32 devices in a mesh: row: 8 (over z, y), col: 4 (over x, core).
Axes of the slice: x: 2, y: 2, z: 4, core: 2. Of those that a mesh axis runs over, the one named last changes fastest.
Arguments:
- frames: bfloat16 [2, 16, 128, 1280], P(None, 'row', 'col'), may hold values from -6 to 6
- targets: bfloat16 [2, 2, 16, 128, 1280], P(None, None, 'row', 'col'), may hold values from -6 to 6
- regions: int32 [2, 4], replicated, may hold values from 0 to 128, as said below
- master: float32 [12017664], P(('row', 'col')), as said below
- first_moment: float32 [12017664], P(('row', 'col')), may hold values from -9.1552734e-05 to 9.1552734e-05
- second_moment: float32 [12017664], P(('row', 'col')), may hold values from 8.737883e-11 to 1.4147049e-09
Outputs:
- master_out: float32 [12017664], P(('row', 'col'))
- first_out: float32 [12017664], P(('row', 'col'))
- second_out: float32 [12017664], P(('row', 'col'))
- weights_out: bfloat16 [12017664], P(('row', 'col'))
- loss_sum: float32 [], replicated
- loss_weight: float32 [], replicated
- grad_norm: float32 [], replicated
The draws below stay inside these ranges and needn't reach their ends.
Inputs may be any that keep to these rules, and one draw needn't show every extreme that they name: `regions`: rows stay within the grid; a row count is 8 or more, a column count 128 // 2 or more; one micro-batch covers the whole grid. `master`: entries from 12016640 on are padding.
All inputs are finite; a program needn't handle non-finite values.
Results may differ from the reference program's by a relative error of at most 0.03.
Values may be sent and summed in bfloat16 or wider, within the bound.
A program may use at most 320 MiB of HBM per device.

```python
import math
import jax
import jax.numpy as jnp
from jax import lax

D = 768
FF = 3072
NBLK = 8
BS = 96
PIN = 1280
LAYERS = 2
STEPS = 2
MB = 2
ADAM_STEP = 5
H = 16
W = 128
NPAR = 12016640
NPAD = 12017664


def draw_regions(key, part):
    key = jax.random.fold_in(key, 7)
    keys = jax.random.split(key, 5)
    row_start = jax.random.randint(keys[0], (MB,), 0, H // 8 + 1)
    row_span = jax.random.randint(keys[1], (MB,), H // 2, H + 1)
    row_span = jnp.minimum(row_span, H - row_start)
    col_start = jax.random.randint(keys[2], (MB,), 0, W)
    col_span = jax.random.randint(keys[3], (MB,), W // 2, W + 1)
    chosen = jax.random.randint(keys[4], (), 0, MB)
    whole = jnp.arange(MB) == chosen
    row_start = jnp.where(whole, 0, row_start)
    row_span = jnp.where(whole, H, row_span)
    col_span = jnp.where(whole, W, col_span)
    return jnp.stack([row_start, row_span, col_start, col_span], axis=1).astype(jnp.int32)


def draw_master(key, part):
    key = jax.random.fold_in(key, 11)
    layer_parts = [(D, 0.1, 1.0), (D, 0.1, 0.0), (2 * NBLK * BS * BS, BS ** (-0.5), 0.0), (2 * NBLK * BS, 0.1, 0.0), (2 * NBLK * BS * BS, BS ** (-0.5), 0.0), (2 * NBLK * BS, 0.1, 0.0), (D, 0.1, 1.0), (D, 0.1, 0.0), (D * FF, D ** (-0.5), 0.0), (FF, 0.1, 0.0), (FF * D, FF ** (-0.5), 0.0), (D, 0.1, 0.0)]
    segments = [(PIN * D, PIN ** (-0.5), 0.0), (D, 0.1, 0.0)] + layer_parts * LAYERS
    segments = segments + [(D, 0.1, 1.0), (D, 0.1, 0.0), (D * PIN, D ** (-0.5), 0.0), (PIN, 0.1, 0.0), (NPAD - NPAR, 0.02, 0.0)]
    scales = jnp.concatenate([jnp.full((length,), scale, jnp.float32) for length, scale, center in segments])
    centers = jnp.concatenate([jnp.full((length,), center, jnp.float32) for length, scale, center in segments])
    return jax.random.normal(key, (NPAD,), jnp.float32) * scales + centers


def block_levels(own_key, extent, shards, low, top_value):
    gain = 1.0
    for dim, parts in shards:
        steps = jax.random.uniform(jax.random.fold_in(jax.random.fold_in(own_key, 6), dim), (parts,), jnp.float32, low / len(shards), top_value / len(shards))
        gain = gain * jnp.repeat(jnp.exp(steps), extent[dim] // parts).reshape((-1,) + (1,) * (len(extent) - 1 - dim))
    return gain


def scatter_about(rng, extent, scale, limit, cuts=(), kind=jnp.bfloat16):
    gain = block_levels(rng, extent, cuts, -0.22, 0.18) if cuts else 1.0
    values = jax.random.normal(rng, extent, jnp.float32) * scale * gain
    return jnp.minimum(jnp.maximum(values, -limit), limit).astype(kind)


def setup_inputs(seed: int = 0) -> dict:
    seeds = jax.random.split(jax.random.key(seed), 7)
    return {
        "frames": scatter_about(seeds[0], (MB, H, W, PIN), 1.0, 6.0, ((1, 8), (2, 4))),
        "targets": scatter_about(seeds[1], (MB, STEPS, H, W, PIN), 1.0, 6.0, ((2, 8), (3, 4))),
        "regions": draw_regions(jax.random.fold_in(seeds[6], 71), 0),
        "master": draw_master(jax.random.fold_in(seeds[6], 71), 0),
        "first_moment": scatter_about(seeds[4], (NPAD,), (0.022 / NPAR ** 0.5), 9.1552734375e-05, ((0, 32),), jnp.float32),
        "second_moment": jnp.clip(jnp.exp(math.log(1.4147049087753771e-09) - 2.784423 * jax.random.uniform(seeds[5], (NPAD,), jnp.float32) ** block_levels(seeds[5], (NPAD,), ((0, 32),), -0.2, 0.2)), 8.737883333553853e-11, 1.4147049087753771e-09),
    }


highest = lax.Precision.HIGHEST
NORM_EPS = 1e-05
BETA_ONE = 0.9
BETA_TWO = 0.95
ADAM_EPS = 1e-08
RATE = 0.03
DECAY = 0.05
CLIP = 0.2

@jax.custom_vjp
def low(v):
    return lax.optimization_barrier(v.astype(jnp.bfloat16)).astype(jnp.float32)

@jax.custom_vjp
def low_back(v):
    return v

def low_keep(v):
    return (low(v), None)

def low_pass(kept, grad):
    return (grad,)

def back_keep(v):
    return (v, None)

def back_low(kept, grad):
    return (low(grad),)
low.defvjp(low_keep, low_pass)
low_back.defvjp(back_keep, back_low)

def both_low(value):
    return low_back(low(value))

def block_shapes():
    return [(D,), (D,), (2, NBLK, BS, BS), (2, NBLK, BS), (2, NBLK, BS, BS), (2, NBLK, BS), (D,), (D,), (D, FF), (FF,), (FF, D), (D,)]

def all_shapes():
    return [(PIN, D), (D,)] + block_shapes() * LAYERS + [(D,), (D,), (D, PIN), (PIN,)]

def unpack(flat_vec):
    pieces = []
    offset = 0
    for layout in all_shapes():
        length = math.prod(layout)
        pieces.append(flat_vec[offset:offset + length].reshape(layout))
        offset += length
    return pieces

def layer_norm(values, gain_vec, shift_vec):
    center = values - lax.optimization_barrier(jnp.mean(values, axis=-1, keepdims=True))
    spread = lax.optimization_barrier(jnp.mean(center * center, axis=-1, keepdims=True))
    return center * lax.rsqrt(spread + NORM_EPS) * gain_vec + shift_vec

def dft_tables(length, direction):
    positions = jnp.arange(length, dtype=jnp.int32)
    phases = (positions[:, None] * positions[None, :] % length).astype(jnp.float32) * (2.0 * math.pi / length)
    factor = 1.0 / math.sqrt(length)
    return (jnp.cos(phases) * factor, direction * jnp.sin(phases) * factor)

def along(tables, real_part, imag_part, form):

    def contract(table, values):
        return jnp.einsum(form, table, values, precision=highest)
    return (contract(tables[0], real_part) - contract(tables[1], imag_part), contract(tables[1], real_part) + contract(tables[0], imag_part))

def spectral(real_part, imag_part, weight, bias_vec):
    blocks = (weight.shape[1], weight.shape[2])
    block_re = real_part.reshape(real_part.shape[:-1] + blocks)
    block_im = imag_part.reshape(imag_part.shape[:-1] + blocks)
    form = '...kb,kbc->...kc'
    out_re = jnp.einsum(form, block_re, weight[0], precision=highest) - jnp.einsum(form, block_im, weight[1], precision=highest) + bias_vec[0]
    out_im = jnp.einsum(form, block_im, weight[0], precision=highest) + jnp.einsum(form, block_re, weight[1], precision=highest) + bias_vec[1]
    return (out_re.reshape(real_part.shape), out_im.reshape(imag_part.shape))

def region_masks(regions, row_ids, col_ids, width):
    row_start = regions[:, 0, None, None]
    row_span = regions[:, 1, None, None]
    col_start = regions[:, 2, None, None]
    col_span = regions[:, 3, None, None]
    row_inside = (row_ids[None, :, None] >= row_start) & (row_ids[None, :, None] < row_start + row_span)
    col_inside = (col_ids[None, None, :] - col_start) % width < col_span
    return (row_inside & col_inside).astype(jnp.float32)

def latitude(row_ids, height):
    return jnp.cos(-1.3 + 1.3 * (row_ids.astype(jnp.float32) + 0.5) / height)

def layer(stream, params, forward_w, forward_h, inverse_w, inverse_h):
    gain_one, shift_one, spec_w1, spec_b1, spec_w2, spec_b2, gain_two, shift_two, weight_in, bias_in, weight_out, bias_out = params
    normed = both_low(layer_norm(stream, gain_one, shift_one))
    wave_re, wave_im = along(forward_w, normed, jnp.zeros_like(normed), 'kw,hwc->hkc')
    wave_re, wave_im = (both_low(wave_re), both_low(wave_im))
    wave_re, wave_im = along(forward_h, wave_re, wave_im, 'kh,hwc->kwc')
    wave_re, wave_im = (both_low(wave_re), both_low(wave_im))
    hid_re, hid_im = spectral(wave_re, wave_im, spec_w1, spec_b1)
    hid_re = both_low(jax.nn.gelu(hid_re, approximate=False))
    hid_im = both_low(jax.nn.gelu(hid_im, approximate=False))
    spec_re, spec_im = spectral(hid_re, hid_im, spec_w2, spec_b2)
    spec_re, spec_im = (both_low(spec_re), both_low(spec_im))
    back_re, back_im = along(inverse_h, spec_re, spec_im, 'kh,hwc->kwc')
    back_re, back_im = (both_low(back_re), both_low(back_im))
    filtered, _ = along(inverse_w, back_re, back_im, 'kw,hwc->hkc')
    mixed = stream + both_low(filtered)
    normed_two = both_low(layer_norm(mixed, gain_two, shift_two))
    hidden = both_low(jax.nn.gelu(jnp.einsum('hwd,df->hwf', normed_two, weight_in, precision=highest) + bias_in, approximate=False))
    return mixed + jnp.einsum('hwf,fd->hwd', hidden, weight_out, precision=highest) + bias_out

def objective(master, frame_one, target, mask_grid, lat_weight, total_weight):
    pieces = unpack(low(master))
    tables = (dft_tables(W, -1.0), dft_tables(H, -1.0), dft_tables(W, 1.0), dft_tables(H, 1.0))
    layer_fn = jax.checkpoint(layer)
    inputs = frame_one * mask_grid[:, :, None]
    loss_sum = jnp.zeros((), jnp.float32)
    tail_params = pieces[2 + 12 * LAYERS:]
    for roll_step in range(STEPS):
        stream = jnp.einsum('hwp,pd->hwd', inputs, pieces[0], precision=highest) + pieces[1]
        for layer_idx in range(LAYERS):
            stream = layer_fn(stream, pieces[2 + 12 * layer_idx:14 + 12 * layer_idx], *tables)
        normed = both_low(layer_norm(stream, tail_params[0], tail_params[1]))
        predicted = jnp.einsum('hwd,dp->hwp', normed, tail_params[2], precision=highest) + tail_params[3]
        errors = predicted - target[roll_step]
        loss_sum = loss_sum + jnp.sum(lat_weight[:, None] * mask_grid * lax.optimization_barrier(jnp.sum(errors * errors, axis=-1)))
        inputs = both_low(predicted * mask_grid[:, :, None])
    return (loss_sum / total_weight, loss_sum)

def reference(frames, targets, regions, master, first_moment, second_moment):
    row_ids = jnp.arange(H, dtype=jnp.int32)
    col_ids = jnp.arange(W, dtype=jnp.int32)
    cell_masks = region_masks(regions, row_ids, col_ids, W)
    lat_weight = latitude(row_ids, H)
    total_weight = jnp.sum(lat_weight[None, :, None] * cell_masks) * STEPS

    def accumulate(running, items):
        frame_one, target, mask_grid = items

        def wrapped(params):
            return objective(params, frame_one, target, mask_grid, lat_weight, total_weight)
        _, pullback, loss_part = jax.vjp(wrapped, master, has_aux=True)
        gradient, = pullback(jnp.ones((), jnp.float32))
        return ((running[0] + gradient, running[1] + loss_part), None)
    start = (jnp.zeros_like(master), jnp.zeros((), jnp.float32))
    (gradients, loss_sum), _ = lax.scan(accumulate, start, (frames.astype(jnp.float32), targets.astype(jnp.float32), cell_masks))
    grad_norm = jnp.sqrt(jnp.sum(gradients * gradients))
    clipped = gradients * (CLIP / jnp.maximum(grad_norm, CLIP))
    first_out = BETA_ONE * first_moment + (1.0 - BETA_ONE) * clipped
    second_out = BETA_TWO * second_moment + (1.0 - BETA_TWO) * clipped * clipped
    corrected_one = first_out / (1.0 - BETA_ONE ** ADAM_STEP)
    corrected_two = second_out / (1.0 - BETA_TWO ** ADAM_STEP)
    master_out = master - RATE * (corrected_one / (jnp.sqrt(corrected_two) + ADAM_EPS) + DECAY * master)
    return (master_out, first_out, second_out, master_out.astype(jnp.bfloat16), loss_sum, total_weight, grad_norm)
```

```python
import functools
import math

import jax
import jax.numpy as jnp
import numpy as np
from jax import lax
from jax.sharding import PartitionSpec as P
from jax.experimental import pallas as pl
from jax.experimental.pallas import tpu as pltpu

D = 768
FF = 3072
NBLK = 8
BS = 96
PIN = 1280
LAYERS = 2
STEPS = 2
ADAM_STEP = 5


highest = lax.Precision.HIGHEST
NORM_EPS = 1e-05
BETA_ONE = 0.9
BETA_TWO = 0.95
ADAM_EPS = 1e-08
RATE = 0.03
DECAY = 0.05
CLIP = 0.2
LANES = 128


def block_shapes():
    return [
        (D,),
        (D,),
        (2, NBLK, BS, BS),
        (2, NBLK, BS),
        (2, NBLK, BS, BS),
        (2, NBLK, BS),
        (D,),
        (D,),
        (D, FF),
        (FF,),
        (FF, D),
        (D,),
    ]


def all_shapes():
    return [(PIN, D), (D,)] + block_shapes() * LAYERS + [(D,), (D,), (D, PIN), (PIN,)]


def unpack(flat_vec):
    pieces = []
    offset = 0
    for layout in all_shapes():
        length = math.prod(layout)
        pieces.append(flat_vec[offset : offset + length].reshape(layout))
        offset += length
    return pieces


def rounded(value):
    return lax.optimization_barrier(value.astype(jnp.bfloat16)).astype(jnp.float32)


def mult(form, left, right):
    return jnp.einsum(
        form,
        left.astype(jnp.bfloat16),
        right.astype(jnp.bfloat16),
        preferred_element_type=jnp.float32,
    )


def mult_exact(form, grad_value, other):
    upper = grad_value.astype(jnp.bfloat16)
    lower = (grad_value - upper.astype(jnp.float32)).astype(jnp.bfloat16)
    return mult(form, upper, other) + mult(form, lower, other)


def layer_norm(values, gain_vec, shift_vec):
    center = values - jnp.mean(values, axis=-1, keepdims=True)
    spread = jnp.mean(center * center, axis=-1, keepdims=True)
    return center * lax.rsqrt(spread + NORM_EPS) * gain_vec + shift_vec


def dft_tables(length, direction):
    positions = jnp.arange(length, dtype=jnp.int32)
    phases = (positions[:, None] * positions[None, :] % length).astype(jnp.float32) * (
        2.0 * math.pi / length
    )
    factor = 1.0 / math.sqrt(length)
    return (jnp.cos(phases) * factor, direction * jnp.sin(phases) * factor)


def apply_pair(tables, real_part, imag_part, form):

    def contract(table, values):
        return jnp.einsum(form, table, values, precision=highest)

    return (
        contract(tables[0], real_part) - contract(tables[1], imag_part),
        contract(tables[1], real_part) + contract(tables[0], imag_part),
    )


def spectral(real_part, imag_part, weight, bias_vec):
    blocks = (weight.shape[1], weight.shape[2])
    block_re = real_part.reshape(real_part.shape[:-1] + blocks)
    block_im = imag_part.reshape(imag_part.shape[:-1] + blocks)
    form = "...kb,kbc->...kc"
    out_re = (
        jnp.einsum(form, block_re, weight[0], precision=highest)
        - jnp.einsum(form, block_im, weight[1], precision=highest)
        + bias_vec[0]
    )
    out_im = (
        jnp.einsum(form, block_im, weight[0], precision=highest)
        + jnp.einsum(form, block_re, weight[1], precision=highest)
        + bias_vec[1]
    )
    return (out_re.reshape(real_part.shape), out_im.reshape(imag_part.shape))


def first_spectral(real_part, imag_part, weight, bias_vec):
    out_re, out_im = spectral(real_part, imag_part, weight, bias_vec)
    return (jax.nn.gelu(out_re, approximate=False), jax.nn.gelu(out_im, approximate=False))


def region_masks(regions, row_ids, col_ids, width):
    row_start = regions[:, 0, None, None]
    row_span = regions[:, 1, None, None]
    col_start = regions[:, 2, None, None]
    col_span = regions[:, 3, None, None]
    row_inside = (row_ids[None, :, None] >= row_start) & (
        row_ids[None, :, None] < row_start + row_span
    )
    col_inside = (col_ids[None, None, :] - col_start) % width < col_span
    return (row_inside & col_inside).astype(jnp.float32)


def latitude(row_ids, height):
    return jnp.cos(-1.3 + 1.3 * (row_ids.astype(jnp.float32) + 0.5) / height)


def linear_forward(values, weight16, bias_vec):
    return mult("brci,io->brco", values, weight16) + bias_vec


def linear_backward(grad_value, values, weight16):
    grad_values = mult_exact("brco,io->brci", grad_value, weight16)
    grad_weight = mult_exact("brco,brci->io", grad_value, values)
    return (grad_values, grad_weight, jnp.sum(grad_value, axis=(0, 1, 2)))


def spectrum(field, forward_w, forward_h):
    values = lax.all_to_all(field, "col", split_axis=3, concat_axis=2, tiled=True).astype(
        jnp.float32
    )
    real_part = jnp.einsum("kw,bnwc->bnkc", forward_w[0], values, precision=highest)
    imag_part = jnp.einsum("kw,bnwc->bnkc", forward_w[1], values, precision=highest)
    real_part, imag_part = apply_pair(
        forward_h,
        lax.all_to_all(
            real_part.astype(jnp.bfloat16), "row", split_axis=2, concat_axis=1, tiled=True
        ).astype(jnp.float32),
        lax.all_to_all(
            imag_part.astype(jnp.bfloat16), "row", split_axis=2, concat_axis=1, tiled=True
        ).astype(jnp.float32),
        "kh,bhwc->bkwc",
    )
    return (real_part.astype(jnp.bfloat16), imag_part.astype(jnp.bfloat16))


def grid(real_part, imag_part, inverse_w, inverse_h):
    back_re, back_im = apply_pair(
        inverse_h, real_part.astype(jnp.float32), imag_part.astype(jnp.float32), "kh,bhwc->bkwc"
    )
    values_re = lax.all_to_all(
        back_re.astype(jnp.bfloat16), "row", split_axis=1, concat_axis=2, tiled=True
    ).astype(jnp.float32)
    values_im = lax.all_to_all(
        back_im.astype(jnp.bfloat16), "row", split_axis=1, concat_axis=2, tiled=True
    ).astype(jnp.float32)
    result = jnp.einsum("kw,bnwc->bnkc", inverse_w[0], values_re, precision=highest) - jnp.einsum(
        "kw,bnwc->bnkc", inverse_w[1], values_im, precision=highest
    )
    columns_back = result.astype(jnp.bfloat16)
    return lax.all_to_all(columns_back, "col", split_axis=2, concat_axis=3, tiled=True)


def local_blocks(params):
    block_count = D // lax.axis_size("col") // BS
    first_block = lax.axis_index("col") * block_count
    chosen = [
        lax.dynamic_slice_in_dim(params[index_pos], first_block, block_count, 1)
        for index_pos in (2, 3, 4, 5)
    ]
    return (chosen, first_block)


def layer_forward(stream, params, params16, tables):
    gain_one, shift_one, _, _, _, _, gain_two, shift_two, _, bias_in, _, bias_out = params
    (local_w1, local_b1, local_w2, local_b2), _ = local_blocks(params)
    normed = layer_norm(stream, gain_one, shift_one).astype(jnp.bfloat16)
    wave_re, wave_im = spectrum(normed, tables[0], tables[1])
    hid_re, hid_im = first_spectral(
        wave_re.astype(jnp.float32), wave_im.astype(jnp.float32), local_w1, local_b1
    )
    hid_re, hid_im = (rounded(hid_re), rounded(hid_im))
    spec_re, spec_im = spectral(hid_re, hid_im, local_w2, local_b2)
    filtered = grid(
        spec_re.astype(jnp.bfloat16), spec_im.astype(jnp.bfloat16), tables[2], tables[3]
    )
    mixed = stream + filtered.astype(jnp.float32)
    normed_two = rounded(layer_norm(mixed, gain_two, shift_two))
    hidden = rounded(
        jax.nn.gelu(linear_forward(normed_two, params16[8], bias_in), approximate=False)
    )
    output = mixed + linear_forward(hidden, params16[10], bias_out)
    return (output, (stream, wave_re, wave_im, hid_re, hid_im, mixed, normed_two, hidden))


def place_blocks(local_grad, full_like, first_block):
    return lax.dynamic_update_slice_in_dim(jnp.zeros_like(full_like), local_grad, first_block, 1)


def layer_backward(grad_out, saved, params, params16, tables):
    stream, wave_re, wave_im, hid_re, hid_im, mixed, normed_two, hidden = saved
    (
        gain_one,
        shift_one,
        spec_w1,
        spec_b1,
        spec_w2,
        spec_b2,
        gain_two,
        shift_two,
        weight_in,
        bias_in,
        weight_out,
        bias_out,
    ) = params
    (local_w1, local_b1, local_w2, local_b2), first_block = local_blocks(params)
    grad_hidden, grad_wout, grad_bout = linear_backward(grad_out, hidden, params16[10])
    grad_mixed = grad_out
    before = linear_forward(normed_two, params16[8], bias_in)
    _, pullback = jax.vjp(lambda value: jax.nn.gelu(value, approximate=False), before)
    (grad_before,) = pullback(rounded(grad_hidden))
    grad_normed, grad_win, grad_bin = linear_backward(grad_before, normed_two, params16[8])
    _, pullback = jax.vjp(layer_norm, mixed, gain_two, shift_two)
    grad_extra, grad_gain2, grad_shift2 = pullback(rounded(grad_normed))
    grad_mixed = grad_mixed + grad_extra
    back_re, back_im = spectrum(grad_mixed.astype(jnp.bfloat16), tables[0], tables[1])
    _, pullback = jax.vjp(spectral, hid_re, hid_im, local_w2, local_b2)
    grad_hre, grad_him, grad_lw2, grad_lb2 = pullback(
        (back_re.astype(jnp.float32), back_im.astype(jnp.float32))
    )
    _, pullback = jax.vjp(
        first_spectral, wave_re.astype(jnp.float32), wave_im.astype(jnp.float32), local_w1, local_b1
    )
    grad_wre, grad_wim, grad_lw1, grad_lb1 = pullback((rounded(grad_hre), rounded(grad_him)))
    grad_first = grid(
        grad_wre.astype(jnp.bfloat16), grad_wim.astype(jnp.bfloat16), tables[2], tables[3]
    )
    _, pullback = jax.vjp(layer_norm, stream, gain_one, shift_one)
    grad_stream, grad_gain1, grad_shift1 = pullback(grad_first.astype(jnp.float32))
    layer_grads = [
        grad_gain1,
        grad_shift1,
        place_blocks(grad_lw1, spec_w1, first_block),
        place_blocks(grad_lb1, spec_b1, first_block),
        place_blocks(grad_lw2, spec_w2, first_block),
        place_blocks(grad_lb2, spec_b2, first_block),
        grad_gain2,
        grad_shift2,
        grad_win,
        grad_bin,
        grad_wout,
        grad_bout,
    ]
    return (grad_stream + grad_mixed, layer_grads)


def add_into(gradients, start, values):
    middle = [left + right for left, right in zip(gradients[start : start + len(values)], values)]
    return gradients[:start] + middle + gradients[start + len(values) :]


MESH = pl.DeviceIdType.MESH
CH = 2944
OWN = 2934
CHR = 2960
GROWS = 93904


CHIPS = 16
UNIT = 64
PADC = 128
f32 = jnp.float32
bf16 = jnp.bfloat16


def remote(src, dst, send_sem, recv_sem, device):
    return pltpu.make_async_remote_copy(
        src_ref=src,
        dst_ref=dst,
        send_sem=send_sem,
        recv_sem=recv_sem,
        device_id=device,
        device_id_type=MESH,
    )


def chip_device(chip, core):
    return chip // 2, (chip % 2) * 2 + core


def place():
    row = lax.axis_index("row")
    col = lax.axis_index("col")
    core = col % 2
    return row, row * 2 + col // 2, core, (row, col + 1 - 2 * core)


def greet_chips(me, core, sibling):
    barrier = pltpu.get_barrier_semaphore()

    def one(k, carry):
        pl.semaphore_signal(
            barrier,
            inc=1,
            device_id=chip_device(lax.rem(me + k, CHIPS), core),
            device_id_type=MESH,
        )
        return carry

    lax.fori_loop(1, CHIPS, one, 0)
    pl.semaphore_signal(barrier, inc=1, device_id=sibling, device_id_type=MESH)
    return barrier


def split_units(values, units):
    blank = jnp.zeros((UNIT, PADC - BS), f32)
    for part in range(2):
        for block in range(NBLK):
            piece = values[part * UNIT : (part + 1) * UNIT, block * BS : (block + 1) * BS]
            units[part * NBLK + block] = jnp.concatenate([piece, blank], axis=1).astype(bf16)


def join_units(units, joined):
    for part in range(2):
        for block in range(NBLK):
            joined[part * UNIT : (part + 1) * UNIT, block * BS : (block + 1) * BS] = units[
                part * NBLK + block, :, 0:BS
            ].astype(f32)


def normalize(values):
    center = values - jnp.mean(values, axis=-1, keepdims=True)
    spread = jnp.mean(center * center, axis=-1, keepdims=True)
    scale = lax.rsqrt(spread + NORM_EPS)
    return center * scale, scale


def gelu_of(value):
    return 0.5 * value * (1.0 + lax.erf(value * math.sqrt(0.5)))


def gelu_slope(value):
    bell = jnp.exp(-0.5 * value * value) * (1.0 / math.sqrt(2.0 * math.pi))
    return 0.5 * (1.0 + lax.erf(value * math.sqrt(0.5))) + value * bell


def dot(left, right):
    return jnp.dot(left, right, preferred_element_type=f32)


def dot_rows(left, right):
    return lax.dot_general(left, right, (((0,), (0,)), ((), ())), preferred_element_type=f32)


def dot_cols(left, right):
    return lax.dot_general(left, right, (((1,), (1,)), ((), ())), preferred_element_type=f32)


def spread_units(me, core, sibling, units, mine, others, sems):
    send_a, recv_a, send_f, recv_f, local_sem = sems

    def out(k):
        chip = lax.rem(me + k, CHIPS)
        return remote(
            units.at[chip], mine.at[me], send_a.at[k], recv_a.at[k], chip_device(chip, core)
        )

    def handed(k):
        chip = lax.rem(me + CHIPS - k, CHIPS)
        return remote(mine.at[chip], others.at[chip], send_f.at[k], recv_f.at[k], sibling)

    own = pltpu.make_async_copy(units.at[me], mine.at[me], local_sem)
    own.start()

    def begin(k, carry):
        out(k).start()
        return carry

    lax.fori_loop(1, CHIPS, begin, 0)
    own.wait()
    handed(0).start()

    def hand(k, carry):
        out(k).wait_recv()
        handed(k).start()
        return carry

    lax.fori_loop(1, CHIPS, hand, 0)

    def arrive(k, carry):
        handed(k).wait_recv()
        return carry

    lax.fori_loop(0, CHIPS, arrive, 0)

    def finish():
        def sent(k, carry):
            out(k).wait_send()
            return carry

        lax.fori_loop(1, CHIPS, sent, 0)

        def sent_on(k, carry):
            handed(k).wait_send()
            return carry

        lax.fori_loop(0, CHIPS, sent_on, 0)

    return finish


def to_spectrum(mine, others, column_table, row_table, waves):
    for h in range(16):
        pair, part = h // 2, pl.ds(32 * (h % 2), 32)
        cells = jnp.concatenate(
            [
                mine[2 * pair, part],
                mine[2 * pair + 1, part],
                others[2 * pair, part],
                others[2 * pair + 1, part],
            ],
            axis=0,
        )
        wave = dot(column_table[...], cells).astype(bf16)
        for g in range(4):
            rows = pl.ds(16 * h, 16)
            waves[g, rows, 0:PADC] = wave[16 * g : 16 * g + 16]
            waves[g, rows, PADC : 2 * PADC] = wave[64 + 16 * g : 80 + 16 * g]
    results = []
    for g in range(4):
        both = dot(row_table[...], waves[g])
        real = both[:256, :PADC] + both[256:, PADC:]
        imag = both[:256, PADC:] - both[256:, :PADC]
        results.append(jnp.concatenate([real, imag], axis=1).astype(bf16))
    return results


def from_spectrum(g, spec, row_table, back):
    both = dot(row_table[...], spec)
    real = (both[:256, :PADC] - both[256:, PADC:]).astype(bf16)
    imag = (both[:256, PADC:] + both[256:, :PADC]).astype(bf16)
    for h in range(16):
        back[h, 16 * g : 16 * g + 16] = real[16 * h : 16 * h + 16]
        back[h, 64 + 16 * g : 80 + 16 * g] = imag[16 * h : 16 * h + 16]


def gather_units(row, me, core, sibling, back, inverse_table, bufs, sems):
    own_sum, to_sib, from_sib, ready, landed = bufs
    send_s, recv_s, send_b, recv_b, local_sem = sems

    def swap(pair):
        rows = pl.ds(2 * pair, 2)
        return remote(
            to_sib.at[rows], from_sib.at[rows], send_s.at[pair], recv_s.at[pair], sibling
        )

    def partial(j, carry):
        pair = lax.rem(row + 1 + j, 8)
        for half in range(2):
            sums = dot(inverse_table[...], back[2 * pair + half])
            part = pl.ds(32 * half, 32)
            for x in range(2):
                own_sum[2 * pair + x, part] = sums[32 * x : 32 * x + 32]
                to_sib[2 * pair + x, part] = sums[64 + 32 * x : 96 + 32 * x].astype(bf16)
        swap(pair).start()
        return carry

    lax.fori_loop(0, 8, partial, 0)

    def home(chip, k):
        return remote(
            ready.at[chip], landed.at[me], send_b.at[k], recv_b.at[k], chip_device(chip, core)
        )

    own = pltpu.make_async_copy(ready.at[me], landed.at[me], local_sem)

    def total(j, carry):
        pair = lax.rem(row + 1 + j, 8)
        swap(pair).wait_recv()
        rows = pl.ds(2 * pair, 2)
        ready[rows] = (own_sum[rows] + from_sib[rows].astype(f32)).astype(bf16)
        for x in range(2):
            chip = 2 * pair + x
            k = lax.rem(chip - me + CHIPS, CHIPS)

            @pl.when(k != 0)
            def _():
                home(chip, k).start()

        return carry

    lax.fori_loop(0, 8, total, 0)
    own.start()

    def landed_all(k, carry):
        home(lax.rem(me + k, CHIPS), k).wait_recv()
        return carry

    lax.fori_loop(1, CHIPS, landed_all, 0)
    own.wait()

    def finish():
        def sent(k, carry):
            home(lax.rem(me + k, CHIPS), k).wait_send()
            return carry

        lax.fori_loop(1, CHIPS, sent, 0)

        def swapped(pair, carry):
            swap(pair).wait_send()
            return carry

        lax.fori_loop(0, 8, swapped, 0)

    return finish


def filter_forward_kernel(
    stream,
    gain,
    shift,
    column_table,
    inverse_table,
    row_table,
    w1,
    b1,
    w2,
    b2,
    mixed,
    saved,
    units,
    mine,
    others,
    waves,
    back,
    own_sum,
    to_sib,
    from_sib,
    ready,
    landed,
    joined,
    *sems,
):
    row, me, core, sibling = place()
    barrier = greet_chips(me, core, sibling)
    normed, _ = normalize(stream[...])
    split_units(normed * gain[...] + shift[...], units)
    pl.semaphore_wait(barrier, CHIPS)
    finish_one = spread_units(me, core, sibling, units, mine, others, sems[:5])
    groups = to_spectrum(mine, others, column_table, row_table, waves)
    for g in range(4):
        saved[g] = groups[g]
        hidden = gelu_of(dot(groups[g], w1[...]) + b1[...]).astype(bf16)
        spec = (dot(hidden, w2[...]) + b2[...]).astype(bf16)
        from_spectrum(g, spec, row_table, back)
    finish_two = gather_units(
        row, me, core, sibling, back, inverse_table,
        (own_sum, to_sib, from_sib, ready, landed), sems[5:],
    )
    join_units(landed, joined)
    mixed[...] = stream[...] + joined[...]
    finish_one()
    finish_two()


def filter_backward_kernel(
    grad,
    stream,
    gain,
    saved,
    column_table,
    inverse_table,
    row_table,
    w1,
    b1,
    w2,
    grad_out,
    grad_norm,
    grad_w1,
    grad_w2,
    grad_b,
    units,
    mine,
    others,
    waves,
    back,
    own_sum,
    to_sib,
    from_sib,
    ready,
    landed,
    joined,
    *sems,
):
    row, me, core, sibling = place()
    barrier = greet_chips(me, core, sibling)
    split_units(grad[...], units)
    pl.semaphore_wait(barrier, CHIPS)
    finish_one = spread_units(me, core, sibling, units, mine, others, sems[:5])
    groups = to_spectrum(mine, others, column_table, row_table, waves)
    grad_w1[...] = jnp.zeros_like(grad_w1)
    grad_w2[...] = jnp.zeros_like(grad_w2)
    grad_b[...] = jnp.zeros_like(grad_b)
    for g in range(4):
        before = dot(saved[g], w1[...]) + b1[...]
        hidden = gelu_of(before).astype(bf16)
        grad_hidden = dot_cols(groups[g], w2[...]).astype(bf16).astype(f32)
        grad_before = grad_hidden * gelu_slope(before)
        grad_before16 = grad_before.astype(bf16)
        grad_w2[...] += dot_rows(hidden, groups[g])
        grad_w1[...] += dot_rows(saved[g], grad_before16)
        grad_b[0:1] += jnp.sum(grad_before, axis=0, keepdims=True)
        grad_b[1:2] += jnp.sum(groups[g].astype(f32), axis=0, keepdims=True)
        from_spectrum(g, dot_cols(grad_before16, w1[...]).astype(bf16), row_table, back)
    finish_two = gather_units(
        row, me, core, sibling, back, inverse_table,
        (own_sum, to_sib, from_sib, ready, landed), sems[5:],
    )
    join_units(landed, joined)
    values = joined[...]
    normed, scale = normalize(stream[...])
    grad_norm[0:1] = jnp.sum(values * normed, axis=0, keepdims=True)
    grad_norm[1:2] = jnp.sum(values, axis=0, keepdims=True)
    grad_norm[2:8] = jnp.zeros((6, D), f32)
    inner = values * gain[...]
    along = jnp.mean(inner * normed, axis=-1, keepdims=True)
    flat = jnp.mean(inner, axis=-1, keepdims=True)
    grad_out[...] = grad[...] + scale * (inner - flat - normed * along)
    finish_one()
    finish_two()


def filter_scratch():
    vm = pltpu.VMEM
    dma = pltpu.SemaphoreType.DMA
    block = (CHIPS, UNIT, PADC)
    return [
        vm(block, bf16),
        vm(block, bf16),
        vm(block, bf16),
        vm((4, 256, 256), bf16),
        vm((16, 128, PADC), bf16),
        vm(block, f32),
        vm(block, bf16),
        vm(block, bf16),
        vm(block, bf16),
        vm(block, bf16),
        vm((2 * UNIT, D), f32),
        dma((CHIPS,)),
        dma((CHIPS,)),
        dma((CHIPS,)),
        dma((CHIPS,)),
        dma,
        dma((8,)),
        dma((8,)),
        dma((CHIPS,)),
        dma((CHIPS,)),
        dma,
    ]


def filter_call(kernel, outs, collective_id, name, *args):
    spec = pl.BlockSpec(memory_space=pltpu.VMEM)
    return pl.pallas_call(
        kernel,
        out_shape=outs,
        in_specs=[spec] * len(args),
        out_specs=[spec] * len(outs),
        scratch_shapes=filter_scratch(),
        compiler_params=pltpu.CompilerParams(
            collective_id=collective_id, has_side_effects=True, vmem_limit_bytes=48 << 20
        ),
        name=name,
    )(*args)


def filter_forward(stream, gain, shift, tables, weights):
    column, inverse, rows = tables
    w1, b1, w2, b2 = weights
    shape = jax.ShapeDtypeStruct
    return filter_call(
        filter_forward_kernel,
        [shape((2 * UNIT, D), f32), shape((4, 256, 256), bf16)],
        2,
        "filter_forward",
        stream, gain, shift, column, inverse, rows, w1, b1, w2, b2,
    )


def filter_backward(grad, stream, gain, saved, tables, weights):
    column, inverse, rows = tables
    w1, b1, w2, _ = weights
    shape = jax.ShapeDtypeStruct
    return filter_call(
        filter_backward_kernel,
        [
            shape((2 * UNIT, D), f32),
            shape((8, D), f32),
            shape((256, 256), f32),
            shape((256, 256), f32),
            shape((8, 256), f32),
        ],
        3,
        "filter_backward",
        grad, stream, gain, saved, column, inverse, rows, w1, b1, w2,
    )


def transform_tables(core):
    width, height = 128, 16
    order = []
    for side in range(2):
        cols = [[32 * (2 * x + (c if side == 0 else 1 - c)) + i for x in range(2) for i in range(32)] for c in range(2)]
        order.append(cols)
    column, inverse = [], []
    for c in range(2):
        cells = np.array(order[0][c] + order[1][c])
        waves = 64 * c + np.arange(64)
        angle = 2.0 * np.pi * (np.outer(waves, cells) % width) / width
        cos, sin = np.cos(angle) / np.sqrt(width), np.sin(angle) / np.sqrt(width)
        column.append(np.concatenate([cos, -sin], axis=0))
        inverse.append(np.concatenate([cos, -sin], axis=0).T)
    steps = np.arange(height)
    angle = 2.0 * np.pi * (np.outer(steps, steps) % height) / height
    eye = np.eye(16)
    rows = np.concatenate(
        [np.kron(np.cos(angle), eye), np.kron(np.sin(angle), eye)], axis=0
    ) / np.sqrt(height)
    pick = lambda both: lax.dynamic_index_in_dim(jnp.asarray(np.stack(both), bf16), core, 0, False)
    return pick(column), pick(inverse), jnp.asarray(rows, bf16)


def spread_weight(re, im):
    def at(block, top, left):
        return jnp.pad(block, ((top, PADC - BS), (left, PADC - BS)))

    pad = lambda m: jnp.pad(m, ((0, PADC - BS), (0, PADC - BS)))
    re, im = pad(re), pad(im)
    return jnp.concatenate(
        [jnp.concatenate([re, im], axis=1), jnp.concatenate([-im, re], axis=1)], axis=0
    )


def spread_bias(bias):
    return jnp.pad(bias, ((0, 0), (0, PADC - BS))).reshape(1, 2 * PADC)


def fold_weight(grad):
    a, b = grad[:BS, :BS], grad[PADC : PADC + BS, PADC : PADC + BS]
    c, d = grad[:BS, PADC : PADC + BS], grad[PADC : PADC + BS, :BS]
    return jnp.stack([a + b, c - d])


def fold_bias(grad):
    return jnp.stack([grad[:BS], grad[PADC : PADC + BS]])


RING = 8
GATHER_CUTS = (0, 640, 1280, 2112, 2944)
SUM_CUTS = (0, 640, 1280, 2128, 2960)


def ring_place(row):
    return jnp.where(row % 2 == 0, row // 2, 7 - row // 2)


def ring_row(spot):
    return jnp.where(spot < 4, 2 * spot, 2 * (7 - spot) + 1)


def gather_kernel(shard, flat, ring_s, ring_r, x_s, x_r, sib_s, sib_r, own_sem):
    row, me, core, sibling = place()
    x = me % 2
    spot = ring_place(row)
    beside = (row, (1 - x) * 2 + core)
    ahead = (ring_row((spot + 1) % RING), x * 2 + core)
    behind = (ring_row((spot + RING - 1) % RING), x * 2 + core)
    ways = (ahead, behind)
    barrier = pltpu.get_barrier_semaphore()
    for device in (ahead, behind, beside, sibling):
        pl.semaphore_signal(barrier, inc=1, device_id=device, device_id_type=MESH)

    def span(part):
        return GATHER_CUTS[part], GATHER_CUTS[part + 1] - GATHER_CUTS[part]

    def piece(source_spot, source_x, part):
        low, size = span(part)
        base = (ring_row(source_spot) * 4 + source_x * 2 + core) * CH
        return flat.at[pl.ds(pl.multiple_of(base + low, 16), size)]

    def mine(part):
        low, size = span(part)
        return shard.at[pl.ds(low, size)]

    def origin(hop, way):
        return (spot - hop + RING) % RING if way == 0 else (spot + hop) % RING

    def item(hop, way, what):
        part = way if what else 2 + way
        return origin(hop, way), (1 - x if what == 2 else x), part

    def ring(hop, way, what, first=False):
        to = piece(*item(hop, way, what))
        source = mine(item(hop, way, what)[2]) if first and what < 2 else to
        return remote(
            source, to, ring_s.at[what, way, hop], ring_r.at[what, way, hop], ways[way]
        )

    def cross(slot, way, first=False):
        if isinstance(slot, int) and slot == 8:
            to, source = piece(spot, x, way), mine(way)
        else:
            to = piece(origin(slot, way), x, 2 + way)
            source = mine(2 + way) if first else to
        return remote(source, to, x_s.at[way, slot], x_r.at[way, slot], beside)

    def share(where, slot, way, what):
        return remote(where, where, sib_s.at[what, way, slot], sib_r.at[what, way, slot], sibling)

    def from_beside(slot, way):
        if isinstance(slot, int) and slot == 8:
            return piece(spot, 1 - x, way)
        return piece(origin(slot, way), 1 - x, 2 + way)

    base = pl.multiple_of((row * 4 + x * 2 + core) * CH, 16)
    whole = flat.at[pl.ds(base, CH)]
    own = pltpu.make_async_copy(shard, whole, own_sem)
    own.start()
    pl.semaphore_wait(barrier, 4)
    for way in range(2):
        ring(0, way, 0, True).start()
        cross(8, way).start()
    for way in range(2):
        ring(0, way, 1, True).start()
        cross(0, way, True).start()
    given = remote(shard, whole, sib_s.at[3, 0, 9], sib_r.at[3, 0, 9], sibling)
    given.start()
    for way in range(2):
        cross(8, way).wait_recv()
        ring(0, way, 2).start()
        share(from_beside(8, way), 8, way, 3).start()

    def step(hop, carry):
        for what in range(3):
            for way in range(2):
                ring(hop - 1, way, what).wait_recv()

                @pl.when(hop < RING - 1)
                def _():
                    ring(hop, way, what).start()

                if what == 0:
                    cross(hop, way).start()
                share(piece(*item(hop, way, what)), hop - 1, way, what).start()
        for way in range(2):
            cross(hop - 1, way).wait_recv()
            share(from_beside(hop - 1, way), hop - 1, way, 3).start()
        return carry

    lax.fori_loop(1, RING, step, 0)
    for way in range(2):
        cross(RING - 1, way).wait_recv()
        share(from_beside(RING - 1, way), RING - 1, way, 3).start()
    own.wait()

    def settle(hop, carry):
        for way in range(2):
            for what in range(3):
                ring(hop, way, what).wait_send()
                share(piece(*item(hop + 1, way, what)), hop, way, what).wait()
        return carry

    lax.fori_loop(0, RING - 1, settle, 0)

    def settle_cross(slot, carry):
        for way in range(2):
            cross(slot, way).wait_send()
            share(from_beside(slot, way), slot, way, 3).wait()
        return carry

    lax.fori_loop(0, RING, settle_cross, 0)
    for way in range(2):
        cross(8, way).wait_send()
        share(from_beside(8, way), 8, way, 3).wait()
    given.wait()


def ag(shard):
    anywhere = pl.BlockSpec(memory_space=pl.ANY)
    dma = pltpu.SemaphoreType.DMA
    return pl.pallas_call(
        gather_kernel,
        out_shape=jax.ShapeDtypeStruct((32 * CH, 128), bf16),
        in_specs=[anywhere],
        out_specs=anywhere,
        scratch_shapes=[
            dma((3, 2, 7)),
            dma((3, 2, 7)),
            dma((2, 9)),
            dma((2, 9)),
            dma((4, 2, 10)),
            dma((4, 2, 10)),
            dma,
        ],
        compiler_params=pltpu.CompilerParams(collective_id=0, has_side_effects=True),
        name="gather_weights",
    )(shard)


def sum_kernel(
    grad, loss, total, stats,
    own, sib, xin, rin_b, rin_a, xlast, st_mine, st_sib, st_sum, st_all,
    own_s, sib_s, sib_r, x_s, x_r, last_s, last_r, ring_s, ring_r, tell_s, tell_r, pair_s, pair_r,
):
    row, me, core, sibling = place()
    x = me % 2
    spot = ring_place(row)
    beside = (row, (1 - x) * 2 + core)
    ahead = (ring_row((spot + 1) % RING), x * 2 + core)
    behind = (ring_row((spot + RING - 1) % RING), x * 2 + core)
    ways = (ahead, behind)
    barrier = greet_chips(me, core, sibling)
    sizes = [SUM_CUTS[k + 1] - SUM_CUTS[k] for k in range(4)]

    def owner(turn, way):
        return (spot - 1 - turn + 2 * RING) % RING if way == 0 else (spot + 1 + turn) % RING

    def source(turn, way, other_x, part, side):
        owner_x = (1 - x) if other_x else x
        base = (ring_row(owner(turn, way)) * 4 + owner_x * 2 + side) * OWN // 16 * 16
        return grad.at[pl.ds(pl.multiple_of(base + SUM_CUTS[part], 16), sizes[part])]

    def part_of(way, what):
        return way if what >= 2 else 2 + way

    def held(buf, turn, way, what):
        part = part_of(way, what)
        return buf.at[what % 2, turn, pl.ds(SUM_CUTS[part], sizes[part])]

    def load(turn, way, what):
        return pltpu.make_async_copy(
            source(turn, way, what % 2, part_of(way, what), core),
            held(own, turn, way, what),
            own_s.at[what, way, turn],
        )

    def give(turn, way, what):
        return remote(
            source(turn, way, what % 2, part_of(way, what), 1 - core),
            held(sib, turn, way, what),
            sib_s.at[what, way, turn],
            sib_r.at[what, way, turn],
            sibling,
        )

    def cross(turn, way):
        return remote(
            held(own, turn, way, 1),
            xin.at[turn, pl.ds(SUM_CUTS[2 + way] - SUM_CUTS[2], sizes[2 + way])],
            x_s.at[way, turn],
            x_r.at[way, turn],
            beside,
        )

    def got(way, slot, what):
        if what == 0:
            return rin_b.at[slot, pl.ds(SUM_CUTS[2 + way] - SUM_CUTS[2], sizes[2 + way])]
        return rin_a.at[what - 2, slot, pl.ds(SUM_CUTS[way], sizes[way])]

    def ring(turn, way, what, first=False):
        where = held(own, turn, way, what) if first else got(way, turn - 1, what)
        return remote(
            where,
            got(way, turn, what),
            ring_s.at[what, way, turn],
            ring_r.at[what, way, turn],
            ways[way],
        )

    order = (1, 2, 3, 0)

    def begin_own(turn, carry):
        for what in order:
            for way in range(2):
                load(turn, way, what).start()
        return carry

    def begin_sib(turn, carry):
        for what in order:
            for way in range(2):
                give(turn, way, what).start()
        return carry

    begin_own(0, 0)
    pl.semaphore_wait(barrier, CHIPS)
    begin_sib(0, 0)
    lax.fori_loop(1, RING, lambda t, c: begin_sib(t, begin_own(t, c)), 0)

    def both(turn, way, what):
        load(turn, way, what).wait()
        give(turn, way, what).wait_recv()
        return held(own, turn, way, what)[...].astype(f32) + held(sib, turn, way, what)[...].astype(f32)

    def send_across(turn):
        for way in range(2):
            held(own, turn, way, 1)[...] = both(turn, way, 1).astype(bf16)
            cross(turn, way).start()

    def across(turn, way):
        cross(turn, way).wait_recv()
        return xin[turn, pl.ds(SUM_CUTS[2 + way] - SUM_CUTS[2], sizes[2 + way])].astype(f32)

    send_across(0)
    for what in (2, 3):
        for way in range(2):
            held(own, 0, way, what)[...] = both(0, way, what).astype(bf16)
            ring(0, way, what, True).start()
    send_across(1)
    for way in range(2):
        held(own, 0, way, 0)[...] = (both(0, way, 0) + across(0, way)).astype(bf16)
        ring(0, way, 0, True).start()

    def step(turn, carry):
        send_across(turn + 1)
        for what in (2, 3, 0):
            for way in range(2):
                part = both(turn, way, what)
                if what == 0:
                    part = part + across(turn, way)
                ring(turn - 1, way, what, True).wait_recv()
                where = got(way, turn - 1, what)
                where[...] = (where[...].astype(f32) + part).astype(bf16)
                ring(turn, way, what).start()
        return carry

    lax.fori_loop(1, RING - 1, step, 0)
    last = RING - 1
    def to_beside(way):
        return remote(
            got(way, last - 1, 3),
            xlast.at[pl.ds(SUM_CUTS[way], sizes[way])],
            last_s.at[way],
            last_r.at[way],
            beside,
        )

    for way in range(2):
        part = both(last, way, 3)
        ring(last - 1, way, 3, True).wait_recv()
        where = got(way, last - 1, 3)
        where[...] = (where[...].astype(f32) + part).astype(bf16)
        to_beside(way).start()
    for what in (2, 0):
        for way in range(2):
            part = both(last, way, what)
            if what == 0:
                part = part + across(last, way)
            ring(last - 1, way, what, True).wait_recv()
            low = SUM_CUTS[part_of(way, what)]
            total[low : low + sizes[part_of(way, what)]] = got(way, last - 1, what)[...].astype(f32) + part
    for way in range(2):
        to_beside(way).wait_recv()
        low = SUM_CUTS[way]
        total[low : low + sizes[way]] += xlast[low : low + sizes[way]].astype(f32)

    first = ((row * 4 + x * 2 + core) * OWN) % 16
    rows = lax.broadcasted_iota(jnp.int32, (CHR, 128), 0)
    value = total[...]
    squares = jnp.where((rows >= first) & (rows < first + OWN), value * value, 0.0)
    st_mine[0:8] = jnp.sum(squares.reshape(CHR // 8, 8, 128), axis=0)
    st_mine[8:16] = loss[...]
    pair = remote(st_mine, st_sib, pair_s, pair_r, sibling)
    pair.start()
    pair.wait_recv()
    st_sum[...] = st_mine[...] + st_sib[...]
    st_all[me] = st_sum[...]

    def tell(k):
        return remote(
            st_sum, st_all.at[me], tell_s.at[k], tell_r.at[k],
            chip_device(lax.rem(me + k, CHIPS), core),
        )

    def tell_one(k, carry):
        tell(k).start()
        return carry

    lax.fori_loop(1, CHIPS, tell_one, 0)

    def settle(turn, carry):
        for way in range(2):
            for what in range(4):
                give(turn, way, what).wait_send()
            cross(turn, way).wait_send()

            @pl.when(turn < RING - 1)
            def _():
                for what in (0, 2, 3):
                    ring(turn, way, what, True).wait_send()

        return carry

    lax.fori_loop(0, RING, settle, 0)
    for way in range(2):
        to_beside(way).wait_send()

    def told(k, carry):
        tell(k).wait_recv()
        return carry

    lax.fori_loop(1, CHIPS, told, 0)
    everything = st_all[0]
    for k in range(1, CHIPS):
        everything = everything + st_all[k]
    stats[...] = everything

    def tell_done(k, carry):
        tell(k).wait_send()
        return carry

    lax.fori_loop(1, CHIPS, tell_done, 0)
    pair.wait_send()


def rs(grad, loss):
    vm, dma = pltpu.VMEM, pltpu.SemaphoreType.DMA
    first, second = SUM_CUTS[2], SUM_CUTS[4] - SUM_CUTS[2]
    shape = jax.ShapeDtypeStruct
    return pl.pallas_call(
        sum_kernel,
        out_shape=[shape((CHR, 128), f32), shape((16, 128), f32)],
        in_specs=[pl.BlockSpec(memory_space=pl.ANY), pl.BlockSpec(memory_space=vm)],
        out_specs=[pl.BlockSpec(memory_space=vm)] * 2,
        scratch_shapes=[
            vm((2, RING, CHR, 128), bf16),
            vm((2, RING, CHR, 128), bf16),
            vm((RING, second, 128), bf16),
            vm((RING - 1, second, 128), bf16),
            vm((2, RING - 1, first, 128), bf16),
            vm((first, 128), bf16),
            vm((16, 128), f32),
            vm((16, 128), f32),
            vm((16, 128), f32),
            vm((CHIPS, 16, 128), f32),
            dma((4, 2, RING)),
            dma((4, 2, RING)),
            dma((4, 2, RING)),
            dma((2, RING)),
            dma((2, RING)),
            dma((2,)),
            dma((2,)),
            dma((4, 2, RING - 1)),
            dma((4, 2, RING - 1)),
            dma((CHIPS,)),
            dma((CHIPS,)),
            dma,
            dma,
        ],
        compiler_params=pltpu.CompilerParams(
            collective_id=1, has_side_effects=True, vmem_limit_bytes=56 << 20
        ),
        name="sum_gradients",
    )(grad, loss)


MATS = [(PIN, D), (D, FF), (FF, D), (D, FF), (FF, D), (D, PIN)]
SMALL_LAYER = 2352
SMALLS = [6 + SMALL_LAYER, 24, 6 + SMALL_LAYER, 24, 18, 10]
PIECE = 256


def flat_sections():
    at = 0
    found = []
    for (depth, cols), small in zip(MATS, SMALLS):
        per_row = cols // LANES
        found.append((at, depth, per_row, at + depth * per_row, small))
        at += depth * per_row + small
    return found


def piece_rows(depth, per_row):
    rows = depth
    while rows * per_row > 7680:
        rows -= PIECE
        while depth % rows:
            rows -= PIECE
    return rows


def unpack_kernel(flat, *refs):
    mats, smalls = refs[:6], refs[6:12]
    raw, wide, out24, out6, out10, in_sem, out_sem = refs[12:]
    outs = {24: out24, 6: out6, 10: out10}
    steps = []
    for i, (start, depth, per_row, small_at, small) in enumerate(flat_sections()):
        rows = piece_rows(depth, per_row)
        for top in range(0, depth, rows):
            steps.append((i, start + top * per_row, rows * per_row, per_row, top, rows))
        steps.append((i, small_at, small, 0, 0, 0))

    def fetch(n):
        _, at, count, *_ = steps[n]
        low = at // 16 * 16
        size = -(-(at + count - low) // 16) * 16
        return pltpu.make_async_copy(
            flat.at[pl.ds(low, size)], raw.at[n % 2, pl.ds(0, size)], in_sem.at[n % 2]
        ), size

    fetch(0)[0].start()
    pending = {}
    for n, (i, at, count, per_row, top, rows) in enumerate(steps):
        if n + 1 < len(steps):
            fetch(n + 1)[0].start()
        copy, size = fetch(n)
        copy.wait()
        wide[0:size] = raw[n % 2, 0:size].astype(f32)
        shift = at % 16
        if not per_row:
            smalls[i][0:count] = wide[shift : shift + count]
            continue
        out = outs[per_row]
        if per_row in pending:
            pending.pop(per_row).wait()
        for part in range(0, rows, PIECE):
            for j in range(per_row):
                out[part : part + PIECE, j * LANES : (j + 1) * LANES] = wide[
                    pl.ds(shift + part * per_row + j, PIECE, stride=per_row), :
                ].astype(bf16)
        done = pltpu.make_async_copy(
            out.at[pl.ds(0, rows)], mats[i].at[pl.ds(top, rows)], out_sem.at[(24, 6, 10).index(per_row)]
        )
        done.start()
        pending[per_row] = done
    for done in pending.values():
        done.wait()


def unpack_flat(flat):
    vm, anywhere = pltpu.VMEM, pl.BlockSpec(memory_space=pl.ANY)
    shape = jax.ShapeDtypeStruct
    padded = [-(-count // 8) * 8 for count in SMALLS]
    return pl.pallas_call(
        unpack_kernel,
        out_shape=[shape(m, bf16) for m in MATS] + [shape((n, LANES), f32) for n in padded],
        in_specs=[anywhere],
        out_specs=[anywhere] * 6 + [pl.BlockSpec(memory_space=vm)] * 6,
        scratch_shapes=[
            vm((2, 7696, LANES), bf16),
            vm((7696, LANES), f32),
            vm((256, FF), bf16),
            vm((1280, D), bf16),
            vm((768, PIN), bf16),
            pltpu.SemaphoreType.DMA((2,)),
            pltpu.SemaphoreType.DMA((3,)),
        ],
        compiler_params=pltpu.CompilerParams(vmem_limit_bytes=48 << 20),
        name="unpack_flat",
    )(flat)


def pack_kernel(counts, *refs):
    pairs = [refs[4 * i : 4 * i + 4] for i in range(6)]
    smalls, rest = [], refs[24:]
    for number in counts:
        smalls.append(rest[:number])
        rest = rest[number:]
    flat, across, side, wide, narrow, sem = rest
    pending = []

    def emit(at, full):
        return pltpu.make_async_copy(narrow.at[pl.ds(0, full)], flat.at[pl.ds(at, full)], sem)

    for i, (start, depth, per_row, small_at, small) in enumerate(flat_sections()):
        x0, x1, g0, g1 = pairs[i]
        cols = per_row * LANES
        for half, (x, g) in enumerate(((x0, g0), (x1, g1))):
            for part in range(0, depth, PIECE):
                across[part : part + PIECE, half * 128 : half * 128 + 128] = x[
                    :, part : part + PIECE
                ].T
            side[half * 128 : half * 128 + 128, 0:cols] = g[...]
        rows = piece_rows(depth, per_row)
        full = rows * per_row
        shift = start % 16
        before = pending.pop() if pending else None

        def step(it, carry):
            top = pl.multiple_of(it * rows, PIECE)
            for part in range(0, rows, PIECE):
                left = across[pl.ds(pl.multiple_of(top + part, PIECE), PIECE), :]
                for j in range(0, per_row, 2):
                    value = dot(left, side[:, j * LANES : (j + 2) * LANES])
                    for side_by in range(2):
                        wide[
                            pl.ds(shift + part * per_row + j + side_by, PIECE, stride=per_row), :
                        ] = value[:, side_by * LANES : (side_by + 1) * LANES]
            if before is not None:
                @pl.when(it == 0)
                def _():
                    before.wait()

            @pl.when(it > 0)
            def _():
                emit(0, full).wait()

            narrow[0:full] = wide[0:full].astype(bf16)
            emit(pl.multiple_of(start - shift + it * full, 16), full).start()
            wide[0:16] = wide[full : full + 16]
            return carry

        lax.fori_loop(0, depth // rows, step, 0)
        shift = small_at % 16
        into = shift
        for piece in smalls[i]:
            wide[into : into + piece.shape[0]] = piece[...]
            into += piece.shape[0]
        full = (shift + small) // 16 * 16
        if i == 5:
            wide[shift + small : GROWS - small_at + shift] = jnp.zeros(
                (GROWS - small_at - small, LANES), f32
            )
            full = GROWS - small_at + shift
        emit(0, rows * per_row).wait()
        narrow[0:full] = wide[0:full].astype(bf16)
        done = emit(small_at - shift, full)
        done.start()
        pending.append(done)
        if i < 5:
            wide[0:16] = wide[full : full + 16]
    pending.pop().wait()


def pack_flat(pairs, smalls):
    vm, whole = pltpu.VMEM, pl.BlockSpec(memory_space=pltpu.VMEM)
    args = [a for four in pairs for a in four] + [a for some in smalls for a in some]
    return pl.pallas_call(
        functools.partial(pack_kernel, [len(some) for some in smalls]),
        out_shape=jax.ShapeDtypeStruct((GROWS, LANES), bf16),
        in_specs=[whole] * len(args),
        out_specs=pl.BlockSpec(memory_space=pl.ANY),
        scratch_shapes=[
            vm((FF, 256), bf16),
            vm((256, FF), bf16),
            vm((7712, LANES), f32),
            vm((7712, LANES), bf16),
            pltpu.SemaphoreType.DMA,
        ],
        compiler_params=pltpu.CompilerParams(vmem_limit_bytes=52 << 20),
        name="pack_flat",
    )(*args)


def split_small(rows, layouts):
    found, at = [], 0
    for layout in layouts:
        count = math.prod(layout) // LANES
        found.append(rows[at : at + count].reshape(layout))
        at += count
    return found


SPEC_ROWS = (2, NBLK, BS * BS // LANES, LANES)
LAYER_SMALL = [(D,), (D,), SPEC_ROWS, (2, NBLK, BS), SPEC_ROWS, (2, NBLK, BS), (D,), (D,)]


def local_fast(frames, targets, regions, master, first_moment, second_moment):
    height, width = 16, 128
    device = lax.axis_index("row") * 4 + lax.axis_index("col")
    _, chip, core, _ = place()
    block = chip % NBLK
    shard = master.astype(bf16).reshape(OWN, LANES)
    halo = lax.ppermute(shard[:320], ("row", "col"), [(k + 1, k) for k in range(31)])
    chunk = lax.dynamic_slice_in_dim(jnp.concatenate([shard, halo]), 10 * device, CH, 0)
    unpacked = unpack_flat(ag(chunk))
    embed, in0, out0, in1, out1, head = unpacked[:6]
    smalls = unpacked[6:]
    embed_bias, *layer0 = split_small(smalls[0], [(D,)] + LAYER_SMALL)
    (c1_0,) = split_small(smalls[1], [(FF,)])
    c2_0, *layer1 = split_small(smalls[2], [(D,)] + LAYER_SMALL)
    (c1_1,) = split_small(smalls[3], [(FF,)])
    c2_1, gain3, shift3 = split_small(smalls[4], [(D,)] * 3)
    (head_bias,) = split_small(smalls[5], [(PIN,)])
    layers = [(layer0, in0, c1_0, out0, c2_0), (layer1, in1, c1_1, out1, c2_1)]
    tables = transform_tables(core)
    row_ids = lax.axis_index("row") * 2 + jnp.arange(2, dtype=jnp.int32)
    col_ids = lax.axis_index("col") * 32 + jnp.arange(32, dtype=jnp.int32)
    cell_masks = region_masks(regions, row_ids, col_ids, width)
    weighted = latitude(row_ids, height)[None, :, None] * cell_masks
    every_row = jnp.arange(height, dtype=jnp.int32)
    every_col = jnp.arange(width, dtype=jnp.int32)
    total_weight = (
        jnp.sum(
            latitude(every_row, height)[None, :, None]
            * region_masks(regions, every_row, every_col, width)
        )
        * STEPS
    )
    flat_mask = cell_masks.reshape(128, 1)
    flat_weight = weighted.reshape(128, 1)
    inputs = (frames.reshape(128, PIN).astype(f32) * flat_mask).astype(bf16)
    goals = [targets[:, s].reshape(128, PIN).astype(f32) for s in range(STEPS)]
    spectral_weights = []
    for small, *_ in layers:
        found = []
        for j in (2, 4):
            w = lax.dynamic_index_in_dim(small[j], block, 1, False).reshape(2, BS, BS)
            b = lax.dynamic_index_in_dim(small[j + 1], block, 1, False)
            found += [spread_weight(w[0], w[1]).astype(bf16), spread_bias(b)]
        spectral_weights.append(found)

    def lin(values, weight16, bias_vec):
        return mult("ci,io->co", values, weight16) + bias_vec

    loss_cells = jnp.zeros((128,), f32)
    history = []
    for roll_step in range(STEPS):
        stream = lin(inputs, embed, embed_bias)
        saved = []
        for (small, w_in, c1, w_out, c2), spectral_w in zip(layers, spectral_weights):
            mixed, waves = filter_forward(
                stream, small[0][None], small[1][None], tables, spectral_w
            )
            normed = layer_norm(mixed, small[6], small[7]).astype(bf16)
            before = lin(normed, w_in, c1)
            hidden = jax.nn.gelu(before, approximate=False).astype(bf16)
            saved.append((stream, waves, mixed, normed, before, hidden))
            stream = mixed + lin(hidden, w_out, c2)
        normed = layer_norm(stream, gain3, shift3).astype(bf16)
        predicted = lin(normed, head, head_bias)
        errors = predicted - goals[roll_step]
        loss_cells = loss_cells + flat_weight[:, 0] * jnp.sum(errors * errors, axis=-1)
        history.append((inputs, saved, stream, normed, errors))
        inputs = (predicted * flat_mask).astype(bf16)
    carried = jnp.zeros((128, PIN), f32)
    pairs = [[None] * 4 for _ in range(6)]
    parts = []

    def keep(i, step, values, grad):
        pairs[i][step] = values.astype(bf16)
        pairs[i][2 + step] = grad.astype(bf16)

    for roll_step in reversed(range(STEPS)):
        inputs, saved, stream, normed, errors = history[roll_step]
        grad_pred = 2.0 * flat_weight * errors / total_weight + carried
        keep(5, roll_step, normed, grad_pred)
        _, pullback = jax.vjp(layer_norm, stream, gain3, shift3)
        grad_stream, grad_gain3, grad_shift3 = pullback(
            rounded(mult("co,io->ci", grad_pred, head))
        )
        found = {"hb": jnp.sum(grad_pred, axis=0), "g3": grad_gain3, "s3": grad_shift3}
        for idx in reversed(range(LAYERS)):
            small, w_in, c1, w_out, c2 = layers[idx]
            stream, waves, mixed, normed, before, hidden = saved[idx]
            keep(2 + 2 * idx, roll_step, hidden, grad_stream)
            grad_hidden = mult("co,io->ci", grad_stream, w_out)
            _, pullback = jax.vjp(lambda value: jax.nn.gelu(value, approximate=False), before)
            (grad_before,) = pullback(rounded(grad_hidden))
            keep(1 + 2 * idx, roll_step, normed, grad_before)
            _, pullback = jax.vjp(layer_norm, mixed, small[6], small[7])
            grad_extra, grad_gain2, grad_shift2 = pullback(
                rounded(mult("co,io->ci", grad_before, w_in))
            )
            found[f"c2{idx}"] = jnp.sum(grad_stream, axis=0)
            found[f"c1{idx}"] = jnp.sum(grad_before, axis=0)
            grad_stream, norm_grads, gw1, gw2, gb = filter_backward(
                grad_stream + grad_extra, stream, small[0][None], waves, tables,
                spectral_weights[idx],
            )
            found[f"layer{idx}"] = (norm_grads, gw1, gw2, gb, grad_gain2, grad_shift2)
        keep(0, roll_step, inputs, grad_stream)
        found["eb"] = jnp.sum(grad_stream, axis=0)
        parts.append(found)
        if roll_step:
            carried = flat_mask * rounded(mult("co,io->ci", grad_stream, embed))
    sums = jax.tree.map(jnp.add, parts[0], parts[1])

    def as_rows(value):
        return value.reshape(-1, LANES)

    def placed(local_grad):
        local_grad = local_grad.reshape(2, 1, -1)
        whole = jnp.zeros((2, NBLK, local_grad.shape[2]), f32)
        return as_rows(lax.dynamic_update_slice_in_dim(whole, local_grad, block, 1))

    def layer_rows(idx):
        norm_grads, gw1, gw2, gb, gain2, shift2 = sums[f"layer{idx}"]
        return [
            as_rows(norm_grads[0]),
            as_rows(norm_grads[1]),
            placed(fold_weight(gw1)),
            placed(fold_bias(gb[0])),
            placed(fold_weight(gw2)),
            placed(fold_bias(gb[1])),
            as_rows(gain2),
            as_rows(shift2),
        ]

    small_grads = [
        [as_rows(sums["eb"])] + layer_rows(0),
        [as_rows(sums["c10"])],
        [as_rows(sums["c20"])] + layer_rows(1),
        [as_rows(sums["c11"])],
        [as_rows(sums[k]) for k in ("c21", "g3", "s3")],
        [as_rows(sums["hb"])],
    ]
    flat_grad = pack_flat(pairs, small_grads)
    loss_tile = jnp.concatenate([loss_cells[None], jnp.zeros((7, LANES), f32)])
    summed, stats = rs(flat_grad, loss_tile)
    reduced = lax.dynamic_slice_in_dim(summed, (device * OWN) % 16, OWN, 0).reshape(-1)
    grad_norm = jnp.sqrt(jnp.sum(stats[:8]))
    return finish_step(
        reduced, grad_norm, master, first_moment, second_moment, jnp.sum(stats[8:]), total_weight
    )


def finish_step(reduced, grad_norm, master, first_moment, second_moment, loss_all, total_weight):
    clipped = reduced * (CLIP / jnp.maximum(grad_norm, CLIP))
    first_out = BETA_ONE * first_moment + (1.0 - BETA_ONE) * clipped
    second_out = BETA_TWO * second_moment + (1.0 - BETA_TWO) * clipped * clipped
    corrected_one = first_out / (1.0 - BETA_ONE**ADAM_STEP)
    corrected_two = second_out / (1.0 - BETA_TWO**ADAM_STEP)
    master_out = master - RATE * (
        corrected_one / (jnp.sqrt(corrected_two) + ADAM_EPS) + DECAY * master
    )
    return (
        master_out,
        first_out,
        second_out,
        master_out.astype(bf16),
        loss_all,
        total_weight,
        grad_norm,
    )


def local(frames, targets, regions, master, first_moment, second_moment):
    row_devices = lax.axis_size("row")
    col_devices = lax.axis_size("col")
    local_rows = frames.shape[1]
    local_cols = frames.shape[2]
    height = local_rows * row_devices
    width = local_cols * col_devices
    weights = lax.all_gather(master.astype(jnp.bfloat16), ("row", "col"), axis=0, tiled=True)
    pieces16 = unpack(weights)
    pieces = unpack(weights.astype(jnp.float32))
    tail_params = pieces[2 + 12 * LAYERS :]
    tail16 = pieces16[2 + 12 * LAYERS :]
    tables = (
        dft_tables(width, -1.0),
        dft_tables(height, -1.0),
        dft_tables(width, 1.0),
        dft_tables(height, 1.0),
    )
    row_ids = lax.axis_index("row") * local_rows + jnp.arange(local_rows, dtype=jnp.int32)
    col_ids = lax.axis_index("col") * local_cols + jnp.arange(local_cols, dtype=jnp.int32)
    cell_masks = region_masks(regions, row_ids, col_ids, width)
    weighted = latitude(row_ids, height)[None, :, None] * cell_masks
    every_row = jnp.arange(height, dtype=jnp.int32)
    every_col = jnp.arange(width, dtype=jnp.int32)
    total_weight = (
        jnp.sum(
            latitude(every_row, height)[None, :, None]
            * region_masks(regions, every_row, every_col, width)
        )
        * STEPS
    )
    inputs = frames.astype(jnp.float32) * cell_masks[..., None]
    loss_sum = jnp.zeros((), jnp.float32)
    history = []
    for roll_step in range(STEPS):
        stream = linear_forward(inputs, pieces16[0], pieces[1])
        saved_layers = []
        for layer_idx in range(LAYERS):
            span = slice(2 + 12 * layer_idx, 14 + 12 * layer_idx)
            stream, saved = layer_forward(stream, pieces[span], pieces16[span], tables)
            saved_layers.append(saved)
        normed = rounded(layer_norm(stream, tail_params[0], tail_params[1]))
        predicted = linear_forward(normed, tail16[2], tail_params[3])
        errors = predicted - targets[:, roll_step].astype(jnp.float32)
        loss_sum = loss_sum + jnp.sum(weighted * jnp.sum(errors * errors, axis=-1))
        history.append((inputs, saved_layers, stream, normed, errors))
        inputs = rounded(predicted * cell_masks[..., None])
    loss_all = lax.psum(loss_sum, ("row", "col"))
    gradients = [jnp.zeros_like(piece) for piece in pieces]
    carried = jnp.zeros_like(inputs)
    for roll_step in reversed(range(STEPS)):
        inputs, saved_layers, stream, normed, errors = history[roll_step]
        grad_pred = 2.0 * weighted[..., None] * errors / total_weight + carried
        grad_normed, grad_head, grad_hbias = linear_backward(grad_pred, normed, tail16[2])
        _, pullback = jax.vjp(layer_norm, stream, tail_params[0], tail_params[1])
        grad_stream, grad_gain3, grad_shift3 = pullback(rounded(grad_normed))
        gradients = add_into(
            gradients, 2 + 12 * LAYERS, [grad_gain3, grad_shift3, grad_head, grad_hbias]
        )
        for layer_idx in reversed(range(LAYERS)):
            span = slice(2 + 12 * layer_idx, 14 + 12 * layer_idx)
            grad_stream, layer_grads = layer_backward(
                grad_stream, saved_layers[layer_idx], pieces[span], pieces16[span], tables
            )
            gradients = add_into(gradients, 2 + 12 * layer_idx, layer_grads)
        grad_inputs, grad_embed, grad_ebias = linear_backward(grad_stream, inputs, pieces16[0])
        gradients = add_into(gradients, 0, [grad_embed, grad_ebias])
        carried = cell_masks[..., None] * rounded(grad_inputs)
    flat_grad = jnp.concatenate([piece.ravel() for piece in gradients])
    padding = master.shape[0] * row_devices * col_devices - flat_grad.shape[0]
    flat_grad = jnp.concatenate([flat_grad, jnp.zeros((padding,), jnp.float32)])
    grad_table = flat_grad.reshape(-1, LANES)
    reduced = lax.psum_scatter(grad_table, ("row", "col"), scatter_dimension=0, tiled=True).reshape(
        -1
    )
    squares = jnp.sum(reduced * reduced)
    square_all = lax.psum(squares, ("row", "col"))
    grad_norm = jnp.sqrt(square_all)
    clipped = reduced * (CLIP / jnp.maximum(grad_norm, CLIP))
    first_out = BETA_ONE * first_moment + (1.0 - BETA_ONE) * clipped
    second_out = BETA_TWO * second_moment + (1.0 - BETA_TWO) * clipped * clipped
    corrected_one = first_out / (1.0 - BETA_ONE**ADAM_STEP)
    corrected_two = second_out / (1.0 - BETA_TWO**ADAM_STEP)
    master_out = master - RATE * (
        corrected_one / (jnp.sqrt(corrected_two) + ADAM_EPS) + DECAY * master
    )
    return (
        master_out,
        first_out,
        second_out,
        master_out.astype(jnp.bfloat16),
        loss_all,
        total_weight,
        grad_norm,
    )


def solution(mesh):
    in_specs = (
        P(None, "row", "col", None),
        P(None, None, "row", "col", None),
        P(),
        P(("row", "col")),
        P(("row", "col")),
        P(("row", "col")),
    )
    out_specs = (
        P(("row", "col")),
        P(("row", "col")),
        P(("row", "col")),
        P(("row", "col")),
        P(),
        P(),
        P(),
    )
    body = local_fast if dict(mesh.shape) == {"row": 8, "col": 4} else local
    return jax.shard_map(body, mesh=mesh, in_specs=in_specs, out_specs=out_specs, check_vma=False)
```

```python
import functools
import math

import jax
import jax.numpy as jnp
import numpy as np
from jax import lax
from jax.sharding import PartitionSpec as P
from jax.experimental import pallas as pl
from jax.experimental.pallas import tpu as pltpu

D = 768
FF = 3072
NBLK = 8
BS = 96
PIN = 1280
LAYERS = 2
STEPS = 2
ADAM_STEP = 5


highest = lax.Precision.HIGHEST
NORM_EPS = 1e-05
BETA_ONE = 0.9
BETA_TWO = 0.95
ADAM_EPS = 1e-08
RATE = 0.03
DECAY = 0.05
CLIP = 0.2
LANES = 128


def block_shapes():
    return [
        (D,),
        (D,),
        (2, NBLK, BS, BS),
        (2, NBLK, BS),
        (2, NBLK, BS, BS),
        (2, NBLK, BS),
        (D,),
        (D,),
        (D, FF),
        (FF,),
        (FF, D),
        (D,),
    ]


def all_shapes():
    return [(PIN, D), (D,)] + block_shapes() * LAYERS + [(D,), (D,), (D, PIN), (PIN,)]


def unpack(flat_vec):
    pieces = []
    offset = 0
    for layout in all_shapes():
        length = math.prod(layout)
        pieces.append(flat_vec[offset : offset + length].reshape(layout))
        offset += length
    return pieces


def rounded(value):
    return lax.optimization_barrier(value.astype(jnp.bfloat16)).astype(jnp.float32)


def mult(form, left, right):
    return jnp.einsum(
        form,
        left.astype(jnp.bfloat16),
        right.astype(jnp.bfloat16),
        preferred_element_type=jnp.float32,
    )


def mult_exact(form, grad_value, other):
    upper = grad_value.astype(jnp.bfloat16)
    lower = (grad_value - upper.astype(jnp.float32)).astype(jnp.bfloat16)
    return mult(form, upper, other) + mult(form, lower, other)


def layer_norm(values, gain_vec, shift_vec):
    center = values - jnp.mean(values, axis=-1, keepdims=True)
    spread = jnp.mean(center * center, axis=-1, keepdims=True)
    return center * lax.rsqrt(spread + NORM_EPS) * gain_vec + shift_vec


def dft_tables(length, direction):
    positions = jnp.arange(length, dtype=jnp.int32)
    phases = (positions[:, None] * positions[None, :] % length).astype(jnp.float32) * (
        2.0 * math.pi / length
    )
    factor = 1.0 / math.sqrt(length)
    return (jnp.cos(phases) * factor, direction * jnp.sin(phases) * factor)


def apply_pair(tables, real_part, imag_part, form):

    def contract(table, values):
        return jnp.einsum(form, table, values, precision=highest)

    return (
        contract(tables[0], real_part) - contract(tables[1], imag_part),
        contract(tables[1], real_part) + contract(tables[0], imag_part),
    )


def spectral(real_part, imag_part, weight, bias_vec):
    blocks = (weight.shape[1], weight.shape[2])
    block_re = real_part.reshape(real_part.shape[:-1] + blocks)
    block_im = imag_part.reshape(imag_part.shape[:-1] + blocks)
    form = "...kb,kbc->...kc"
    out_re = (
        jnp.einsum(form, block_re, weight[0], precision=highest)
        - jnp.einsum(form, block_im, weight[1], precision=highest)
        + bias_vec[0]
    )
    out_im = (
        jnp.einsum(form, block_im, weight[0], precision=highest)
        + jnp.einsum(form, block_re, weight[1], precision=highest)
        + bias_vec[1]
    )
    return (out_re.reshape(real_part.shape), out_im.reshape(imag_part.shape))


def first_spectral(real_part, imag_part, weight, bias_vec):
    out_re, out_im = spectral(real_part, imag_part, weight, bias_vec)
    return (jax.nn.gelu(out_re, approximate=False), jax.nn.gelu(out_im, approximate=False))


def region_masks(regions, row_ids, col_ids, width):
    row_start = regions[:, 0, None, None]
    row_span = regions[:, 1, None, None]
    col_start = regions[:, 2, None, None]
    col_span = regions[:, 3, None, None]
    row_inside = (row_ids[None, :, None] >= row_start) & (
        row_ids[None, :, None] < row_start + row_span
    )
    col_inside = (col_ids[None, None, :] - col_start) % width < col_span
    return (row_inside & col_inside).astype(jnp.float32)


def latitude(row_ids, height):
    return jnp.cos(-1.3 + 1.3 * (row_ids.astype(jnp.float32) + 0.5) / height)


def linear_forward(values, weight16, bias_vec):
    return mult("brci,io->brco", values, weight16) + bias_vec


def linear_backward(grad_value, values, weight16):
    grad_values = mult_exact("brco,io->brci", grad_value, weight16)
    grad_weight = mult_exact("brco,brci->io", grad_value, values)
    return (grad_values, grad_weight, jnp.sum(grad_value, axis=(0, 1, 2)))


def spectrum(field, forward_w, forward_h):
    values = lax.all_to_all(field, "col", split_axis=3, concat_axis=2, tiled=True).astype(
        jnp.float32
    )
    real_part = jnp.einsum("kw,bnwc->bnkc", forward_w[0], values, precision=highest)
    imag_part = jnp.einsum("kw,bnwc->bnkc", forward_w[1], values, precision=highest)
    real_part, imag_part = apply_pair(
        forward_h,
        lax.all_to_all(
            real_part.astype(jnp.bfloat16), "row", split_axis=2, concat_axis=1, tiled=True
        ).astype(jnp.float32),
        lax.all_to_all(
            imag_part.astype(jnp.bfloat16), "row", split_axis=2, concat_axis=1, tiled=True
        ).astype(jnp.float32),
        "kh,bhwc->bkwc",
    )
    return (real_part.astype(jnp.bfloat16), imag_part.astype(jnp.bfloat16))


def grid(real_part, imag_part, inverse_w, inverse_h):
    back_re, back_im = apply_pair(
        inverse_h, real_part.astype(jnp.float32), imag_part.astype(jnp.float32), "kh,bhwc->bkwc"
    )
    values_re = lax.all_to_all(
        back_re.astype(jnp.bfloat16), "row", split_axis=1, concat_axis=2, tiled=True
    ).astype(jnp.float32)
    values_im = lax.all_to_all(
        back_im.astype(jnp.bfloat16), "row", split_axis=1, concat_axis=2, tiled=True
    ).astype(jnp.float32)
    result = jnp.einsum("kw,bnwc->bnkc", inverse_w[0], values_re, precision=highest) - jnp.einsum(
        "kw,bnwc->bnkc", inverse_w[1], values_im, precision=highest
    )
    columns_back = result.astype(jnp.bfloat16)
    return lax.all_to_all(columns_back, "col", split_axis=2, concat_axis=3, tiled=True)


def local_blocks(params):
    block_count = D // lax.axis_size("col") // BS
    first_block = lax.axis_index("col") * block_count
    chosen = [
        lax.dynamic_slice_in_dim(params[index_pos], first_block, block_count, 1)
        for index_pos in (2, 3, 4, 5)
    ]
    return (chosen, first_block)


def layer_forward(stream, params, params16, tables):
    gain_one, shift_one, _, _, _, _, gain_two, shift_two, _, bias_in, _, bias_out = params
    (local_w1, local_b1, local_w2, local_b2), _ = local_blocks(params)
    normed = layer_norm(stream, gain_one, shift_one).astype(jnp.bfloat16)
    wave_re, wave_im = spectrum(normed, tables[0], tables[1])
    hid_re, hid_im = first_spectral(
        wave_re.astype(jnp.float32), wave_im.astype(jnp.float32), local_w1, local_b1
    )
    hid_re, hid_im = (rounded(hid_re), rounded(hid_im))
    spec_re, spec_im = spectral(hid_re, hid_im, local_w2, local_b2)
    filtered = grid(
        spec_re.astype(jnp.bfloat16), spec_im.astype(jnp.bfloat16), tables[2], tables[3]
    )
    mixed = stream + filtered.astype(jnp.float32)
    normed_two = rounded(layer_norm(mixed, gain_two, shift_two))
    hidden = rounded(
        jax.nn.gelu(linear_forward(normed_two, params16[8], bias_in), approximate=False)
    )
    output = mixed + linear_forward(hidden, params16[10], bias_out)
    return (output, (stream, wave_re, wave_im, hid_re, hid_im, mixed, normed_two, hidden))


def place_blocks(local_grad, full_like, first_block):
    return lax.dynamic_update_slice_in_dim(jnp.zeros_like(full_like), local_grad, first_block, 1)


def layer_backward(grad_out, saved, params, params16, tables):
    stream, wave_re, wave_im, hid_re, hid_im, mixed, normed_two, hidden = saved
    (
        gain_one,
        shift_one,
        spec_w1,
        spec_b1,
        spec_w2,
        spec_b2,
        gain_two,
        shift_two,
        weight_in,
        bias_in,
        weight_out,
        bias_out,
    ) = params
    (local_w1, local_b1, local_w2, local_b2), first_block = local_blocks(params)
    grad_hidden, grad_wout, grad_bout = linear_backward(grad_out, hidden, params16[10])
    grad_mixed = grad_out
    before = linear_forward(normed_two, params16[8], bias_in)
    _, pullback = jax.vjp(lambda value: jax.nn.gelu(value, approximate=False), before)
    (grad_before,) = pullback(rounded(grad_hidden))
    grad_normed, grad_win, grad_bin = linear_backward(grad_before, normed_two, params16[8])
    _, pullback = jax.vjp(layer_norm, mixed, gain_two, shift_two)
    grad_extra, grad_gain2, grad_shift2 = pullback(rounded(grad_normed))
    grad_mixed = grad_mixed + grad_extra
    back_re, back_im = spectrum(grad_mixed.astype(jnp.bfloat16), tables[0], tables[1])
    _, pullback = jax.vjp(spectral, hid_re, hid_im, local_w2, local_b2)
    grad_hre, grad_him, grad_lw2, grad_lb2 = pullback(
        (back_re.astype(jnp.float32), back_im.astype(jnp.float32))
    )
    _, pullback = jax.vjp(
        first_spectral, wave_re.astype(jnp.float32), wave_im.astype(jnp.float32), local_w1, local_b1
    )
    grad_wre, grad_wim, grad_lw1, grad_lb1 = pullback((rounded(grad_hre), rounded(grad_him)))
    grad_first = grid(
        grad_wre.astype(jnp.bfloat16), grad_wim.astype(jnp.bfloat16), tables[2], tables[3]
    )
    _, pullback = jax.vjp(layer_norm, stream, gain_one, shift_one)
    grad_stream, grad_gain1, grad_shift1 = pullback(grad_first.astype(jnp.float32))
    layer_grads = [
        grad_gain1,
        grad_shift1,
        place_blocks(grad_lw1, spec_w1, first_block),
        place_blocks(grad_lb1, spec_b1, first_block),
        place_blocks(grad_lw2, spec_w2, first_block),
        place_blocks(grad_lb2, spec_b2, first_block),
        grad_gain2,
        grad_shift2,
        grad_win,
        grad_bin,
        grad_wout,
        grad_bout,
    ]
    return (grad_stream + grad_mixed, layer_grads)


def add_into(gradients, start, values):
    middle = [left + right for left, right in zip(gradients[start : start + len(values)], values)]
    return gradients[:start] + middle + gradients[start + len(values) :]


MESH = pl.DeviceIdType.MESH
CH = 2944
OWN = 2934
CHR = 2960
GROWS = 93904


CHIPS = 16
UNIT = 64
PADC = 128
f32 = jnp.float32
bf16 = jnp.bfloat16


def remote(src, dst, send_sem, recv_sem, device):
    return pltpu.make_async_remote_copy(
        src_ref=src,
        dst_ref=dst,
        send_sem=send_sem,
        recv_sem=recv_sem,
        device_id=device,
        device_id_type=MESH,
    )


def chip_device(chip, core):
    return chip // 2, (chip % 2) * 2 + core


def place():
    row = lax.axis_index("row")
    col = lax.axis_index("col")
    core = col % 2
    return row, row * 2 + col // 2, core, (row, col + 1 - 2 * core)


def greet_chips(me, core, sibling):
    barrier = pltpu.get_barrier_semaphore()

    def one(k, carry):
        pl.semaphore_signal(
            barrier,
            inc=1,
            device_id=chip_device(lax.rem(me + k, CHIPS), core),
            device_id_type=MESH,
        )
        return carry

    lax.fori_loop(1, CHIPS, one, 0)
    pl.semaphore_signal(barrier, inc=1, device_id=sibling, device_id_type=MESH)
    return barrier


def split_units(values, units):
    blank = jnp.zeros((UNIT, PADC - BS), f32)
    for part in range(2):
        for block in range(NBLK):
            piece = values[part * UNIT : (part + 1) * UNIT, block * BS : (block + 1) * BS]
            units[part * NBLK + block] = jnp.concatenate([piece, blank], axis=1).astype(bf16)


def join_units(units, joined):
    for part in range(2):
        for block in range(NBLK):
            joined[part * UNIT : (part + 1) * UNIT, block * BS : (block + 1) * BS] = units[
                part * NBLK + block, :, 0:BS
            ].astype(f32)


def normalize(values):
    center = values - jnp.mean(values, axis=-1, keepdims=True)
    spread = jnp.mean(center * center, axis=-1, keepdims=True)
    scale = lax.rsqrt(spread + NORM_EPS)
    return center * scale, scale


def gelu_of(value):
    return 0.5 * value * (1.0 + lax.erf(value * math.sqrt(0.5)))


def gelu_slope(value):
    bell = jnp.exp(-0.5 * value * value) * (1.0 / math.sqrt(2.0 * math.pi))
    return 0.5 * (1.0 + lax.erf(value * math.sqrt(0.5))) + value * bell


def dot(left, right):
    return jnp.dot(left, right, preferred_element_type=f32)


def dot_rows(left, right):
    return lax.dot_general(left, right, (((0,), (0,)), ((), ())), preferred_element_type=f32)


def dot_cols(left, right):
    return lax.dot_general(left, right, (((1,), (1,)), ((), ())), preferred_element_type=f32)


def spread_units(me, core, sibling, units, mine, others, sems):
    send_a, recv_a, send_f, recv_f, local_sem = sems

    def out(k):
        chip = lax.rem(me + k, CHIPS)
        return remote(
            units.at[chip], mine.at[me], send_a.at[k], recv_a.at[k], chip_device(chip, core)
        )

    def handed(k):
        chip = lax.rem(me + CHIPS - k, CHIPS)
        return remote(mine.at[chip], others.at[chip], send_f.at[k], recv_f.at[k], sibling)

    own = pltpu.make_async_copy(units.at[me], mine.at[me], local_sem)
    own.start()

    def begin(k, carry):
        out(k).start()
        return carry

    lax.fori_loop(1, CHIPS, begin, 0)
    own.wait()
    handed(0).start()

    def hand(k, carry):
        out(k).wait_recv()
        handed(k).start()
        return carry

    lax.fori_loop(1, CHIPS, hand, 0)

    def arrive(k, carry):
        handed(k).wait_recv()
        return carry

    lax.fori_loop(0, CHIPS, arrive, 0)

    def finish():
        def sent(k, carry):
            out(k).wait_send()
            return carry

        lax.fori_loop(1, CHIPS, sent, 0)

        def sent_on(k, carry):
            handed(k).wait_send()
            return carry

        lax.fori_loop(0, CHIPS, sent_on, 0)

    return finish


def to_spectrum(mine, others, column_table, row_table, waves):
    for h in range(16):
        pair, part = h // 2, pl.ds(32 * (h % 2), 32)
        cells = jnp.concatenate(
            [
                mine[2 * pair, part],
                mine[2 * pair + 1, part],
                others[2 * pair, part],
                others[2 * pair + 1, part],
            ],
            axis=0,
        )
        wave = dot(column_table[...], cells).astype(bf16)
        for g in range(4):
            rows = pl.ds(16 * h, 16)
            waves[g, rows, 0:PADC] = wave[16 * g : 16 * g + 16]
            waves[g, rows, PADC : 2 * PADC] = wave[64 + 16 * g : 80 + 16 * g]
    results = []
    for g in range(4):
        both = dot(row_table[...], waves[g])
        real = both[:256, :PADC] + both[256:, PADC:]
        imag = both[:256, PADC:] - both[256:, :PADC]
        results.append(jnp.concatenate([real, imag], axis=1).astype(bf16))
    return results


def from_spectrum(g, spec, row_table, back):
    both = dot(row_table[...], spec)
    real = (both[:256, :PADC] - both[256:, PADC:]).astype(bf16)
    imag = (both[:256, PADC:] + both[256:, :PADC]).astype(bf16)
    for h in range(16):
        back[h, 16 * g : 16 * g + 16] = real[16 * h : 16 * h + 16]
        back[h, 64 + 16 * g : 80 + 16 * g] = imag[16 * h : 16 * h + 16]


def gather_units(row, me, core, sibling, back, inverse_table, bufs, sems, settle):
    own_sum, to_sib, from_sib, ready, landed = bufs
    send_s, recv_s, send_b, recv_b, local_sem = sems

    def swap(pair):
        rows = pl.ds(2 * pair, 2)
        return remote(
            to_sib.at[rows], from_sib.at[rows], send_s.at[pair], recv_s.at[pair], sibling
        )

    def partial(j, carry):
        pair = lax.rem(row + 1 + j, 8)
        for half in range(2):
            sums = dot(inverse_table[...], back[2 * pair + half])
            part = pl.ds(32 * half, 32)
            for x in range(2):
                own_sum[2 * pair + x, part] = sums[32 * x : 32 * x + 32]
                to_sib[2 * pair + x, part] = sums[64 + 32 * x : 96 + 32 * x].astype(bf16)
        swap(pair).start()
        return carry

    lax.fori_loop(0, 8, partial, 0)
    settle()

    def home(chip, k):
        return remote(
            ready.at[chip], landed.at[me], send_b.at[k], recv_b.at[k], chip_device(chip, core)
        )

    own = pltpu.make_async_copy(ready.at[me], landed.at[me], local_sem)

    def total(j, carry):
        pair = lax.rem(row + 1 + j, 8)
        swap(pair).wait_recv()
        rows = pl.ds(2 * pair, 2)
        ready[rows] = (own_sum[rows] + from_sib[rows].astype(f32)).astype(bf16)
        for x in range(2):
            chip = 2 * pair + x
            k = lax.rem(chip - me + CHIPS, CHIPS)

            @pl.when(k != 0)
            def _():
                home(chip, k).start()

        return carry

    lax.fori_loop(0, 8, total, 0)
    own.start()

    def landed_all(k, carry):
        home(lax.rem(me + k, CHIPS), k).wait_recv()
        return carry

    lax.fori_loop(1, CHIPS, landed_all, 0)
    own.wait()

    def finish():
        def sent(k, carry):
            home(lax.rem(me + k, CHIPS), k).wait_send()
            return carry

        lax.fori_loop(1, CHIPS, sent, 0)

        def swapped(pair, carry):
            swap(pair).wait_send()
            return carry

        lax.fori_loop(0, 8, swapped, 0)

    return finish


def filter_scratch():
    vm = pltpu.VMEM
    dma = pltpu.SemaphoreType.DMA
    block = (CHIPS, UNIT, PADC)
    return [
        vm(block, bf16),
        vm(block, bf16),
        vm(block, bf16),
        vm((4, 256, 256), bf16),
        vm((16, 128, PADC), bf16),
        vm(block, f32),
        vm(block, bf16),
        vm(block, bf16),
        vm(block, bf16),
        vm(block, bf16),
        vm((2 * UNIT, D), f32),
        dma((CHIPS,)),
        dma((CHIPS,)),
        dma((CHIPS,)),
        dma((CHIPS,)),
        dma,
        dma((8,)),
        dma((8,)),
        dma((CHIPS,)),
        dma((CHIPS,)),
        dma,
    ]


def transform_tables(core):
    width, height = 128, 16
    order = []
    for side in range(2):
        cols = [[32 * (2 * x + (c if side == 0 else 1 - c)) + i for x in range(2) for i in range(32)] for c in range(2)]
        order.append(cols)
    column, inverse = [], []
    for c in range(2):
        cells = np.array(order[0][c] + order[1][c])
        waves = 64 * c + np.arange(64)
        angle = 2.0 * np.pi * (np.outer(waves, cells) % width) / width
        cos, sin = np.cos(angle) / np.sqrt(width), np.sin(angle) / np.sqrt(width)
        column.append(np.concatenate([cos, -sin], axis=0))
        inverse.append(np.concatenate([cos, -sin], axis=0).T)
    steps = np.arange(height)
    angle = 2.0 * np.pi * (np.outer(steps, steps) % height) / height
    eye = np.eye(16)
    rows = np.concatenate(
        [np.kron(np.cos(angle), eye), np.kron(np.sin(angle), eye)], axis=0
    ) / np.sqrt(height)
    pick = lambda both: lax.dynamic_index_in_dim(jnp.asarray(np.stack(both), bf16), core, 0, False)
    return pick(column), pick(inverse), jnp.asarray(rows, bf16)


def spread_weight(re, im):
    def at(block, top, left):
        return jnp.pad(block, ((top, PADC - BS), (left, PADC - BS)))

    pad = lambda m: jnp.pad(m, ((0, PADC - BS), (0, PADC - BS)))
    re, im = pad(re), pad(im)
    return jnp.concatenate(
        [jnp.concatenate([re, im], axis=1), jnp.concatenate([-im, re], axis=1)], axis=0
    )


def spread_bias(bias):
    return jnp.pad(bias, ((0, 0), (0, PADC - BS))).reshape(1, 2 * PADC)


def fold_weight(grad):
    a, b = grad[:BS, :BS], grad[PADC : PADC + BS, PADC : PADC + BS]
    c, d = grad[:BS, PADC : PADC + BS], grad[PADC : PADC + BS, :BS]
    return jnp.stack([a + b, c - d])


def fold_bias(grad):
    return jnp.stack([grad[:BS], grad[PADC : PADC + BS]])


RING = 8
GATHER_CUTS = (0, 640, 1280, 2112, 2944)
SUM_CUTS = (0, 640, 1280, 2128, 2960)


def ring_place(row):
    return jnp.where(row % 2 == 0, row // 2, 7 - row // 2)


def ring_row(spot):
    return jnp.where(spot < 4, 2 * spot, 2 * (7 - spot) + 1)


def gather_kernel(shard, flat, ring_s, ring_r, x_s, x_r, sib_s, sib_r, own_sem):
    row, me, core, sibling = place()
    x = me % 2
    spot = ring_place(row)
    beside = (row, (1 - x) * 2 + core)
    ahead = (ring_row((spot + 1) % RING), x * 2 + core)
    behind = (ring_row((spot + RING - 1) % RING), x * 2 + core)
    ways = (ahead, behind)
    barrier = pltpu.get_barrier_semaphore()
    for device in (ahead, behind, beside, sibling):
        pl.semaphore_signal(barrier, inc=1, device_id=device, device_id_type=MESH)

    def span(part):
        return GATHER_CUTS[part], GATHER_CUTS[part + 1] - GATHER_CUTS[part]

    def piece(source_spot, source_x, part):
        low, size = span(part)
        base = (ring_row(source_spot) * 4 + source_x * 2 + core) * CH
        return flat.at[pl.ds(pl.multiple_of(base + low, 16), size)]

    def mine(part):
        low, size = span(part)
        return shard.at[pl.ds(low, size)]

    def origin(hop, way):
        return (spot - hop + RING) % RING if way == 0 else (spot + hop) % RING

    def item(hop, way, what):
        part = way if what else 2 + way
        return origin(hop, way), (1 - x if what == 2 else x), part

    def ring(hop, way, what, first=False):
        to = piece(*item(hop, way, what))
        source = mine(item(hop, way, what)[2]) if first and what < 2 else to
        return remote(
            source, to, ring_s.at[what, way, hop], ring_r.at[what, way, hop], ways[way]
        )

    def cross(slot, way, first=False):
        if isinstance(slot, int) and slot == 8:
            to, source = piece(spot, x, way), mine(way)
        else:
            to = piece(origin(slot, way), x, 2 + way)
            source = mine(2 + way) if first else to
        return remote(source, to, x_s.at[way, slot], x_r.at[way, slot], beside)

    def share(where, slot, way, what):
        return remote(where, where, sib_s.at[what, way, slot], sib_r.at[what, way, slot], sibling)

    def from_beside(slot, way):
        if isinstance(slot, int) and slot == 8:
            return piece(spot, 1 - x, way)
        return piece(origin(slot, way), 1 - x, 2 + way)

    base = pl.multiple_of((row * 4 + x * 2 + core) * CH, 16)
    whole = flat.at[pl.ds(base, CH)]
    own = pltpu.make_async_copy(shard, whole, own_sem)
    own.start()
    pl.semaphore_wait(barrier, 4)
    for way in range(2):
        ring(0, way, 0, True).start()
        cross(8, way).start()
    for way in range(2):
        ring(0, way, 1, True).start()
        cross(0, way, True).start()
    given = remote(shard, whole, sib_s.at[3, 0, 9], sib_r.at[3, 0, 9], sibling)
    given.start()
    for way in range(2):
        cross(8, way).wait_recv()
        ring(0, way, 2).start()
        share(from_beside(8, way), 8, way, 3).start()

    def step(hop, carry):
        for what in range(3):
            for way in range(2):
                ring(hop - 1, way, what).wait_recv()

                @pl.when(hop < RING - 1)
                def _():
                    ring(hop, way, what).start()

                if what == 0:
                    cross(hop, way).start()
                share(piece(*item(hop, way, what)), hop - 1, way, what).start()
        for way in range(2):
            cross(hop - 1, way).wait_recv()
            share(from_beside(hop - 1, way), hop - 1, way, 3).start()
        return carry

    lax.fori_loop(1, RING, step, 0)
    for way in range(2):
        cross(RING - 1, way).wait_recv()
        share(from_beside(RING - 1, way), RING - 1, way, 3).start()
    own.wait()

    def settle(hop, carry):
        for way in range(2):
            for what in range(3):
                ring(hop, way, what).wait_send()
                share(piece(*item(hop + 1, way, what)), hop, way, what).wait()
        return carry

    lax.fori_loop(0, RING - 1, settle, 0)

    def settle_cross(slot, carry):
        for way in range(2):
            cross(slot, way).wait_send()
            share(from_beside(slot, way), slot, way, 3).wait()
        return carry

    lax.fori_loop(0, RING, settle_cross, 0)
    for way in range(2):
        cross(8, way).wait_send()
        share(from_beside(8, way), 8, way, 3).wait()
    given.wait()


def ag(shard):
    anywhere = pl.BlockSpec(memory_space=pl.ANY)
    dma = pltpu.SemaphoreType.DMA
    return pl.pallas_call(
        gather_kernel,
        out_shape=jax.ShapeDtypeStruct((32 * CH, 128), bf16),
        in_specs=[anywhere],
        out_specs=anywhere,
        scratch_shapes=[
            dma((3, 2, 7)),
            dma((3, 2, 7)),
            dma((2, 9)),
            dma((2, 9)),
            dma((4, 2, 10)),
            dma((4, 2, 10)),
            dma,
        ],
        compiler_params=pltpu.CompilerParams(collective_id=0, has_side_effects=True),
        name="gather_weights",
    )(shard)


def sum_kernel(
    grad, loss, total, stats,
    own, sib, xin, rin_b, rin_a, xlast, st_mine, st_sib, st_sum, st_all,
    own_s, sib_s, sib_r, x_s, x_r, last_s, last_r, ring_s, ring_r, tell_s, tell_r, pair_s, pair_r,
):
    row, me, core, sibling = place()
    x = me % 2
    spot = ring_place(row)
    beside = (row, (1 - x) * 2 + core)
    ahead = (ring_row((spot + 1) % RING), x * 2 + core)
    behind = (ring_row((spot + RING - 1) % RING), x * 2 + core)
    ways = (ahead, behind)
    barrier = greet_chips(me, core, sibling)
    sizes = [SUM_CUTS[k + 1] - SUM_CUTS[k] for k in range(4)]

    def owner(turn, way):
        return (spot - 1 - turn + 2 * RING) % RING if way == 0 else (spot + 1 + turn) % RING

    def source(turn, way, other_x, part, side):
        owner_x = (1 - x) if other_x else x
        base = (ring_row(owner(turn, way)) * 4 + owner_x * 2 + side) * OWN // 16 * 16
        return grad.at[pl.ds(pl.multiple_of(base + SUM_CUTS[part], 16), sizes[part])]

    def part_of(way, what):
        return way if what >= 2 else 2 + way

    def held(buf, turn, way, what):
        part = part_of(way, what)
        return buf.at[what % 2, turn, pl.ds(SUM_CUTS[part], sizes[part])]

    def load(turn, way, what):
        return pltpu.make_async_copy(
            source(turn, way, what % 2, part_of(way, what), core),
            held(own, turn, way, what),
            own_s.at[what, way, turn],
        )

    def give(turn, way, what):
        return remote(
            source(turn, way, what % 2, part_of(way, what), 1 - core),
            held(sib, turn, way, what),
            sib_s.at[what, way, turn],
            sib_r.at[what, way, turn],
            sibling,
        )

    def cross(turn, way):
        return remote(
            held(own, turn, way, 1),
            xin.at[turn, pl.ds(SUM_CUTS[2 + way] - SUM_CUTS[2], sizes[2 + way])],
            x_s.at[way, turn],
            x_r.at[way, turn],
            beside,
        )

    def got(way, slot, what):
        if what == 0:
            return rin_b.at[slot, pl.ds(SUM_CUTS[2 + way] - SUM_CUTS[2], sizes[2 + way])]
        return rin_a.at[what - 2, slot, pl.ds(SUM_CUTS[way], sizes[way])]

    def ring(turn, way, what, first=False):
        where = held(own, turn, way, what) if first else got(way, turn - 1, what)
        return remote(
            where,
            got(way, turn, what),
            ring_s.at[what, way, turn],
            ring_r.at[what, way, turn],
            ways[way],
        )

    order = (1, 2, 3, 0)

    def begin_own(turn, carry):
        for what in order:
            for way in range(2):
                load(turn, way, what).start()
        return carry

    def begin_sib(turn, carry):
        for what in order:
            for way in range(2):
                give(turn, way, what).start()
        return carry

    begin_own(0, 0)
    pl.semaphore_wait(barrier, CHIPS)
    begin_sib(0, 0)
    lax.fori_loop(1, RING, lambda t, c: begin_sib(t, begin_own(t, c)), 0)

    def both(turn, way, what):
        load(turn, way, what).wait()
        give(turn, way, what).wait_recv()
        return held(own, turn, way, what)[...].astype(f32) + held(sib, turn, way, what)[...].astype(f32)

    def send_across(turn):
        for way in range(2):
            held(own, turn, way, 1)[...] = both(turn, way, 1).astype(bf16)
            cross(turn, way).start()

    def across(turn, way):
        cross(turn, way).wait_recv()
        return xin[turn, pl.ds(SUM_CUTS[2 + way] - SUM_CUTS[2], sizes[2 + way])].astype(f32)

    send_across(0)
    for what in (2, 3):
        for way in range(2):
            held(own, 0, way, what)[...] = both(0, way, what).astype(bf16)
            ring(0, way, what, True).start()
    send_across(1)
    for way in range(2):
        held(own, 0, way, 0)[...] = (both(0, way, 0) + across(0, way)).astype(bf16)
        ring(0, way, 0, True).start()

    def step(turn, carry):
        send_across(turn + 1)
        for what in (2, 3, 0):
            for way in range(2):
                part = both(turn, way, what)
                if what == 0:
                    part = part + across(turn, way)
                ring(turn - 1, way, what, True).wait_recv()
                where = got(way, turn - 1, what)
                where[...] = (where[...].astype(f32) + part).astype(bf16)
                ring(turn, way, what).start()
        return carry

    lax.fori_loop(1, RING - 1, step, 0)
    last = RING - 1
    def to_beside(way):
        return remote(
            got(way, last - 1, 3),
            xlast.at[pl.ds(SUM_CUTS[way], sizes[way])],
            last_s.at[way],
            last_r.at[way],
            beside,
        )

    for way in range(2):
        part = both(last, way, 3)
        ring(last - 1, way, 3, True).wait_recv()
        where = got(way, last - 1, 3)
        where[...] = (where[...].astype(f32) + part).astype(bf16)
        to_beside(way).start()
    for what in (2, 0):
        for way in range(2):
            part = both(last, way, what)
            if what == 0:
                part = part + across(last, way)
            ring(last - 1, way, what, True).wait_recv()
            low = SUM_CUTS[part_of(way, what)]
            total[low : low + sizes[part_of(way, what)]] = got(way, last - 1, what)[...].astype(f32) + part
    for way in range(2):
        to_beside(way).wait_recv()
        low = SUM_CUTS[way]
        total[low : low + sizes[way]] += xlast[low : low + sizes[way]].astype(f32)

    first = ((row * 4 + x * 2 + core) * OWN) % 16
    rows = lax.broadcasted_iota(jnp.int32, (CHR, 128), 0)
    value = total[...]
    squares = jnp.where((rows >= first) & (rows < first + OWN), value * value, 0.0)
    st_mine[0:8] = jnp.sum(squares.reshape(CHR // 8, 8, 128), axis=0)
    st_mine[8:16] = loss[...]
    pair = remote(st_mine, st_sib, pair_s, pair_r, sibling)
    pair.start()
    pair.wait_recv()
    st_sum[...] = st_mine[...] + st_sib[...]
    st_all[me] = st_sum[...]

    def tell(k):
        return remote(
            st_sum, st_all.at[me], tell_s.at[k], tell_r.at[k],
            chip_device(lax.rem(me + k, CHIPS), core),
        )

    def tell_one(k, carry):
        tell(k).start()
        return carry

    lax.fori_loop(1, CHIPS, tell_one, 0)

    def settle(turn, carry):
        for way in range(2):
            for what in range(4):
                give(turn, way, what).wait_send()
            cross(turn, way).wait_send()

            @pl.when(turn < RING - 1)
            def _():
                for what in (0, 2, 3):
                    ring(turn, way, what, True).wait_send()

        return carry

    lax.fori_loop(0, RING, settle, 0)
    for way in range(2):
        to_beside(way).wait_send()

    def told(k, carry):
        tell(k).wait_recv()
        return carry

    lax.fori_loop(1, CHIPS, told, 0)
    everything = st_all[0]
    for k in range(1, CHIPS):
        everything = everything + st_all[k]
    stats[...] = everything

    def tell_done(k, carry):
        tell(k).wait_send()
        return carry

    lax.fori_loop(1, CHIPS, tell_done, 0)
    pair.wait_send()


def rs(grad, loss):
    vm, dma = pltpu.VMEM, pltpu.SemaphoreType.DMA
    first, second = SUM_CUTS[2], SUM_CUTS[4] - SUM_CUTS[2]
    shape = jax.ShapeDtypeStruct
    return pl.pallas_call(
        sum_kernel,
        out_shape=[shape((CHR, 128), f32), shape((16, 128), f32)],
        in_specs=[pl.BlockSpec(memory_space=pl.ANY), pl.BlockSpec(memory_space=vm)],
        out_specs=[pl.BlockSpec(memory_space=vm)] * 2,
        scratch_shapes=[
            vm((2, RING, CHR, 128), bf16),
            vm((2, RING, CHR, 128), bf16),
            vm((RING, second, 128), bf16),
            vm((RING - 1, second, 128), bf16),
            vm((2, RING - 1, first, 128), bf16),
            vm((first, 128), bf16),
            vm((16, 128), f32),
            vm((16, 128), f32),
            vm((16, 128), f32),
            vm((CHIPS, 16, 128), f32),
            dma((4, 2, RING)),
            dma((4, 2, RING)),
            dma((4, 2, RING)),
            dma((2, RING)),
            dma((2, RING)),
            dma((2,)),
            dma((2,)),
            dma((4, 2, RING - 1)),
            dma((4, 2, RING - 1)),
            dma((CHIPS,)),
            dma((CHIPS,)),
            dma,
            dma,
        ],
        compiler_params=pltpu.CompilerParams(
            collective_id=1, has_side_effects=True, vmem_limit_bytes=56 << 20
        ),
        name="sum_gradients",
    )(grad, loss)


CELLS = 2 * UNIT
FCHUNK = 768
FILTER_SEMS = 10


def norm_adjoint(values, gain, grad):
    normed, scale = normalize(values)
    inner = grad * gain
    along = jnp.mean(inner * normed, axis=-1, keepdims=True)
    flat = jnp.mean(inner, axis=-1, keepdims=True)
    return (
        scale * (inner - flat - normed * along),
        jnp.sum(grad * normed, axis=0, keepdims=True),
        jnp.sum(grad, axis=0, keepdims=True),
    )


def forward_kernel(*refs):
    (x0, goals, mask, weight, embed_b, norms, c1, c2, tail, head_b, column, inverse, rows,
     w1, b1, w2, b2, embed_h, in0, out0, in1, out1, head_h) = refs[:23]
    streams, waves_o, mixeds, normeds, befores, hiddens, lasts, tails, errors, x1, loss = refs[23:34]
    (embed, w_in, w_out, head, flow, x_now, s_stream, s_waves, s_mixed, s_norm, s_before, s_hidden,
     s_tail, s_error, weight_sem, out_sem, tail_sem) = refs[34:51]
    units, mine, others, waves, back, own_sum, to_sib, from_sib, ready, landed, joined = refs[51:62]
    sems = refs[62:]
    row, me, core, sibling = place()
    barrier = greet_chips(me, core, sibling)
    loads = [
        pltpu.make_async_copy(source, target, weight_sem.at[k])
        for k, (source, target) in enumerate(
            [(embed_h, embed), (in0, w_in.at[0]), (out0, w_out.at[0]), (in1, w_in.at[1]),
             (out1, w_out.at[1]), (head_h, head)]
        )
    ]
    for load in loads:
        load.start()
    x_now[...] = x0[...]
    loss[...] = jnp.zeros_like(loss)

    def saves(it):
        pairs = [(s_stream, streams), (s_waves, waves_o), (s_mixed, mixeds), (s_norm, normeds),
                 (s_before, befores), (s_hidden, hiddens)]
        return [
            pltpu.make_async_copy(source, target.at[it], out_sem.at[k])
            for k, (source, target) in enumerate(pairs)
        ]

    def tail_saves(step):
        pairs = [(flow, lasts), (s_tail, tails), (s_error, errors)]
        return [
            pltpu.make_async_copy(source, target.at[step], tail_sem.at[k])
            for k, (source, target) in enumerate(pairs)
        ]

    def when_it(cond, action):
        @pl.when(cond)
        def _():
            action()

    def body(it, carry):
        step, layer = it // 2, it % 2

        def start_step():
            flow[...] = dot(x_now[...], embed[...]) + embed_b[...]

        when_it(it == 0, loads[0].wait)

        def tail_done():
            for save in tail_saves(0):
                save.wait()

        when_it(it == 2, tail_done)
        when_it(layer == 0, start_step)

        def saved():
            for save in saves(it):
                save.wait()

        when_it(it > 0, saved)
        s_stream[...] = flow[...]
        normed, _ = normalize(flow[...])
        split_units(normed * norms[layer, 0:1] + norms[layer, 1:2], units)
        when_it(it == 0, lambda: pl.semaphore_wait(barrier, CHIPS))
        finish_one = spread_units(me, core, sibling, units, mine, others, sems[:5])
        groups = to_spectrum(mine, others, column, rows, waves)
        for g in range(4):
            s_waves[g] = groups[g]
            hidden = gelu_of(dot(groups[g], w1[layer]) + b1[layer]).astype(bf16)
            spec = (dot(hidden, w2[layer]) + b2[layer]).astype(bf16)
            from_spectrum(g, spec, rows, back)
        finish_two = gather_units(
            row, me, core, sibling, back, inverse,
            (own_sum, to_sib, from_sib, ready, landed), sems[5:], finish_one,
        )
        join_units(landed, joined)
        mixed = flow[...] + joined[...]
        s_mixed[...] = mixed
        normed, _ = normalize(mixed)
        s_norm[...] = (normed * norms[layer, 2:3] + norms[layer, 3:4]).astype(bf16)
        flow[...] = mixed + c2[layer]

        def first_layer():
            loads[1].wait()
            loads[2].wait()

        def second_layer():
            loads[3].wait()
            loads[4].wait()

        when_it(it == 0, first_layer)
        when_it(it == 1, second_layer)

        def chunk(c, carry):
            part = pl.ds(pl.multiple_of(c * FCHUNK, FCHUNK), FCHUNK)
            before = dot(s_norm[...], w_in[layer, :, part]) + c1[layer, :, part]
            s_before[:, part] = before.astype(bf16)
            hidden = gelu_of(before).astype(bf16)
            s_hidden[:, part] = hidden
            flow[...] += dot(hidden, w_out[layer, part, :])
            return carry

        lax.fori_loop(0, FF // FCHUNK, chunk, 0)
        for save in saves(it):
            save.start()
        finish_two()
        when_it(it == 1, loads[5].wait)

        def end_step():
            normed, _ = normalize(flow[...])
            s_tail[...] = (normed * tail[0:1] + tail[1:2]).astype(bf16)
            predicted = dot(s_tail[...], head[...]) + head_b[...]
            error = predicted - goals[step].astype(f32)
            s_error[...] = error
            loss[...] += weight[...] * jnp.sum(error * error, axis=-1, keepdims=True)
            x_now[...] = (predicted * mask[...]).astype(bf16)
            for save in tail_saves(step):
                save.start()

        when_it(layer == 1, end_step)
        when_it(it == 1, lambda: x1.__setitem__(Ellipsis, x_now[...]))
        return carry

    lax.fori_loop(0, 4, body, 0)
    for save in saves(3):
        save.wait()
    for save in tail_saves(1):
        save.wait()


def forward_pass(*args):
    vm, dma = pltpu.VMEM, pltpu.SemaphoreType.DMA
    whole, anywhere = pl.BlockSpec(memory_space=vm), pl.BlockSpec(memory_space=pl.ANY)
    shape = jax.ShapeDtypeStruct
    return pl.pallas_call(
        forward_kernel,
        out_shape=[
            shape((4, CELLS, D), f32),
            shape((4, 4, 256, 256), bf16),
            shape((4, CELLS, D), f32),
            shape((4, CELLS, D), bf16),
            shape((4, CELLS, FF), bf16),
            shape((4, CELLS, FF), bf16),
            shape((2, CELLS, D), f32),
            shape((2, CELLS, D), bf16),
            shape((2, CELLS, PIN), f32),
            shape((CELLS, PIN), bf16),
            shape((CELLS, 1), f32),
        ],
        in_specs=[whole] * 17 + [anywhere] * 6,
        out_specs=[anywhere] * 9 + [whole] * 2,
        scratch_shapes=[
            vm((PIN, D), bf16),
            vm((2, D, FF), bf16),
            vm((2, FF, D), bf16),
            vm((D, PIN), bf16),
            vm((CELLS, D), f32),
            vm((CELLS, PIN), bf16),
            vm((CELLS, D), f32),
            vm((4, 256, 256), bf16),
            vm((CELLS, D), f32),
            vm((CELLS, D), bf16),
            vm((CELLS, FF), bf16),
            vm((CELLS, FF), bf16),
            vm((CELLS, D), bf16),
            vm((CELLS, PIN), f32),
            dma((6,)),
            dma((6,)),
            dma((3,)),
        ]
        + filter_scratch(),
        compiler_params=pltpu.CompilerParams(
            collective_id=2, has_side_effects=True, vmem_limit_bytes=56 << 20
        ),
        name="forward_pass",
    )(*args)


def backward_kernel(*refs):
    (gscale, mask, norms, tail, column, inverse, rows, w1, b1, w2,
     embed_h, in0, out0, in1, out1, head_h,
     streams, waves_h, mixeds, befores, lasts, errors) = refs[:22]
    (g_pred, g_out, g_pre, g_embed, sum_norm, sum_c1, sum_tail, sum_head, grad_w1, grad_w2, grad_b) = refs[22:33]
    (embed, w_in, w_out, head, flow, carried, i_stream, i_waves, i_mixed, i_before, i_last, i_error,
     s_pred, s_out, s_pre, s_embed, g_norm, weight_sem, in_sem, tail_in, out_sem, tail_sem) = refs[33:55]
    units, mine, others, waves, back, own_sum, to_sib, from_sib, ready, landed, joined = refs[55:66]
    sems = refs[66:]
    row, me, core, sibling = place()
    barrier = greet_chips(me, core, sibling)

    def when_it(cond, action):
        @pl.when(cond)
        def _():
            action()

    loads = [
        pltpu.make_async_copy(source, target, weight_sem.at[k])
        for k, (source, target) in enumerate(
            [(head_h, head), (out1, w_out.at[1]), (in1, w_in.at[1]), (out0, w_out.at[0]),
             (in0, w_in.at[0]), (embed_h, embed)]
        )
    ]

    def inst(it):
        return 3 - it

    def fetch(it):
        slot = it % 2
        pairs = [(streams, i_stream), (waves_h, i_waves), (mixeds, i_mixed), (befores, i_before)]
        return [
            pltpu.make_async_copy(source.at[inst(it)], target.at[slot], in_sem.at[k, slot])
            for k, (source, target) in enumerate(pairs)
        ]

    tail_loads = [
        pltpu.make_async_copy(lasts, i_last, tail_in.at[0]),
        pltpu.make_async_copy(errors, i_error, tail_in.at[1]),
    ]
    for load in tail_loads:
        load.start()
    loads[0].start()
    for load in fetch(0):
        load.start()
    for load in loads[1:]:
        load.start()
    for target in (sum_norm, sum_c1, sum_tail, sum_head, grad_w1, grad_w2, grad_b, carried):
        target[...] = jnp.zeros_like(target)

    def saves(it):
        pairs = [(s_out, g_out), (s_pre, g_pre)]
        return [
            pltpu.make_async_copy(source, target.at[inst(it)], out_sem.at[k])
            for k, (source, target) in enumerate(pairs)
        ]

    def pred_save(step):
        return pltpu.make_async_copy(s_pred, g_pred.at[step], tail_sem.at[0])

    def embed_save(step):
        return pltpu.make_async_copy(s_embed, g_embed.at[step], tail_sem.at[1])

    def body(it, carry):
        step, layer, slot = 1 - it // 2, 1 - it % 2, it % 2

        def first():
            for load in tail_loads:
                load.wait()
            loads[0].wait()

        when_it(it == 0, first)
        when_it(it == 2, lambda: pred_save(1).wait())

        def head_adjoint():
            grad = i_error[step] * gscale[...] + carried[...]
            grad16 = grad.astype(bf16)
            s_pred[...] = grad16
            pred_save(step).start()
            sum_head[0:1] += jnp.sum(grad, axis=0, keepdims=True)
            back_n = dot_cols(grad16, head[...]).astype(bf16).astype(f32)
            value, gain, shift = norm_adjoint(i_last[step], tail[0:1], back_n)
            flow[...] = value
            sum_tail[0:1] += gain
            sum_tail[1:2] += shift

        when_it(layer == 1, head_adjoint)

        def prefetch():
            for load in fetch(it + 1):
                load.start()

        when_it(it < 3, prefetch)

        def saved():
            for save in saves(it):
                save.wait()

        when_it(it > 0, saved)
        s_out[...] = flow[...].astype(bf16)
        sum_norm[layer, 4:5] += jnp.sum(flow[...], axis=0, keepdims=True)
        for load in fetch(it):
            load.wait()

        def second_layer():
            loads[1].wait()
            loads[2].wait()

        def first_layer():
            loads[3].wait()
            loads[4].wait()

        when_it(it == 0, second_layer)
        when_it(it == 1, first_layer)
        g_norm[...] = jnp.zeros_like(g_norm)

        def chunk(c, carry):
            part = pl.ds(pl.multiple_of(c * FCHUNK, FCHUNK), FCHUNK)
            grad = dot_cols(s_out[...], w_out[layer, part, :]).astype(bf16).astype(f32)
            grad = grad * gelu_slope(i_before[slot, :, part].astype(f32))
            sum_c1[layer, 0:1, part] += jnp.sum(grad, axis=0, keepdims=True)
            grad16 = grad.astype(bf16)
            s_pre[:, part] = grad16
            g_norm[...] += dot_cols(grad16, w_in[layer, :, part])
            return carry

        lax.fori_loop(0, FF // FCHUNK, chunk, 0)
        for save in saves(it):
            save.start()
        value, gain, shift = norm_adjoint(
            i_mixed[slot], norms[layer, 2:3], g_norm[...].astype(bf16).astype(f32)
        )
        flow[...] += value
        sum_norm[layer, 2:3] += gain
        sum_norm[layer, 3:4] += shift
        split_units(flow[...], units)
        when_it(it == 0, lambda: pl.semaphore_wait(barrier, CHIPS))
        finish_one = spread_units(me, core, sibling, units, mine, others, sems[:5])
        groups = to_spectrum(mine, others, column, rows, waves)
        for g in range(4):
            before = dot(i_waves[slot, g], w1[layer]) + b1[layer]
            hidden = gelu_of(before).astype(bf16)
            grad_hidden = dot_cols(groups[g], w2[layer]).astype(bf16).astype(f32)
            grad_before = grad_hidden * gelu_slope(before)
            grad_before16 = grad_before.astype(bf16)
            grad_w2[layer] += dot_rows(hidden, groups[g])
            grad_w1[layer] += dot_rows(i_waves[slot, g], grad_before16)
            grad_b[layer, 0:1] += jnp.sum(grad_before, axis=0, keepdims=True)
            grad_b[layer, 1:2] += jnp.sum(groups[g].astype(f32), axis=0, keepdims=True)
            from_spectrum(g, dot_cols(grad_before16, w1[layer]).astype(bf16), rows, back)
        finish_two = gather_units(
            row, me, core, sibling, back, inverse,
            (own_sum, to_sib, from_sib, ready, landed), sems[5:], finish_one,
        )
        join_units(landed, joined)
        value, gain, shift = norm_adjoint(i_stream[slot], norms[layer, 0:1], joined[...])
        flow[...] += value
        sum_norm[layer, 0:1] += gain
        sum_norm[layer, 1:2] += shift
        when_it(it == 1, loads[5].wait)
        when_it(it == 3, lambda: embed_save(1).wait())

        def embed_adjoint():
            s_embed[...] = flow[...].astype(bf16)
            sum_tail[2:3] += jnp.sum(flow[...], axis=0, keepdims=True)
            embed_save(step).start()

        when_it(layer == 0, embed_adjoint)

        def carry_back():
            carried[...] = mask[...] * dot_cols(s_embed[...], embed[...]).astype(bf16).astype(f32)

        when_it(it == 1, carry_back)
        finish_two()
        return carry

    lax.fori_loop(0, 4, body, 0)
    for save in saves(3):
        save.wait()
    pred_save(0).wait()
    embed_save(0).wait()


def backward_pass(*args):
    vm, dma = pltpu.VMEM, pltpu.SemaphoreType.DMA
    whole, anywhere = pl.BlockSpec(memory_space=vm), pl.BlockSpec(memory_space=pl.ANY)
    shape = jax.ShapeDtypeStruct
    return pl.pallas_call(
        backward_kernel,
        out_shape=[
            shape((2, CELLS, PIN), bf16),
            shape((4, CELLS, D), bf16),
            shape((4, CELLS, FF), bf16),
            shape((2, CELLS, D), bf16),
            shape((2, 8, D), f32),
            shape((2, 8, FF), f32),
            shape((8, D), f32),
            shape((8, PIN), f32),
            shape((2, 256, 256), f32),
            shape((2, 256, 256), f32),
            shape((2, 8, 256), f32),
        ],
        in_specs=[whole] * 10 + [anywhere] * 12,
        out_specs=[anywhere] * 4 + [whole] * 7,
        scratch_shapes=[
            vm((PIN, D), bf16),
            vm((2, D, FF), bf16),
            vm((2, FF, D), bf16),
            vm((D, PIN), bf16),
            vm((CELLS, D), f32),
            vm((CELLS, PIN), f32),
            vm((2, CELLS, D), f32),
            vm((2, 4, 256, 256), bf16),
            vm((2, CELLS, D), f32),
            vm((2, CELLS, FF), bf16),
            vm((2, CELLS, D), f32),
            vm((2, CELLS, PIN), f32),
            vm((CELLS, PIN), bf16),
            vm((CELLS, D), bf16),
            vm((CELLS, FF), bf16),
            vm((CELLS, D), bf16),
            vm((CELLS, D), f32),
            dma((6,)),
            dma((4, 2)),
            dma((2,)),
            dma((2,)),
            dma((2,)),
        ]
        + filter_scratch(),
        compiler_params=pltpu.CompilerParams(
            collective_id=3, has_side_effects=True, vmem_limit_bytes=56 << 20
        ),
        name="backward_pass",
    )(*args)


MATS = [(PIN, D), (D, FF), (FF, D), (D, FF), (FF, D), (D, PIN)]
SMALL_LAYER = 2352
SMALLS = [6 + SMALL_LAYER, 24, 6 + SMALL_LAYER, 24, 18, 10]
PIECE = 256


def flat_sections():
    at = 0
    found = []
    for (depth, cols), small in zip(MATS, SMALLS):
        per_row = cols // LANES
        found.append((at, depth, per_row, at + depth * per_row, small))
        at += depth * per_row + small
    return found


def piece_rows(depth, per_row):
    rows = depth
    while rows * per_row > 7680:
        rows -= PIECE
        while depth % rows:
            rows -= PIECE
    return rows


def unpack_kernel(flat, *refs):
    mats, smalls = refs[:6], refs[6:12]
    raw, wide, out24, out6, out10, in_sem, out_sem = refs[12:]
    outs = {24: out24, 6: out6, 10: out10}
    steps = []
    for i, (start, depth, per_row, small_at, small) in enumerate(flat_sections()):
        rows = piece_rows(depth, per_row)
        for top in range(0, depth, rows):
            steps.append((i, start + top * per_row, rows * per_row, per_row, top, rows))
        steps.append((i, small_at, small, 0, 0, 0))

    def fetch(n):
        _, at, count, *_ = steps[n]
        low = at // 16 * 16
        size = -(-(at + count - low) // 16) * 16
        return pltpu.make_async_copy(
            flat.at[pl.ds(low, size)], raw.at[n % 2, pl.ds(0, size)], in_sem.at[n % 2]
        ), size

    fetch(0)[0].start()
    pending = {}
    for n, (i, at, count, per_row, top, rows) in enumerate(steps):
        if n + 1 < len(steps):
            fetch(n + 1)[0].start()
        copy, size = fetch(n)
        copy.wait()
        wide[0:size] = raw[n % 2, 0:size].astype(f32)
        shift = at % 16
        if not per_row:
            smalls[i][0:count] = wide[shift : shift + count]
            continue
        out = outs[per_row]
        if per_row in pending:
            pending.pop(per_row).wait()
        for part in range(0, rows, PIECE):
            for j in range(per_row):
                out[part : part + PIECE, j * LANES : (j + 1) * LANES] = wide[
                    pl.ds(shift + part * per_row + j, PIECE, stride=per_row), :
                ].astype(bf16)
        done = pltpu.make_async_copy(
            out.at[pl.ds(0, rows)], mats[i].at[pl.ds(top, rows)], out_sem.at[(24, 6, 10).index(per_row)]
        )
        done.start()
        pending[per_row] = done
    for done in pending.values():
        done.wait()


def unpack_flat(flat):
    vm, anywhere = pltpu.VMEM, pl.BlockSpec(memory_space=pl.ANY)
    shape = jax.ShapeDtypeStruct
    padded = [-(-count // 8) * 8 for count in SMALLS]
    return pl.pallas_call(
        unpack_kernel,
        out_shape=[shape(m, bf16) for m in MATS] + [shape((n, LANES), f32) for n in padded],
        in_specs=[anywhere],
        out_specs=[anywhere] * 6 + [pl.BlockSpec(memory_space=vm)] * 6,
        scratch_shapes=[
            vm((2, 7696, LANES), bf16),
            vm((7696, LANES), f32),
            vm((256, FF), bf16),
            vm((1280, D), bf16),
            vm((768, PIN), bf16),
            pltpu.SemaphoreType.DMA((2,)),
            pltpu.SemaphoreType.DMA((3,)),
        ],
        compiler_params=pltpu.CompilerParams(vmem_limit_bytes=48 << 20),
        name="unpack_flat",
    )(flat)


def pack_kernel(counts, *refs):
    pairs = [refs[4 * i : 4 * i + 4] for i in range(6)]
    smalls, rest = [], refs[24:]
    for number in counts:
        smalls.append(rest[:number])
        rest = rest[number:]
    flat, across, side, wide, narrow, sem = rest
    pending = []

    def emit(at, full):
        return pltpu.make_async_copy(narrow.at[pl.ds(0, full)], flat.at[pl.ds(at, full)], sem)

    for i, (start, depth, per_row, small_at, small) in enumerate(flat_sections()):
        x0, x1, g0, g1 = pairs[i]
        cols = per_row * LANES
        for half, (x, g) in enumerate(((x0, g0), (x1, g1))):
            for part in range(0, depth, PIECE):
                across[part : part + PIECE, half * 128 : half * 128 + 128] = x[
                    :, part : part + PIECE
                ].T
            side[half * 128 : half * 128 + 128, 0:cols] = g[...]
        rows = piece_rows(depth, per_row)
        full = rows * per_row
        shift = start % 16
        before = pending.pop() if pending else None

        def step(it, carry):
            top = pl.multiple_of(it * rows, PIECE)
            for part in range(0, rows, PIECE):
                left = across[pl.ds(pl.multiple_of(top + part, PIECE), PIECE), :]
                for j in range(0, per_row, 2):
                    value = dot(left, side[:, j * LANES : (j + 2) * LANES])
                    for side_by in range(2):
                        wide[
                            pl.ds(shift + part * per_row + j + side_by, PIECE, stride=per_row), :
                        ] = value[:, side_by * LANES : (side_by + 1) * LANES]
            if before is not None:
                @pl.when(it == 0)
                def _():
                    before.wait()

            @pl.when(it > 0)
            def _():
                emit(0, full).wait()

            narrow[0:full] = wide[0:full].astype(bf16)
            emit(pl.multiple_of(start - shift + it * full, 16), full).start()
            wide[0:16] = wide[full : full + 16]
            return carry

        lax.fori_loop(0, depth // rows, step, 0)
        shift = small_at % 16
        into = shift
        for piece in smalls[i]:
            wide[into : into + piece.shape[0]] = piece[...]
            into += piece.shape[0]
        full = (shift + small) // 16 * 16
        if i == 5:
            wide[shift + small : GROWS - small_at + shift] = jnp.zeros(
                (GROWS - small_at - small, LANES), f32
            )
            full = GROWS - small_at + shift
        emit(0, rows * per_row).wait()
        narrow[0:full] = wide[0:full].astype(bf16)
        done = emit(small_at - shift, full)
        done.start()
        pending.append(done)
        if i < 5:
            wide[0:16] = wide[full : full + 16]
    pending.pop().wait()


def pack_flat(pairs, smalls):
    vm, whole = pltpu.VMEM, pl.BlockSpec(memory_space=pltpu.VMEM)
    args = [a for four in pairs for a in four] + [a for some in smalls for a in some]
    return pl.pallas_call(
        functools.partial(pack_kernel, [len(some) for some in smalls]),
        out_shape=jax.ShapeDtypeStruct((GROWS, LANES), bf16),
        in_specs=[whole] * len(args),
        out_specs=pl.BlockSpec(memory_space=pl.ANY),
        scratch_shapes=[
            vm((FF, 256), bf16),
            vm((256, FF), bf16),
            vm((7712, LANES), f32),
            vm((7712, LANES), bf16),
            pltpu.SemaphoreType.DMA,
        ],
        compiler_params=pltpu.CompilerParams(vmem_limit_bytes=52 << 20),
        name="pack_flat",
    )(*args)


def split_small(rows, layouts):
    found, at = [], 0
    for layout in layouts:
        count = math.prod(layout) // LANES
        found.append(rows[at : at + count].reshape(layout))
        at += count
    return found


SPEC_ROWS = (2, NBLK, BS * BS // LANES, LANES)
LAYER_SMALL = [(D,), (D,), SPEC_ROWS, (2, NBLK, BS), SPEC_ROWS, (2, NBLK, BS), (D,), (D,)]


def local_fast(frames, targets, regions, master, first_moment, second_moment):
    height, width = 16, 128
    device = lax.axis_index("row") * 4 + lax.axis_index("col")
    _, chip, core, _ = place()
    block = chip % NBLK
    shard = master.astype(bf16).reshape(OWN, LANES)
    halo = lax.ppermute(shard[:320], ("row", "col"), [(k + 1, k) for k in range(31)])
    chunk = lax.dynamic_slice_in_dim(jnp.concatenate([shard, halo]), 10 * device, CH, 0)
    unpacked = unpack_flat(ag(chunk))
    embed, in0, out0, in1, out1, head = unpacked[:6]
    smalls = unpacked[6:]
    embed_bias, *layer0 = split_small(smalls[0], [(D,)] + LAYER_SMALL)
    (c1_0,) = split_small(smalls[1], [(FF,)])
    c2_0, *layer1 = split_small(smalls[2], [(D,)] + LAYER_SMALL)
    (c1_1,) = split_small(smalls[3], [(FF,)])
    c2_1, gain3, shift3 = split_small(smalls[4], [(D,)] * 3)
    (head_bias,) = split_small(smalls[5], [(PIN,)])
    layers = [(layer0, in0, c1_0, out0, c2_0), (layer1, in1, c1_1, out1, c2_1)]
    tables = transform_tables(core)
    row_ids = lax.axis_index("row") * 2 + jnp.arange(2, dtype=jnp.int32)
    col_ids = lax.axis_index("col") * 32 + jnp.arange(32, dtype=jnp.int32)
    cell_masks = region_masks(regions, row_ids, col_ids, width)
    weighted = latitude(row_ids, height)[None, :, None] * cell_masks
    every_row = jnp.arange(height, dtype=jnp.int32)
    every_col = jnp.arange(width, dtype=jnp.int32)
    total_weight = (
        jnp.sum(
            latitude(every_row, height)[None, :, None]
            * region_masks(regions, every_row, every_col, width)
        )
        * STEPS
    )
    flat_mask = cell_masks.reshape(128, 1)
    flat_weight = weighted.reshape(128, 1)
    inputs = (frames.reshape(128, PIN).astype(f32) * flat_mask).astype(bf16)
    goals = jnp.stack([targets[:, s].reshape(128, PIN) for s in range(STEPS)])
    spectral_weights = []
    for small, *_ in layers:
        found = []
        for j in (2, 4):
            w = lax.dynamic_index_in_dim(small[j], block, 1, False).reshape(2, BS, BS)
            b = lax.dynamic_index_in_dim(small[j + 1], block, 1, False)
            found += [spread_weight(w[0], w[1]).astype(bf16), spread_bias(b)]
        spectral_weights.append(found)
    w1, b1, w2, b2 = (jnp.stack(both) for both in zip(*spectral_weights))
    norms = jnp.stack([jnp.stack([small[k] for k in (0, 1, 6, 7)]) for small, *_ in layers])
    tail = jnp.stack([gain3, shift3])
    mats = (embed, in0, out0, in1, out1, head)
    streams, waves, mixeds, normeds, befores, hiddens, lasts, tails, errors, x1, loss = forward_pass(
        inputs, goals, flat_mask, flat_weight, embed_bias[None], norms,
        jnp.stack([c1_0, c1_1])[:, None], jnp.stack([c2_0, c2_1])[:, None], tail, head_bias[None],
        *tables, w1, b1, w2, b2, *mats,
    )
    (g_pred, g_out, g_pre, g_embed, sum_norm, sum_c1, sum_tail, sum_head, grad_w1, grad_w2, grad_b) = (
        backward_pass(
            flat_weight * (2.0 / total_weight), flat_mask, norms, tail, *tables, w1, b1, w2, *mats,
            streams, waves, mixeds, befores, lasts, errors,
        )
    )
    pairs = [[inputs, x1, g_embed[0], g_embed[1]]]
    for idx in range(LAYERS):
        pairs.append([normeds[idx], normeds[2 + idx], g_pre[idx], g_pre[2 + idx]])
        pairs.append([hiddens[idx], hiddens[2 + idx], g_out[idx], g_out[2 + idx]])
    pairs.append([tails[0], tails[1], g_pred[0], g_pred[1]])

    def as_rows(value):
        return value.reshape(-1, LANES)

    def placed(local_grad):
        local_grad = local_grad.reshape(2, 1, -1)
        whole = jnp.zeros((2, NBLK, local_grad.shape[2]), f32)
        return as_rows(lax.dynamic_update_slice_in_dim(whole, local_grad, block, 1))

    def layer_rows(idx):
        gb = grad_b[idx]
        return [
            as_rows(sum_norm[idx, 0]),
            as_rows(sum_norm[idx, 1]),
            placed(fold_weight(grad_w1[idx])),
            placed(fold_bias(gb[0])),
            placed(fold_weight(grad_w2[idx])),
            placed(fold_bias(gb[1])),
            as_rows(sum_norm[idx, 2]),
            as_rows(sum_norm[idx, 3]),
        ]

    small_grads = [
        [as_rows(sum_tail[2])] + layer_rows(0),
        [as_rows(sum_c1[0, 0])],
        [as_rows(sum_norm[0, 4])] + layer_rows(1),
        [as_rows(sum_c1[1, 0])],
        [as_rows(v) for v in (sum_norm[1, 4], sum_tail[0], sum_tail[1])],
        [as_rows(sum_head[0])],
    ]
    flat_grad = pack_flat(pairs, small_grads)
    loss_tile = jnp.concatenate([loss.reshape(1, LANES), jnp.zeros((7, LANES), f32)])
    summed, stats = rs(flat_grad, loss_tile)
    reduced = lax.dynamic_slice_in_dim(summed, (device * OWN) % 16, OWN, 0).reshape(-1)
    grad_norm = jnp.sqrt(jnp.sum(stats[:8]))
    return finish_step(
        reduced, grad_norm, master, first_moment, second_moment, jnp.sum(stats[8:]), total_weight
    )


def finish_step(reduced, grad_norm, master, first_moment, second_moment, loss_all, total_weight):
    clipped = reduced * (CLIP / jnp.maximum(grad_norm, CLIP))
    first_out = BETA_ONE * first_moment + (1.0 - BETA_ONE) * clipped
    second_out = BETA_TWO * second_moment + (1.0 - BETA_TWO) * clipped * clipped
    corrected_one = first_out / (1.0 - BETA_ONE**ADAM_STEP)
    corrected_two = second_out / (1.0 - BETA_TWO**ADAM_STEP)
    master_out = master - RATE * (
        corrected_one / (jnp.sqrt(corrected_two) + ADAM_EPS) + DECAY * master
    )
    return (
        master_out,
        first_out,
        second_out,
        master_out.astype(bf16),
        loss_all,
        total_weight,
        grad_norm,
    )


def local(frames, targets, regions, master, first_moment, second_moment):
    row_devices = lax.axis_size("row")
    col_devices = lax.axis_size("col")
    local_rows = frames.shape[1]
    local_cols = frames.shape[2]
    height = local_rows * row_devices
    width = local_cols * col_devices
    weights = lax.all_gather(master.astype(jnp.bfloat16), ("row", "col"), axis=0, tiled=True)
    pieces16 = unpack(weights)
    pieces = unpack(weights.astype(jnp.float32))
    tail_params = pieces[2 + 12 * LAYERS :]
    tail16 = pieces16[2 + 12 * LAYERS :]
    tables = (
        dft_tables(width, -1.0),
        dft_tables(height, -1.0),
        dft_tables(width, 1.0),
        dft_tables(height, 1.0),
    )
    row_ids = lax.axis_index("row") * local_rows + jnp.arange(local_rows, dtype=jnp.int32)
    col_ids = lax.axis_index("col") * local_cols + jnp.arange(local_cols, dtype=jnp.int32)
    cell_masks = region_masks(regions, row_ids, col_ids, width)
    weighted = latitude(row_ids, height)[None, :, None] * cell_masks
    every_row = jnp.arange(height, dtype=jnp.int32)
    every_col = jnp.arange(width, dtype=jnp.int32)
    total_weight = (
        jnp.sum(
            latitude(every_row, height)[None, :, None]
            * region_masks(regions, every_row, every_col, width)
        )
        * STEPS
    )
    inputs = frames.astype(jnp.float32) * cell_masks[..., None]
    loss_sum = jnp.zeros((), jnp.float32)
    history = []
    for roll_step in range(STEPS):
        stream = linear_forward(inputs, pieces16[0], pieces[1])
        saved_layers = []
        for layer_idx in range(LAYERS):
            span = slice(2 + 12 * layer_idx, 14 + 12 * layer_idx)
            stream, saved = layer_forward(stream, pieces[span], pieces16[span], tables)
            saved_layers.append(saved)
        normed = rounded(layer_norm(stream, tail_params[0], tail_params[1]))
        predicted = linear_forward(normed, tail16[2], tail_params[3])
        errors = predicted - targets[:, roll_step].astype(jnp.float32)
        loss_sum = loss_sum + jnp.sum(weighted * jnp.sum(errors * errors, axis=-1))
        history.append((inputs, saved_layers, stream, normed, errors))
        inputs = rounded(predicted * cell_masks[..., None])
    loss_all = lax.psum(loss_sum, ("row", "col"))
    gradients = [jnp.zeros_like(piece) for piece in pieces]
    carried = jnp.zeros_like(inputs)
    for roll_step in reversed(range(STEPS)):
        inputs, saved_layers, stream, normed, errors = history[roll_step]
        grad_pred = 2.0 * weighted[..., None] * errors / total_weight + carried
        grad_normed, grad_head, grad_hbias = linear_backward(grad_pred, normed, tail16[2])
        _, pullback = jax.vjp(layer_norm, stream, tail_params[0], tail_params[1])
        grad_stream, grad_gain3, grad_shift3 = pullback(rounded(grad_normed))
        gradients = add_into(
            gradients, 2 + 12 * LAYERS, [grad_gain3, grad_shift3, grad_head, grad_hbias]
        )
        for layer_idx in reversed(range(LAYERS)):
            span = slice(2 + 12 * layer_idx, 14 + 12 * layer_idx)
            grad_stream, layer_grads = layer_backward(
                grad_stream, saved_layers[layer_idx], pieces[span], pieces16[span], tables
            )
            gradients = add_into(gradients, 2 + 12 * layer_idx, layer_grads)
        grad_inputs, grad_embed, grad_ebias = linear_backward(grad_stream, inputs, pieces16[0])
        gradients = add_into(gradients, 0, [grad_embed, grad_ebias])
        carried = cell_masks[..., None] * rounded(grad_inputs)
    flat_grad = jnp.concatenate([piece.ravel() for piece in gradients])
    padding = master.shape[0] * row_devices * col_devices - flat_grad.shape[0]
    flat_grad = jnp.concatenate([flat_grad, jnp.zeros((padding,), jnp.float32)])
    grad_table = flat_grad.reshape(-1, LANES)
    reduced = lax.psum_scatter(grad_table, ("row", "col"), scatter_dimension=0, tiled=True).reshape(
        -1
    )
    squares = jnp.sum(reduced * reduced)
    square_all = lax.psum(squares, ("row", "col"))
    grad_norm = jnp.sqrt(square_all)
    clipped = reduced * (CLIP / jnp.maximum(grad_norm, CLIP))
    first_out = BETA_ONE * first_moment + (1.0 - BETA_ONE) * clipped
    second_out = BETA_TWO * second_moment + (1.0 - BETA_TWO) * clipped * clipped
    corrected_one = first_out / (1.0 - BETA_ONE**ADAM_STEP)
    corrected_two = second_out / (1.0 - BETA_TWO**ADAM_STEP)
    master_out = master - RATE * (
        corrected_one / (jnp.sqrt(corrected_two) + ADAM_EPS) + DECAY * master
    )
    return (
        master_out,
        first_out,
        second_out,
        master_out.astype(jnp.bfloat16),
        loss_all,
        total_weight,
        grad_norm,
    )


def solution(mesh):
    in_specs = (
        P(None, "row", "col", None),
        P(None, None, "row", "col", None),
        P(),
        P(("row", "col")),
        P(("row", "col")),
        P(("row", "col")),
    )
    out_specs = (
        P(("row", "col")),
        P(("row", "col")),
        P(("row", "col")),
        P(("row", "col")),
        P(),
        P(),
        P(),
    )
    body = local_fast if dict(mesh.shape) == {"row": 8, "col": 4} else local
    return jax.shard_map(body, mesh=mesh, in_specs=in_specs, out_specs=out_specs, check_vma=False)
```

```python
import functools
import math

import jax
import jax.numpy as jnp
import numpy as np
from jax import lax
from jax.sharding import PartitionSpec as P
from jax.experimental import pallas as pl
from jax.experimental.pallas import tpu as pltpu

D = 768
FF = 3072
NBLK = 8
BS = 96
PIN = 1280
LAYERS = 2
STEPS = 2
ADAM_STEP = 5


highest = lax.Precision.HIGHEST
NORM_EPS = 1e-05
BETA_ONE = 0.9
BETA_TWO = 0.95
ADAM_EPS = 1e-08
RATE = 0.03
DECAY = 0.05
CLIP = 0.2
LANES = 128


def block_shapes():
    return [
        (D,),
        (D,),
        (2, NBLK, BS, BS),
        (2, NBLK, BS),
        (2, NBLK, BS, BS),
        (2, NBLK, BS),
        (D,),
        (D,),
        (D, FF),
        (FF,),
        (FF, D),
        (D,),
    ]


def all_shapes():
    return [(PIN, D), (D,)] + block_shapes() * LAYERS + [(D,), (D,), (D, PIN), (PIN,)]


def unpack(flat_vec):
    pieces = []
    offset = 0
    for layout in all_shapes():
        length = math.prod(layout)
        pieces.append(flat_vec[offset : offset + length].reshape(layout))
        offset += length
    return pieces


def rounded(value):
    return lax.optimization_barrier(value.astype(jnp.bfloat16)).astype(jnp.float32)


def mult(form, left, right):
    return jnp.einsum(
        form,
        left.astype(jnp.bfloat16),
        right.astype(jnp.bfloat16),
        preferred_element_type=jnp.float32,
    )


def mult_exact(form, grad_value, other):
    upper = grad_value.astype(jnp.bfloat16)
    lower = (grad_value - upper.astype(jnp.float32)).astype(jnp.bfloat16)
    return mult(form, upper, other) + mult(form, lower, other)


def layer_norm(values, gain_vec, shift_vec):
    center = values - jnp.mean(values, axis=-1, keepdims=True)
    spread = jnp.mean(center * center, axis=-1, keepdims=True)
    return center * lax.rsqrt(spread + NORM_EPS) * gain_vec + shift_vec


def dft_tables(length, direction):
    positions = jnp.arange(length, dtype=jnp.int32)
    phases = (positions[:, None] * positions[None, :] % length).astype(jnp.float32) * (
        2.0 * math.pi / length
    )
    factor = 1.0 / math.sqrt(length)
    return (jnp.cos(phases) * factor, direction * jnp.sin(phases) * factor)


def apply_pair(tables, real_part, imag_part, form):

    def contract(table, values):
        return jnp.einsum(form, table, values, precision=highest)

    return (
        contract(tables[0], real_part) - contract(tables[1], imag_part),
        contract(tables[1], real_part) + contract(tables[0], imag_part),
    )


def spectral(real_part, imag_part, weight, bias_vec):
    blocks = (weight.shape[1], weight.shape[2])
    block_re = real_part.reshape(real_part.shape[:-1] + blocks)
    block_im = imag_part.reshape(imag_part.shape[:-1] + blocks)
    form = "...kb,kbc->...kc"
    out_re = (
        jnp.einsum(form, block_re, weight[0], precision=highest)
        - jnp.einsum(form, block_im, weight[1], precision=highest)
        + bias_vec[0]
    )
    out_im = (
        jnp.einsum(form, block_im, weight[0], precision=highest)
        + jnp.einsum(form, block_re, weight[1], precision=highest)
        + bias_vec[1]
    )
    return (out_re.reshape(real_part.shape), out_im.reshape(imag_part.shape))


def first_spectral(real_part, imag_part, weight, bias_vec):
    out_re, out_im = spectral(real_part, imag_part, weight, bias_vec)
    return (jax.nn.gelu(out_re, approximate=False), jax.nn.gelu(out_im, approximate=False))


def region_masks(regions, row_ids, col_ids, width):
    row_start = regions[:, 0, None, None]
    row_span = regions[:, 1, None, None]
    col_start = regions[:, 2, None, None]
    col_span = regions[:, 3, None, None]
    row_inside = (row_ids[None, :, None] >= row_start) & (
        row_ids[None, :, None] < row_start + row_span
    )
    col_inside = (col_ids[None, None, :] - col_start) % width < col_span
    return (row_inside & col_inside).astype(jnp.float32)


def latitude(row_ids, height):
    return jnp.cos(-1.3 + 1.3 * (row_ids.astype(jnp.float32) + 0.5) / height)


def linear_forward(values, weight16, bias_vec):
    return mult("brci,io->brco", values, weight16) + bias_vec


def linear_backward(grad_value, values, weight16):
    grad_values = mult_exact("brco,io->brci", grad_value, weight16)
    grad_weight = mult_exact("brco,brci->io", grad_value, values)
    return (grad_values, grad_weight, jnp.sum(grad_value, axis=(0, 1, 2)))


def spectrum(field, forward_w, forward_h):
    values = lax.all_to_all(field, "col", split_axis=3, concat_axis=2, tiled=True).astype(
        jnp.float32
    )
    real_part = jnp.einsum("kw,bnwc->bnkc", forward_w[0], values, precision=highest)
    imag_part = jnp.einsum("kw,bnwc->bnkc", forward_w[1], values, precision=highest)
    real_part, imag_part = apply_pair(
        forward_h,
        lax.all_to_all(
            real_part.astype(jnp.bfloat16), "row", split_axis=2, concat_axis=1, tiled=True
        ).astype(jnp.float32),
        lax.all_to_all(
            imag_part.astype(jnp.bfloat16), "row", split_axis=2, concat_axis=1, tiled=True
        ).astype(jnp.float32),
        "kh,bhwc->bkwc",
    )
    return (real_part.astype(jnp.bfloat16), imag_part.astype(jnp.bfloat16))


def grid(real_part, imag_part, inverse_w, inverse_h):
    back_re, back_im = apply_pair(
        inverse_h, real_part.astype(jnp.float32), imag_part.astype(jnp.float32), "kh,bhwc->bkwc"
    )
    values_re = lax.all_to_all(
        back_re.astype(jnp.bfloat16), "row", split_axis=1, concat_axis=2, tiled=True
    ).astype(jnp.float32)
    values_im = lax.all_to_all(
        back_im.astype(jnp.bfloat16), "row", split_axis=1, concat_axis=2, tiled=True
    ).astype(jnp.float32)
    result = jnp.einsum("kw,bnwc->bnkc", inverse_w[0], values_re, precision=highest) - jnp.einsum(
        "kw,bnwc->bnkc", inverse_w[1], values_im, precision=highest
    )
    columns_back = result.astype(jnp.bfloat16)
    return lax.all_to_all(columns_back, "col", split_axis=2, concat_axis=3, tiled=True)


def local_blocks(params):
    block_count = D // lax.axis_size("col") // BS
    first_block = lax.axis_index("col") * block_count
    chosen = [
        lax.dynamic_slice_in_dim(params[index_pos], first_block, block_count, 1)
        for index_pos in (2, 3, 4, 5)
    ]
    return (chosen, first_block)


def layer_forward(stream, params, params16, tables):
    gain_one, shift_one, _, _, _, _, gain_two, shift_two, _, bias_in, _, bias_out = params
    (local_w1, local_b1, local_w2, local_b2), _ = local_blocks(params)
    normed = layer_norm(stream, gain_one, shift_one).astype(jnp.bfloat16)
    wave_re, wave_im = spectrum(normed, tables[0], tables[1])
    hid_re, hid_im = first_spectral(
        wave_re.astype(jnp.float32), wave_im.astype(jnp.float32), local_w1, local_b1
    )
    hid_re, hid_im = (rounded(hid_re), rounded(hid_im))
    spec_re, spec_im = spectral(hid_re, hid_im, local_w2, local_b2)
    filtered = grid(
        spec_re.astype(jnp.bfloat16), spec_im.astype(jnp.bfloat16), tables[2], tables[3]
    )
    mixed = stream + filtered.astype(jnp.float32)
    normed_two = rounded(layer_norm(mixed, gain_two, shift_two))
    hidden = rounded(
        jax.nn.gelu(linear_forward(normed_two, params16[8], bias_in), approximate=False)
    )
    output = mixed + linear_forward(hidden, params16[10], bias_out)
    return (output, (stream, wave_re, wave_im, hid_re, hid_im, mixed, normed_two, hidden))


def place_blocks(local_grad, full_like, first_block):
    return lax.dynamic_update_slice_in_dim(jnp.zeros_like(full_like), local_grad, first_block, 1)


def layer_backward(grad_out, saved, params, params16, tables):
    stream, wave_re, wave_im, hid_re, hid_im, mixed, normed_two, hidden = saved
    (
        gain_one,
        shift_one,
        spec_w1,
        spec_b1,
        spec_w2,
        spec_b2,
        gain_two,
        shift_two,
        weight_in,
        bias_in,
        weight_out,
        bias_out,
    ) = params
    (local_w1, local_b1, local_w2, local_b2), first_block = local_blocks(params)
    grad_hidden, grad_wout, grad_bout = linear_backward(grad_out, hidden, params16[10])
    grad_mixed = grad_out
    before = linear_forward(normed_two, params16[8], bias_in)
    _, pullback = jax.vjp(lambda value: jax.nn.gelu(value, approximate=False), before)
    (grad_before,) = pullback(rounded(grad_hidden))
    grad_normed, grad_win, grad_bin = linear_backward(grad_before, normed_two, params16[8])
    _, pullback = jax.vjp(layer_norm, mixed, gain_two, shift_two)
    grad_extra, grad_gain2, grad_shift2 = pullback(rounded(grad_normed))
    grad_mixed = grad_mixed + grad_extra
    back_re, back_im = spectrum(grad_mixed.astype(jnp.bfloat16), tables[0], tables[1])
    _, pullback = jax.vjp(spectral, hid_re, hid_im, local_w2, local_b2)
    grad_hre, grad_him, grad_lw2, grad_lb2 = pullback(
        (back_re.astype(jnp.float32), back_im.astype(jnp.float32))
    )
    _, pullback = jax.vjp(
        first_spectral, wave_re.astype(jnp.float32), wave_im.astype(jnp.float32), local_w1, local_b1
    )
    grad_wre, grad_wim, grad_lw1, grad_lb1 = pullback((rounded(grad_hre), rounded(grad_him)))
    grad_first = grid(
        grad_wre.astype(jnp.bfloat16), grad_wim.astype(jnp.bfloat16), tables[2], tables[3]
    )
    _, pullback = jax.vjp(layer_norm, stream, gain_one, shift_one)
    grad_stream, grad_gain1, grad_shift1 = pullback(grad_first.astype(jnp.float32))
    layer_grads = [
        grad_gain1,
        grad_shift1,
        place_blocks(grad_lw1, spec_w1, first_block),
        place_blocks(grad_lb1, spec_b1, first_block),
        place_blocks(grad_lw2, spec_w2, first_block),
        place_blocks(grad_lb2, spec_b2, first_block),
        grad_gain2,
        grad_shift2,
        grad_win,
        grad_bin,
        grad_wout,
        grad_bout,
    ]
    return (grad_stream + grad_mixed, layer_grads)


def add_into(gradients, start, values):
    middle = [left + right for left, right in zip(gradients[start : start + len(values)], values)]
    return gradients[:start] + middle + gradients[start + len(values) :]


MESH = pl.DeviceIdType.MESH
CH = 2944
OWN = 2934
CHR = 2960
GROWS = 93904


CHIPS = 16
UNIT = 64
PADC = 128
f32 = jnp.float32
bf16 = jnp.bfloat16


def remote(src, dst, send_sem, recv_sem, device):
    return pltpu.make_async_remote_copy(
        src_ref=src,
        dst_ref=dst,
        send_sem=send_sem,
        recv_sem=recv_sem,
        device_id=device,
        device_id_type=MESH,
    )


def chip_device(chip, core):
    return chip // 2, (chip % 2) * 2 + core


def place():
    row = lax.axis_index("row")
    col = lax.axis_index("col")
    core = col % 2
    return row, row * 2 + col // 2, core, (row, col + 1 - 2 * core)


def greet_chips(me, core, sibling):
    barrier = pltpu.get_barrier_semaphore()

    def one(k, carry):
        pl.semaphore_signal(
            barrier,
            inc=1,
            device_id=chip_device(lax.rem(me + k, CHIPS), core),
            device_id_type=MESH,
        )
        return carry

    lax.fori_loop(1, CHIPS, one, 0)
    pl.semaphore_signal(barrier, inc=1, device_id=sibling, device_id_type=MESH)
    return barrier


def split_units(values, units):
    blank = jnp.zeros((UNIT, PADC - BS), f32)
    for part in range(2):
        for block in range(NBLK):
            piece = values[part * UNIT : (part + 1) * UNIT, block * BS : (block + 1) * BS]
            units[part * NBLK + block] = jnp.concatenate([piece, blank], axis=1).astype(bf16)


def join_units(units, joined):
    for part in range(2):
        for block in range(NBLK):
            joined[part * UNIT : (part + 1) * UNIT, block * BS : (block + 1) * BS] = units[
                part * NBLK + block, :, 0:BS
            ].astype(f32)


def normalize(values):
    center = values - jnp.mean(values, axis=-1, keepdims=True)
    spread = jnp.mean(center * center, axis=-1, keepdims=True)
    scale = lax.rsqrt(spread + NORM_EPS)
    return center * scale, scale


def gelu_of(value):
    return 0.5 * value * (1.0 + lax.erf(value * math.sqrt(0.5)))


def gelu_slope(value):
    bell = jnp.exp(-0.5 * value * value) * (1.0 / math.sqrt(2.0 * math.pi))
    return 0.5 * (1.0 + lax.erf(value * math.sqrt(0.5))) + value * bell


def dot(left, right):
    return jnp.dot(left, right, preferred_element_type=f32)


def dot_rows(left, right):
    return lax.dot_general(left, right, (((0,), (0,)), ((), ())), preferred_element_type=f32)


def dot_cols(left, right):
    return lax.dot_general(left, right, (((1,), (1,)), ((), ())), preferred_element_type=f32)


def spread_units(me, core, sibling, units, mine, others, sems, meanwhile):
    send_a, recv_a, send_f, recv_f, local_sem = sems

    def out(k):
        chip = lax.rem(me + k, CHIPS)
        return remote(
            units.at[chip], mine.at[me], send_a.at[k], recv_a.at[k], chip_device(chip, core)
        )

    def handed(k):
        chip = lax.rem(me + CHIPS - k, CHIPS)
        return remote(mine.at[chip], others.at[chip], send_f.at[k], recv_f.at[k], sibling)

    own = pltpu.make_async_copy(units.at[me], mine.at[me], local_sem)
    own.start()

    def begin(k, carry):
        out(k).start()
        return carry

    lax.fori_loop(1, CHIPS, begin, 0)
    meanwhile()
    own.wait()
    handed(0).start()

    def hand(k, carry):
        out(k).wait_recv()
        handed(k).start()
        return carry

    lax.fori_loop(1, CHIPS, hand, 0)

    def arrive(k, carry):
        handed(k).wait_recv()
        return carry

    lax.fori_loop(0, CHIPS, arrive, 0)

    def finish():
        def sent(k, carry):
            out(k).wait_send()
            return carry

        lax.fori_loop(1, CHIPS, sent, 0)

        def sent_on(k, carry):
            handed(k).wait_send()
            return carry

        lax.fori_loop(0, CHIPS, sent_on, 0)

    return finish


def to_spectrum(mine, others, column_table, row_table, waves):
    for h in range(16):
        pair, part = h // 2, pl.ds(32 * (h % 2), 32)
        cells = jnp.concatenate(
            [
                mine[2 * pair, part],
                mine[2 * pair + 1, part],
                others[2 * pair, part],
                others[2 * pair + 1, part],
            ],
            axis=0,
        )
        wave = dot(column_table[...], cells).astype(bf16)
        for g in range(4):
            rows = pl.ds(16 * h, 16)
            waves[g, rows, 0:PADC] = wave[16 * g : 16 * g + 16]
            waves[g, rows, PADC : 2 * PADC] = wave[64 + 16 * g : 80 + 16 * g]
    results = []
    for g in range(4):
        both = dot(row_table[...], waves[g])
        real = both[:256, :PADC] + both[256:, PADC:]
        imag = both[:256, PADC:] - both[256:, :PADC]
        results.append(jnp.concatenate([real, imag], axis=1).astype(bf16))
    return results


def from_spectrum(g, spec, row_table, back):
    both = dot(row_table[...], spec)
    real = (both[:256, :PADC] - both[256:, PADC:]).astype(bf16)
    imag = (both[:256, PADC:] + both[256:, :PADC]).astype(bf16)
    for h in range(16):
        back[h, 16 * g : 16 * g + 16] = real[16 * h : 16 * h + 16]
        back[h, 64 + 16 * g : 80 + 16 * g] = imag[16 * h : 16 * h + 16]


def gather_units(row, me, core, sibling, back, inverse_table, bufs, sems, settle, meanwhile):
    own_sum, to_sib, from_sib, ready, landed = bufs
    send_s, recv_s, send_b, recv_b, local_sem = sems

    def swap(pair):
        rows = pl.ds(2 * pair, 2)
        return remote(
            to_sib.at[rows], from_sib.at[rows], send_s.at[pair], recv_s.at[pair], sibling
        )

    def partial(j, carry):
        pair = lax.rem(row + 1 + j, 8)
        for half in range(2):
            sums = dot(inverse_table[...], back[2 * pair + half])
            part = pl.ds(32 * half, 32)
            for x in range(2):
                own_sum[2 * pair + x, part] = sums[32 * x : 32 * x + 32]
                to_sib[2 * pair + x, part] = sums[64 + 32 * x : 96 + 32 * x].astype(bf16)
        swap(pair).start()
        return carry

    lax.fori_loop(0, 8, partial, 0)
    settle()

    def home(chip, k):
        return remote(
            ready.at[chip], landed.at[me], send_b.at[k], recv_b.at[k], chip_device(chip, core)
        )

    own = pltpu.make_async_copy(ready.at[me], landed.at[me], local_sem)

    def total(j, carry):
        pair = lax.rem(row + 1 + j, 8)
        swap(pair).wait_recv()
        rows = pl.ds(2 * pair, 2)
        ready[rows] = (own_sum[rows] + from_sib[rows].astype(f32)).astype(bf16)
        for x in range(2):
            chip = 2 * pair + x
            k = lax.rem(chip - me + CHIPS, CHIPS)

            @pl.when(k != 0)
            def _():
                home(chip, k).start()

        return carry

    lax.fori_loop(0, 8, total, 0)
    own.start()
    meanwhile()

    def landed_all(k, carry):
        home(lax.rem(me + k, CHIPS), k).wait_recv()
        return carry

    lax.fori_loop(1, CHIPS, landed_all, 0)
    own.wait()

    def finish():
        def sent(k, carry):
            home(lax.rem(me + k, CHIPS), k).wait_send()
            return carry

        lax.fori_loop(1, CHIPS, sent, 0)

        def swapped(pair, carry):
            swap(pair).wait_send()
            return carry

        lax.fori_loop(0, 8, swapped, 0)

    return finish


def filter_scratch():
    vm = pltpu.VMEM
    dma = pltpu.SemaphoreType.DMA
    block = (CHIPS, UNIT, PADC)
    return [
        vm(block, bf16),
        vm(block, bf16),
        vm(block, bf16),
        vm((4, 256, 256), bf16),
        vm((16, 128, PADC), bf16),
        vm(block, f32),
        vm(block, bf16),
        vm(block, bf16),
        vm(block, bf16),
        vm(block, bf16),
        vm((2 * UNIT, D), f32),
        dma((CHIPS,)),
        dma((CHIPS,)),
        dma((CHIPS,)),
        dma((CHIPS,)),
        dma,
        dma((8,)),
        dma((8,)),
        dma((CHIPS,)),
        dma((CHIPS,)),
        dma,
    ]


def transform_tables(core):
    width, height = 128, 16
    order = []
    for side in range(2):
        cols = [[32 * (2 * x + (c if side == 0 else 1 - c)) + i for x in range(2) for i in range(32)] for c in range(2)]
        order.append(cols)
    column, inverse = [], []
    for c in range(2):
        cells = np.array(order[0][c] + order[1][c])
        waves = 64 * c + np.arange(64)
        angle = 2.0 * np.pi * (np.outer(waves, cells) % width) / width
        cos, sin = np.cos(angle) / np.sqrt(width), np.sin(angle) / np.sqrt(width)
        column.append(np.concatenate([cos, -sin], axis=0))
        inverse.append(np.concatenate([cos, -sin], axis=0).T)
    steps = np.arange(height)
    angle = 2.0 * np.pi * (np.outer(steps, steps) % height) / height
    eye = np.eye(16)
    rows = np.concatenate(
        [np.kron(np.cos(angle), eye), np.kron(np.sin(angle), eye)], axis=0
    ) / np.sqrt(height)
    pick = lambda both: lax.dynamic_index_in_dim(jnp.asarray(np.stack(both), bf16), core, 0, False)
    return pick(column), pick(inverse), jnp.asarray(rows, bf16)


RING = 8
GATHER_CUTS = (0, 640, 1280, 2112, 2944)
SUM_CUTS = (0, 640, 1280, 2128, 2960)


def ring_place(row):
    return jnp.where(row % 2 == 0, row // 2, 7 - row // 2)


def ring_row(spot):
    return jnp.where(spot < 4, 2 * spot, 2 * (7 - spot) + 1)


def gather_kernel(shard, flat, ring_s, ring_r, x_s, x_r, sib_s, sib_r, own_sem):
    row, me, core, sibling = place()
    x = me % 2
    spot = ring_place(row)
    beside = (row, (1 - x) * 2 + core)
    ahead = (ring_row((spot + 1) % RING), x * 2 + core)
    behind = (ring_row((spot + RING - 1) % RING), x * 2 + core)
    ways = (ahead, behind)
    barrier = pltpu.get_barrier_semaphore()
    for device in (ahead, behind, beside, sibling):
        pl.semaphore_signal(barrier, inc=1, device_id=device, device_id_type=MESH)

    def span(part):
        return GATHER_CUTS[part], GATHER_CUTS[part + 1] - GATHER_CUTS[part]

    def piece(source_spot, source_x, part):
        low, size = span(part)
        base = (ring_row(source_spot) * 4 + source_x * 2 + core) * CH
        return flat.at[pl.ds(pl.multiple_of(base + low, 16), size)]

    def mine(part):
        low, size = span(part)
        return shard.at[pl.ds(low, size)]

    def origin(hop, way):
        return (spot - hop + RING) % RING if way == 0 else (spot + hop) % RING

    def item(hop, way, what):
        part = way if what else 2 + way
        return origin(hop, way), (1 - x if what == 2 else x), part

    def ring(hop, way, what, first=False):
        to = piece(*item(hop, way, what))
        source = mine(item(hop, way, what)[2]) if first and what < 2 else to
        return remote(
            source, to, ring_s.at[what, way, hop], ring_r.at[what, way, hop], ways[way]
        )

    def cross(slot, way, first=False):
        if isinstance(slot, int) and slot == 8:
            to, source = piece(spot, x, way), mine(way)
        else:
            to = piece(origin(slot, way), x, 2 + way)
            source = mine(2 + way) if first else to
        return remote(source, to, x_s.at[way, slot], x_r.at[way, slot], beside)

    def share(where, slot, way, what):
        return remote(where, where, sib_s.at[what, way, slot], sib_r.at[what, way, slot], sibling)

    def from_beside(slot, way):
        if isinstance(slot, int) and slot == 8:
            return piece(spot, 1 - x, way)
        return piece(origin(slot, way), 1 - x, 2 + way)

    base = pl.multiple_of((row * 4 + x * 2 + core) * CH, 16)
    whole = flat.at[pl.ds(base, CH)]
    own = pltpu.make_async_copy(shard, whole, own_sem)
    own.start()
    pl.semaphore_wait(barrier, 4)
    for way in range(2):
        ring(0, way, 0, True).start()
        cross(8, way).start()
    for way in range(2):
        ring(0, way, 1, True).start()
        cross(0, way, True).start()
    given = remote(shard, whole, sib_s.at[3, 0, 9], sib_r.at[3, 0, 9], sibling)
    given.start()
    for way in range(2):
        cross(8, way).wait_recv()
        ring(0, way, 2).start()
        share(from_beside(8, way), 8, way, 3).start()

    def step(hop, carry):
        for what in range(3):
            for way in range(2):
                ring(hop - 1, way, what).wait_recv()

                @pl.when(hop < RING - 1)
                def _():
                    ring(hop, way, what).start()

                if what == 0:
                    cross(hop, way).start()
                share(piece(*item(hop, way, what)), hop - 1, way, what).start()
        for way in range(2):
            cross(hop - 1, way).wait_recv()
            share(from_beside(hop - 1, way), hop - 1, way, 3).start()
        return carry

    lax.fori_loop(1, RING, step, 0)
    for way in range(2):
        cross(RING - 1, way).wait_recv()
        share(from_beside(RING - 1, way), RING - 1, way, 3).start()
    own.wait()

    def settle(hop, carry):
        for way in range(2):
            for what in range(3):
                ring(hop, way, what).wait_send()
                share(piece(*item(hop + 1, way, what)), hop, way, what).wait()
        return carry

    lax.fori_loop(0, RING - 1, settle, 0)

    def settle_cross(slot, carry):
        for way in range(2):
            cross(slot, way).wait_send()
            share(from_beside(slot, way), slot, way, 3).wait()
        return carry

    lax.fori_loop(0, RING, settle_cross, 0)
    for way in range(2):
        cross(8, way).wait_send()
        share(from_beside(8, way), 8, way, 3).wait()
    given.wait()


def ag(shard):
    anywhere = pl.BlockSpec(memory_space=pl.ANY)
    dma = pltpu.SemaphoreType.DMA
    return pl.pallas_call(
        gather_kernel,
        out_shape=jax.ShapeDtypeStruct((32 * CH, 128), bf16),
        in_specs=[anywhere],
        out_specs=anywhere,
        scratch_shapes=[
            dma((3, 2, 7)),
            dma((3, 2, 7)),
            dma((2, 9)),
            dma((2, 9)),
            dma((4, 2, 10)),
            dma((4, 2, 10)),
            dma,
        ],
        compiler_params=pltpu.CompilerParams(collective_id=0, has_side_effects=True),
        name="gather_weights",
    )(shard)


def sum_kernel(
    grad, loss, total, stats,
    own, sib, xin, rin_b, rin_a, xlast, st_mine, st_sib, st_sum, st_all,
    own_s, sib_s, sib_r, x_s, x_r, last_s, last_r, ring_s, ring_r, tell_s, tell_r, pair_s, pair_r,
):
    row, me, core, sibling = place()
    x = me % 2
    spot = ring_place(row)
    beside = (row, (1 - x) * 2 + core)
    ahead = (ring_row((spot + 1) % RING), x * 2 + core)
    behind = (ring_row((spot + RING - 1) % RING), x * 2 + core)
    ways = (ahead, behind)
    barrier = greet_chips(me, core, sibling)
    sizes = [SUM_CUTS[k + 1] - SUM_CUTS[k] for k in range(4)]

    def owner(turn, way):
        return (spot - 1 - turn + 2 * RING) % RING if way == 0 else (spot + 1 + turn) % RING

    def source(turn, way, other_x, part, side):
        owner_x = (1 - x) if other_x else x
        base = (ring_row(owner(turn, way)) * 4 + owner_x * 2 + side) * OWN // 16 * 16
        return grad.at[pl.ds(pl.multiple_of(base + SUM_CUTS[part], 16), sizes[part])]

    def part_of(way, what):
        return way if what >= 2 else 2 + way

    def held(buf, turn, way, what):
        part = part_of(way, what)
        return buf.at[what % 2, turn, pl.ds(SUM_CUTS[part], sizes[part])]

    def load(turn, way, what):
        return pltpu.make_async_copy(
            source(turn, way, what % 2, part_of(way, what), core),
            held(own, turn, way, what),
            own_s.at[what, way, turn],
        )

    def give(turn, way, what):
        return remote(
            source(turn, way, what % 2, part_of(way, what), 1 - core),
            held(sib, turn, way, what),
            sib_s.at[what, way, turn],
            sib_r.at[what, way, turn],
            sibling,
        )

    def cross(turn, way):
        return remote(
            held(own, turn, way, 1),
            xin.at[turn, pl.ds(SUM_CUTS[2 + way] - SUM_CUTS[2], sizes[2 + way])],
            x_s.at[way, turn],
            x_r.at[way, turn],
            beside,
        )

    def got(way, slot, what):
        if what == 0:
            return rin_b.at[slot, pl.ds(SUM_CUTS[2 + way] - SUM_CUTS[2], sizes[2 + way])]
        return rin_a.at[what - 2, slot, pl.ds(SUM_CUTS[way], sizes[way])]

    def ring(turn, way, what, first=False):
        where = held(own, turn, way, what) if first else got(way, turn - 1, what)
        return remote(
            where,
            got(way, turn, what),
            ring_s.at[what, way, turn],
            ring_r.at[what, way, turn],
            ways[way],
        )

    order = (1, 2, 3, 0)

    def begin_own(turn, carry):
        for what in order:
            for way in range(2):
                load(turn, way, what).start()
        return carry

    def begin_sib(turn, carry):
        for what in order:
            for way in range(2):
                give(turn, way, what).start()
        return carry

    begin_own(0, 0)
    pl.semaphore_wait(barrier, CHIPS)
    begin_sib(0, 0)
    lax.fori_loop(1, RING, lambda t, c: begin_sib(t, begin_own(t, c)), 0)

    def both(turn, way, what):
        load(turn, way, what).wait()
        give(turn, way, what).wait_recv()
        return held(own, turn, way, what)[...].astype(f32) + held(sib, turn, way, what)[...].astype(f32)

    def send_across(turn):
        for way in range(2):
            held(own, turn, way, 1)[...] = both(turn, way, 1).astype(bf16)
            cross(turn, way).start()

    def across(turn, way):
        cross(turn, way).wait_recv()
        return xin[turn, pl.ds(SUM_CUTS[2 + way] - SUM_CUTS[2], sizes[2 + way])].astype(f32)

    send_across(0)
    for what in (2, 3):
        for way in range(2):
            held(own, 0, way, what)[...] = both(0, way, what).astype(bf16)
            ring(0, way, what, True).start()
    send_across(1)
    for way in range(2):
        held(own, 0, way, 0)[...] = (both(0, way, 0) + across(0, way)).astype(bf16)
        ring(0, way, 0, True).start()

    def step(turn, carry):
        send_across(turn + 1)
        for what in (2, 3, 0):
            for way in range(2):
                part = both(turn, way, what)
                if what == 0:
                    part = part + across(turn, way)
                ring(turn - 1, way, what, True).wait_recv()
                where = got(way, turn - 1, what)
                where[...] = (where[...].astype(f32) + part).astype(bf16)
                ring(turn, way, what).start()
        return carry

    lax.fori_loop(1, RING - 1, step, 0)
    last = RING - 1
    def to_beside(way):
        return remote(
            got(way, last - 1, 3),
            xlast.at[pl.ds(SUM_CUTS[way], sizes[way])],
            last_s.at[way],
            last_r.at[way],
            beside,
        )

    for way in range(2):
        part = both(last, way, 3)
        ring(last - 1, way, 3, True).wait_recv()
        where = got(way, last - 1, 3)
        where[...] = (where[...].astype(f32) + part).astype(bf16)
        to_beside(way).start()
    for what in (2, 0):
        for way in range(2):
            part = both(last, way, what)
            if what == 0:
                part = part + across(last, way)
            ring(last - 1, way, what, True).wait_recv()
            low = SUM_CUTS[part_of(way, what)]
            total[low : low + sizes[part_of(way, what)]] = got(way, last - 1, what)[...].astype(f32) + part
    for way in range(2):
        to_beside(way).wait_recv()
        low = SUM_CUTS[way]
        total[low : low + sizes[way]] += xlast[low : low + sizes[way]].astype(f32)

    first = ((row * 4 + x * 2 + core) * OWN) % 16
    rows = lax.broadcasted_iota(jnp.int32, (CHR, 128), 0)
    value = total[...]
    squares = jnp.where((rows >= first) & (rows < first + OWN), value * value, 0.0)
    st_mine[0:8] = jnp.sum(squares.reshape(CHR // 8, 8, 128), axis=0)
    st_mine[8:16] = loss[...]
    pair = remote(st_mine, st_sib, pair_s, pair_r, sibling)
    pair.start()
    pair.wait_recv()
    st_sum[...] = st_mine[...] + st_sib[...]
    st_all[me] = st_sum[...]

    def tell(k):
        return remote(
            st_sum, st_all.at[me], tell_s.at[k], tell_r.at[k],
            chip_device(lax.rem(me + k, CHIPS), core),
        )

    def tell_one(k, carry):
        tell(k).start()
        return carry

    lax.fori_loop(1, CHIPS, tell_one, 0)

    def settle(turn, carry):
        for way in range(2):
            for what in range(4):
                give(turn, way, what).wait_send()
            cross(turn, way).wait_send()

            @pl.when(turn < RING - 1)
            def _():
                for what in (0, 2, 3):
                    ring(turn, way, what, True).wait_send()

        return carry

    lax.fori_loop(0, RING, settle, 0)
    for way in range(2):
        to_beside(way).wait_send()

    def told(k, carry):
        tell(k).wait_recv()
        return carry

    lax.fori_loop(1, CHIPS, told, 0)
    everything = st_all[0]
    for k in range(1, CHIPS):
        everything = everything + st_all[k]
    stats[...] = everything

    def tell_done(k, carry):
        tell(k).wait_send()
        return carry

    lax.fori_loop(1, CHIPS, tell_done, 0)
    pair.wait_send()


def rs(grad, loss):
    vm, dma = pltpu.VMEM, pltpu.SemaphoreType.DMA
    first, second = SUM_CUTS[2], SUM_CUTS[4] - SUM_CUTS[2]
    shape = jax.ShapeDtypeStruct
    return pl.pallas_call(
        sum_kernel,
        out_shape=[shape((CHR, 128), f32), shape((16, 128), f32)],
        in_specs=[pl.BlockSpec(memory_space=pl.ANY), pl.BlockSpec(memory_space=vm)],
        out_specs=[pl.BlockSpec(memory_space=vm)] * 2,
        scratch_shapes=[
            vm((2, RING, CHR, 128), bf16),
            vm((2, RING, CHR, 128), bf16),
            vm((RING, second, 128), bf16),
            vm((RING - 1, second, 128), bf16),
            vm((2, RING - 1, first, 128), bf16),
            vm((first, 128), bf16),
            vm((16, 128), f32),
            vm((16, 128), f32),
            vm((16, 128), f32),
            vm((CHIPS, 16, 128), f32),
            dma((4, 2, RING)),
            dma((4, 2, RING)),
            dma((4, 2, RING)),
            dma((2, RING)),
            dma((2, RING)),
            dma((2,)),
            dma((2,)),
            dma((4, 2, RING - 1)),
            dma((4, 2, RING - 1)),
            dma((CHIPS,)),
            dma((CHIPS,)),
            dma,
            dma,
        ],
        compiler_params=pltpu.CompilerParams(
            collective_id=1, has_side_effects=True, vmem_limit_bytes=56 << 20
        ),
        name="sum_gradients",
    )(grad, loss)


MATS = [(PIN, D), (D, FF), (FF, D), (D, FF), (FF, D), (D, PIN)]
SMALL_LAYER = 2352
SMALLS = [6 + SMALL_LAYER, 24, 6 + SMALL_LAYER, 24, 18, 10]
PIECE = 256


def flat_sections():
    at = 0
    found = []
    for (depth, cols), small in zip(MATS, SMALLS):
        per_row = cols // LANES
        found.append((at, depth, per_row, at + depth * per_row, small))
        at += depth * per_row + small
    return found


def piece_rows(depth, per_row):
    rows = depth
    while rows * per_row > 7680:
        rows -= PIECE
        while depth % rows:
            rows -= PIECE
    return rows


def put_rows(wide, at, value):
    for k in range(value.shape[1] // LANES):
        wide[at + k : at + k + 1] = value[:, k * LANES : (k + 1) * LANES]


def put_block_weight(wide, at, block, grad, square):
    wide[at : at + 2 * NBLK * BLOCK_ROWS] = jnp.zeros((2 * NBLK * BLOCK_ROWS, LANES), f32)
    square[0] = grad[:PADC, :PADC] + grad[PADC:, PADC:]
    square[1] = grad[:PADC, PADC:] - grad[PADC:, :PADC]
    for part in range(2):
        a, b, c, d = (square[part, pl.ds(q, 24, stride=4), :] for q in range(4))
        rows = (
            jnp.concatenate([a[:, :96], b[:, :32]], axis=1),
            jnp.concatenate([b[:, 32:96], c[:, :64]], axis=1),
            jnp.concatenate([c[:, 64:96], d[:, :96]], axis=1),
        )
        for q, value in enumerate(rows):
            wide[pl.ds(at + (part * NBLK + block) * BLOCK_ROWS + q, 24, stride=3), :] = value


def put_block_bias(wide, at, block, grad):
    found = []
    for part in range(2):
        piece = grad[:, part * PADC : part * PADC + BS]
        found += [jnp.where(block == k, piece, 0.0) for k in range(NBLK)]
    put_rows(wide, at, jnp.concatenate(found, axis=1))


def pack_kernel(*refs):
    sources, refs = refs[:9], refs[9:]
    sum_norm, sum_c1, sum_tail, sum_head, grad_w1, grad_w2, grad_b = refs[:7]
    flat = refs[7]
    held, refs = refs[8:17], refs[17:]
    across, side, wide, narrow, square, sem, in_sem = refs
    inputs, x1, normeds, hiddens, tails, g_embed, g_pre, g_out, g_pred = held
    _, me, _, _ = place()
    block = me % NBLK
    loads = [
        pltpu.make_async_copy(source, target, in_sem.at[k])
        for k, (source, target) in enumerate(zip(sources, held))
    ]
    order = (0, 1, 5, 2, 6, 3, 7, 4, 8)
    for k in order:
        loads[k].start()
    needs = ((0, 1, 5), (2, 6), (3, 7), (), (), (4, 8))
    pairs = [(inputs, x1, g_embed.at[0], g_embed.at[1])]
    for idx in range(LAYERS):
        pairs.append((normeds.at[idx], normeds.at[2 + idx], g_pre.at[idx], g_pre.at[2 + idx]))
        pairs.append((hiddens.at[idx], hiddens.at[2 + idx], g_out.at[idx], g_out.at[2 + idx]))
    pairs.append((tails.at[0], tails.at[1], g_pred.at[0], g_pred.at[1]))

    def put_layer(at, idx):
        put_rows(wide, at, sum_norm[idx, 0:1])
        put_rows(wide, at + 6, sum_norm[idx, 1:2])
        put_block_weight(wide, at + AT_W1, block, grad_w1[idx], square)
        put_block_bias(wide, at + AT_B1, block, grad_b[idx, 0:1])
        put_block_weight(wide, at + AT_W2, block, grad_w2[idx], square)
        put_block_bias(wide, at + AT_B2, block, grad_b[idx, 1:2])
        put_rows(wide, at + AT_NORM[2], sum_norm[idx, 2:3])
        put_rows(wide, at + AT_NORM[3], sum_norm[idx, 3:4])

    def put_small(i, at):
        if i == 0:
            put_rows(wide, at, sum_tail[2:3])
            put_layer(at + 6, 0)
        elif i == 2:
            put_rows(wide, at, sum_norm[0, 4:5])
            put_layer(at + 6, 1)
        elif i == 4:
            put_rows(wide, at, sum_norm[1, 4:5])
            put_rows(wide, at + 6, sum_tail[0:1])
            put_rows(wide, at + 12, sum_tail[1:2])
        elif i == 5:
            put_rows(wide, at, sum_head[0:1])
        else:
            put_rows(wide, at, sum_c1[i // 2, 0:1])

    pending = []

    def emit(at, full):
        return pltpu.make_async_copy(narrow.at[pl.ds(0, full)], flat.at[pl.ds(at, full)], sem)

    for i, (start, depth, per_row, small_at, small) in enumerate(flat_sections()):
        for k in needs[i]:
            loads[k].wait()
        x0, x1_, g0, g1 = pairs[i]
        cols = per_row * LANES
        for half, (x, g) in enumerate(((x0, g0), (x1_, g1))):
            for part in range(0, depth, PIECE):
                across[part : part + PIECE, half * 128 : half * 128 + 128] = x[
                    :, part : part + PIECE
                ].T
            side[half * 128 : half * 128 + 128, 0:cols] = g[...]
        rows = piece_rows(depth, per_row)
        full = rows * per_row
        shift = start % 16
        before = pending.pop() if pending else None

        def step(it, carry):
            top = pl.multiple_of(it * rows, PIECE)
            for part in range(0, rows, PIECE):
                left = across[pl.ds(pl.multiple_of(top + part, PIECE), PIECE), :]
                for j in range(0, per_row, 2):
                    value = dot(left, side[:, j * LANES : (j + 2) * LANES])
                    for side_by in range(2):
                        wide[
                            pl.ds(shift + part * per_row + j + side_by, PIECE, stride=per_row), :
                        ] = value[:, side_by * LANES : (side_by + 1) * LANES]
            if before is not None:
                @pl.when(it == 0)
                def _():
                    before.wait()

            @pl.when(it > 0)
            def _():
                emit(0, full).wait()

            narrow[0:full] = wide[0:full].astype(bf16)
            emit(pl.multiple_of(start - shift + it * full, 16), full).start()
            wide[0:16] = wide[full : full + 16]
            return carry

        lax.fori_loop(0, depth // rows, step, 0)
        shift = small_at % 16
        put_small(i, shift)
        full = (shift + small) // 16 * 16
        if i == 5:
            wide[shift + small : GROWS - small_at + shift] = jnp.zeros(
                (GROWS - small_at - small, LANES), f32
            )
            full = GROWS - small_at + shift
        emit(0, rows * per_row).wait()
        narrow[0:full] = wide[0:full].astype(bf16)
        done = emit(small_at - shift, full)
        done.start()
        pending.append(done)
        if i < 5:
            wide[0:16] = wide[full : full + 16]
    pending.pop().wait()


def pack_flat(*args):
    vm, whole = pltpu.VMEM, pl.BlockSpec(memory_space=pltpu.VMEM)
    anywhere = pl.BlockSpec(memory_space=pl.ANY)
    return pl.pallas_call(
        pack_kernel,
        out_shape=jax.ShapeDtypeStruct((GROWS, LANES), bf16),
        in_specs=[anywhere] * 9 + [whole] * 7,
        out_specs=anywhere,
        scratch_shapes=[vm(a.shape, a.dtype) for a in args[:9]]
        + [
            vm((FF, 256), bf16),
            vm((256, FF), bf16),
            vm((7712, LANES), f32),
            vm((7712, LANES), bf16),
            vm((2, PADC, PADC), f32),
            pltpu.SemaphoreType.DMA,
            pltpu.SemaphoreType.DMA((9,)),
        ],
        compiler_params=pltpu.CompilerParams(vmem_limit_bytes=52 << 20),
        name="pack_flat",
    )(*args)


CELLS = 2 * UNIT
FCHUNK = 768
FILTER_SEMS = 10


def norm_adjoint(values, gain, grad):
    normed, scale = normalize(values)
    inner = grad * gain
    along = jnp.mean(inner * normed, axis=-1, keepdims=True)
    flat = jnp.mean(inner, axis=-1, keepdims=True)
    return (
        scale * (inner - flat - normed * along),
        jnp.sum(grad * normed, axis=0, keepdims=True),
        jnp.sum(grad, axis=0, keepdims=True),
    )


SMALL_AT = []
for _count in SMALLS:
    SMALL_AT.append(SMALL_AT[-1] + -(-SMALLS[len(SMALL_AT) - 1] // 8) * 8 if SMALL_AT else 0)
SMALL_ROWS = SMALL_AT[-1] + 16
AT_NORM = (0, 6, 2340, 2346)
AT_W1, AT_B1, AT_W2, AT_B2 = 12, 1164, 1176, 2328
BLOCK_ROWS = BS * BS // LANES


def aligned_part(at, count):
    low = at // 16 * 16
    return low, -(-(at + count - low) // 16) * 16


def unpack_sections(flat, raw, wide, in_sem, wanted):
    steps = []
    for i, target in wanted:
        start, depth, per_row, _, _ = flat_sections()[i]
        rows = piece_rows(depth, per_row)
        for top in range(0, depth, rows):
            steps.append((start + top * per_row, per_row, top, rows, target))

    def fetch(n):
        at, per_row, _, rows, _ = steps[n]
        low, size = aligned_part(at, rows * per_row)
        return pltpu.make_async_copy(
            flat.at[pl.ds(low, size)], raw.at[n % 2, pl.ds(0, size)], in_sem.at[n % 2]
        ), size

    fetch(0)[0].start()
    for n, (at, per_row, top, rows, target) in enumerate(steps):
        if n + 1 < len(steps):
            fetch(n + 1)[0].start()
        copy, size = fetch(n)
        copy.wait()
        wide[0:size] = raw[n % 2, 0:size].astype(f32)
        for part in range(0, rows, PIECE):
            for j in range(per_row):
                target[top + part : top + part + PIECE, j * LANES : (j + 1) * LANES] = wide[
                    pl.ds(at % 16 + part * per_row + j, PIECE, stride=per_row), :
                ].astype(bf16)


def unpack_small(flat, raw, wide, in_sem, small):
    def fetch(n):
        _, _, _, at, count = flat_sections()[n]
        low, size = aligned_part(at, count)
        return pltpu.make_async_copy(
            flat.at[pl.ds(low, size)], raw.at[n % 2, pl.ds(0, size)], in_sem.at[n % 2]
        ), size, at - low, count

    fetch(0)[0].start()
    for n in range(6):
        if n < 5:
            fetch(n + 1)[0].start()
        copy, size, shift, count = fetch(n)
        copy.wait()
        wide[0:size] = raw[n % 2, 0:size].astype(f32)
        small[SMALL_AT[n] : SMALL_AT[n] + count] = wide[shift : shift + count]


def long_row(small, at, count):
    return jnp.concatenate([small[at + k : at + k + 1] for k in range(count)], axis=1)


def block_weight(small, at, block, square, out):
    blank = jnp.zeros((24, PADC - BS), f32)
    square[...] = jnp.zeros_like(square)
    for part in range(2):
        base = at + (part * NBLK + block) * BLOCK_ROWS
        a, b, c = (small[pl.ds(base + q, 24, stride=3), :] for q in range(3))
        pieces = (
            a[:, :96],
            jnp.concatenate([a[:, 96:], b[:, :64]], axis=1),
            jnp.concatenate([b[:, 64:], c[:, :32]], axis=1),
            c[:, 32:],
        )
        for q, piece in enumerate(pieces):
            piece = jnp.concatenate([piece, blank], axis=1)
            if part == 0:
                square[0, pl.ds(q, 24, stride=4), :] = piece
                square[3, pl.ds(q, 24, stride=4), :] = piece
            else:
                square[1, pl.ds(q, 24, stride=4), :] = piece
                square[2, pl.ds(q, 24, stride=4), :] = -piece
    for quarter in range(4):
        top, left = quarter // 2 * PADC, quarter % 2 * PADC
        out[top : top + PADC, left : left + PADC] = square[quarter].astype(bf16)


def block_bias(small, at, block):
    blank = jnp.zeros((1, PADC - BS), f32)
    both = long_row(small, at, 12)
    found = []
    for part in range(2):
        value = jnp.zeros((1, BS), f32)
        for k in range(NBLK):
            low = (part * NBLK + k) * BS
            value = value + jnp.where(block == k, both[:, low : low + BS], 0.0)
        found += [value, blank]
    return jnp.concatenate(found, axis=1)


def forward_kernel(*refs):
    x0, goals, mask, weight, column, inverse, rows, flat = refs[:8]
    (streams, waves_o, mixeds, normeds, befores, hiddens, lasts, tails, errors,
     embed_h, in0, out0, in1, out1, head_h, x1, loss, norms, tail, w1, b1, w2) = refs[8:30]
    (embed, w_in, w_out, head, flow, x_now, s_stream, s_waves, s_mixed, s_norm, s_before, s_hidden,
     s_tail, s_error, raw, wide, small, square, b2, c1, c2, embed_b, head_b,
     weight_sem, out_sem, tail_sem, in_sem) = refs[30:57]
    units, mine, others, waves, back, own_sum, to_sib, from_sib, ready, landed, joined = refs[57:68]
    sems = refs[68:]
    row, me, core, sibling = place()
    barrier = greet_chips(me, core, sibling)
    stores = [
        pltpu.make_async_copy(source, target, weight_sem.at[k])
        for k, (source, target) in enumerate(
            [(embed, embed_h), (w_in.at[0], in0), (w_out.at[0], out0), (w_in.at[1], in1),
             (w_out.at[1], out1), (head, head_h)]
        )
    ]
    block = me % NBLK
    unpack_small(flat, raw, wide, in_sem, small)
    embed_b[...] = long_row(small, SMALL_AT[0], 6)
    head_b[...] = long_row(small, SMALL_AT[5], 10)
    for layer in range(LAYERS):
        base = SMALL_AT[2 * layer] + 6
        for k, at in enumerate(AT_NORM):
            norms[layer, k : k + 1] = long_row(small, base + at, 6)
        c1[layer] = long_row(small, SMALL_AT[2 * layer + 1], 24)
        c2[layer] = long_row(small, SMALL_AT[2 * layer + 2], 6)
        block_weight(small, base + AT_W1, block, square, w1.at[layer])
        block_weight(small, base + AT_W2, block, square, w2.at[layer])
        b1[layer] = block_bias(small, base + AT_B1, block)
        b2[layer] = block_bias(small, base + AT_B2, block)
    tail[0:1] = long_row(small, SMALL_AT[4] + 6, 6)
    tail[1:2] = long_row(small, SMALL_AT[4] + 12, 6)
    unpack_sections(flat, raw, wide, in_sem, [(0, embed)])
    stores[0].start()
    x_now[...] = x0[...]
    loss[...] = jnp.zeros_like(loss)

    def saves(it):
        pairs = [(s_stream, streams), (s_waves, waves_o), (s_mixed, mixeds), (s_norm, normeds),
                 (s_before, befores), (s_hidden, hiddens)]
        return [
            pltpu.make_async_copy(source, target.at[it], out_sem.at[k])
            for k, (source, target) in enumerate(pairs)
        ]

    def tail_saves(step):
        pairs = [(flow, lasts), (s_tail, tails), (s_error, errors)]
        return [
            pltpu.make_async_copy(source, target.at[step], tail_sem.at[k])
            for k, (source, target) in enumerate(pairs)
        ]

    def when_it(cond, action):
        @pl.when(cond)
        def _():
            action()

    def unpack_when(it, number, wanted, done):
        def go():
            unpack_sections(flat, raw, wide, in_sem, wanted)
            for k in done:
                stores[k].start()

        when_it(it == number, go)

    def meanwhile_in(it):
        unpack_when(it, 0, [(1, w_in.at[0])], [1])
        unpack_when(it, 1, [(3, w_in.at[1])], [3])

    def meanwhile_out(it):
        unpack_when(it, 0, [(2, w_out.at[0])], [2])
        unpack_when(it, 1, [(4, w_out.at[1]), (5, head)], [4, 5])

    def body(it, carry):
        step, layer = it // 2, it % 2

        def start_step():
            flow[...] = dot(x_now[...], embed[...]) + embed_b[...]

        def tail_done():
            for save in tail_saves(0):
                save.wait()

        when_it(it == 2, tail_done)
        when_it(layer == 0, start_step)

        def saved():
            for save in saves(it):
                save.wait()

        when_it(it > 0, saved)
        s_stream[...] = flow[...]
        normed, _ = normalize(flow[...])
        split_units(normed * norms[layer, 0:1] + norms[layer, 1:2], units)
        when_it(it == 0, lambda: pl.semaphore_wait(barrier, CHIPS))

        finish_one = spread_units(
            me, core, sibling, units, mine, others, sems[:5], lambda: meanwhile_in(it)
        )
        groups = to_spectrum(mine, others, column, rows, waves)
        for g in range(4):
            s_waves[g] = groups[g]
            hidden = gelu_of(dot(groups[g], w1[layer]) + b1[layer]).astype(bf16)
            spec = (dot(hidden, w2[layer]) + b2[layer]).astype(bf16)
            from_spectrum(g, spec, rows, back)
        finish_two = gather_units(
            row, me, core, sibling, back, inverse,
            (own_sum, to_sib, from_sib, ready, landed), sems[5:], finish_one,
            lambda: meanwhile_out(it),
        )
        join_units(landed, joined)
        mixed = flow[...] + joined[...]
        s_mixed[...] = mixed
        normed, _ = normalize(mixed)
        s_norm[...] = (normed * norms[layer, 2:3] + norms[layer, 3:4]).astype(bf16)
        flow[...] = mixed + c2[layer]

        def chunk(c, carry):
            part = pl.ds(pl.multiple_of(c * FCHUNK, FCHUNK), FCHUNK)
            before = dot(s_norm[...], w_in[layer, :, part]) + c1[layer, :, part]
            s_before[:, part] = before.astype(bf16)
            hidden = gelu_of(before).astype(bf16)
            s_hidden[:, part] = hidden
            flow[...] += dot(hidden, w_out[layer, part, :])
            return carry

        lax.fori_loop(0, FF // FCHUNK, chunk, 0)
        for save in saves(it):
            save.start()
        finish_two()
        def end_step():
            normed, _ = normalize(flow[...])
            s_tail[...] = (normed * tail[0:1] + tail[1:2]).astype(bf16)
            predicted = dot(s_tail[...], head[...]) + head_b[...]
            error = predicted - goals[step].astype(f32)
            s_error[...] = error
            loss[...] += weight[...] * jnp.sum(error * error, axis=-1, keepdims=True)
            x_now[...] = (predicted * mask[...]).astype(bf16)
            for save in tail_saves(step):
                save.start()

        when_it(layer == 1, end_step)
        when_it(it == 1, lambda: x1.__setitem__(Ellipsis, x_now[...]))
        return carry

    lax.fori_loop(0, 4, body, 0)
    for save in saves(3):
        save.wait()
    for save in tail_saves(1):
        save.wait()
    for store in stores:
        store.wait()


def forward_pass(*args):
    vm, dma = pltpu.VMEM, pltpu.SemaphoreType.DMA
    whole, anywhere = pl.BlockSpec(memory_space=vm), pl.BlockSpec(memory_space=pl.ANY)
    shape = jax.ShapeDtypeStruct
    return pl.pallas_call(
        forward_kernel,
        out_shape=[
            shape((4, CELLS, D), f32),
            shape((4, 4, 256, 256), bf16),
            shape((4, CELLS, D), f32),
            shape((4, CELLS, D), bf16),
            shape((4, CELLS, FF), bf16),
            shape((4, CELLS, FF), bf16),
            shape((2, CELLS, D), f32),
            shape((2, CELLS, D), bf16),
            shape((2, CELLS, PIN), f32),
            *[shape(dims, bf16) for dims in MATS],
            shape((CELLS, PIN), bf16),
            shape((CELLS, 1), f32),
            shape((2, 4, D), f32),
            shape((2, D), f32),
            shape((2, 256, 256), bf16),
            shape((2, 1, 256), f32),
            shape((2, 256, 256), bf16),
        ],
        in_specs=[whole] * 7 + [anywhere],
        out_specs=[anywhere] * 15 + [whole] * 7,
        scratch_shapes=[
            vm((PIN, D), bf16),
            vm((2, D, FF), bf16),
            vm((2, FF, D), bf16),
            vm((D, PIN), bf16),
            vm((CELLS, D), f32),
            vm((CELLS, PIN), bf16),
            vm((CELLS, D), f32),
            vm((4, 256, 256), bf16),
            vm((CELLS, D), f32),
            vm((CELLS, D), bf16),
            vm((CELLS, FF), bf16),
            vm((CELLS, FF), bf16),
            vm((CELLS, D), bf16),
            vm((CELLS, PIN), f32),
            vm((2, 7696, LANES), bf16),
            vm((7696, LANES), f32),
            vm((SMALL_ROWS, LANES), f32),
            vm((4, PADC, PADC), f32),
            vm((2, 1, 256), f32),
            vm((2, 1, FF), f32),
            vm((2, 1, D), f32),
            vm((1, D), f32),
            vm((1, PIN), f32),
            dma((6,)),
            dma((6,)),
            dma((3,)),
            dma((2,)),
        ]
        + filter_scratch(),
        compiler_params=pltpu.CompilerParams(
            collective_id=2, has_side_effects=True, vmem_limit_bytes=56 << 20
        ),
        name="forward_pass",
    )(*args)


def backward_kernel(*refs):
    (gscale, mask, norms, tail, column, inverse, rows, w1, b1, w2,
     embed_h, in0, out0, in1, out1, head_h,
     streams, waves_h, mixeds, befores, lasts, errors) = refs[:22]
    (g_pred, g_out, g_pre, g_embed, sum_norm, sum_c1, sum_tail, sum_head, grad_w1, grad_w2, grad_b) = refs[22:33]
    (embed, w_in, w_out, head, flow, carried, i_stream, i_waves, i_mixed, i_before, i_last, i_error,
     s_pred, s_out, s_pre, s_embed, g_norm, weight_sem, in_sem, tail_in, out_sem, tail_sem) = refs[33:55]
    units, mine, others, waves, back, own_sum, to_sib, from_sib, ready, landed, joined = refs[55:66]
    sems = refs[66:]
    row, me, core, sibling = place()
    barrier = greet_chips(me, core, sibling)

    def when_it(cond, action):
        @pl.when(cond)
        def _():
            action()

    loads = [
        pltpu.make_async_copy(source, target, weight_sem.at[k])
        for k, (source, target) in enumerate(
            [(head_h, head), (out1, w_out.at[1]), (in1, w_in.at[1]), (out0, w_out.at[0]),
             (in0, w_in.at[0]), (embed_h, embed)]
        )
    ]

    def inst(it):
        return 3 - it

    def fetch(it):
        slot = it % 2
        pairs = [(streams, i_stream), (waves_h, i_waves), (mixeds, i_mixed), (befores, i_before)]
        return [
            pltpu.make_async_copy(source.at[inst(it)], target.at[slot], in_sem.at[k, slot])
            for k, (source, target) in enumerate(pairs)
        ]

    tail_loads = [
        pltpu.make_async_copy(lasts, i_last, tail_in.at[0]),
        pltpu.make_async_copy(errors, i_error, tail_in.at[1]),
    ]
    for load in tail_loads:
        load.start()
    loads[0].start()
    for load in fetch(0):
        load.start()
    for load in loads[1:]:
        load.start()
    for target in (sum_norm, sum_c1, sum_tail, sum_head, grad_w1, grad_w2, grad_b, carried):
        target[...] = jnp.zeros_like(target)

    def saves(it):
        pairs = [(s_out, g_out), (s_pre, g_pre)]
        return [
            pltpu.make_async_copy(source, target.at[inst(it)], out_sem.at[k])
            for k, (source, target) in enumerate(pairs)
        ]

    def pred_save(step):
        return pltpu.make_async_copy(s_pred, g_pred.at[step], tail_sem.at[0])

    def embed_save(step):
        return pltpu.make_async_copy(s_embed, g_embed.at[step], tail_sem.at[1])

    def body(it, carry):
        step, layer, slot = 1 - it // 2, 1 - it % 2, it % 2

        def first():
            for load in tail_loads:
                load.wait()
            loads[0].wait()

        when_it(it == 0, first)
        when_it(it == 2, lambda: pred_save(1).wait())

        def head_adjoint():
            grad = i_error[step] * gscale[...] + carried[...]
            grad16 = grad.astype(bf16)
            s_pred[...] = grad16
            pred_save(step).start()
            sum_head[0:1] += jnp.sum(grad, axis=0, keepdims=True)
            back_n = dot_cols(grad16, head[...]).astype(bf16).astype(f32)
            value, gain, shift = norm_adjoint(i_last[step], tail[0:1], back_n)
            flow[...] = value
            sum_tail[0:1] += gain
            sum_tail[1:2] += shift

        when_it(layer == 1, head_adjoint)

        def prefetch():
            for load in fetch(it + 1):
                load.start()

        when_it(it < 3, prefetch)

        def saved():
            for save in saves(it):
                save.wait()

        when_it(it > 0, saved)
        s_out[...] = flow[...].astype(bf16)
        sum_norm[layer, 4:5] += jnp.sum(flow[...], axis=0, keepdims=True)
        for load in fetch(it):
            load.wait()

        def second_layer():
            loads[1].wait()
            loads[2].wait()

        def first_layer():
            loads[3].wait()
            loads[4].wait()

        when_it(it == 0, second_layer)
        when_it(it == 1, first_layer)
        g_norm[...] = jnp.zeros_like(g_norm)

        def chunk(c, carry):
            part = pl.ds(pl.multiple_of(c * FCHUNK, FCHUNK), FCHUNK)
            grad = dot_cols(s_out[...], w_out[layer, part, :]).astype(bf16).astype(f32)
            grad = grad * gelu_slope(i_before[slot, :, part].astype(f32))
            sum_c1[layer, 0:1, part] += jnp.sum(grad, axis=0, keepdims=True)
            grad16 = grad.astype(bf16)
            s_pre[:, part] = grad16
            g_norm[...] += dot_cols(grad16, w_in[layer, :, part])
            return carry

        lax.fori_loop(0, FF // FCHUNK, chunk, 0)
        for save in saves(it):
            save.start()
        value, gain, shift = norm_adjoint(
            i_mixed[slot], norms[layer, 2:3], g_norm[...].astype(bf16).astype(f32)
        )
        flow[...] += value
        sum_norm[layer, 2:3] += gain
        sum_norm[layer, 3:4] += shift
        split_units(flow[...], units)
        when_it(it == 0, lambda: pl.semaphore_wait(barrier, CHIPS))
        finish_one = spread_units(
            me, core, sibling, units, mine, others, sems[:5], lambda: None
        )
        groups = to_spectrum(mine, others, column, rows, waves)
        for g in range(4):
            before = dot(i_waves[slot, g], w1[layer]) + b1[layer]
            hidden = gelu_of(before).astype(bf16)
            grad_hidden = dot_cols(groups[g], w2[layer]).astype(bf16).astype(f32)
            grad_before = grad_hidden * gelu_slope(before)
            grad_before16 = grad_before.astype(bf16)
            grad_w2[layer] += dot_rows(hidden, groups[g])
            grad_w1[layer] += dot_rows(i_waves[slot, g], grad_before16)
            grad_b[layer, 0:1] += jnp.sum(grad_before, axis=0, keepdims=True)
            grad_b[layer, 1:2] += jnp.sum(groups[g].astype(f32), axis=0, keepdims=True)
            from_spectrum(g, dot_cols(grad_before16, w1[layer]).astype(bf16), rows, back)
        finish_two = gather_units(
            row, me, core, sibling, back, inverse,
            (own_sum, to_sib, from_sib, ready, landed), sems[5:], finish_one, lambda: None,
        )
        join_units(landed, joined)
        value, gain, shift = norm_adjoint(i_stream[slot], norms[layer, 0:1], joined[...])
        flow[...] += value
        sum_norm[layer, 0:1] += gain
        sum_norm[layer, 1:2] += shift
        when_it(it == 1, loads[5].wait)
        when_it(it == 3, lambda: embed_save(1).wait())

        def embed_adjoint():
            s_embed[...] = flow[...].astype(bf16)
            sum_tail[2:3] += jnp.sum(flow[...], axis=0, keepdims=True)
            embed_save(step).start()

        when_it(layer == 0, embed_adjoint)

        def carry_back():
            carried[...] = mask[...] * dot_cols(s_embed[...], embed[...]).astype(bf16).astype(f32)

        when_it(it == 1, carry_back)
        finish_two()
        return carry

    lax.fori_loop(0, 4, body, 0)
    for save in saves(3):
        save.wait()
    pred_save(0).wait()
    embed_save(0).wait()


def backward_pass(*args):
    vm, dma = pltpu.VMEM, pltpu.SemaphoreType.DMA
    whole, anywhere = pl.BlockSpec(memory_space=vm), pl.BlockSpec(memory_space=pl.ANY)
    shape = jax.ShapeDtypeStruct
    return pl.pallas_call(
        backward_kernel,
        out_shape=[
            shape((2, CELLS, PIN), bf16),
            shape((4, CELLS, D), bf16),
            shape((4, CELLS, FF), bf16),
            shape((2, CELLS, D), bf16),
            shape((2, 8, D), f32),
            shape((2, 8, FF), f32),
            shape((8, D), f32),
            shape((8, PIN), f32),
            shape((2, 256, 256), f32),
            shape((2, 256, 256), f32),
            shape((2, 8, 256), f32),
        ],
        in_specs=[whole] * 10 + [anywhere] * 12,
        out_specs=[anywhere] * 4 + [whole] * 7,
        scratch_shapes=[
            vm((PIN, D), bf16),
            vm((2, D, FF), bf16),
            vm((2, FF, D), bf16),
            vm((D, PIN), bf16),
            vm((CELLS, D), f32),
            vm((CELLS, PIN), f32),
            vm((2, CELLS, D), f32),
            vm((2, 4, 256, 256), bf16),
            vm((2, CELLS, D), f32),
            vm((2, CELLS, FF), bf16),
            vm((2, CELLS, D), f32),
            vm((2, CELLS, PIN), f32),
            vm((CELLS, PIN), bf16),
            vm((CELLS, D), bf16),
            vm((CELLS, FF), bf16),
            vm((CELLS, D), bf16),
            vm((CELLS, D), f32),
            dma((6,)),
            dma((4, 2)),
            dma((2,)),
            dma((2,)),
            dma((2,)),
        ]
        + filter_scratch(),
        compiler_params=pltpu.CompilerParams(
            collective_id=3, has_side_effects=True, vmem_limit_bytes=56 << 20
        ),
        name="backward_pass",
    )(*args)


def local_fast(frames, targets, regions, master, first_moment, second_moment):
    height, width = 16, 128
    device = lax.axis_index("row") * 4 + lax.axis_index("col")
    core = lax.axis_index("col") % 2
    shard = master.astype(bf16).reshape(OWN, LANES)
    halo = lax.ppermute(shard[:320], ("row", "col"), [(k + 1, k) for k in range(31)])
    chunk = lax.dynamic_slice_in_dim(jnp.concatenate([shard, halo]), 10 * device, CH, 0)
    flat = ag(chunk)
    tables = transform_tables(core)
    row_ids = lax.axis_index("row") * 2 + jnp.arange(2, dtype=jnp.int32)
    col_ids = lax.axis_index("col") * 32 + jnp.arange(32, dtype=jnp.int32)
    cell_masks = region_masks(regions, row_ids, col_ids, width)
    weighted = latitude(row_ids, height)[None, :, None] * cell_masks
    every_row = jnp.arange(height, dtype=jnp.int32)
    every_col = jnp.arange(width, dtype=jnp.int32)
    total_weight = (
        jnp.sum(
            latitude(every_row, height)[None, :, None]
            * region_masks(regions, every_row, every_col, width)
        )
        * STEPS
    )
    flat_mask = cell_masks.reshape(128, 1)
    flat_weight = weighted.reshape(128, 1)
    inputs = (frames.reshape(128, PIN).astype(f32) * flat_mask).astype(bf16)
    goals = jnp.stack([targets[:, s].reshape(128, PIN) for s in range(STEPS)])
    (streams, waves, mixeds, normeds, befores, hiddens, lasts, tails, errors, *rest) = forward_pass(
        inputs, goals, flat_mask, flat_weight, *tables, flat
    )
    mats, (x1, loss, norms, tail, w1, b1, w2) = rest[:6], rest[6:]
    (g_pred, g_out, g_pre, g_embed, sum_norm, sum_c1, sum_tail, sum_head, grad_w1, grad_w2, grad_b) = (
        backward_pass(
            flat_weight * (2.0 / total_weight), flat_mask, norms, tail, *tables, w1, b1, w2, *mats,
            streams, waves, mixeds, befores, lasts, errors,
        )
    )
    flat_grad = pack_flat(
        inputs, x1, normeds, hiddens, tails, g_embed, g_pre, g_out, g_pred,
        sum_norm, sum_c1, sum_tail, sum_head, grad_w1, grad_w2, grad_b,
    )
    loss_tile = jnp.concatenate([loss.reshape(1, LANES), jnp.zeros((7, LANES), f32)])
    summed, stats = rs(flat_grad, loss_tile)
    reduced = lax.dynamic_slice_in_dim(summed, (device * OWN) % 16, OWN, 0).reshape(-1)
    grad_norm = jnp.sqrt(jnp.sum(stats[:8]))
    return finish_step(
        reduced, grad_norm, master, first_moment, second_moment, jnp.sum(stats[8:]), total_weight
    )


def finish_step(reduced, grad_norm, master, first_moment, second_moment, loss_all, total_weight):
    clipped = reduced * (CLIP / jnp.maximum(grad_norm, CLIP))
    first_out = BETA_ONE * first_moment + (1.0 - BETA_ONE) * clipped
    second_out = BETA_TWO * second_moment + (1.0 - BETA_TWO) * clipped * clipped
    corrected_one = first_out / (1.0 - BETA_ONE**ADAM_STEP)
    corrected_two = second_out / (1.0 - BETA_TWO**ADAM_STEP)
    master_out = master - RATE * (
        corrected_one / (jnp.sqrt(corrected_two) + ADAM_EPS) + DECAY * master
    )
    return (
        master_out,
        first_out,
        second_out,
        master_out.astype(bf16),
        loss_all,
        total_weight,
        grad_norm,
    )


def local(frames, targets, regions, master, first_moment, second_moment):
    row_devices = lax.axis_size("row")
    col_devices = lax.axis_size("col")
    local_rows = frames.shape[1]
    local_cols = frames.shape[2]
    height = local_rows * row_devices
    width = local_cols * col_devices
    weights = lax.all_gather(master.astype(jnp.bfloat16), ("row", "col"), axis=0, tiled=True)
    pieces16 = unpack(weights)
    pieces = unpack(weights.astype(jnp.float32))
    tail_params = pieces[2 + 12 * LAYERS :]
    tail16 = pieces16[2 + 12 * LAYERS :]
    tables = (
        dft_tables(width, -1.0),
        dft_tables(height, -1.0),
        dft_tables(width, 1.0),
        dft_tables(height, 1.0),
    )
    row_ids = lax.axis_index("row") * local_rows + jnp.arange(local_rows, dtype=jnp.int32)
    col_ids = lax.axis_index("col") * local_cols + jnp.arange(local_cols, dtype=jnp.int32)
    cell_masks = region_masks(regions, row_ids, col_ids, width)
    weighted = latitude(row_ids, height)[None, :, None] * cell_masks
    every_row = jnp.arange(height, dtype=jnp.int32)
    every_col = jnp.arange(width, dtype=jnp.int32)
    total_weight = (
        jnp.sum(
            latitude(every_row, height)[None, :, None]
            * region_masks(regions, every_row, every_col, width)
        )
        * STEPS
    )
    inputs = frames.astype(jnp.float32) * cell_masks[..., None]
    loss_sum = jnp.zeros((), jnp.float32)
    history = []
    for roll_step in range(STEPS):
        stream = linear_forward(inputs, pieces16[0], pieces[1])
        saved_layers = []
        for layer_idx in range(LAYERS):
            span = slice(2 + 12 * layer_idx, 14 + 12 * layer_idx)
            stream, saved = layer_forward(stream, pieces[span], pieces16[span], tables)
            saved_layers.append(saved)
        normed = rounded(layer_norm(stream, tail_params[0], tail_params[1]))
        predicted = linear_forward(normed, tail16[2], tail_params[3])
        errors = predicted - targets[:, roll_step].astype(jnp.float32)
        loss_sum = loss_sum + jnp.sum(weighted * jnp.sum(errors * errors, axis=-1))
        history.append((inputs, saved_layers, stream, normed, errors))
        inputs = rounded(predicted * cell_masks[..., None])
    loss_all = lax.psum(loss_sum, ("row", "col"))
    gradients = [jnp.zeros_like(piece) for piece in pieces]
    carried = jnp.zeros_like(inputs)
    for roll_step in reversed(range(STEPS)):
        inputs, saved_layers, stream, normed, errors = history[roll_step]
        grad_pred = 2.0 * weighted[..., None] * errors / total_weight + carried
        grad_normed, grad_head, grad_hbias = linear_backward(grad_pred, normed, tail16[2])
        _, pullback = jax.vjp(layer_norm, stream, tail_params[0], tail_params[1])
        grad_stream, grad_gain3, grad_shift3 = pullback(rounded(grad_normed))
        gradients = add_into(
            gradients, 2 + 12 * LAYERS, [grad_gain3, grad_shift3, grad_head, grad_hbias]
        )
        for layer_idx in reversed(range(LAYERS)):
            span = slice(2 + 12 * layer_idx, 14 + 12 * layer_idx)
            grad_stream, layer_grads = layer_backward(
                grad_stream, saved_layers[layer_idx], pieces[span], pieces16[span], tables
            )
            gradients = add_into(gradients, 2 + 12 * layer_idx, layer_grads)
        grad_inputs, grad_embed, grad_ebias = linear_backward(grad_stream, inputs, pieces16[0])
        gradients = add_into(gradients, 0, [grad_embed, grad_ebias])
        carried = cell_masks[..., None] * rounded(grad_inputs)
    flat_grad = jnp.concatenate([piece.ravel() for piece in gradients])
    padding = master.shape[0] * row_devices * col_devices - flat_grad.shape[0]
    flat_grad = jnp.concatenate([flat_grad, jnp.zeros((padding,), jnp.float32)])
    grad_table = flat_grad.reshape(-1, LANES)
    reduced = lax.psum_scatter(grad_table, ("row", "col"), scatter_dimension=0, tiled=True).reshape(
        -1
    )
    squares = jnp.sum(reduced * reduced)
    square_all = lax.psum(squares, ("row", "col"))
    grad_norm = jnp.sqrt(square_all)
    clipped = reduced * (CLIP / jnp.maximum(grad_norm, CLIP))
    first_out = BETA_ONE * first_moment + (1.0 - BETA_ONE) * clipped
    second_out = BETA_TWO * second_moment + (1.0 - BETA_TWO) * clipped * clipped
    corrected_one = first_out / (1.0 - BETA_ONE**ADAM_STEP)
    corrected_two = second_out / (1.0 - BETA_TWO**ADAM_STEP)
    master_out = master - RATE * (
        corrected_one / (jnp.sqrt(corrected_two) + ADAM_EPS) + DECAY * master
    )
    return (
        master_out,
        first_out,
        second_out,
        master_out.astype(jnp.bfloat16),
        loss_all,
        total_weight,
        grad_norm,
    )


def solution(mesh):
    in_specs = (
        P(None, "row", "col", None),
        P(None, None, "row", "col", None),
        P(),
        P(("row", "col")),
        P(("row", "col")),
        P(("row", "col")),
    )
    out_specs = (
        P(("row", "col")),
        P(("row", "col")),
        P(("row", "col")),
        P(("row", "col")),
        P(),
        P(),
        P(),
    )
    body = local_fast if dict(mesh.shape) == {"row": 8, "col": 4} else local
    return jax.shard_map(body, mesh=mesh, in_specs=in_specs, out_specs=out_specs, check_vma=False)
```

```python
import functools
import math

import jax
import jax.numpy as jnp
import numpy as np
from jax import lax
from jax.sharding import PartitionSpec as P
from jax.experimental import pallas as pl
from jax.experimental.pallas import tpu as pltpu

D = 768
FF = 3072
NBLK = 8
BS = 96
PIN = 1280
LAYERS = 2
STEPS = 2
ADAM_STEP = 5


highest = lax.Precision.HIGHEST
NORM_EPS = 1e-05
BETA_ONE = 0.9
BETA_TWO = 0.95
ADAM_EPS = 1e-08
RATE = 0.03
DECAY = 0.05
CLIP = 0.2
LANES = 128


def block_shapes():
    return [
        (D,),
        (D,),
        (2, NBLK, BS, BS),
        (2, NBLK, BS),
        (2, NBLK, BS, BS),
        (2, NBLK, BS),
        (D,),
        (D,),
        (D, FF),
        (FF,),
        (FF, D),
        (D,),
    ]


def all_shapes():
    return [(PIN, D), (D,)] + block_shapes() * LAYERS + [(D,), (D,), (D, PIN), (PIN,)]


def unpack(flat_vec):
    pieces = []
    offset = 0
    for layout in all_shapes():
        length = math.prod(layout)
        pieces.append(flat_vec[offset : offset + length].reshape(layout))
        offset += length
    return pieces


def rounded(value):
    return lax.optimization_barrier(value.astype(jnp.bfloat16)).astype(jnp.float32)


def mult(form, left, right):
    return jnp.einsum(
        form,
        left.astype(jnp.bfloat16),
        right.astype(jnp.bfloat16),
        preferred_element_type=jnp.float32,
    )


def mult_exact(form, grad_value, other):
    upper = grad_value.astype(jnp.bfloat16)
    lower = (grad_value - upper.astype(jnp.float32)).astype(jnp.bfloat16)
    return mult(form, upper, other) + mult(form, lower, other)


def layer_norm(values, gain_vec, shift_vec):
    center = values - jnp.mean(values, axis=-1, keepdims=True)
    spread = jnp.mean(center * center, axis=-1, keepdims=True)
    return center * lax.rsqrt(spread + NORM_EPS) * gain_vec + shift_vec


def dft_tables(length, direction):
    positions = jnp.arange(length, dtype=jnp.int32)
    phases = (positions[:, None] * positions[None, :] % length).astype(jnp.float32) * (
        2.0 * math.pi / length
    )
    factor = 1.0 / math.sqrt(length)
    return (jnp.cos(phases) * factor, direction * jnp.sin(phases) * factor)


def apply_pair(tables, real_part, imag_part, form):

    def contract(table, values):
        return jnp.einsum(form, table, values, precision=highest)

    return (
        contract(tables[0], real_part) - contract(tables[1], imag_part),
        contract(tables[1], real_part) + contract(tables[0], imag_part),
    )


def spectral(real_part, imag_part, weight, bias_vec):
    blocks = (weight.shape[1], weight.shape[2])
    block_re = real_part.reshape(real_part.shape[:-1] + blocks)
    block_im = imag_part.reshape(imag_part.shape[:-1] + blocks)
    form = "...kb,kbc->...kc"
    out_re = (
        jnp.einsum(form, block_re, weight[0], precision=highest)
        - jnp.einsum(form, block_im, weight[1], precision=highest)
        + bias_vec[0]
    )
    out_im = (
        jnp.einsum(form, block_im, weight[0], precision=highest)
        + jnp.einsum(form, block_re, weight[1], precision=highest)
        + bias_vec[1]
    )
    return (out_re.reshape(real_part.shape), out_im.reshape(imag_part.shape))


def first_spectral(real_part, imag_part, weight, bias_vec):
    out_re, out_im = spectral(real_part, imag_part, weight, bias_vec)
    return (jax.nn.gelu(out_re, approximate=False), jax.nn.gelu(out_im, approximate=False))


def region_masks(regions, row_ids, col_ids, width):
    row_start = regions[:, 0, None, None]
    row_span = regions[:, 1, None, None]
    col_start = regions[:, 2, None, None]
    col_span = regions[:, 3, None, None]
    row_inside = (row_ids[None, :, None] >= row_start) & (
        row_ids[None, :, None] < row_start + row_span
    )
    col_inside = (col_ids[None, None, :] - col_start) % width < col_span
    return (row_inside & col_inside).astype(jnp.float32)


def latitude(row_ids, height):
    return jnp.cos(-1.3 + 1.3 * (row_ids.astype(jnp.float32) + 0.5) / height)


def linear_forward(values, weight16, bias_vec):
    return mult("brci,io->brco", values, weight16) + bias_vec


def linear_backward(grad_value, values, weight16):
    grad_values = mult_exact("brco,io->brci", grad_value, weight16)
    grad_weight = mult_exact("brco,brci->io", grad_value, values)
    return (grad_values, grad_weight, jnp.sum(grad_value, axis=(0, 1, 2)))


def spectrum(field, forward_w, forward_h):
    values = lax.all_to_all(field, "col", split_axis=3, concat_axis=2, tiled=True).astype(
        jnp.float32
    )
    real_part = jnp.einsum("kw,bnwc->bnkc", forward_w[0], values, precision=highest)
    imag_part = jnp.einsum("kw,bnwc->bnkc", forward_w[1], values, precision=highest)
    real_part, imag_part = apply_pair(
        forward_h,
        lax.all_to_all(
            real_part.astype(jnp.bfloat16), "row", split_axis=2, concat_axis=1, tiled=True
        ).astype(jnp.float32),
        lax.all_to_all(
            imag_part.astype(jnp.bfloat16), "row", split_axis=2, concat_axis=1, tiled=True
        ).astype(jnp.float32),
        "kh,bhwc->bkwc",
    )
    return (real_part.astype(jnp.bfloat16), imag_part.astype(jnp.bfloat16))


def grid(real_part, imag_part, inverse_w, inverse_h):
    back_re, back_im = apply_pair(
        inverse_h, real_part.astype(jnp.float32), imag_part.astype(jnp.float32), "kh,bhwc->bkwc"
    )
    values_re = lax.all_to_all(
        back_re.astype(jnp.bfloat16), "row", split_axis=1, concat_axis=2, tiled=True
    ).astype(jnp.float32)
    values_im = lax.all_to_all(
        back_im.astype(jnp.bfloat16), "row", split_axis=1, concat_axis=2, tiled=True
    ).astype(jnp.float32)
    result = jnp.einsum("kw,bnwc->bnkc", inverse_w[0], values_re, precision=highest) - jnp.einsum(
        "kw,bnwc->bnkc", inverse_w[1], values_im, precision=highest
    )
    columns_back = result.astype(jnp.bfloat16)
    return lax.all_to_all(columns_back, "col", split_axis=2, concat_axis=3, tiled=True)


def local_blocks(params):
    block_count = D // lax.axis_size("col") // BS
    first_block = lax.axis_index("col") * block_count
    chosen = [
        lax.dynamic_slice_in_dim(params[index_pos], first_block, block_count, 1)
        for index_pos in (2, 3, 4, 5)
    ]
    return (chosen, first_block)


def layer_forward(stream, params, params16, tables):
    gain_one, shift_one, _, _, _, _, gain_two, shift_two, _, bias_in, _, bias_out = params
    (local_w1, local_b1, local_w2, local_b2), _ = local_blocks(params)
    normed = layer_norm(stream, gain_one, shift_one).astype(jnp.bfloat16)
    wave_re, wave_im = spectrum(normed, tables[0], tables[1])
    hid_re, hid_im = first_spectral(
        wave_re.astype(jnp.float32), wave_im.astype(jnp.float32), local_w1, local_b1
    )
    hid_re, hid_im = (rounded(hid_re), rounded(hid_im))
    spec_re, spec_im = spectral(hid_re, hid_im, local_w2, local_b2)
    filtered = grid(
        spec_re.astype(jnp.bfloat16), spec_im.astype(jnp.bfloat16), tables[2], tables[3]
    )
    mixed = stream + filtered.astype(jnp.float32)
    normed_two = rounded(layer_norm(mixed, gain_two, shift_two))
    hidden = rounded(
        jax.nn.gelu(linear_forward(normed_two, params16[8], bias_in), approximate=False)
    )
    output = mixed + linear_forward(hidden, params16[10], bias_out)
    return (output, (stream, wave_re, wave_im, hid_re, hid_im, mixed, normed_two, hidden))


def place_blocks(local_grad, full_like, first_block):
    return lax.dynamic_update_slice_in_dim(jnp.zeros_like(full_like), local_grad, first_block, 1)


def layer_backward(grad_out, saved, params, params16, tables):
    stream, wave_re, wave_im, hid_re, hid_im, mixed, normed_two, hidden = saved
    (
        gain_one,
        shift_one,
        spec_w1,
        spec_b1,
        spec_w2,
        spec_b2,
        gain_two,
        shift_two,
        weight_in,
        bias_in,
        weight_out,
        bias_out,
    ) = params
    (local_w1, local_b1, local_w2, local_b2), first_block = local_blocks(params)
    grad_hidden, grad_wout, grad_bout = linear_backward(grad_out, hidden, params16[10])
    grad_mixed = grad_out
    before = linear_forward(normed_two, params16[8], bias_in)
    _, pullback = jax.vjp(lambda value: jax.nn.gelu(value, approximate=False), before)
    (grad_before,) = pullback(rounded(grad_hidden))
    grad_normed, grad_win, grad_bin = linear_backward(grad_before, normed_two, params16[8])
    _, pullback = jax.vjp(layer_norm, mixed, gain_two, shift_two)
    grad_extra, grad_gain2, grad_shift2 = pullback(rounded(grad_normed))
    grad_mixed = grad_mixed + grad_extra
    back_re, back_im = spectrum(grad_mixed.astype(jnp.bfloat16), tables[0], tables[1])
    _, pullback = jax.vjp(spectral, hid_re, hid_im, local_w2, local_b2)
    grad_hre, grad_him, grad_lw2, grad_lb2 = pullback(
        (back_re.astype(jnp.float32), back_im.astype(jnp.float32))
    )
    _, pullback = jax.vjp(
        first_spectral, wave_re.astype(jnp.float32), wave_im.astype(jnp.float32), local_w1, local_b1
    )
    grad_wre, grad_wim, grad_lw1, grad_lb1 = pullback((rounded(grad_hre), rounded(grad_him)))
    grad_first = grid(
        grad_wre.astype(jnp.bfloat16), grad_wim.astype(jnp.bfloat16), tables[2], tables[3]
    )
    _, pullback = jax.vjp(layer_norm, stream, gain_one, shift_one)
    grad_stream, grad_gain1, grad_shift1 = pullback(grad_first.astype(jnp.float32))
    layer_grads = [
        grad_gain1,
        grad_shift1,
        place_blocks(grad_lw1, spec_w1, first_block),
        place_blocks(grad_lb1, spec_b1, first_block),
        place_blocks(grad_lw2, spec_w2, first_block),
        place_blocks(grad_lb2, spec_b2, first_block),
        grad_gain2,
        grad_shift2,
        grad_win,
        grad_bin,
        grad_wout,
        grad_bout,
    ]
    return (grad_stream + grad_mixed, layer_grads)


def add_into(gradients, start, values):
    middle = [left + right for left, right in zip(gradients[start : start + len(values)], values)]
    return gradients[:start] + middle + gradients[start + len(values) :]


MESH = pl.DeviceIdType.MESH
CH = 2944
OWN = 2934
CHR = 2960
GROWS = 93904


CHIPS = 16
UNIT = 64
PADC = 128
f32 = jnp.float32
bf16 = jnp.bfloat16


def remote(src, dst, send_sem, recv_sem, device):
    return pltpu.make_async_remote_copy(
        src_ref=src,
        dst_ref=dst,
        send_sem=send_sem,
        recv_sem=recv_sem,
        device_id=device,
        device_id_type=MESH,
    )


def chip_device(chip, core):
    return chip // 2, (chip % 2) * 2 + core


def place():
    row = lax.axis_index("row")
    col = lax.axis_index("col")
    core = col % 2
    return row, row * 2 + col // 2, core, (row, col + 1 - 2 * core)


def greet_chips(me, core, sibling):
    barrier = pltpu.get_barrier_semaphore()

    def one(k, carry):
        pl.semaphore_signal(
            barrier,
            inc=1,
            device_id=chip_device(lax.rem(me + k, CHIPS), core),
            device_id_type=MESH,
        )
        return carry

    lax.fori_loop(1, CHIPS, one, 0)
    pl.semaphore_signal(barrier, inc=1, device_id=sibling, device_id_type=MESH)
    return barrier


def split_units(values, units):
    blank = jnp.zeros((UNIT, PADC - BS), f32)
    for part in range(2):
        for block in range(NBLK):
            piece = values[part * UNIT : (part + 1) * UNIT, block * BS : (block + 1) * BS]
            units[part * NBLK + block] = jnp.concatenate([piece, blank], axis=1).astype(bf16)


def join_units(units, joined):
    for part in range(2):
        for block in range(NBLK):
            joined[part * UNIT : (part + 1) * UNIT, block * BS : (block + 1) * BS] = units[
                part * NBLK + block, :, 0:BS
            ].astype(f32)


def normalize(values):
    center = values - jnp.mean(values, axis=-1, keepdims=True)
    spread = jnp.mean(center * center, axis=-1, keepdims=True)
    scale = lax.rsqrt(spread + NORM_EPS)
    return center * scale, scale


def gelu_of(value):
    return 0.5 * value * (1.0 + lax.erf(value * math.sqrt(0.5)))


def gelu_slope(value):
    bell = jnp.exp(-0.5 * value * value) * (1.0 / math.sqrt(2.0 * math.pi))
    return 0.5 * (1.0 + lax.erf(value * math.sqrt(0.5))) + value * bell


def dot(left, right):
    return jnp.dot(left, right, preferred_element_type=f32)


def dot_rows(left, right):
    return lax.dot_general(left, right, (((0,), (0,)), ((), ())), preferred_element_type=f32)


def dot_cols(left, right):
    return lax.dot_general(left, right, (((1,), (1,)), ((), ())), preferred_element_type=f32)


def spread_units(me, core, sibling, units, mine, others, sems, meanwhile):
    send_a, recv_a, send_f, recv_f, local_sem = sems

    def out(k):
        chip = lax.rem(me + k, CHIPS)
        return remote(
            units.at[chip], mine.at[me], send_a.at[k], recv_a.at[k], chip_device(chip, core)
        )

    def handed(k):
        chip = lax.rem(me + CHIPS - k, CHIPS)
        return remote(mine.at[chip], others.at[chip], send_f.at[k], recv_f.at[k], sibling)

    own = pltpu.make_async_copy(units.at[me], mine.at[me], local_sem)
    own.start()

    def begin(k, carry):
        out(k).start()
        return carry

    lax.fori_loop(1, CHIPS, begin, 0)
    meanwhile()
    own.wait()
    handed(0).start()

    def hand(k, carry):
        out(k).wait_recv()
        handed(k).start()
        return carry

    lax.fori_loop(1, CHIPS, hand, 0)

    def arrive(k, carry):
        handed(k).wait_recv()
        return carry

    lax.fori_loop(0, CHIPS, arrive, 0)

    def finish():
        def sent(k, carry):
            out(k).wait_send()
            return carry

        lax.fori_loop(1, CHIPS, sent, 0)

        def sent_on(k, carry):
            handed(k).wait_send()
            return carry

        lax.fori_loop(0, CHIPS, sent_on, 0)

    return finish


def to_spectrum(mine, others, column_table, row_table, waves):
    for h in range(16):
        pair, part = h // 2, pl.ds(32 * (h % 2), 32)
        cells = jnp.concatenate(
            [
                mine[2 * pair, part],
                mine[2 * pair + 1, part],
                others[2 * pair, part],
                others[2 * pair + 1, part],
            ],
            axis=0,
        )
        wave = dot(column_table[...], cells).astype(bf16)
        for g in range(4):
            rows = pl.ds(16 * h, 16)
            waves[g, rows, 0:PADC] = wave[16 * g : 16 * g + 16]
            waves[g, rows, PADC : 2 * PADC] = wave[64 + 16 * g : 80 + 16 * g]
    results = []
    for g in range(4):
        both = dot(row_table[...], waves[g])
        real = both[:256, :PADC] + both[256:, PADC:]
        imag = both[:256, PADC:] - both[256:, :PADC]
        results.append(jnp.concatenate([real, imag], axis=1).astype(bf16))
    return results


def from_spectrum(g, spec, row_table, back):
    both = dot(row_table[...], spec)
    real = (both[:256, :PADC] - both[256:, PADC:]).astype(bf16)
    imag = (both[:256, PADC:] + both[256:, :PADC]).astype(bf16)
    for h in range(16):
        back[h, 16 * g : 16 * g + 16] = real[16 * h : 16 * h + 16]
        back[h, 64 + 16 * g : 80 + 16 * g] = imag[16 * h : 16 * h + 16]


def gather_units(row, me, core, sibling, back, inverse_table, bufs, sems, settle, meanwhile):
    own_sum, to_sib, from_sib, ready, landed = bufs
    send_s, recv_s, send_b, recv_b, local_sem = sems

    def swap(pair):
        rows = pl.ds(2 * pair, 2)
        return remote(
            to_sib.at[rows], from_sib.at[rows], send_s.at[pair], recv_s.at[pair], sibling
        )

    def partial(j, carry):
        pair = lax.rem(row + 1 + j, 8)
        for half in range(2):
            sums = dot(inverse_table[...], back[2 * pair + half])
            part = pl.ds(32 * half, 32)
            for x in range(2):
                own_sum[2 * pair + x, part] = sums[32 * x : 32 * x + 32]
                to_sib[2 * pair + x, part] = sums[64 + 32 * x : 96 + 32 * x].astype(bf16)
        swap(pair).start()
        return carry

    lax.fori_loop(0, 8, partial, 0)
    settle()

    def home(chip, k):
        return remote(
            ready.at[chip], landed.at[me], send_b.at[k], recv_b.at[k], chip_device(chip, core)
        )

    own = pltpu.make_async_copy(ready.at[me], landed.at[me], local_sem)

    def total(j, carry):
        pair = lax.rem(row + 1 + j, 8)
        swap(pair).wait_recv()
        rows = pl.ds(2 * pair, 2)
        ready[rows] = (own_sum[rows] + from_sib[rows].astype(f32)).astype(bf16)
        for x in range(2):
            chip = 2 * pair + x
            k = lax.rem(chip - me + CHIPS, CHIPS)

            @pl.when(k != 0)
            def _():
                home(chip, k).start()

        return carry

    lax.fori_loop(0, 8, total, 0)
    own.start()
    meanwhile()

    def landed_all(k, carry):
        home(lax.rem(me + k, CHIPS), k).wait_recv()
        return carry

    lax.fori_loop(1, CHIPS, landed_all, 0)
    own.wait()

    def finish():
        def sent(k, carry):
            home(lax.rem(me + k, CHIPS), k).wait_send()
            return carry

        lax.fori_loop(1, CHIPS, sent, 0)

        def swapped(pair, carry):
            swap(pair).wait_send()
            return carry

        lax.fori_loop(0, 8, swapped, 0)

    return finish


def filter_scratch():
    vm = pltpu.VMEM
    dma = pltpu.SemaphoreType.DMA
    block = (CHIPS, UNIT, PADC)
    return [
        vm(block, bf16),
        vm(block, bf16),
        vm(block, bf16),
        vm((4, 256, 256), bf16),
        vm((16, 128, PADC), bf16),
        vm(block, f32),
        vm(block, bf16),
        vm(block, bf16),
        vm(block, bf16),
        vm(block, bf16),
        vm((2 * UNIT, D), f32),
        dma((CHIPS,)),
        dma((CHIPS,)),
        dma((CHIPS,)),
        dma((CHIPS,)),
        dma,
        dma((8,)),
        dma((8,)),
        dma((CHIPS,)),
        dma((CHIPS,)),
        dma,
    ]


def transform_tables(core):
    width, height = 128, 16
    order = []
    for side in range(2):
        cols = [[32 * (2 * x + (c if side == 0 else 1 - c)) + i for x in range(2) for i in range(32)] for c in range(2)]
        order.append(cols)
    column, inverse = [], []
    for c in range(2):
        cells = np.array(order[0][c] + order[1][c])
        waves = 64 * c + np.arange(64)
        angle = 2.0 * np.pi * (np.outer(waves, cells) % width) / width
        cos, sin = np.cos(angle) / np.sqrt(width), np.sin(angle) / np.sqrt(width)
        column.append(np.concatenate([cos, -sin], axis=0))
        inverse.append(np.concatenate([cos, -sin], axis=0).T)
    steps = np.arange(height)
    angle = 2.0 * np.pi * (np.outer(steps, steps) % height) / height
    eye = np.eye(16)
    rows = np.concatenate(
        [np.kron(np.cos(angle), eye), np.kron(np.sin(angle), eye)], axis=0
    ) / np.sqrt(height)
    pick = lambda both: lax.dynamic_index_in_dim(jnp.asarray(np.stack(both), bf16), core, 0, False)
    return pick(column), pick(inverse), jnp.asarray(rows, bf16)


RING = 8
GATHER_CUTS = (0, 640, 1280, 2112, 2944)
SUM_CUTS = (0, 640, 1280, 2128, 2960)


def ring_place(row):
    return jnp.where(row % 2 == 0, row // 2, 7 - row // 2)


def ring_row(spot):
    return jnp.where(spot < 4, 2 * spot, 2 * (7 - spot) + 1)


def gather_kernel(shard, flat, ring_s, ring_r, x_s, x_r, sib_s, sib_r, own_sem):
    row, me, core, sibling = place()
    x = me % 2
    spot = ring_place(row)
    beside = (row, (1 - x) * 2 + core)
    ahead = (ring_row((spot + 1) % RING), x * 2 + core)
    behind = (ring_row((spot + RING - 1) % RING), x * 2 + core)
    ways = (ahead, behind)
    barrier = pltpu.get_barrier_semaphore()
    for device in (ahead, behind, beside, sibling):
        pl.semaphore_signal(barrier, inc=1, device_id=device, device_id_type=MESH)

    def span(part):
        return GATHER_CUTS[part], GATHER_CUTS[part + 1] - GATHER_CUTS[part]

    def piece(source_spot, source_x, part):
        low, size = span(part)
        base = (ring_row(source_spot) * 4 + source_x * 2 + core) * CH
        return flat.at[pl.ds(pl.multiple_of(base + low, 16), size)]

    def mine(part):
        low, size = span(part)
        return shard.at[pl.ds(low, size)]

    def origin(hop, way):
        return (spot - hop + RING) % RING if way == 0 else (spot + hop) % RING

    def item(hop, way, what):
        part = way if what else 2 + way
        return origin(hop, way), (1 - x if what == 2 else x), part

    def ring(hop, way, what, first=False):
        to = piece(*item(hop, way, what))
        source = mine(item(hop, way, what)[2]) if first and what < 2 else to
        return remote(
            source, to, ring_s.at[what, way, hop], ring_r.at[what, way, hop], ways[way]
        )

    def cross(slot, way, first=False):
        if isinstance(slot, int) and slot == 8:
            to, source = piece(spot, x, way), mine(way)
        else:
            to = piece(origin(slot, way), x, 2 + way)
            source = mine(2 + way) if first else to
        return remote(source, to, x_s.at[way, slot], x_r.at[way, slot], beside)

    def share(where, slot, way, what):
        return remote(where, where, sib_s.at[what, way, slot], sib_r.at[what, way, slot], sibling)

    def from_beside(slot, way):
        if isinstance(slot, int) and slot == 8:
            return piece(spot, 1 - x, way)
        return piece(origin(slot, way), 1 - x, 2 + way)

    base = pl.multiple_of((row * 4 + x * 2 + core) * CH, 16)
    whole = flat.at[pl.ds(base, CH)]
    own = pltpu.make_async_copy(shard, whole, own_sem)
    own.start()
    pl.semaphore_wait(barrier, 4)
    for way in range(2):
        ring(0, way, 0, True).start()
        cross(8, way).start()
    for way in range(2):
        ring(0, way, 1, True).start()
        cross(0, way, True).start()
    given = remote(shard, whole, sib_s.at[3, 0, 9], sib_r.at[3, 0, 9], sibling)
    given.start()
    for way in range(2):
        cross(8, way).wait_recv()
        ring(0, way, 2).start()
        share(from_beside(8, way), 8, way, 3).start()

    def step(hop, carry):
        for what in range(3):
            for way in range(2):
                ring(hop - 1, way, what).wait_recv()

                @pl.when(hop < RING - 1)
                def _():
                    ring(hop, way, what).start()

                if what == 0:
                    cross(hop, way).start()
                share(piece(*item(hop, way, what)), hop - 1, way, what).start()
        for way in range(2):
            cross(hop - 1, way).wait_recv()
            share(from_beside(hop - 1, way), hop - 1, way, 3).start()
        return carry

    lax.fori_loop(1, RING, step, 0)
    for way in range(2):
        cross(RING - 1, way).wait_recv()
        share(from_beside(RING - 1, way), RING - 1, way, 3).start()
    own.wait()

    def settle(hop, carry):
        for way in range(2):
            for what in range(3):
                ring(hop, way, what).wait_send()
                share(piece(*item(hop + 1, way, what)), hop, way, what).wait()
        return carry

    lax.fori_loop(0, RING - 1, settle, 0)

    def settle_cross(slot, carry):
        for way in range(2):
            cross(slot, way).wait_send()
            share(from_beside(slot, way), slot, way, 3).wait()
        return carry

    lax.fori_loop(0, RING, settle_cross, 0)
    for way in range(2):
        cross(8, way).wait_send()
        share(from_beside(8, way), 8, way, 3).wait()
    given.wait()


def ag(shard):
    anywhere = pl.BlockSpec(memory_space=pl.ANY)
    dma = pltpu.SemaphoreType.DMA
    return pl.pallas_call(
        gather_kernel,
        out_shape=jax.ShapeDtypeStruct((32 * CH, 128), bf16),
        in_specs=[anywhere],
        out_specs=anywhere,
        scratch_shapes=[
            dma((3, 2, 7)),
            dma((3, 2, 7)),
            dma((2, 9)),
            dma((2, 9)),
            dma((4, 2, 10)),
            dma((4, 2, 10)),
            dma,
        ],
        compiler_params=pltpu.CompilerParams(collective_id=0, has_side_effects=True),
        name="gather_weights",
    )(shard)


def sum_kernel(
    grad, loss, total, stats,
    own, sib, xin, rin_b, rin_a, xlast, st_mine, st_sib, st_sum, st_all,
    own_s, sib_s, sib_r, x_s, x_r, last_s, last_r, ring_s, ring_r, tell_s, tell_r, pair_s, pair_r,
):
    row, me, core, sibling = place()
    x = me % 2
    spot = ring_place(row)
    beside = (row, (1 - x) * 2 + core)
    ahead = (ring_row((spot + 1) % RING), x * 2 + core)
    behind = (ring_row((spot + RING - 1) % RING), x * 2 + core)
    ways = (ahead, behind)
    barrier = greet_chips(me, core, sibling)
    sizes = [SUM_CUTS[k + 1] - SUM_CUTS[k] for k in range(4)]

    def owner(turn, way):
        return (spot - 1 - turn + 2 * RING) % RING if way == 0 else (spot + 1 + turn) % RING

    def source(turn, way, other_x, part, side):
        owner_x = (1 - x) if other_x else x
        base = (ring_row(owner(turn, way)) * 4 + owner_x * 2 + side) * OWN // 16 * 16
        return grad.at[pl.ds(pl.multiple_of(base + SUM_CUTS[part], 16), sizes[part])]

    def part_of(way, what):
        return way if what >= 2 else 2 + way

    def held(buf, turn, way, what):
        part = part_of(way, what)
        return buf.at[what % 2, turn, pl.ds(SUM_CUTS[part], sizes[part])]

    def load(turn, way, what):
        return pltpu.make_async_copy(
            source(turn, way, what % 2, part_of(way, what), core),
            held(own, turn, way, what),
            own_s.at[what, way, turn],
        )

    def give(turn, way, what):
        return remote(
            source(turn, way, what % 2, part_of(way, what), 1 - core),
            held(sib, turn, way, what),
            sib_s.at[what, way, turn],
            sib_r.at[what, way, turn],
            sibling,
        )

    def cross(turn, way):
        return remote(
            held(own, turn, way, 1),
            xin.at[turn, pl.ds(SUM_CUTS[2 + way] - SUM_CUTS[2], sizes[2 + way])],
            x_s.at[way, turn],
            x_r.at[way, turn],
            beside,
        )

    def got(way, slot, what):
        if what == 0:
            return rin_b.at[slot, pl.ds(SUM_CUTS[2 + way] - SUM_CUTS[2], sizes[2 + way])]
        return rin_a.at[what - 2, slot, pl.ds(SUM_CUTS[way], sizes[way])]

    def ring(turn, way, what, first=False):
        where = held(own, turn, way, what) if first else got(way, turn - 1, what)
        return remote(
            where,
            got(way, turn, what),
            ring_s.at[what, way, turn],
            ring_r.at[what, way, turn],
            ways[way],
        )

    order = (1, 2, 3, 0)

    def begin_own(turn, carry):
        for what in order:
            for way in range(2):
                load(turn, way, what).start()
        return carry

    def begin_sib(turn, carry):
        for what in order:
            for way in range(2):
                give(turn, way, what).start()
        return carry

    begin_own(0, 0)
    pl.semaphore_wait(barrier, CHIPS)
    begin_sib(0, 0)
    lax.fori_loop(1, RING, lambda t, c: begin_sib(t, begin_own(t, c)), 0)

    def both(turn, way, what):
        load(turn, way, what).wait()
        give(turn, way, what).wait_recv()
        return held(own, turn, way, what)[...].astype(f32) + held(sib, turn, way, what)[...].astype(f32)

    def send_across(turn):
        for way in range(2):
            held(own, turn, way, 1)[...] = both(turn, way, 1).astype(bf16)
            cross(turn, way).start()

    def across(turn, way):
        cross(turn, way).wait_recv()
        return xin[turn, pl.ds(SUM_CUTS[2 + way] - SUM_CUTS[2], sizes[2 + way])].astype(f32)

    send_across(0)
    for what in (2, 3):
        for way in range(2):
            held(own, 0, way, what)[...] = both(0, way, what).astype(bf16)
            ring(0, way, what, True).start()
    send_across(1)
    for way in range(2):
        held(own, 0, way, 0)[...] = (both(0, way, 0) + across(0, way)).astype(bf16)
        ring(0, way, 0, True).start()

    def step(turn, carry):
        send_across(turn + 1)
        for what in (2, 3, 0):
            for way in range(2):
                part = both(turn, way, what)
                if what == 0:
                    part = part + across(turn, way)
                ring(turn - 1, way, what, True).wait_recv()
                where = got(way, turn - 1, what)
                where[...] = (where[...].astype(f32) + part).astype(bf16)
                ring(turn, way, what).start()
        return carry

    lax.fori_loop(1, RING - 1, step, 0)
    last = RING - 1
    def to_beside(way):
        return remote(
            got(way, last - 1, 3),
            xlast.at[pl.ds(SUM_CUTS[way], sizes[way])],
            last_s.at[way],
            last_r.at[way],
            beside,
        )

    for way in range(2):
        part = both(last, way, 3)
        ring(last - 1, way, 3, True).wait_recv()
        where = got(way, last - 1, 3)
        where[...] = (where[...].astype(f32) + part).astype(bf16)
        to_beside(way).start()
    for what in (2, 0):
        for way in range(2):
            part = both(last, way, what)
            if what == 0:
                part = part + across(last, way)
            ring(last - 1, way, what, True).wait_recv()
            low = SUM_CUTS[part_of(way, what)]
            total[low : low + sizes[part_of(way, what)]] = got(way, last - 1, what)[...].astype(f32) + part
    for way in range(2):
        to_beside(way).wait_recv()
        low = SUM_CUTS[way]
        total[low : low + sizes[way]] += xlast[low : low + sizes[way]].astype(f32)

    first = ((row * 4 + x * 2 + core) * OWN) % 16
    rows = lax.broadcasted_iota(jnp.int32, (CHR, 128), 0)
    value = total[...]
    squares = jnp.where((rows >= first) & (rows < first + OWN), value * value, 0.0)
    st_mine[0:8] = jnp.sum(squares.reshape(CHR // 8, 8, 128), axis=0)
    st_mine[8:16] = loss[...]
    pair = remote(st_mine, st_sib, pair_s, pair_r, sibling)
    pair.start()
    pair.wait_recv()
    st_sum[...] = st_mine[...] + st_sib[...]
    st_all[me] = st_sum[...]

    def tell(k):
        return remote(
            st_sum, st_all.at[me], tell_s.at[k], tell_r.at[k],
            chip_device(lax.rem(me + k, CHIPS), core),
        )

    def tell_one(k, carry):
        tell(k).start()
        return carry

    lax.fori_loop(1, CHIPS, tell_one, 0)

    def settle(turn, carry):
        for way in range(2):
            for what in range(4):
                give(turn, way, what).wait_send()
            cross(turn, way).wait_send()

            @pl.when(turn < RING - 1)
            def _():
                for what in (0, 2, 3):
                    ring(turn, way, what, True).wait_send()

        return carry

    lax.fori_loop(0, RING, settle, 0)
    for way in range(2):
        to_beside(way).wait_send()

    def told(k, carry):
        tell(k).wait_recv()
        return carry

    lax.fori_loop(1, CHIPS, told, 0)
    everything = st_all[0]
    for k in range(1, CHIPS):
        everything = everything + st_all[k]
    stats[...] = everything

    def tell_done(k, carry):
        tell(k).wait_send()
        return carry

    lax.fori_loop(1, CHIPS, tell_done, 0)
    pair.wait_send()


def rs(grad, loss):
    vm, dma = pltpu.VMEM, pltpu.SemaphoreType.DMA
    first, second = SUM_CUTS[2], SUM_CUTS[4] - SUM_CUTS[2]
    shape = jax.ShapeDtypeStruct
    return pl.pallas_call(
        sum_kernel,
        out_shape=[shape((CHR, 128), f32), shape((16, 128), f32)],
        in_specs=[pl.BlockSpec(memory_space=pl.ANY), pl.BlockSpec(memory_space=vm)],
        out_specs=[pl.BlockSpec(memory_space=vm)] * 2,
        scratch_shapes=[
            vm((2, RING, CHR, 128), bf16),
            vm((2, RING, CHR, 128), bf16),
            vm((RING, second, 128), bf16),
            vm((RING - 1, second, 128), bf16),
            vm((2, RING - 1, first, 128), bf16),
            vm((first, 128), bf16),
            vm((16, 128), f32),
            vm((16, 128), f32),
            vm((16, 128), f32),
            vm((CHIPS, 16, 128), f32),
            dma((4, 2, RING)),
            dma((4, 2, RING)),
            dma((4, 2, RING)),
            dma((2, RING)),
            dma((2, RING)),
            dma((2,)),
            dma((2,)),
            dma((4, 2, RING - 1)),
            dma((4, 2, RING - 1)),
            dma((CHIPS,)),
            dma((CHIPS,)),
            dma,
            dma,
        ],
        compiler_params=pltpu.CompilerParams(
            collective_id=1, has_side_effects=True, vmem_limit_bytes=56 << 20
        ),
        name="sum_gradients",
    )(grad, loss)


MATS = [(PIN, D), (D, FF), (FF, D), (D, FF), (FF, D), (D, PIN)]
SMALL_LAYER = 2352
SMALLS = [6 + SMALL_LAYER, 24, 6 + SMALL_LAYER, 24, 18, 10]
PIECE = 256


def flat_sections():
    at = 0
    found = []
    for (depth, cols), small in zip(MATS, SMALLS):
        per_row = cols // LANES
        found.append((at, depth, per_row, at + depth * per_row, small))
        at += depth * per_row + small
    return found


def piece_rows(depth, per_row):
    rows = depth
    while rows * per_row > 7680:
        rows -= PIECE
        while depth % rows:
            rows -= PIECE
    return rows


def put_rows(wide, at, value):
    for k in range(value.shape[1] // LANES):
        wide[at + k : at + k + 1] = value[:, k * LANES : (k + 1) * LANES]


def put_block_weight(wide, at, block, grad, square):
    wide[at : at + 2 * NBLK * BLOCK_ROWS] = jnp.zeros((2 * NBLK * BLOCK_ROWS, LANES), f32)
    square[0] = grad[:PADC, :PADC] + grad[PADC:, PADC:]
    square[1] = grad[:PADC, PADC:] - grad[PADC:, :PADC]
    for part in range(2):
        a, b, c, d = (square[part, pl.ds(q, 24, stride=4), :] for q in range(4))
        rows = (
            jnp.concatenate([a[:, :96], b[:, :32]], axis=1),
            jnp.concatenate([b[:, 32:96], c[:, :64]], axis=1),
            jnp.concatenate([c[:, 64:96], d[:, :96]], axis=1),
        )
        for q, value in enumerate(rows):
            wide[pl.ds(at + (part * NBLK + block) * BLOCK_ROWS + q, 24, stride=3), :] = value


def put_block_bias(wide, at, block, grad):
    found = []
    for part in range(2):
        piece = grad[:, part * PADC : part * PADC + BS]
        found += [jnp.where(block == k, piece, 0.0) for k in range(NBLK)]
    put_rows(wide, at, jnp.concatenate(found, axis=1))


def write_section(i, xs, gs, bufs):
    across, side, wide, narrow, edge, flat, sem = bufs
    start, depth, per_row, _, _ = flat_sections()[i]
    cols = per_row * LANES
    for half in range(2):
        for part in range(0, depth, PIECE):
            across[part : part + PIECE, half * 128 : half * 128 + 128] = xs[half][
                :, part : part + PIECE
            ].T
        side[half * 128 : half * 128 + 128, 0:cols] = gs[half][...]
    rows = piece_rows(depth, per_row)
    full = rows * per_row
    shift = start % 16
    skip = 16 if shift else 0
    turns = depth // rows

    def emit(at, low):
        return pltpu.make_async_copy(
            narrow.at[pl.ds(low, full - low)], flat.at[pl.ds(at + low, full - low)], sem
        )

    def step(it, carry):
        top = pl.multiple_of(it * rows, PIECE)
        for part in range(0, rows, PIECE):
            left = across[pl.ds(pl.multiple_of(top + part, PIECE), PIECE), :]
            for j in range(0, per_row, 2):
                value = dot(left, side[:, j * LANES : (j + 2) * LANES])
                for by in range(2):
                    wide[pl.ds(shift + part * per_row + j + by, PIECE, stride=per_row), :] = value[
                        :, by * LANES : (by + 1) * LANES
                    ]

        @pl.when(it == 1)
        def _():
            emit(0, skip).wait()

        @pl.when(it > 1)
        def _():
            emit(0, 0).wait()

        narrow[0:full] = wide[0:full].astype(bf16)

        @pl.when(it == 0)
        def _():
            edge[2 * i] = wide[0:16]
            emit(start - shift, skip).start()

        @pl.when(it > 0)
        def _():
            emit(pl.multiple_of(start - shift + it * full, 16), 0).start()

        wide[0:16] = wide[full : full + 16]
        return carry

    lax.fori_loop(0, turns, step, 0)
    edge[2 * i + 1] = wide[0:16]
    emit(0, skip if turns == 1 else 0).wait()


def write_small(i, put, bufs):
    _, _, wide, narrow, edge, flat, sem = bufs
    _, _, _, at, count = flat_sections()[i]
    shift = at % 16
    wide[0:16] = edge[2 * i + 1]
    put(i, shift)
    end = shift + count
    total = GROWS - at + shift if i == 5 else -(-end // 16) * 16
    if i == 5:
        wide[end:total] = jnp.zeros((total - end, LANES), f32)
    elif total > end:
        wide[end:total] = edge[2 * i + 2, 16 - (total - end) : 16]
    narrow[0:total] = wide[0:total].astype(bf16)
    done = pltpu.make_async_copy(
        narrow.at[pl.ds(0, total)], flat.at[pl.ds(at - shift, total)], sem
    )
    done.start()
    done.wait()


CELLS = 2 * UNIT
FCHUNK = 768
FILTER_SEMS = 10


def norm_adjoint(values, gain, grad):
    normed, scale = normalize(values)
    inner = grad * gain
    along = jnp.mean(inner * normed, axis=-1, keepdims=True)
    flat = jnp.mean(inner, axis=-1, keepdims=True)
    return (
        scale * (inner - flat - normed * along),
        jnp.sum(grad * normed, axis=0, keepdims=True),
        jnp.sum(grad, axis=0, keepdims=True),
    )


SMALL_AT = []
for _count in SMALLS:
    SMALL_AT.append(SMALL_AT[-1] + -(-SMALLS[len(SMALL_AT) - 1] // 8) * 8 if SMALL_AT else 0)
SMALL_ROWS = SMALL_AT[-1] + 16
AT_NORM = (0, 6, 2340, 2346)
AT_W1, AT_B1, AT_W2, AT_B2 = 12, 1164, 1176, 2328
BLOCK_ROWS = BS * BS // LANES


def aligned_part(at, count):
    low = at // 16 * 16
    return low, -(-(at + count - low) // 16) * 16


def unpack_sections(flat, raw, wide, in_sem, wanted):
    steps = []
    for i, target in wanted:
        start, depth, per_row, _, _ = flat_sections()[i]
        rows = piece_rows(depth, per_row)
        for top in range(0, depth, rows):
            steps.append((start + top * per_row, per_row, top, rows, target))

    def fetch(n):
        at, per_row, _, rows, _ = steps[n]
        low, size = aligned_part(at, rows * per_row)
        return pltpu.make_async_copy(
            flat.at[pl.ds(low, size)], raw.at[n % 2, pl.ds(0, size)], in_sem.at[n % 2]
        ), size

    fetch(0)[0].start()
    for n, (at, per_row, top, rows, target) in enumerate(steps):
        if n + 1 < len(steps):
            fetch(n + 1)[0].start()
        copy, size = fetch(n)
        copy.wait()
        wide[0:size] = raw[n % 2, 0:size].astype(f32)
        for part in range(0, rows, PIECE):
            for j in range(per_row):
                target[top + part : top + part + PIECE, j * LANES : (j + 1) * LANES] = wide[
                    pl.ds(at % 16 + part * per_row + j, PIECE, stride=per_row), :
                ].astype(bf16)


def unpack_small(flat, raw, wide, in_sem, small):
    def fetch(n):
        _, _, _, at, count = flat_sections()[n]
        low, size = aligned_part(at, count)
        return pltpu.make_async_copy(
            flat.at[pl.ds(low, size)], raw.at[n % 2, pl.ds(0, size)], in_sem.at[n % 2]
        ), size, at - low, count

    fetch(0)[0].start()
    for n in range(6):
        if n < 5:
            fetch(n + 1)[0].start()
        copy, size, shift, count = fetch(n)
        copy.wait()
        wide[0:size] = raw[n % 2, 0:size].astype(f32)
        small[SMALL_AT[n] : SMALL_AT[n] + count] = wide[shift : shift + count]


def long_row(small, at, count):
    return jnp.concatenate([small[at + k : at + k + 1] for k in range(count)], axis=1)


def block_weight(small, at, block, square, out):
    blank = jnp.zeros((24, PADC - BS), f32)
    square[...] = jnp.zeros_like(square)
    for part in range(2):
        base = at + (part * NBLK + block) * BLOCK_ROWS
        a, b, c = (small[pl.ds(base + q, 24, stride=3), :] for q in range(3))
        pieces = (
            a[:, :96],
            jnp.concatenate([a[:, 96:], b[:, :64]], axis=1),
            jnp.concatenate([b[:, 64:], c[:, :32]], axis=1),
            c[:, 32:],
        )
        for q, piece in enumerate(pieces):
            piece = jnp.concatenate([piece, blank], axis=1)
            if part == 0:
                square[0, pl.ds(q, 24, stride=4), :] = piece
                square[3, pl.ds(q, 24, stride=4), :] = piece
            else:
                square[1, pl.ds(q, 24, stride=4), :] = piece
                square[2, pl.ds(q, 24, stride=4), :] = -piece
    for quarter in range(4):
        top, left = quarter // 2 * PADC, quarter % 2 * PADC
        out[top : top + PADC, left : left + PADC] = square[quarter].astype(bf16)


def block_bias(small, at, block):
    blank = jnp.zeros((1, PADC - BS), f32)
    both = long_row(small, at, 12)
    found = []
    for part in range(2):
        value = jnp.zeros((1, BS), f32)
        for k in range(NBLK):
            low = (part * NBLK + k) * BS
            value = value + jnp.where(block == k, both[:, low : low + BS], 0.0)
        found += [value, blank]
    return jnp.concatenate(found, axis=1)


def forward_kernel(*refs):
    x0, goals, mask, weight, column, inverse, rows, flat = refs[:8]
    (streams, waves_o, mixeds, normeds, befores, hiddens, lasts, tails, errors,
     embed_h, in0, out0, in1, out1, head_h, x1, loss, norms, tail, w1, b1, w2) = refs[8:30]
    (embed, w_in, w_out, head, flow, x_now, s_stream, s_waves, s_mixed, s_norm, s_before, s_hidden,
     s_tail, s_error, raw, wide, small, square, b2, c1, c2, embed_b, head_b,
     weight_sem, out_sem, tail_sem, in_sem) = refs[30:57]
    units, mine, others, waves, back, own_sum, to_sib, from_sib, ready, landed, joined = refs[57:68]
    sems = refs[68:]
    row, me, core, sibling = place()
    barrier = greet_chips(me, core, sibling)
    stores = [
        pltpu.make_async_copy(source, target, weight_sem.at[k])
        for k, (source, target) in enumerate(
            [(embed, embed_h), (w_in.at[0], in0), (w_out.at[0], out0), (w_in.at[1], in1),
             (w_out.at[1], out1), (head, head_h)]
        )
    ]
    block = me % NBLK
    unpack_small(flat, raw, wide, in_sem, small)
    embed_b[...] = long_row(small, SMALL_AT[0], 6)
    head_b[...] = long_row(small, SMALL_AT[5], 10)
    for layer in range(LAYERS):
        base = SMALL_AT[2 * layer] + 6
        for k, at in enumerate(AT_NORM):
            norms[layer, k : k + 1] = long_row(small, base + at, 6)
        c1[layer] = long_row(small, SMALL_AT[2 * layer + 1], 24)
        c2[layer] = long_row(small, SMALL_AT[2 * layer + 2], 6)
        block_weight(small, base + AT_W1, block, square, w1.at[layer])
        block_weight(small, base + AT_W2, block, square, w2.at[layer])
        b1[layer] = block_bias(small, base + AT_B1, block)
        b2[layer] = block_bias(small, base + AT_B2, block)
    tail[0:1] = long_row(small, SMALL_AT[4] + 6, 6)
    tail[1:2] = long_row(small, SMALL_AT[4] + 12, 6)
    unpack_sections(flat, raw, wide, in_sem, [(0, embed)])
    stores[0].start()
    x_now[...] = x0[...]
    loss[...] = jnp.zeros_like(loss)

    def saves(it):
        pairs = [(s_stream, streams), (s_waves, waves_o), (s_mixed, mixeds), (s_norm, normeds),
                 (s_before, befores), (s_hidden, hiddens)]
        return [
            pltpu.make_async_copy(source, target.at[it], out_sem.at[k])
            for k, (source, target) in enumerate(pairs)
        ]

    def tail_saves(step):
        pairs = [(flow, lasts), (s_tail, tails), (s_error, errors)]
        return [
            pltpu.make_async_copy(source, target.at[step], tail_sem.at[k])
            for k, (source, target) in enumerate(pairs)
        ]

    def when_it(cond, action):
        @pl.when(cond)
        def _():
            action()

    def unpack_when(it, number, wanted, done):
        def go():
            unpack_sections(flat, raw, wide, in_sem, wanted)
            for k in done:
                stores[k].start()

        when_it(it == number, go)

    def meanwhile_in(it):
        unpack_when(it, 0, [(1, w_in.at[0])], [1])
        unpack_when(it, 1, [(3, w_in.at[1])], [3])

    def meanwhile_out(it):
        unpack_when(it, 0, [(2, w_out.at[0])], [2])
        unpack_when(it, 1, [(4, w_out.at[1]), (5, head)], [4, 5])

    def body(it, carry):
        step, layer = it // 2, it % 2

        def start_step():
            flow[...] = dot(x_now[...], embed[...]) + embed_b[...]

        def tail_done():
            for save in tail_saves(0):
                save.wait()

        when_it(it == 2, tail_done)
        when_it(layer == 0, start_step)

        def saved():
            for save in saves(it):
                save.wait()

        when_it(it > 0, saved)
        s_stream[...] = flow[...]
        normed, _ = normalize(flow[...])
        split_units(normed * norms[layer, 0:1] + norms[layer, 1:2], units)
        when_it(it == 0, lambda: pl.semaphore_wait(barrier, CHIPS))

        finish_one = spread_units(
            me, core, sibling, units, mine, others, sems[:5], lambda: meanwhile_in(it)
        )
        groups = to_spectrum(mine, others, column, rows, waves)
        for g in range(4):
            s_waves[g] = groups[g]
            hidden = gelu_of(dot(groups[g], w1[layer]) + b1[layer]).astype(bf16)
            spec = (dot(hidden, w2[layer]) + b2[layer]).astype(bf16)
            from_spectrum(g, spec, rows, back)
        finish_two = gather_units(
            row, me, core, sibling, back, inverse,
            (own_sum, to_sib, from_sib, ready, landed), sems[5:], finish_one,
            lambda: meanwhile_out(it),
        )
        join_units(landed, joined)
        mixed = flow[...] + joined[...]
        s_mixed[...] = mixed
        normed, _ = normalize(mixed)
        s_norm[...] = (normed * norms[layer, 2:3] + norms[layer, 3:4]).astype(bf16)
        flow[...] = mixed + c2[layer]

        def chunk(c, carry):
            part = pl.ds(pl.multiple_of(c * FCHUNK, FCHUNK), FCHUNK)
            before = dot(s_norm[...], w_in[layer, :, part]) + c1[layer, :, part]
            s_before[:, part] = before.astype(bf16)
            hidden = gelu_of(before).astype(bf16)
            s_hidden[:, part] = hidden
            flow[...] += dot(hidden, w_out[layer, part, :])
            return carry

        lax.fori_loop(0, FF // FCHUNK, chunk, 0)
        for save in saves(it):
            save.start()
        finish_two()
        def end_step():
            normed, _ = normalize(flow[...])
            s_tail[...] = (normed * tail[0:1] + tail[1:2]).astype(bf16)
            predicted = dot(s_tail[...], head[...]) + head_b[...]
            error = predicted - goals[step].astype(f32)
            s_error[...] = error
            loss[...] += weight[...] * jnp.sum(error * error, axis=-1, keepdims=True)
            x_now[...] = (predicted * mask[...]).astype(bf16)
            for save in tail_saves(step):
                save.start()

        when_it(layer == 1, end_step)
        when_it(it == 1, lambda: x1.__setitem__(Ellipsis, x_now[...]))
        return carry

    lax.fori_loop(0, 4, body, 0)
    for save in saves(3):
        save.wait()
    for save in tail_saves(1):
        save.wait()
    for store in stores:
        store.wait()


def forward_pass(*args):
    vm, dma = pltpu.VMEM, pltpu.SemaphoreType.DMA
    whole, anywhere = pl.BlockSpec(memory_space=vm), pl.BlockSpec(memory_space=pl.ANY)
    shape = jax.ShapeDtypeStruct
    return pl.pallas_call(
        forward_kernel,
        out_shape=[
            shape((4, CELLS, D), f32),
            shape((4, 4, 256, 256), bf16),
            shape((4, CELLS, D), f32),
            shape((4, CELLS, D), bf16),
            shape((4, CELLS, FF), bf16),
            shape((4, CELLS, FF), bf16),
            shape((2, CELLS, D), f32),
            shape((2, CELLS, D), bf16),
            shape((2, CELLS, PIN), f32),
            *[shape(dims, bf16) for dims in MATS],
            shape((CELLS, PIN), bf16),
            shape((CELLS, 1), f32),
            shape((2, 4, D), f32),
            shape((2, D), f32),
            shape((2, 256, 256), bf16),
            shape((2, 1, 256), f32),
            shape((2, 256, 256), bf16),
        ],
        in_specs=[whole] * 7 + [anywhere],
        out_specs=[anywhere] * 15 + [whole] * 7,
        scratch_shapes=[
            vm((PIN, D), bf16),
            vm((2, D, FF), bf16),
            vm((2, FF, D), bf16),
            vm((D, PIN), bf16),
            vm((CELLS, D), f32),
            vm((CELLS, PIN), bf16),
            vm((CELLS, D), f32),
            vm((4, 256, 256), bf16),
            vm((CELLS, D), f32),
            vm((CELLS, D), bf16),
            vm((CELLS, FF), bf16),
            vm((CELLS, FF), bf16),
            vm((CELLS, D), bf16),
            vm((CELLS, PIN), f32),
            vm((2, 7696, LANES), bf16),
            vm((7696, LANES), f32),
            vm((SMALL_ROWS, LANES), f32),
            vm((4, PADC, PADC), f32),
            vm((2, 1, 256), f32),
            vm((2, 1, FF), f32),
            vm((2, 1, D), f32),
            vm((1, D), f32),
            vm((1, PIN), f32),
            dma((6,)),
            dma((6,)),
            dma((3,)),
            dma((2,)),
        ]
        + filter_scratch(),
        compiler_params=pltpu.CompilerParams(
            collective_id=2, has_side_effects=True, vmem_limit_bytes=56 << 20
        ),
        name="forward_pass",
    )(*args)


def backward_kernel(*refs):
    (gscale, mask, norms, tail, column, inverse, rows, w1, b1, w2,
     embed_h, in0, out0, in1, out1, head_h,
     streams, waves_h, mixeds, befores, lasts, errors, inputs, x1, normeds, hiddens, tails) = refs[:27]
    flat = refs[27]
    (sum_norm, sum_c1, sum_tail, sum_head, grad_w1, grad_w2, grad_b,
     embed, w_in, w_out, head, flow, carried, i_stream, i_waves, i_mixed, i_before, i_last, i_error,
     s_pred, s_out, s_pre, s_embed, g_norm, x_in, x_out, x_tail,
     across, side, wide, narrow, edge, square,
     weight_sem, in_sem, tail_in, section_sem, flat_sem) = refs[28:66]
    units, mine, others, waves, back, own_sum, to_sib, from_sib, ready, landed, joined = refs[66:77]
    sems = refs[77:]
    bufs = (across, side, wide, narrow, edge, flat, flat_sem)
    row, me, core, sibling = place()
    barrier = greet_chips(me, core, sibling)

    def when_it(cond, action):
        @pl.when(cond)
        def _():
            action()

    loads = [
        pltpu.make_async_copy(source, target, weight_sem.at[k])
        for k, (source, target) in enumerate(
            [(head_h, head), (out1, w_out.at[1]), (in1, w_in.at[1]), (out0, w_out.at[0]),
             (in0, w_in.at[0]), (embed_h, embed)]
        )
    ]

    def inst(it):
        return 3 - it

    def fetch(it):
        slot = it % 2
        pairs = [(streams, i_stream), (waves_h, i_waves), (mixeds, i_mixed), (befores, i_before)]
        return [
            pltpu.make_async_copy(source.at[inst(it)], target.at[slot], in_sem.at[k, slot])
            for k, (source, target) in enumerate(pairs)
        ]

    tail_loads = [
        pltpu.make_async_copy(lasts, i_last, tail_in.at[0]),
        pltpu.make_async_copy(errors, i_error, tail_in.at[1]),
    ]
    late_load = pltpu.make_async_copy(tails, x_tail, tail_in.at[2])
    for load in tail_loads:
        load.start()
    loads[0].start()
    for load in fetch(0):
        load.start()
    for load in loads[1:]:
        load.start()
    for target in (sum_norm, sum_c1, sum_tail, sum_head, grad_w1, grad_w2, grad_b, carried):
        target[...] = jnp.zeros_like(target)

    late_load.start()

    def section_loads(layer):
        return [
            pltpu.make_async_copy(source.at[2 * step + layer], target.at[step], section_sem.at[n, step])
            for n, (source, target) in enumerate([(normeds, x_in), (hiddens, x_out)])
            for step in range(2)
        ]

    def write_when(it, number, work):
        when_it(it == number, lambda: [write_section(i, xs, gs, bufs) for i, xs, gs in work] and None)

    def pairs_out(layer):
        return (2 + 2 * layer, (x_out.at[0], x_out.at[1]), (s_out.at[2], s_out.at[layer]))

    def pairs_in(layer):
        return (1 + 2 * layer, (x_in.at[0], x_in.at[1]), (s_pre.at[2], s_pre.at[layer]))

    def meanwhile_in(it):
        write_when(it, 2, [(5, (x_tail.at[0], x_tail.at[1]), (s_pred.at[0], s_pred.at[1])), pairs_out(1)])
        write_when(it, 3, [pairs_out(0)])

    def meanwhile_out(it):
        write_when(it, 2, [pairs_in(1)])
        write_when(it, 3, [pairs_in(0)])

    def body(it, carry):
        step, layer, slot = 1 - it // 2, 1 - it % 2, it % 2
        keep = jnp.where(step == 1, layer, 2)

        def fetch_section(wanted):
            for load in section_loads(wanted):
                load.start()

        when_it(it == 2, lambda: fetch_section(1))
        when_it(it == 3, lambda: fetch_section(0))

        def first():
            for load in tail_loads:
                load.wait()
            loads[0].wait()

        when_it(it == 0, first)

        def head_adjoint():
            grad = i_error[step] * gscale[...] + carried[...]
            grad16 = grad.astype(bf16)
            s_pred[step] = grad16
            sum_head[0:1] += jnp.sum(grad, axis=0, keepdims=True)
            back_n = dot_cols(grad16, head[...]).astype(bf16).astype(f32)
            value, gain, shift = norm_adjoint(i_last[step], tail[0:1], back_n)
            flow[...] = value
            sum_tail[0:1] += gain
            sum_tail[1:2] += shift

        when_it(layer == 1, head_adjoint)

        def prefetch():
            for load in fetch(it + 1):
                load.start()

        when_it(it < 3, prefetch)

        s_out[keep] = flow[...].astype(bf16)
        sum_norm[layer, 4:5] += jnp.sum(flow[...], axis=0, keepdims=True)
        for load in fetch(it):
            load.wait()

        def second_layer():
            loads[1].wait()
            loads[2].wait()

        def first_layer():
            loads[3].wait()
            loads[4].wait()

        when_it(it == 0, second_layer)
        when_it(it == 1, first_layer)
        g_norm[...] = jnp.zeros_like(g_norm)

        def chunk(c, carry):
            part = pl.ds(pl.multiple_of(c * FCHUNK, FCHUNK), FCHUNK)
            grad = dot_cols(s_out[keep], w_out[layer, part, :]).astype(bf16).astype(f32)
            grad = grad * gelu_slope(i_before[slot, :, part].astype(f32))
            sum_c1[layer, 0:1, part] += jnp.sum(grad, axis=0, keepdims=True)
            grad16 = grad.astype(bf16)
            s_pre[keep, :, part] = grad16
            g_norm[...] += dot_cols(grad16, w_in[layer, :, part])
            return carry

        lax.fori_loop(0, FF // FCHUNK, chunk, 0)

        def section_ready():
            for load in section_loads(0):
                load.wait()

        when_it(it >= 2, section_ready)
        when_it(it == 2, late_load.wait)
        value, gain, shift = norm_adjoint(
            i_mixed[slot], norms[layer, 2:3], g_norm[...].astype(bf16).astype(f32)
        )
        flow[...] += value
        sum_norm[layer, 2:3] += gain
        sum_norm[layer, 3:4] += shift
        split_units(flow[...], units)
        when_it(it == 0, lambda: pl.semaphore_wait(barrier, CHIPS))
        finish_one = spread_units(
            me, core, sibling, units, mine, others, sems[:5], lambda: meanwhile_in(it)
        )
        groups = to_spectrum(mine, others, column, rows, waves)
        for g in range(4):
            before = dot(i_waves[slot, g], w1[layer]) + b1[layer]
            hidden = gelu_of(before).astype(bf16)
            grad_hidden = dot_cols(groups[g], w2[layer]).astype(bf16).astype(f32)
            grad_before = grad_hidden * gelu_slope(before)
            grad_before16 = grad_before.astype(bf16)
            grad_w2[layer] += dot_rows(hidden, groups[g])
            grad_w1[layer] += dot_rows(i_waves[slot, g], grad_before16)
            grad_b[layer, 0:1] += jnp.sum(grad_before, axis=0, keepdims=True)
            grad_b[layer, 1:2] += jnp.sum(groups[g].astype(f32), axis=0, keepdims=True)
            from_spectrum(g, dot_cols(grad_before16, w1[layer]).astype(bf16), rows, back)
        finish_two = gather_units(
            row, me, core, sibling, back, inverse,
            (own_sum, to_sib, from_sib, ready, landed), sems[5:], finish_one,
            lambda: meanwhile_out(it),
        )
        join_units(landed, joined)
        value, gain, shift = norm_adjoint(i_stream[slot], norms[layer, 0:1], joined[...])
        flow[...] += value
        sum_norm[layer, 0:1] += gain
        sum_norm[layer, 1:2] += shift
        when_it(it == 1, loads[5].wait)

        def embed_adjoint():
            s_embed[step] = flow[...].astype(bf16)
            sum_tail[2:3] += jnp.sum(flow[...], axis=0, keepdims=True)

        when_it(layer == 0, embed_adjoint)

        def carry_back():
            carried[...] = mask[...] * dot_cols(s_embed[1], embed[...]).astype(bf16).astype(f32)

        when_it(it == 1, carry_back)
        finish_two()
        return carry

    lax.fori_loop(0, 4, body, 0)
    block = me % NBLK

    def put_layer(at, idx):
        put_rows(wide, at, sum_norm[idx, 0:1])
        put_rows(wide, at + 6, sum_norm[idx, 1:2])
        put_block_weight(wide, at + AT_W1, block, grad_w1[idx], square)
        put_block_bias(wide, at + AT_B1, block, grad_b[idx, 0:1])
        put_block_weight(wide, at + AT_W2, block, grad_w2[idx], square)
        put_block_bias(wide, at + AT_B2, block, grad_b[idx, 1:2])
        put_rows(wide, at + AT_NORM[2], sum_norm[idx, 2:3])
        put_rows(wide, at + AT_NORM[3], sum_norm[idx, 3:4])

    def put_small(i, at):
        if i == 0:
            put_rows(wide, at, sum_tail[2:3])
            put_layer(at + 6, 0)
        elif i == 2:
            put_rows(wide, at, sum_norm[0, 4:5])
            put_layer(at + 6, 1)
        elif i == 4:
            put_rows(wide, at, sum_norm[1, 4:5])
            put_rows(wide, at + 6, sum_tail[0:1])
            put_rows(wide, at + 12, sum_tail[1:2])
        elif i == 5:
            put_rows(wide, at, sum_head[0:1])
        else:
            put_rows(wide, at, sum_c1[i // 2, 0:1])

    write_section(0, (inputs, x1), (s_embed.at[0], s_embed.at[1]), bufs)
    for i in range(6):
        write_small(i, put_small, bufs)


def backward_pass(*args):
    vm, dma = pltpu.VMEM, pltpu.SemaphoreType.DMA
    whole, anywhere = pl.BlockSpec(memory_space=vm), pl.BlockSpec(memory_space=pl.ANY)
    shape = jax.ShapeDtypeStruct
    return pl.pallas_call(
        backward_kernel,
        out_shape=shape((GROWS, LANES), bf16),
        in_specs=[whole] * 10 + [anywhere] * 12 + [whole] * 2 + [anywhere] * 3,
        out_specs=anywhere,
        scratch_shapes=[
            vm((2, 8, D), f32),
            vm((2, 8, FF), f32),
            vm((8, D), f32),
            vm((8, PIN), f32),
            vm((2, 256, 256), f32),
            vm((2, 256, 256), f32),
            vm((2, 8, 256), f32),
            vm((PIN, D), bf16),
            vm((2, D, FF), bf16),
            vm((2, FF, D), bf16),
            vm((D, PIN), bf16),
            vm((CELLS, D), f32),
            vm((CELLS, PIN), f32),
            vm((2, CELLS, D), f32),
            vm((2, 4, 256, 256), bf16),
            vm((2, CELLS, D), f32),
            vm((2, CELLS, FF), bf16),
            vm((2, CELLS, D), f32),
            vm((2, CELLS, PIN), f32),
            vm((2, CELLS, PIN), bf16),
            vm((3, CELLS, D), bf16),
            vm((3, CELLS, FF), bf16),
            vm((2, CELLS, D), bf16),
            vm((CELLS, D), f32),
            vm((2, CELLS, D), bf16),
            vm((2, CELLS, FF), bf16),
            vm((2, CELLS, D), bf16),
            vm((FF, 256), bf16),
            vm((256, FF), bf16),
            vm((7712, LANES), f32),
            vm((7712, LANES), bf16),
            vm((12, 16, LANES), f32),
            vm((2, PADC, PADC), f32),
            dma((6,)),
            dma((4, 2)),
            dma((3,)),
            dma((2, 2)),
            dma,
        ]
        + filter_scratch(),
        compiler_params=pltpu.CompilerParams(
            collective_id=3, has_side_effects=True, vmem_limit_bytes=60 << 20
        ),
        name="backward_pass",
    )(*args)


def local_fast(frames, targets, regions, master, first_moment, second_moment):
    height, width = 16, 128
    device = lax.axis_index("row") * 4 + lax.axis_index("col")
    core = lax.axis_index("col") % 2
    shard = master.astype(bf16).reshape(OWN, LANES)
    halo = lax.ppermute(shard[:320], ("row", "col"), [(k + 1, k) for k in range(31)])
    chunk = lax.dynamic_slice_in_dim(jnp.concatenate([shard, halo]), 10 * device, CH, 0)
    flat = ag(chunk)
    tables = transform_tables(core)
    row_ids = lax.axis_index("row") * 2 + jnp.arange(2, dtype=jnp.int32)
    col_ids = lax.axis_index("col") * 32 + jnp.arange(32, dtype=jnp.int32)
    cell_masks = region_masks(regions, row_ids, col_ids, width)
    weighted = latitude(row_ids, height)[None, :, None] * cell_masks
    every_row = jnp.arange(height, dtype=jnp.int32)
    every_col = jnp.arange(width, dtype=jnp.int32)
    total_weight = (
        jnp.sum(
            latitude(every_row, height)[None, :, None]
            * region_masks(regions, every_row, every_col, width)
        )
        * STEPS
    )
    flat_mask = cell_masks.reshape(128, 1)
    flat_weight = weighted.reshape(128, 1)
    inputs = (frames.reshape(128, PIN).astype(f32) * flat_mask).astype(bf16)
    goals = jnp.stack([targets[:, s].reshape(128, PIN) for s in range(STEPS)])
    (streams, waves, mixeds, normeds, befores, hiddens, lasts, tails, errors, *rest) = forward_pass(
        inputs, goals, flat_mask, flat_weight, *tables, flat
    )
    mats, (x1, loss, norms, tail, w1, b1, w2) = rest[:6], rest[6:]
    flat_grad = backward_pass(
        flat_weight * (2.0 / total_weight), flat_mask, norms, tail, *tables, w1, b1, w2, *mats,
        streams, waves, mixeds, befores, lasts, errors, inputs, x1, normeds, hiddens, tails,
    )
    loss_tile = jnp.concatenate([loss.reshape(1, LANES), jnp.zeros((7, LANES), f32)])
    summed, stats = rs(flat_grad, loss_tile)
    reduced = lax.dynamic_slice_in_dim(summed, (device * OWN) % 16, OWN, 0).reshape(-1)
    grad_norm = jnp.sqrt(jnp.sum(stats[:8]))
    return finish_step(
        reduced, grad_norm, master, first_moment, second_moment, jnp.sum(stats[8:]), total_weight
    )


def finish_step(reduced, grad_norm, master, first_moment, second_moment, loss_all, total_weight):
    clipped = reduced * (CLIP / jnp.maximum(grad_norm, CLIP))
    first_out = BETA_ONE * first_moment + (1.0 - BETA_ONE) * clipped
    second_out = BETA_TWO * second_moment + (1.0 - BETA_TWO) * clipped * clipped
    corrected_one = first_out / (1.0 - BETA_ONE**ADAM_STEP)
    corrected_two = second_out / (1.0 - BETA_TWO**ADAM_STEP)
    master_out = master - RATE * (
        corrected_one / (jnp.sqrt(corrected_two) + ADAM_EPS) + DECAY * master
    )
    return (
        master_out,
        first_out,
        second_out,
        master_out.astype(bf16),
        loss_all,
        total_weight,
        grad_norm,
    )


def local(frames, targets, regions, master, first_moment, second_moment):
    row_devices = lax.axis_size("row")
    col_devices = lax.axis_size("col")
    local_rows = frames.shape[1]
    local_cols = frames.shape[2]
    height = local_rows * row_devices
    width = local_cols * col_devices
    weights = lax.all_gather(master.astype(jnp.bfloat16), ("row", "col"), axis=0, tiled=True)
    pieces16 = unpack(weights)
    pieces = unpack(weights.astype(jnp.float32))
    tail_params = pieces[2 + 12 * LAYERS :]
    tail16 = pieces16[2 + 12 * LAYERS :]
    tables = (
        dft_tables(width, -1.0),
        dft_tables(height, -1.0),
        dft_tables(width, 1.0),
        dft_tables(height, 1.0),
    )
    row_ids = lax.axis_index("row") * local_rows + jnp.arange(local_rows, dtype=jnp.int32)
    col_ids = lax.axis_index("col") * local_cols + jnp.arange(local_cols, dtype=jnp.int32)
    cell_masks = region_masks(regions, row_ids, col_ids, width)
    weighted = latitude(row_ids, height)[None, :, None] * cell_masks
    every_row = jnp.arange(height, dtype=jnp.int32)
    every_col = jnp.arange(width, dtype=jnp.int32)
    total_weight = (
        jnp.sum(
            latitude(every_row, height)[None, :, None]
            * region_masks(regions, every_row, every_col, width)
        )
        * STEPS
    )
    inputs = frames.astype(jnp.float32) * cell_masks[..., None]
    loss_sum = jnp.zeros((), jnp.float32)
    history = []
    for roll_step in range(STEPS):
        stream = linear_forward(inputs, pieces16[0], pieces[1])
        saved_layers = []
        for layer_idx in range(LAYERS):
            span = slice(2 + 12 * layer_idx, 14 + 12 * layer_idx)
            stream, saved = layer_forward(stream, pieces[span], pieces16[span], tables)
            saved_layers.append(saved)
        normed = rounded(layer_norm(stream, tail_params[0], tail_params[1]))
        predicted = linear_forward(normed, tail16[2], tail_params[3])
        errors = predicted - targets[:, roll_step].astype(jnp.float32)
        loss_sum = loss_sum + jnp.sum(weighted * jnp.sum(errors * errors, axis=-1))
        history.append((inputs, saved_layers, stream, normed, errors))
        inputs = rounded(predicted * cell_masks[..., None])
    loss_all = lax.psum(loss_sum, ("row", "col"))
    gradients = [jnp.zeros_like(piece) for piece in pieces]
    carried = jnp.zeros_like(inputs)
    for roll_step in reversed(range(STEPS)):
        inputs, saved_layers, stream, normed, errors = history[roll_step]
        grad_pred = 2.0 * weighted[..., None] * errors / total_weight + carried
        grad_normed, grad_head, grad_hbias = linear_backward(grad_pred, normed, tail16[2])
        _, pullback = jax.vjp(layer_norm, stream, tail_params[0], tail_params[1])
        grad_stream, grad_gain3, grad_shift3 = pullback(rounded(grad_normed))
        gradients = add_into(
            gradients, 2 + 12 * LAYERS, [grad_gain3, grad_shift3, grad_head, grad_hbias]
        )
        for layer_idx in reversed(range(LAYERS)):
            span = slice(2 + 12 * layer_idx, 14 + 12 * layer_idx)
            grad_stream, layer_grads = layer_backward(
                grad_stream, saved_layers[layer_idx], pieces[span], pieces16[span], tables
            )
            gradients = add_into(gradients, 2 + 12 * layer_idx, layer_grads)
        grad_inputs, grad_embed, grad_ebias = linear_backward(grad_stream, inputs, pieces16[0])
        gradients = add_into(gradients, 0, [grad_embed, grad_ebias])
        carried = cell_masks[..., None] * rounded(grad_inputs)
    flat_grad = jnp.concatenate([piece.ravel() for piece in gradients])
    padding = master.shape[0] * row_devices * col_devices - flat_grad.shape[0]
    flat_grad = jnp.concatenate([flat_grad, jnp.zeros((padding,), jnp.float32)])
    grad_table = flat_grad.reshape(-1, LANES)
    reduced = lax.psum_scatter(grad_table, ("row", "col"), scatter_dimension=0, tiled=True).reshape(
        -1
    )
    squares = jnp.sum(reduced * reduced)
    square_all = lax.psum(squares, ("row", "col"))
    grad_norm = jnp.sqrt(square_all)
    clipped = reduced * (CLIP / jnp.maximum(grad_norm, CLIP))
    first_out = BETA_ONE * first_moment + (1.0 - BETA_ONE) * clipped
    second_out = BETA_TWO * second_moment + (1.0 - BETA_TWO) * clipped * clipped
    corrected_one = first_out / (1.0 - BETA_ONE**ADAM_STEP)
    corrected_two = second_out / (1.0 - BETA_TWO**ADAM_STEP)
    master_out = master - RATE * (
        corrected_one / (jnp.sqrt(corrected_two) + ADAM_EPS) + DECAY * master
    )
    return (
        master_out,
        first_out,
        second_out,
        master_out.astype(jnp.bfloat16),
        loss_all,
        total_weight,
        grad_norm,
    )


def solution(mesh):
    in_specs = (
        P(None, "row", "col", None),
        P(None, None, "row", "col", None),
        P(),
        P(("row", "col")),
        P(("row", "col")),
        P(("row", "col")),
    )
    out_specs = (
        P(("row", "col")),
        P(("row", "col")),
        P(("row", "col")),
        P(("row", "col")),
        P(),
        P(),
        P(),
    )
    body = local_fast if dict(mesh.shape) == {"row": 8, "col": 4} else local
    return jax.shard_map(body, mesh=mesh, in_specs=in_specs, out_specs=out_specs, check_vma=False)
```

```python
import functools
import math

import jax
import jax.numpy as jnp
import numpy as np
from jax import lax
from jax.sharding import PartitionSpec as P
from jax.experimental import pallas as pl
from jax.experimental.pallas import tpu as pltpu

D = 768
FF = 3072
NBLK = 8
BS = 96
PIN = 1280
LAYERS = 2
STEPS = 2
ADAM_STEP = 5


highest = lax.Precision.HIGHEST
NORM_EPS = 1e-05
BETA_ONE = 0.9
BETA_TWO = 0.95
ADAM_EPS = 1e-08
RATE = 0.03
DECAY = 0.05
CLIP = 0.2
LANES = 128


def block_shapes():
    return [
        (D,),
        (D,),
        (2, NBLK, BS, BS),
        (2, NBLK, BS),
        (2, NBLK, BS, BS),
        (2, NBLK, BS),
        (D,),
        (D,),
        (D, FF),
        (FF,),
        (FF, D),
        (D,),
    ]


def all_shapes():
    return [(PIN, D), (D,)] + block_shapes() * LAYERS + [(D,), (D,), (D, PIN), (PIN,)]


def unpack(flat_vec):
    pieces = []
    offset = 0
    for layout in all_shapes():
        length = math.prod(layout)
        pieces.append(flat_vec[offset : offset + length].reshape(layout))
        offset += length
    return pieces


def rounded(value):
    return lax.optimization_barrier(value.astype(jnp.bfloat16)).astype(jnp.float32)


def mult(form, left, right):
    return jnp.einsum(
        form,
        left.astype(jnp.bfloat16),
        right.astype(jnp.bfloat16),
        preferred_element_type=jnp.float32,
    )


def mult_exact(form, grad_value, other):
    upper = grad_value.astype(jnp.bfloat16)
    lower = (grad_value - upper.astype(jnp.float32)).astype(jnp.bfloat16)
    return mult(form, upper, other) + mult(form, lower, other)


def layer_norm(values, gain_vec, shift_vec):
    center = values - jnp.mean(values, axis=-1, keepdims=True)
    spread = jnp.mean(center * center, axis=-1, keepdims=True)
    return center * lax.rsqrt(spread + NORM_EPS) * gain_vec + shift_vec


def dft_tables(length, direction):
    positions = jnp.arange(length, dtype=jnp.int32)
    phases = (positions[:, None] * positions[None, :] % length).astype(jnp.float32) * (
        2.0 * math.pi / length
    )
    factor = 1.0 / math.sqrt(length)
    return (jnp.cos(phases) * factor, direction * jnp.sin(phases) * factor)


def apply_pair(tables, real_part, imag_part, form):

    def contract(table, values):
        return jnp.einsum(form, table, values, precision=highest)

    return (
        contract(tables[0], real_part) - contract(tables[1], imag_part),
        contract(tables[1], real_part) + contract(tables[0], imag_part),
    )


def spectral(real_part, imag_part, weight, bias_vec):
    blocks = (weight.shape[1], weight.shape[2])
    block_re = real_part.reshape(real_part.shape[:-1] + blocks)
    block_im = imag_part.reshape(imag_part.shape[:-1] + blocks)
    form = "...kb,kbc->...kc"
    out_re = (
        jnp.einsum(form, block_re, weight[0], precision=highest)
        - jnp.einsum(form, block_im, weight[1], precision=highest)
        + bias_vec[0]
    )
    out_im = (
        jnp.einsum(form, block_im, weight[0], precision=highest)
        + jnp.einsum(form, block_re, weight[1], precision=highest)
        + bias_vec[1]
    )
    return (out_re.reshape(real_part.shape), out_im.reshape(imag_part.shape))


def first_spectral(real_part, imag_part, weight, bias_vec):
    out_re, out_im = spectral(real_part, imag_part, weight, bias_vec)
    return (jax.nn.gelu(out_re, approximate=False), jax.nn.gelu(out_im, approximate=False))


def region_masks(regions, row_ids, col_ids, width):
    row_start = regions[:, 0, None, None]
    row_span = regions[:, 1, None, None]
    col_start = regions[:, 2, None, None]
    col_span = regions[:, 3, None, None]
    row_inside = (row_ids[None, :, None] >= row_start) & (
        row_ids[None, :, None] < row_start + row_span
    )
    col_inside = (col_ids[None, None, :] - col_start) % width < col_span
    return (row_inside & col_inside).astype(jnp.float32)


def latitude(row_ids, height):
    return jnp.cos(-1.3 + 1.3 * (row_ids.astype(jnp.float32) + 0.5) / height)


def linear_forward(values, weight16, bias_vec):
    return mult("brci,io->brco", values, weight16) + bias_vec


def linear_backward(grad_value, values, weight16):
    grad_values = mult_exact("brco,io->brci", grad_value, weight16)
    grad_weight = mult_exact("brco,brci->io", grad_value, values)
    return (grad_values, grad_weight, jnp.sum(grad_value, axis=(0, 1, 2)))


def spectrum(field, forward_w, forward_h):
    values = lax.all_to_all(field, "col", split_axis=3, concat_axis=2, tiled=True).astype(
        jnp.float32
    )
    real_part = jnp.einsum("kw,bnwc->bnkc", forward_w[0], values, precision=highest)
    imag_part = jnp.einsum("kw,bnwc->bnkc", forward_w[1], values, precision=highest)
    real_part, imag_part = apply_pair(
        forward_h,
        lax.all_to_all(
            real_part.astype(jnp.bfloat16), "row", split_axis=2, concat_axis=1, tiled=True
        ).astype(jnp.float32),
        lax.all_to_all(
            imag_part.astype(jnp.bfloat16), "row", split_axis=2, concat_axis=1, tiled=True
        ).astype(jnp.float32),
        "kh,bhwc->bkwc",
    )
    return (real_part.astype(jnp.bfloat16), imag_part.astype(jnp.bfloat16))


def grid(real_part, imag_part, inverse_w, inverse_h):
    back_re, back_im = apply_pair(
        inverse_h, real_part.astype(jnp.float32), imag_part.astype(jnp.float32), "kh,bhwc->bkwc"
    )
    values_re = lax.all_to_all(
        back_re.astype(jnp.bfloat16), "row", split_axis=1, concat_axis=2, tiled=True
    ).astype(jnp.float32)
    values_im = lax.all_to_all(
        back_im.astype(jnp.bfloat16), "row", split_axis=1, concat_axis=2, tiled=True
    ).astype(jnp.float32)
    result = jnp.einsum("kw,bnwc->bnkc", inverse_w[0], values_re, precision=highest) - jnp.einsum(
        "kw,bnwc->bnkc", inverse_w[1], values_im, precision=highest
    )
    columns_back = result.astype(jnp.bfloat16)
    return lax.all_to_all(columns_back, "col", split_axis=2, concat_axis=3, tiled=True)


def local_blocks(params):
    block_count = D // lax.axis_size("col") // BS
    first_block = lax.axis_index("col") * block_count
    chosen = [
        lax.dynamic_slice_in_dim(params[index_pos], first_block, block_count, 1)
        for index_pos in (2, 3, 4, 5)
    ]
    return (chosen, first_block)


def layer_forward(stream, params, params16, tables):
    gain_one, shift_one, _, _, _, _, gain_two, shift_two, _, bias_in, _, bias_out = params
    (local_w1, local_b1, local_w2, local_b2), _ = local_blocks(params)
    normed = layer_norm(stream, gain_one, shift_one).astype(jnp.bfloat16)
    wave_re, wave_im = spectrum(normed, tables[0], tables[1])
    hid_re, hid_im = first_spectral(
        wave_re.astype(jnp.float32), wave_im.astype(jnp.float32), local_w1, local_b1
    )
    hid_re, hid_im = (rounded(hid_re), rounded(hid_im))
    spec_re, spec_im = spectral(hid_re, hid_im, local_w2, local_b2)
    filtered = grid(
        spec_re.astype(jnp.bfloat16), spec_im.astype(jnp.bfloat16), tables[2], tables[3]
    )
    mixed = stream + filtered.astype(jnp.float32)
    normed_two = rounded(layer_norm(mixed, gain_two, shift_two))
    hidden = rounded(
        jax.nn.gelu(linear_forward(normed_two, params16[8], bias_in), approximate=False)
    )
    output = mixed + linear_forward(hidden, params16[10], bias_out)
    return (output, (stream, wave_re, wave_im, hid_re, hid_im, mixed, normed_two, hidden))


def place_blocks(local_grad, full_like, first_block):
    return lax.dynamic_update_slice_in_dim(jnp.zeros_like(full_like), local_grad, first_block, 1)


def layer_backward(grad_out, saved, params, params16, tables):
    stream, wave_re, wave_im, hid_re, hid_im, mixed, normed_two, hidden = saved
    (
        gain_one,
        shift_one,
        spec_w1,
        spec_b1,
        spec_w2,
        spec_b2,
        gain_two,
        shift_two,
        weight_in,
        bias_in,
        weight_out,
        bias_out,
    ) = params
    (local_w1, local_b1, local_w2, local_b2), first_block = local_blocks(params)
    grad_hidden, grad_wout, grad_bout = linear_backward(grad_out, hidden, params16[10])
    grad_mixed = grad_out
    before = linear_forward(normed_two, params16[8], bias_in)
    _, pullback = jax.vjp(lambda value: jax.nn.gelu(value, approximate=False), before)
    (grad_before,) = pullback(rounded(grad_hidden))
    grad_normed, grad_win, grad_bin = linear_backward(grad_before, normed_two, params16[8])
    _, pullback = jax.vjp(layer_norm, mixed, gain_two, shift_two)
    grad_extra, grad_gain2, grad_shift2 = pullback(rounded(grad_normed))
    grad_mixed = grad_mixed + grad_extra
    back_re, back_im = spectrum(grad_mixed.astype(jnp.bfloat16), tables[0], tables[1])
    _, pullback = jax.vjp(spectral, hid_re, hid_im, local_w2, local_b2)
    grad_hre, grad_him, grad_lw2, grad_lb2 = pullback(
        (back_re.astype(jnp.float32), back_im.astype(jnp.float32))
    )
    _, pullback = jax.vjp(
        first_spectral, wave_re.astype(jnp.float32), wave_im.astype(jnp.float32), local_w1, local_b1
    )
    grad_wre, grad_wim, grad_lw1, grad_lb1 = pullback((rounded(grad_hre), rounded(grad_him)))
    grad_first = grid(
        grad_wre.astype(jnp.bfloat16), grad_wim.astype(jnp.bfloat16), tables[2], tables[3]
    )
    _, pullback = jax.vjp(layer_norm, stream, gain_one, shift_one)
    grad_stream, grad_gain1, grad_shift1 = pullback(grad_first.astype(jnp.float32))
    layer_grads = [
        grad_gain1,
        grad_shift1,
        place_blocks(grad_lw1, spec_w1, first_block),
        place_blocks(grad_lb1, spec_b1, first_block),
        place_blocks(grad_lw2, spec_w2, first_block),
        place_blocks(grad_lb2, spec_b2, first_block),
        grad_gain2,
        grad_shift2,
        grad_win,
        grad_bin,
        grad_wout,
        grad_bout,
    ]
    return (grad_stream + grad_mixed, layer_grads)


def add_into(gradients, start, values):
    middle = [left + right for left, right in zip(gradients[start : start + len(values)], values)]
    return gradients[:start] + middle + gradients[start + len(values) :]


MESH = pl.DeviceIdType.MESH
CH = 2944
OWN = 2934
CHR = 2960
GROWS = 93904


CHIPS = 16
UNIT = 64
PADC = 128
f32 = jnp.float32
bf16 = jnp.bfloat16


def remote(src, dst, send_sem, recv_sem, device):
    return pltpu.make_async_remote_copy(
        src_ref=src,
        dst_ref=dst,
        send_sem=send_sem,
        recv_sem=recv_sem,
        device_id=device,
        device_id_type=MESH,
    )


def chip_device(chip, core):
    return chip // 2, (chip % 2) * 2 + core


def place():
    row = lax.axis_index("row")
    col = lax.axis_index("col")
    core = col % 2
    return row, row * 2 + col // 2, core, (row, col + 1 - 2 * core)


def greet_chips(me, core, sibling):
    barrier = pltpu.get_barrier_semaphore()

    def one(k, carry):
        pl.semaphore_signal(
            barrier,
            inc=1,
            device_id=chip_device(me ^ (CHIPS - k), core),
            device_id_type=MESH,
        )
        return carry

    lax.fori_loop(1, CHIPS, one, 0)
    pl.semaphore_signal(barrier, inc=1, device_id=sibling, device_id_type=MESH)
    return barrier


def split_units(values, units):
    blank = jnp.zeros((UNIT, PADC - BS), f32)
    for part in range(2):
        for block in range(NBLK):
            piece = values[part * UNIT : (part + 1) * UNIT, block * BS : (block + 1) * BS]
            units[part * NBLK + block] = jnp.concatenate([piece, blank], axis=1).astype(bf16)


def join_units(units, joined):
    for part in range(2):
        for block in range(NBLK):
            joined[part * UNIT : (part + 1) * UNIT, block * BS : (block + 1) * BS] = units[
                part * NBLK + block, :, 0:BS
            ].astype(f32)


def normalize(values):
    center = values - jnp.mean(values, axis=-1, keepdims=True)
    spread = jnp.mean(center * center, axis=-1, keepdims=True)
    scale = lax.rsqrt(spread + NORM_EPS)
    return center * scale, scale


def gelu_of(value):
    return 0.5 * value * (1.0 + lax.erf(value * math.sqrt(0.5)))


def gelu_slope(value):
    bell = jnp.exp(-0.5 * value * value) * (1.0 / math.sqrt(2.0 * math.pi))
    return 0.5 * (1.0 + lax.erf(value * math.sqrt(0.5))) + value * bell


def dot(left, right):
    return jnp.dot(left, right, preferred_element_type=f32)


def dot_rows(left, right):
    return lax.dot_general(left, right, (((0,), (0,)), ((), ())), preferred_element_type=f32)


def dot_cols(left, right):
    return lax.dot_general(left, right, (((1,), (1,)), ((), ())), preferred_element_type=f32)


def spread_units(me, core, sibling, units, mine, others, sems, meanwhile):
    send_a, recv_a, send_f, recv_f, local_sem = sems

    def out(k):
        chip = me ^ k
        return remote(
            units.at[chip], mine.at[me], send_a.at[k], recv_a.at[k], chip_device(chip, core)
        )

    def handed(k):
        chip = me ^ k
        return remote(mine.at[chip], others.at[chip], send_f.at[k], recv_f.at[k], sibling)

    own = pltpu.make_async_copy(units.at[me], mine.at[me], local_sem)
    own.start()

    def begin(k, carry):
        out(CHIPS - k).start()
        return carry

    lax.fori_loop(1, CHIPS, begin, 0)
    meanwhile()
    own.wait()
    handed(0).start()

    def hand(k, carry):
        out(CHIPS - k).wait_recv()
        handed(CHIPS - k).start()
        return carry

    lax.fori_loop(1, CHIPS, hand, 0)

    def arrive(k, carry):
        handed(k).wait_recv()
        return carry

    lax.fori_loop(0, CHIPS, arrive, 0)

    def finish():
        def sent(k, carry):
            out(k).wait_send()
            return carry

        lax.fori_loop(1, CHIPS, sent, 0)

        def sent_on(k, carry):
            handed(k).wait_send()
            return carry

        lax.fori_loop(0, CHIPS, sent_on, 0)

    return finish


def to_spectrum(mine, others, column_table, row_table, waves):
    for h in range(16):
        pair, part = h // 2, pl.ds(32 * (h % 2), 32)
        cells = jnp.concatenate(
            [
                mine[2 * pair, part],
                mine[2 * pair + 1, part],
                others[2 * pair, part],
                others[2 * pair + 1, part],
            ],
            axis=0,
        )
        wave = dot(column_table[...], cells).astype(bf16)
        for g in range(4):
            rows = pl.ds(16 * h, 16)
            waves[g, rows, 0:PADC] = wave[16 * g : 16 * g + 16]
            waves[g, rows, PADC : 2 * PADC] = wave[64 + 16 * g : 80 + 16 * g]
    results = []
    for g in range(4):
        both = dot(row_table[...], waves[g])
        real = both[:256, :PADC] + both[256:, PADC:]
        imag = both[:256, PADC:] - both[256:, :PADC]
        results.append(jnp.concatenate([real, imag], axis=1).astype(bf16))
    return results


def from_spectrum(g, spec, row_table, back):
    both = dot(row_table[...], spec)
    real = (both[:256, :PADC] - both[256:, PADC:]).astype(bf16)
    imag = (both[:256, PADC:] + both[256:, :PADC]).astype(bf16)
    for h in range(16):
        back[h, 16 * g : 16 * g + 16] = real[16 * h : 16 * h + 16]
        back[h, 64 + 16 * g : 80 + 16 * g] = imag[16 * h : 16 * h + 16]


def gather_units(row, me, core, sibling, back, inverse_table, bufs, sems, settle, meanwhile):
    own_sum, to_sib, from_sib, ready, landed = bufs
    send_s, recv_s, send_b, recv_b, local_sem = sems

    def swap(pair):
        rows = pl.ds(2 * pair, 2)
        return remote(
            to_sib.at[rows], from_sib.at[rows], send_s.at[pair], recv_s.at[pair], sibling
        )

    def partial(j, carry):
        pair = row ^ (7 - j)
        for half in range(2):
            sums = dot(inverse_table[...], back[2 * pair + half])
            part = pl.ds(32 * half, 32)
            for x in range(2):
                own_sum[2 * pair + x, part] = sums[32 * x : 32 * x + 32]
                to_sib[2 * pair + x, part] = sums[64 + 32 * x : 96 + 32 * x].astype(bf16)
        swap(pair).start()
        return carry

    lax.fori_loop(0, 8, partial, 0)
    settle()

    def home(chip, k):
        return remote(
            ready.at[chip], landed.at[me], send_b.at[k], recv_b.at[k], chip_device(chip, core)
        )

    own = pltpu.make_async_copy(ready.at[me], landed.at[me], local_sem)

    def total(j, carry):
        pair = row ^ (7 - j)
        swap(pair).wait_recv()
        rows = pl.ds(2 * pair, 2)
        ready[rows] = (own_sum[rows] + from_sib[rows].astype(f32)).astype(bf16)
        for x in range(2):
            chip = 2 * pair + x
            k = chip ^ me

            @pl.when(k != 0)
            def _():
                home(chip, k).start()

        return carry

    lax.fori_loop(0, 8, total, 0)
    own.start()
    meanwhile()

    def landed_all(k, carry):
        home(me ^ k, k).wait_recv()
        return carry

    lax.fori_loop(1, CHIPS, landed_all, 0)
    own.wait()

    def finish():
        def sent(k, carry):
            home(me ^ k, k).wait_send()
            return carry

        lax.fori_loop(1, CHIPS, sent, 0)

        def swapped(pair, carry):
            swap(pair).wait_send()
            return carry

        lax.fori_loop(0, 8, swapped, 0)

    return finish


def filter_scratch():
    vm = pltpu.VMEM
    dma = pltpu.SemaphoreType.DMA
    block = (CHIPS, UNIT, PADC)
    return [
        vm(block, bf16),
        vm(block, bf16),
        vm(block, bf16),
        vm((4, 256, 256), bf16),
        vm((16, 128, PADC), bf16),
        vm(block, f32),
        vm(block, bf16),
        vm(block, bf16),
        vm(block, bf16),
        vm(block, bf16),
        vm((2 * UNIT, D), f32),
        dma((CHIPS,)),
        dma((CHIPS,)),
        dma((CHIPS,)),
        dma((CHIPS,)),
        dma,
        dma((8,)),
        dma((8,)),
        dma((CHIPS,)),
        dma((CHIPS,)),
        dma,
    ]


def transform_tables(core):
    width, height = 128, 16
    order = []
    for side in range(2):
        cols = [[32 * (2 * x + (c if side == 0 else 1 - c)) + i for x in range(2) for i in range(32)] for c in range(2)]
        order.append(cols)
    column, inverse = [], []
    for c in range(2):
        cells = np.array(order[0][c] + order[1][c])
        waves = 64 * c + np.arange(64)
        angle = 2.0 * np.pi * (np.outer(waves, cells) % width) / width
        cos, sin = np.cos(angle) / np.sqrt(width), np.sin(angle) / np.sqrt(width)
        column.append(np.concatenate([cos, -sin], axis=0))
        inverse.append(np.concatenate([cos, -sin], axis=0).T)
    steps = np.arange(height)
    angle = 2.0 * np.pi * (np.outer(steps, steps) % height) / height
    eye = np.eye(16)
    rows = np.concatenate(
        [np.kron(np.cos(angle), eye), np.kron(np.sin(angle), eye)], axis=0
    ) / np.sqrt(height)
    pick = lambda both: lax.dynamic_index_in_dim(jnp.asarray(np.stack(both), bf16), core, 0, False)
    return pick(column), pick(inverse), jnp.asarray(rows, bf16)


RING = 8
GATHER_CUTS = (0, 640, 1280, 2112, 2944)
SUM_CUTS = (0, 640, 1280, 2128, 2960)


def ring_place(row):
    return jnp.where(row % 2 == 0, row // 2, 7 - row // 2)


def ring_row(spot):
    return jnp.where(spot < 4, 2 * spot, 2 * (7 - spot) + 1)


def gather_kernel(shard, flat, ring_s, ring_r, x_s, x_r, sib_s, sib_r, own_sem):
    row, me, core, sibling = place()
    x = me % 2
    spot = ring_place(row)
    beside = (row, (1 - x) * 2 + core)
    ahead = (ring_row((spot + 1) % RING), x * 2 + core)
    behind = (ring_row((spot + RING - 1) % RING), x * 2 + core)
    ways = (ahead, behind)
    barrier = pltpu.get_barrier_semaphore()
    for device in (ahead, behind, beside, sibling):
        pl.semaphore_signal(barrier, inc=1, device_id=device, device_id_type=MESH)

    def span(part):
        return GATHER_CUTS[part], GATHER_CUTS[part + 1] - GATHER_CUTS[part]

    def piece(source_spot, source_x, part):
        low, size = span(part)
        base = (ring_row(source_spot) * 4 + source_x * 2 + core) * CH
        return flat.at[pl.ds(pl.multiple_of(base + low, 16), size)]

    def mine(part):
        low, size = span(part)
        return shard.at[pl.ds(low, size)]

    def origin(hop, way):
        return (spot - hop + RING) % RING if way == 0 else (spot + hop) % RING

    def item(hop, way, what):
        part = way if what else 2 + way
        return origin(hop, way), (1 - x if what == 2 else x), part

    def ring(hop, way, what, first=False):
        to = piece(*item(hop, way, what))
        source = mine(item(hop, way, what)[2]) if first and what < 2 else to
        return remote(
            source, to, ring_s.at[what, way, hop], ring_r.at[what, way, hop], ways[way]
        )

    def cross(slot, way, first=False):
        if isinstance(slot, int) and slot == 8:
            to, source = piece(spot, x, way), mine(way)
        else:
            to = piece(origin(slot, way), x, 2 + way)
            source = mine(2 + way) if first else to
        return remote(source, to, x_s.at[way, slot], x_r.at[way, slot], beside)

    def share(where, slot, way, what):
        return remote(where, where, sib_s.at[what, way, slot], sib_r.at[what, way, slot], sibling)

    def from_beside(slot, way):
        if isinstance(slot, int) and slot == 8:
            return piece(spot, 1 - x, way)
        return piece(origin(slot, way), 1 - x, 2 + way)

    base = pl.multiple_of((row * 4 + x * 2 + core) * CH, 16)
    whole = flat.at[pl.ds(base, CH)]
    own = pltpu.make_async_copy(shard, whole, own_sem)
    own.start()
    pl.semaphore_wait(barrier, 4)
    for way in range(2):
        ring(0, way, 0, True).start()
        cross(8, way).start()
    for way in range(2):
        ring(0, way, 1, True).start()
        cross(0, way, True).start()
    given = remote(shard, whole, sib_s.at[3, 0, 9], sib_r.at[3, 0, 9], sibling)
    given.start()
    for way in range(2):
        cross(8, way).wait_recv()
        ring(0, way, 2).start()
        share(from_beside(8, way), 8, way, 3).start()

    def step(hop, carry):
        for what in range(3):
            for way in range(2):
                ring(hop - 1, way, what).wait_recv()

                @pl.when(hop < RING - 1)
                def _():
                    ring(hop, way, what).start()

                if what == 0:
                    cross(hop, way).start()
                share(piece(*item(hop, way, what)), hop - 1, way, what).start()
        for way in range(2):
            cross(hop - 1, way).wait_recv()
            share(from_beside(hop - 1, way), hop - 1, way, 3).start()
        return carry

    lax.fori_loop(1, RING, step, 0)
    for way in range(2):
        cross(RING - 1, way).wait_recv()
        share(from_beside(RING - 1, way), RING - 1, way, 3).start()
    own.wait()

    def settle(hop, carry):
        for way in range(2):
            for what in range(3):
                ring(hop, way, what).wait_send()
                share(piece(*item(hop + 1, way, what)), hop, way, what).wait()
        return carry

    lax.fori_loop(0, RING - 1, settle, 0)

    def settle_cross(slot, carry):
        for way in range(2):
            cross(slot, way).wait_send()
            share(from_beside(slot, way), slot, way, 3).wait()
        return carry

    lax.fori_loop(0, RING, settle_cross, 0)
    for way in range(2):
        cross(8, way).wait_send()
        share(from_beside(8, way), 8, way, 3).wait()
    given.wait()


def ag(shard):
    anywhere = pl.BlockSpec(memory_space=pl.ANY)
    dma = pltpu.SemaphoreType.DMA
    return pl.pallas_call(
        gather_kernel,
        out_shape=jax.ShapeDtypeStruct((32 * CH, 128), bf16),
        in_specs=[anywhere],
        out_specs=anywhere,
        scratch_shapes=[
            dma((3, 2, 7)),
            dma((3, 2, 7)),
            dma((2, 9)),
            dma((2, 9)),
            dma((4, 2, 10)),
            dma((4, 2, 10)),
            dma,
        ],
        compiler_params=pltpu.CompilerParams(collective_id=0, has_side_effects=True),
        name="gather_weights",
    )(shard)


def sum_kernel(
    grad, loss, total, stats,
    own, sib, xin, rin_b, rin_a, xlast, st_mine, st_sib, st_sum, st_all,
    own_s, sib_s, sib_r, x_s, x_r, last_s, last_r, ring_s, ring_r, tell_s, tell_r, pair_s, pair_r,
):
    row, me, core, sibling = place()
    x = me % 2
    spot = ring_place(row)
    beside = (row, (1 - x) * 2 + core)
    ahead = (ring_row((spot + 1) % RING), x * 2 + core)
    behind = (ring_row((spot + RING - 1) % RING), x * 2 + core)
    ways = (ahead, behind)
    barrier = greet_chips(me, core, sibling)
    sizes = [SUM_CUTS[k + 1] - SUM_CUTS[k] for k in range(4)]

    def owner(turn, way):
        return (spot - 1 - turn + 2 * RING) % RING if way == 0 else (spot + 1 + turn) % RING

    def source(turn, way, other_x, part, side):
        owner_x = (1 - x) if other_x else x
        base = (ring_row(owner(turn, way)) * 4 + owner_x * 2 + side) * OWN // 16 * 16
        return grad.at[pl.ds(pl.multiple_of(base + SUM_CUTS[part], 16), sizes[part])]

    def part_of(way, what):
        return way if what >= 2 else 2 + way

    def held(buf, turn, way, what):
        part = part_of(way, what)
        return buf.at[what % 2, turn, pl.ds(SUM_CUTS[part], sizes[part])]

    def load(turn, way, what):
        return pltpu.make_async_copy(
            source(turn, way, what % 2, part_of(way, what), core),
            held(own, turn, way, what),
            own_s.at[what, way, turn],
        )

    def give(turn, way, what):
        return remote(
            source(turn, way, what % 2, part_of(way, what), 1 - core),
            held(sib, turn, way, what),
            sib_s.at[what, way, turn],
            sib_r.at[what, way, turn],
            sibling,
        )

    def cross(turn, way):
        return remote(
            held(own, turn, way, 1),
            xin.at[turn, pl.ds(SUM_CUTS[2 + way] - SUM_CUTS[2], sizes[2 + way])],
            x_s.at[way, turn],
            x_r.at[way, turn],
            beside,
        )

    def got(way, slot, what):
        if what == 0:
            return rin_b.at[slot, pl.ds(SUM_CUTS[2 + way] - SUM_CUTS[2], sizes[2 + way])]
        return rin_a.at[what - 2, slot, pl.ds(SUM_CUTS[way], sizes[way])]

    def ring(turn, way, what, first=False):
        where = held(own, turn, way, what) if first else got(way, turn - 1, what)
        return remote(
            where,
            got(way, turn, what),
            ring_s.at[what, way, turn],
            ring_r.at[what, way, turn],
            ways[way],
        )

    order = (1, 2, 3, 0)

    def begin_own(turn, carry):
        for what in order:
            for way in range(2):
                load(turn, way, what).start()
        return carry

    def begin_sib(turn, carry):
        for what in order:
            for way in range(2):
                give(turn, way, what).start()
        return carry

    begin_own(0, 0)
    pl.semaphore_wait(barrier, CHIPS)
    begin_sib(0, 0)
    lax.fori_loop(1, RING, lambda t, c: begin_sib(t, begin_own(t, c)), 0)

    def both(turn, way, what):
        load(turn, way, what).wait()
        give(turn, way, what).wait_recv()
        return held(own, turn, way, what)[...].astype(f32) + held(sib, turn, way, what)[...].astype(f32)

    def send_across(turn):
        for way in range(2):
            held(own, turn, way, 1)[...] = both(turn, way, 1).astype(bf16)
            cross(turn, way).start()

    def across(turn, way):
        cross(turn, way).wait_recv()
        return xin[turn, pl.ds(SUM_CUTS[2 + way] - SUM_CUTS[2], sizes[2 + way])].astype(f32)

    send_across(0)
    for what in (2, 3):
        for way in range(2):
            held(own, 0, way, what)[...] = both(0, way, what).astype(bf16)
            ring(0, way, what, True).start()
    send_across(1)
    for way in range(2):
        held(own, 0, way, 0)[...] = (both(0, way, 0) + across(0, way)).astype(bf16)
        ring(0, way, 0, True).start()

    def step(turn, carry):
        send_across(turn + 1)
        for what in (2, 3, 0):
            for way in range(2):
                part = both(turn, way, what)
                if what == 0:
                    part = part + across(turn, way)
                ring(turn - 1, way, what, True).wait_recv()
                where = got(way, turn - 1, what)
                where[...] = (where[...].astype(f32) + part).astype(bf16)
                ring(turn, way, what).start()
        return carry

    lax.fori_loop(1, RING - 1, step, 0)
    last = RING - 1
    def to_beside(way):
        return remote(
            got(way, last - 1, 3),
            xlast.at[pl.ds(SUM_CUTS[way], sizes[way])],
            last_s.at[way],
            last_r.at[way],
            beside,
        )

    for way in range(2):
        part = both(last, way, 3)
        ring(last - 1, way, 3, True).wait_recv()
        where = got(way, last - 1, 3)
        where[...] = (where[...].astype(f32) + part).astype(bf16)
        to_beside(way).start()
    for what in (2, 0):
        for way in range(2):
            part = both(last, way, what)
            if what == 0:
                part = part + across(last, way)
            ring(last - 1, way, what, True).wait_recv()
            low = SUM_CUTS[part_of(way, what)]
            total[low : low + sizes[part_of(way, what)]] = got(way, last - 1, what)[...].astype(f32) + part
    for way in range(2):
        to_beside(way).wait_recv()
        low = SUM_CUTS[way]
        total[low : low + sizes[way]] += xlast[low : low + sizes[way]].astype(f32)

    first = ((row * 4 + x * 2 + core) * OWN) % 16
    rows = lax.broadcasted_iota(jnp.int32, (CHR, 128), 0)
    value = total[...]
    squares = jnp.where((rows >= first) & (rows < first + OWN), value * value, 0.0)
    st_mine[0:8] = jnp.sum(squares.reshape(CHR // 8, 8, 128), axis=0)
    st_mine[8:16] = loss[...]
    pair = remote(st_mine, st_sib, pair_s, pair_r, sibling)
    pair.start()
    pair.wait_recv()
    st_sum[...] = st_mine[...] + st_sib[...]
    st_all[me] = st_sum[...]

    def tell(k):
        return remote(
            st_sum, st_all.at[me], tell_s.at[k], tell_r.at[k],
            chip_device(lax.rem(me + k, CHIPS), core),
        )

    def tell_one(k, carry):
        tell(k).start()
        return carry

    lax.fori_loop(1, CHIPS, tell_one, 0)

    def settle(turn, carry):
        for way in range(2):
            for what in range(4):
                give(turn, way, what).wait_send()
            cross(turn, way).wait_send()

            @pl.when(turn < RING - 1)
            def _():
                for what in (0, 2, 3):
                    ring(turn, way, what, True).wait_send()

        return carry

    lax.fori_loop(0, RING, settle, 0)
    for way in range(2):
        to_beside(way).wait_send()

    def told(k, carry):
        tell(k).wait_recv()
        return carry

    lax.fori_loop(1, CHIPS, told, 0)
    everything = st_all[0]
    for k in range(1, CHIPS):
        everything = everything + st_all[k]
    stats[...] = everything

    def tell_done(k, carry):
        tell(k).wait_send()
        return carry

    lax.fori_loop(1, CHIPS, tell_done, 0)
    pair.wait_send()


def rs(grad, loss):
    vm, dma = pltpu.VMEM, pltpu.SemaphoreType.DMA
    first, second = SUM_CUTS[2], SUM_CUTS[4] - SUM_CUTS[2]
    shape = jax.ShapeDtypeStruct
    return pl.pallas_call(
        sum_kernel,
        out_shape=[shape((CHR, 128), f32), shape((16, 128), f32)],
        in_specs=[pl.BlockSpec(memory_space=pl.ANY), pl.BlockSpec(memory_space=vm)],
        out_specs=[pl.BlockSpec(memory_space=vm)] * 2,
        scratch_shapes=[
            vm((2, RING, CHR, 128), bf16),
            vm((2, RING, CHR, 128), bf16),
            vm((RING, second, 128), bf16),
            vm((RING - 1, second, 128), bf16),
            vm((2, RING - 1, first, 128), bf16),
            vm((first, 128), bf16),
            vm((16, 128), f32),
            vm((16, 128), f32),
            vm((16, 128), f32),
            vm((CHIPS, 16, 128), f32),
            dma((4, 2, RING)),
            dma((4, 2, RING)),
            dma((4, 2, RING)),
            dma((2, RING)),
            dma((2, RING)),
            dma((2,)),
            dma((2,)),
            dma((4, 2, RING - 1)),
            dma((4, 2, RING - 1)),
            dma((CHIPS,)),
            dma((CHIPS,)),
            dma,
            dma,
        ],
        compiler_params=pltpu.CompilerParams(
            collective_id=1, has_side_effects=True, vmem_limit_bytes=56 << 20
        ),
        name="sum_gradients",
    )(grad, loss)


MATS = [(PIN, D), (D, FF), (FF, D), (D, FF), (FF, D), (D, PIN)]
SMALL_LAYER = 2352
SMALLS = [6 + SMALL_LAYER, 24, 6 + SMALL_LAYER, 24, 18, 10]
PIECE = 256


def flat_sections():
    at = 0
    found = []
    for (depth, cols), small in zip(MATS, SMALLS):
        per_row = cols // LANES
        found.append((at, depth, per_row, at + depth * per_row, small))
        at += depth * per_row + small
    return found


def piece_rows(depth, per_row):
    rows = depth
    while rows * per_row > 7680:
        rows -= PIECE
        while depth % rows:
            rows -= PIECE
    return rows


def put_rows(wide, at, value):
    for k in range(value.shape[1] // LANES):
        wide[at + k : at + k + 1] = value[:, k * LANES : (k + 1) * LANES]


def put_block_weight(wide, at, block, grad, square):
    wide[at : at + 2 * NBLK * BLOCK_ROWS] = jnp.zeros((2 * NBLK * BLOCK_ROWS, LANES), f32)
    square[0] = grad[:PADC, :PADC] + grad[PADC:, PADC:]
    square[1] = grad[:PADC, PADC:] - grad[PADC:, :PADC]
    for part in range(2):
        a, b, c, d = (square[part, pl.ds(q, 24, stride=4), :] for q in range(4))
        rows = (
            jnp.concatenate([a[:, :96], b[:, :32]], axis=1),
            jnp.concatenate([b[:, 32:96], c[:, :64]], axis=1),
            jnp.concatenate([c[:, 64:96], d[:, :96]], axis=1),
        )
        for q, value in enumerate(rows):
            wide[pl.ds(at + (part * NBLK + block) * BLOCK_ROWS + q, 24, stride=3), :] = value


def put_block_bias(wide, at, block, grad):
    found = []
    for part in range(2):
        piece = grad[:, part * PADC : part * PADC + BS]
        found += [jnp.where(block == k, piece, 0.0) for k in range(NBLK)]
    put_rows(wide, at, jnp.concatenate(found, axis=1))


def write_section(i, xs, gs, bufs):
    across, side, wide, narrow, edge, flat, sem = bufs
    start, depth, per_row, _, _ = flat_sections()[i]
    cols = per_row * LANES
    for half in range(2):
        for part in range(0, depth, PIECE):
            across[part : part + PIECE, half * 128 : half * 128 + 128] = xs[half][
                :, part : part + PIECE
            ].T
        side[half * 128 : half * 128 + 128, 0:cols] = gs[half][...]
    rows = piece_rows(depth, per_row)
    full = rows * per_row
    shift = start % 16
    skip = 16 if shift else 0
    turns = depth // rows

    def emit(at, low):
        return pltpu.make_async_copy(
            narrow.at[pl.ds(low, full - low)], flat.at[pl.ds(at + low, full - low)], sem
        )

    def step(it, carry):
        top = pl.multiple_of(it * rows, PIECE)
        for part in range(0, rows, PIECE):
            left = across[pl.ds(pl.multiple_of(top + part, PIECE), PIECE), :]
            for j in range(0, per_row, 2):
                value = dot(left, side[:, j * LANES : (j + 2) * LANES])
                for by in range(2):
                    wide[pl.ds(shift + part * per_row + j + by, PIECE, stride=per_row), :] = value[
                        :, by * LANES : (by + 1) * LANES
                    ]

        @pl.when(it == 1)
        def _():
            emit(0, skip).wait()

        @pl.when(it > 1)
        def _():
            emit(0, 0).wait()

        narrow[0:full] = wide[0:full].astype(bf16)

        @pl.when(it == 0)
        def _():
            edge[2 * i] = wide[0:16]
            emit(start - shift, skip).start()

        @pl.when(it > 0)
        def _():
            emit(pl.multiple_of(start - shift + it * full, 16), 0).start()

        wide[0:16] = wide[full : full + 16]
        return carry

    lax.fori_loop(0, turns, step, 0)
    edge[2 * i + 1] = wide[0:16]
    emit(0, skip if turns == 1 else 0).wait()


def write_small(i, put, bufs):
    _, _, wide, narrow, edge, flat, sem = bufs
    _, _, _, at, count = flat_sections()[i]
    shift = at % 16
    wide[0:16] = edge[2 * i + 1]
    put(i, shift)
    end = shift + count
    total = GROWS - at + shift if i == 5 else -(-end // 16) * 16
    if i == 5:
        wide[end:total] = jnp.zeros((total - end, LANES), f32)
    elif total > end:
        wide[end:total] = edge[2 * i + 2, 16 - (total - end) : 16]
    narrow[0:total] = wide[0:total].astype(bf16)
    done = pltpu.make_async_copy(
        narrow.at[pl.ds(0, total)], flat.at[pl.ds(at - shift, total)], sem
    )
    done.start()
    done.wait()


CELLS = 2 * UNIT
FCHUNK = 1024
FILTER_SEMS = 10


def norm_adjoint(values, gain, grad):
    normed, scale = normalize(values)
    inner = grad * gain
    along = jnp.mean(inner * normed, axis=-1, keepdims=True)
    flat = jnp.mean(inner, axis=-1, keepdims=True)
    return (
        scale * (inner - flat - normed * along),
        jnp.sum(grad * normed, axis=0, keepdims=True),
        jnp.sum(grad, axis=0, keepdims=True),
    )


SMALL_AT = []
for _count in SMALLS:
    SMALL_AT.append(SMALL_AT[-1] + -(-SMALLS[len(SMALL_AT) - 1] // 8) * 8 if SMALL_AT else 0)
SMALL_ROWS = SMALL_AT[-1] + 16
AT_NORM = (0, 6, 2340, 2346)
AT_W1, AT_B1, AT_W2, AT_B2 = 12, 1164, 1176, 2328
BLOCK_ROWS = BS * BS // LANES


def aligned_part(at, count):
    low = at // 16 * 16
    return low, -(-(at + count - low) // 16) * 16


def unpack_sections(flat, raw, wide, in_sem, wanted):
    steps = []
    for i, target in wanted:
        start, depth, per_row, _, _ = flat_sections()[i]
        rows = piece_rows(depth, per_row)
        for top in range(0, depth, rows):
            steps.append((start + top * per_row, per_row, top, rows, target))

    def fetch(n):
        at, per_row, _, rows, _ = steps[n]
        low, size = aligned_part(at, rows * per_row)
        return pltpu.make_async_copy(
            flat.at[pl.ds(low, size)], raw.at[n % 2, pl.ds(0, size)], in_sem.at[n % 2]
        ), size

    fetch(0)[0].start()
    for n, (at, per_row, top, rows, target) in enumerate(steps):
        if n + 1 < len(steps):
            fetch(n + 1)[0].start()
        copy, size = fetch(n)
        copy.wait()
        wide[0:size] = raw[n % 2, 0:size].astype(f32)
        for part in range(0, rows, PIECE):
            for j in range(per_row):
                target[top + part : top + part + PIECE, j * LANES : (j + 1) * LANES] = wide[
                    pl.ds(at % 16 + part * per_row + j, PIECE, stride=per_row), :
                ].astype(bf16)


def unpack_small(flat, raw, wide, in_sem, small):
    def fetch(n):
        _, _, _, at, count = flat_sections()[n]
        low, size = aligned_part(at, count)
        return pltpu.make_async_copy(
            flat.at[pl.ds(low, size)], raw.at[n % 2, pl.ds(0, size)], in_sem.at[n % 2]
        ), size, at - low, count

    fetch(0)[0].start()
    for n in range(6):
        if n < 5:
            fetch(n + 1)[0].start()
        copy, size, shift, count = fetch(n)
        copy.wait()
        wide[0:size] = raw[n % 2, 0:size].astype(f32)
        small[SMALL_AT[n] : SMALL_AT[n] + count] = wide[shift : shift + count]


def long_row(small, at, count):
    return jnp.concatenate([small[at + k : at + k + 1] for k in range(count)], axis=1)


def block_weight(small, at, block, square, out):
    blank = jnp.zeros((24, PADC - BS), f32)
    square[...] = jnp.zeros_like(square)
    for part in range(2):
        base = at + (part * NBLK + block) * BLOCK_ROWS
        a, b, c = (small[pl.ds(base + q, 24, stride=3), :] for q in range(3))
        pieces = (
            a[:, :96],
            jnp.concatenate([a[:, 96:], b[:, :64]], axis=1),
            jnp.concatenate([b[:, 64:], c[:, :32]], axis=1),
            c[:, 32:],
        )
        for q, piece in enumerate(pieces):
            piece = jnp.concatenate([piece, blank], axis=1)
            if part == 0:
                square[0, pl.ds(q, 24, stride=4), :] = piece
                square[3, pl.ds(q, 24, stride=4), :] = piece
            else:
                square[1, pl.ds(q, 24, stride=4), :] = piece
                square[2, pl.ds(q, 24, stride=4), :] = -piece
    for quarter in range(4):
        top, left = quarter // 2 * PADC, quarter % 2 * PADC
        out[top : top + PADC, left : left + PADC] = square[quarter].astype(bf16)


def block_bias(small, at, block):
    blank = jnp.zeros((1, PADC - BS), f32)
    both = long_row(small, at, 12)
    found = []
    for part in range(2):
        value = jnp.zeros((1, BS), f32)
        for k in range(NBLK):
            low = (part * NBLK + k) * BS
            value = value + jnp.where(block == k, both[:, low : low + BS], 0.0)
        found += [value, blank]
    return jnp.concatenate(found, axis=1)


def forward_kernel(*refs):
    x0, goals, mask, weight, column, inverse, rows, flat = refs[:8]
    (streams, waves_o, mixeds, normeds, befores, hiddens, lasts, tails, errors,
     embed_h, in0, out0, in1, out1, head_h, x1, loss, norms, tail, w1, b1, w2) = refs[8:30]
    (embed, w_in, w_out, head, flow, x_now, s_stream, s_waves, s_mixed, s_norm, s_before, s_hidden,
     s_tail, s_error, raw, wide, small, square, b2, c1, c2, embed_b, head_b,
     weight_sem, out_sem, tail_sem, in_sem) = refs[30:57]
    units, mine, others, waves, back, own_sum, to_sib, from_sib, ready, landed, joined = refs[57:68]
    sems = refs[68:]
    row, me, core, sibling = place()
    barrier = greet_chips(me, core, sibling)
    stores = [
        pltpu.make_async_copy(source, target, weight_sem.at[k])
        for k, (source, target) in enumerate(
            [(embed, embed_h), (w_in.at[0], in0), (w_out.at[0], out0), (w_in.at[1], in1),
             (w_out.at[1], out1), (head, head_h)]
        )
    ]
    block = me % NBLK
    unpack_small(flat, raw, wide, in_sem, small)
    embed_b[...] = long_row(small, SMALL_AT[0], 6)
    head_b[...] = long_row(small, SMALL_AT[5], 10)
    for layer in range(LAYERS):
        base = SMALL_AT[2 * layer] + 6
        for k, at in enumerate(AT_NORM):
            norms[layer, k : k + 1] = long_row(small, base + at, 6)
        c1[layer] = long_row(small, SMALL_AT[2 * layer + 1], 24)
        c2[layer] = long_row(small, SMALL_AT[2 * layer + 2], 6)
        block_weight(small, base + AT_W1, block, square, w1.at[layer])
        block_weight(small, base + AT_W2, block, square, w2.at[layer])
        b1[layer] = block_bias(small, base + AT_B1, block)
        b2[layer] = block_bias(small, base + AT_B2, block)
    tail[0:1] = long_row(small, SMALL_AT[4] + 6, 6)
    tail[1:2] = long_row(small, SMALL_AT[4] + 12, 6)
    unpack_sections(flat, raw, wide, in_sem, [(0, embed)])
    stores[0].start()
    x_now[...] = x0[...]
    loss[...] = jnp.zeros_like(loss)

    def saves(it):
        pairs = [(s_stream, streams), (s_waves, waves_o), (s_mixed, mixeds), (s_norm, normeds),
                 (s_before, befores), (s_hidden, hiddens)]
        return [
            pltpu.make_async_copy(source, target.at[it], out_sem.at[k])
            for k, (source, target) in enumerate(pairs)
        ]

    def tail_saves(step):
        pairs = [(flow, lasts), (s_tail, tails), (s_error, errors)]
        return [
            pltpu.make_async_copy(source, target.at[step], tail_sem.at[k])
            for k, (source, target) in enumerate(pairs)
        ]

    def when_it(cond, action):
        @pl.when(cond)
        def _():
            action()

    def unpack_when(it, number, wanted, done):
        def go():
            unpack_sections(flat, raw, wide, in_sem, wanted)
            for k in done:
                stores[k].start()

        when_it(it == number, go)

    def meanwhile_in(it):
        unpack_when(it, 0, [(1, w_in.at[0])], [1])
        unpack_when(it, 1, [(3, w_in.at[1])], [3])

    def meanwhile_out(it):
        unpack_when(it, 0, [(2, w_out.at[0])], [2])
        unpack_when(it, 1, [(4, w_out.at[1]), (5, head)], [4, 5])

    def body(it, carry):
        step, layer = it // 2, it % 2

        def start_step():
            flow[...] = dot(x_now[...], embed[...]) + embed_b[...]

        def tail_done():
            for save in tail_saves(0):
                save.wait()

        when_it(it == 2, tail_done)
        when_it(layer == 0, start_step)

        def saved():
            for save in saves(it):
                save.wait()

        when_it(it > 0, saved)
        s_stream[...] = flow[...]
        normed, _ = normalize(flow[...])
        split_units(normed * norms[layer, 0:1] + norms[layer, 1:2], units)
        when_it(it == 0, lambda: pl.semaphore_wait(barrier, CHIPS))

        finish_one = spread_units(
            me, core, sibling, units, mine, others, sems[:5], lambda: meanwhile_in(it)
        )
        groups = to_spectrum(mine, others, column, rows, waves)
        for g in range(4):
            s_waves[g] = groups[g]
            hidden = gelu_of(dot(groups[g], w1[layer]) + b1[layer]).astype(bf16)
            spec = (dot(hidden, w2[layer]) + b2[layer]).astype(bf16)
            from_spectrum(g, spec, rows, back)
        finish_two = gather_units(
            row, me, core, sibling, back, inverse,
            (own_sum, to_sib, from_sib, ready, landed), sems[5:], finish_one,
            lambda: meanwhile_out(it),
        )
        join_units(landed, joined)
        mixed = flow[...] + joined[...]
        s_mixed[...] = mixed
        normed, _ = normalize(mixed)
        s_norm[...] = (normed * norms[layer, 2:3] + norms[layer, 3:4]).astype(bf16)
        flow[...] = mixed + c2[layer]

        def chunk(c, carry):
            part = pl.ds(c * FCHUNK, FCHUNK)
            before = dot(s_norm[...], w_in[layer, :, part]) + c1[layer, :, part]
            s_before[:, part] = before.astype(bf16)
            hidden = gelu_of(before).astype(bf16)
            s_hidden[:, part] = hidden
            flow[...] += dot(hidden, w_out[layer, part, :])
            return carry

        for c in range(FF // FCHUNK):
            chunk(c, 0)
        for save in saves(it):
            save.start()
        finish_two()
        def end_step():
            normed, _ = normalize(flow[...])
            s_tail[...] = (normed * tail[0:1] + tail[1:2]).astype(bf16)
            predicted = dot(s_tail[...], head[...]) + head_b[...]
            error = predicted - goals[step].astype(f32)
            s_error[...] = error
            loss[...] += weight[...] * jnp.sum(error * error, axis=-1, keepdims=True)
            x_now[...] = (predicted * mask[...]).astype(bf16)
            for save in tail_saves(step):
                save.start()

        when_it(layer == 1, end_step)
        when_it(it == 1, lambda: x1.__setitem__(Ellipsis, x_now[...]))
        return carry

    lax.fori_loop(0, 4, body, 0)
    for save in saves(3):
        save.wait()
    for save in tail_saves(1):
        save.wait()
    for store in stores:
        store.wait()


def forward_pass(*args):
    vm, dma = pltpu.VMEM, pltpu.SemaphoreType.DMA
    whole, anywhere = pl.BlockSpec(memory_space=vm), pl.BlockSpec(memory_space=pl.ANY)
    shape = jax.ShapeDtypeStruct
    return pl.pallas_call(
        forward_kernel,
        out_shape=[
            shape((4, CELLS, D), f32),
            shape((4, 4, 256, 256), bf16),
            shape((4, CELLS, D), f32),
            shape((4, CELLS, D), bf16),
            shape((4, CELLS, FF), bf16),
            shape((4, CELLS, FF), bf16),
            shape((2, CELLS, D), f32),
            shape((2, CELLS, D), bf16),
            shape((2, CELLS, PIN), f32),
            *[shape(dims, bf16) for dims in MATS],
            shape((CELLS, PIN), bf16),
            shape((CELLS, 1), f32),
            shape((2, 4, D), f32),
            shape((2, D), f32),
            shape((2, 256, 256), bf16),
            shape((2, 1, 256), f32),
            shape((2, 256, 256), bf16),
        ],
        in_specs=[whole] * 7 + [anywhere],
        out_specs=[anywhere] * 15 + [whole] * 7,
        scratch_shapes=[
            vm((PIN, D), bf16),
            vm((2, D, FF), bf16),
            vm((2, FF, D), bf16),
            vm((D, PIN), bf16),
            vm((CELLS, D), f32),
            vm((CELLS, PIN), bf16),
            vm((CELLS, D), f32),
            vm((4, 256, 256), bf16),
            vm((CELLS, D), f32),
            vm((CELLS, D), bf16),
            vm((CELLS, FF), bf16),
            vm((CELLS, FF), bf16),
            vm((CELLS, D), bf16),
            vm((CELLS, PIN), f32),
            vm((2, 7696, LANES), bf16),
            vm((7696, LANES), f32),
            vm((SMALL_ROWS, LANES), f32),
            vm((4, PADC, PADC), f32),
            vm((2, 1, 256), f32),
            vm((2, 1, FF), f32),
            vm((2, 1, D), f32),
            vm((1, D), f32),
            vm((1, PIN), f32),
            dma((6,)),
            dma((6,)),
            dma((3,)),
            dma((2,)),
        ]
        + filter_scratch(),
        compiler_params=pltpu.CompilerParams(
            collective_id=2, has_side_effects=True, vmem_limit_bytes=56 << 20
        ),
        name="forward_pass",
    )(*args)


def backward_kernel(*refs):
    (gscale, mask, norms, tail, column, inverse, rows, w1, b1, w2,
     embed_h, in0, out0, in1, out1, head_h,
     streams, waves_h, mixeds, befores, lasts, errors, inputs, x1, normeds, hiddens, tails) = refs[:27]
    flat = refs[27]
    (sum_norm, sum_c1, sum_tail, sum_head, grad_w1, grad_w2, grad_b,
     embed, w_in, w_out, head, flow, carried, i_stream, i_waves, i_mixed, i_before, i_last, i_error,
     s_pred, s_out, s_pre, s_embed, g_norm, x_in, x_out, x_tail,
     across, side, wide, narrow, edge, square,
     weight_sem, in_sem, tail_in, section_sem, flat_sem) = refs[28:66]
    units, mine, others, waves, back, own_sum, to_sib, from_sib, ready, landed, joined = refs[66:77]
    sems = refs[77:]
    bufs = (across, side, wide, narrow, edge, flat, flat_sem)
    row, me, core, sibling = place()
    barrier = greet_chips(me, core, sibling)

    def when_it(cond, action):
        @pl.when(cond)
        def _():
            action()

    loads = [
        pltpu.make_async_copy(source, target, weight_sem.at[k])
        for k, (source, target) in enumerate(
            [(head_h, head), (out1, w_out.at[1]), (in1, w_in.at[1]), (out0, w_out.at[0]),
             (in0, w_in.at[0]), (embed_h, embed)]
        )
    ]

    def inst(it):
        return 3 - it

    def fetch(it):
        slot = it % 2
        pairs = [(streams, i_stream), (waves_h, i_waves), (mixeds, i_mixed), (befores, i_before)]
        return [
            pltpu.make_async_copy(source.at[inst(it)], target.at[slot], in_sem.at[k, slot])
            for k, (source, target) in enumerate(pairs)
        ]

    tail_loads = [
        pltpu.make_async_copy(lasts, i_last, tail_in.at[0]),
        pltpu.make_async_copy(errors, i_error, tail_in.at[1]),
    ]
    late_load = pltpu.make_async_copy(tails, x_tail, tail_in.at[2])
    for load in tail_loads:
        load.start()
    loads[0].start()
    for load in fetch(0):
        load.start()
    for load in loads[1:]:
        load.start()
    for target in (sum_norm, sum_c1, sum_tail, sum_head, grad_w1, grad_w2, grad_b, carried):
        target[...] = jnp.zeros_like(target)

    late_load.start()

    def section_loads(layer):
        return [
            pltpu.make_async_copy(source.at[2 * step + layer], target.at[step], section_sem.at[n, step])
            for n, (source, target) in enumerate([(normeds, x_in), (hiddens, x_out)])
            for step in range(2)
        ]

    def write_when(it, number, work):
        when_it(it == number, lambda: [write_section(i, xs, gs, bufs) for i, xs, gs in work] and None)

    def pairs_out(layer):
        return (2 + 2 * layer, (x_out.at[0], x_out.at[1]), (s_out.at[2], s_out.at[layer]))

    def pairs_in(layer):
        return (1 + 2 * layer, (x_in.at[0], x_in.at[1]), (s_pre.at[2], s_pre.at[layer]))

    def meanwhile_in(it):
        write_when(it, 2, [(5, (x_tail.at[0], x_tail.at[1]), (s_pred.at[0], s_pred.at[1])), pairs_out(1)])
        write_when(it, 3, [pairs_out(0)])

    def meanwhile_out(it):
        write_when(it, 2, [pairs_in(1)])
        write_when(it, 3, [pairs_in(0)])

    def body(it, carry):
        step, layer, slot = 1 - it // 2, 1 - it % 2, it % 2
        keep = jnp.where(step == 1, layer, 2)

        def fetch_section(wanted):
            for load in section_loads(wanted):
                load.start()

        when_it(it == 2, lambda: fetch_section(1))
        when_it(it == 3, lambda: fetch_section(0))

        def first():
            for load in tail_loads:
                load.wait()
            loads[0].wait()

        when_it(it == 0, first)

        def head_adjoint():
            grad = i_error[step] * gscale[...] + carried[...]
            grad16 = grad.astype(bf16)
            s_pred[step] = grad16
            sum_head[0:1] += jnp.sum(grad, axis=0, keepdims=True)
            back_n = dot_cols(grad16, head[...]).astype(bf16).astype(f32)
            value, gain, shift = norm_adjoint(i_last[step], tail[0:1], back_n)
            flow[...] = value
            sum_tail[0:1] += gain
            sum_tail[1:2] += shift

        when_it(layer == 1, head_adjoint)

        def prefetch():
            for load in fetch(it + 1):
                load.start()

        when_it(it < 3, prefetch)

        s_out[keep] = flow[...].astype(bf16)
        sum_norm[layer, 4:5] += jnp.sum(flow[...], axis=0, keepdims=True)
        for load in fetch(it):
            load.wait()

        def second_layer():
            loads[1].wait()
            loads[2].wait()

        def first_layer():
            loads[3].wait()
            loads[4].wait()

        when_it(it == 0, second_layer)
        when_it(it == 1, first_layer)
        g_norm[...] = jnp.zeros_like(g_norm)

        def chunk(c, carry):
            part = pl.ds(c * FCHUNK, FCHUNK)
            grad = dot_cols(s_out[keep], w_out[layer, part, :]).astype(bf16).astype(f32)
            grad = grad * gelu_slope(i_before[slot, :, part].astype(f32))
            sum_c1[layer, 0:1, part] += jnp.sum(grad, axis=0, keepdims=True)
            grad16 = grad.astype(bf16)
            s_pre[keep, :, part] = grad16
            g_norm[...] += dot_cols(grad16, w_in[layer, :, part])
            return carry

        for c in range(FF // FCHUNK):
            chunk(c, 0)

        def section_ready():
            for load in section_loads(0):
                load.wait()

        when_it(it >= 2, section_ready)
        when_it(it == 2, late_load.wait)
        value, gain, shift = norm_adjoint(
            i_mixed[slot], norms[layer, 2:3], g_norm[...].astype(bf16).astype(f32)
        )
        flow[...] += value
        sum_norm[layer, 2:3] += gain
        sum_norm[layer, 3:4] += shift
        split_units(flow[...], units)
        when_it(it == 0, lambda: pl.semaphore_wait(barrier, CHIPS))
        finish_one = spread_units(
            me, core, sibling, units, mine, others, sems[:5], lambda: meanwhile_in(it)
        )
        groups = to_spectrum(mine, others, column, rows, waves)
        for g in range(4):
            before = dot(i_waves[slot, g], w1[layer]) + b1[layer]
            hidden = gelu_of(before).astype(bf16)
            grad_hidden = dot_cols(groups[g], w2[layer]).astype(bf16).astype(f32)
            grad_before = grad_hidden * gelu_slope(before)
            grad_before16 = grad_before.astype(bf16)
            grad_w2[layer] += dot_rows(hidden, groups[g])
            grad_w1[layer] += dot_rows(i_waves[slot, g], grad_before16)
            grad_b[layer, 0:1] += jnp.sum(grad_before, axis=0, keepdims=True)
            grad_b[layer, 1:2] += jnp.sum(groups[g].astype(f32), axis=0, keepdims=True)
            from_spectrum(g, dot_cols(grad_before16, w1[layer]).astype(bf16), rows, back)
        finish_two = gather_units(
            row, me, core, sibling, back, inverse,
            (own_sum, to_sib, from_sib, ready, landed), sems[5:], finish_one,
            lambda: meanwhile_out(it),
        )
        join_units(landed, joined)
        value, gain, shift = norm_adjoint(i_stream[slot], norms[layer, 0:1], joined[...])
        flow[...] += value
        sum_norm[layer, 0:1] += gain
        sum_norm[layer, 1:2] += shift
        when_it(it == 1, loads[5].wait)

        def embed_adjoint():
            s_embed[step] = flow[...].astype(bf16)
            sum_tail[2:3] += jnp.sum(flow[...], axis=0, keepdims=True)

        when_it(layer == 0, embed_adjoint)

        def carry_back():
            carried[...] = mask[...] * dot_cols(s_embed[1], embed[...]).astype(bf16).astype(f32)

        when_it(it == 1, carry_back)
        finish_two()
        return carry

    lax.fori_loop(0, 4, body, 0)
    block = me % NBLK

    def put_layer(at, idx):
        put_rows(wide, at, sum_norm[idx, 0:1])
        put_rows(wide, at + 6, sum_norm[idx, 1:2])
        put_block_weight(wide, at + AT_W1, block, grad_w1[idx], square)
        put_block_bias(wide, at + AT_B1, block, grad_b[idx, 0:1])
        put_block_weight(wide, at + AT_W2, block, grad_w2[idx], square)
        put_block_bias(wide, at + AT_B2, block, grad_b[idx, 1:2])
        put_rows(wide, at + AT_NORM[2], sum_norm[idx, 2:3])
        put_rows(wide, at + AT_NORM[3], sum_norm[idx, 3:4])

    def put_small(i, at):
        if i == 0:
            put_rows(wide, at, sum_tail[2:3])
            put_layer(at + 6, 0)
        elif i == 2:
            put_rows(wide, at, sum_norm[0, 4:5])
            put_layer(at + 6, 1)
        elif i == 4:
            put_rows(wide, at, sum_norm[1, 4:5])
            put_rows(wide, at + 6, sum_tail[0:1])
            put_rows(wide, at + 12, sum_tail[1:2])
        elif i == 5:
            put_rows(wide, at, sum_head[0:1])
        else:
            put_rows(wide, at, sum_c1[i // 2, 0:1])

    write_section(0, (inputs, x1), (s_embed.at[0], s_embed.at[1]), bufs)
    for i in range(6):
        write_small(i, put_small, bufs)


def backward_pass(*args):
    vm, dma = pltpu.VMEM, pltpu.SemaphoreType.DMA
    whole, anywhere = pl.BlockSpec(memory_space=vm), pl.BlockSpec(memory_space=pl.ANY)
    shape = jax.ShapeDtypeStruct
    return pl.pallas_call(
        backward_kernel,
        out_shape=shape((GROWS, LANES), bf16),
        in_specs=[whole] * 10 + [anywhere] * 12 + [whole] * 2 + [anywhere] * 3,
        out_specs=anywhere,
        scratch_shapes=[
            vm((2, 8, D), f32),
            vm((2, 8, FF), f32),
            vm((8, D), f32),
            vm((8, PIN), f32),
            vm((2, 256, 256), f32),
            vm((2, 256, 256), f32),
            vm((2, 8, 256), f32),
            vm((PIN, D), bf16),
            vm((2, D, FF), bf16),
            vm((2, FF, D), bf16),
            vm((D, PIN), bf16),
            vm((CELLS, D), f32),
            vm((CELLS, PIN), f32),
            vm((2, CELLS, D), f32),
            vm((2, 4, 256, 256), bf16),
            vm((2, CELLS, D), f32),
            vm((2, CELLS, FF), bf16),
            vm((2, CELLS, D), f32),
            vm((2, CELLS, PIN), f32),
            vm((2, CELLS, PIN), bf16),
            vm((3, CELLS, D), bf16),
            vm((3, CELLS, FF), bf16),
            vm((2, CELLS, D), bf16),
            vm((CELLS, D), f32),
            vm((2, CELLS, D), bf16),
            vm((2, CELLS, FF), bf16),
            vm((2, CELLS, D), bf16),
            vm((FF, 256), bf16),
            vm((256, FF), bf16),
            vm((7712, LANES), f32),
            vm((7712, LANES), bf16),
            vm((12, 16, LANES), f32),
            vm((2, PADC, PADC), f32),
            dma((6,)),
            dma((4, 2)),
            dma((3,)),
            dma((2, 2)),
            dma,
        ]
        + filter_scratch(),
        compiler_params=pltpu.CompilerParams(
            collective_id=3, has_side_effects=True, vmem_limit_bytes=60 << 20
        ),
        name="backward_pass",
    )(*args)


def local_fast(frames, targets, regions, master, first_moment, second_moment):
    height, width = 16, 128
    device = lax.axis_index("row") * 4 + lax.axis_index("col")
    core = lax.axis_index("col") % 2
    shard = master.astype(bf16).reshape(OWN, LANES)
    halo = lax.ppermute(shard[:320], ("row", "col"), [(k + 1, k) for k in range(31)])
    chunk = lax.dynamic_slice_in_dim(jnp.concatenate([shard, halo]), 10 * device, CH, 0)
    flat = ag(chunk)
    tables = transform_tables(core)
    row_ids = lax.axis_index("row") * 2 + jnp.arange(2, dtype=jnp.int32)
    col_ids = lax.axis_index("col") * 32 + jnp.arange(32, dtype=jnp.int32)
    cell_masks = region_masks(regions, row_ids, col_ids, width)
    weighted = latitude(row_ids, height)[None, :, None] * cell_masks
    every_row = jnp.arange(height, dtype=jnp.int32)
    every_col = jnp.arange(width, dtype=jnp.int32)
    total_weight = (
        jnp.sum(
            latitude(every_row, height)[None, :, None]
            * region_masks(regions, every_row, every_col, width)
        )
        * STEPS
    )
    flat_mask = cell_masks.reshape(128, 1)
    flat_weight = weighted.reshape(128, 1)
    inputs = (frames.reshape(128, PIN).astype(f32) * flat_mask).astype(bf16)
    goals = jnp.stack([targets[:, s].reshape(128, PIN) for s in range(STEPS)])
    (streams, waves, mixeds, normeds, befores, hiddens, lasts, tails, errors, *rest) = forward_pass(
        inputs, goals, flat_mask, flat_weight, *tables, flat
    )
    mats, (x1, loss, norms, tail, w1, b1, w2) = rest[:6], rest[6:]
    flat_grad = backward_pass(
        flat_weight * (2.0 / total_weight), flat_mask, norms, tail, *tables, w1, b1, w2, *mats,
        streams, waves, mixeds, befores, lasts, errors, inputs, x1, normeds, hiddens, tails,
    )
    loss_tile = jnp.concatenate([loss.reshape(1, LANES), jnp.zeros((7, LANES), f32)])
    summed, stats = rs(flat_grad, loss_tile)
    reduced = lax.dynamic_slice_in_dim(summed, (device * OWN) % 16, OWN, 0).reshape(-1)
    grad_norm = jnp.sqrt(jnp.sum(stats[:8]))
    return finish_step(
        reduced, grad_norm, master, first_moment, second_moment, jnp.sum(stats[8:]), total_weight
    )


def finish_step(reduced, grad_norm, master, first_moment, second_moment, loss_all, total_weight):
    clipped = reduced * (CLIP / jnp.maximum(grad_norm, CLIP))
    first_out = BETA_ONE * first_moment + (1.0 - BETA_ONE) * clipped
    second_out = BETA_TWO * second_moment + (1.0 - BETA_TWO) * clipped * clipped
    corrected_one = first_out / (1.0 - BETA_ONE**ADAM_STEP)
    corrected_two = second_out / (1.0 - BETA_TWO**ADAM_STEP)
    master_out = master - RATE * (
        corrected_one / (jnp.sqrt(corrected_two) + ADAM_EPS) + DECAY * master
    )
    return (
        master_out,
        first_out,
        second_out,
        master_out.astype(bf16),
        loss_all,
        total_weight,
        grad_norm,
    )


def local(frames, targets, regions, master, first_moment, second_moment):
    row_devices = lax.axis_size("row")
    col_devices = lax.axis_size("col")
    local_rows = frames.shape[1]
    local_cols = frames.shape[2]
    height = local_rows * row_devices
    width = local_cols * col_devices
    weights = lax.all_gather(master.astype(jnp.bfloat16), ("row", "col"), axis=0, tiled=True)
    pieces16 = unpack(weights)
    pieces = unpack(weights.astype(jnp.float32))
    tail_params = pieces[2 + 12 * LAYERS :]
    tail16 = pieces16[2 + 12 * LAYERS :]
    tables = (
        dft_tables(width, -1.0),
        dft_tables(height, -1.0),
        dft_tables(width, 1.0),
        dft_tables(height, 1.0),
    )
    row_ids = lax.axis_index("row") * local_rows + jnp.arange(local_rows, dtype=jnp.int32)
    col_ids = lax.axis_index("col") * local_cols + jnp.arange(local_cols, dtype=jnp.int32)
    cell_masks = region_masks(regions, row_ids, col_ids, width)
    weighted = latitude(row_ids, height)[None, :, None] * cell_masks
    every_row = jnp.arange(height, dtype=jnp.int32)
    every_col = jnp.arange(width, dtype=jnp.int32)
    total_weight = (
        jnp.sum(
            latitude(every_row, height)[None, :, None]
            * region_masks(regions, every_row, every_col, width)
        )
        * STEPS
    )
    inputs = frames.astype(jnp.float32) * cell_masks[..., None]
    loss_sum = jnp.zeros((), jnp.float32)
    history = []
    for roll_step in range(STEPS):
        stream = linear_forward(inputs, pieces16[0], pieces[1])
        saved_layers = []
        for layer_idx in range(LAYERS):
            span = slice(2 + 12 * layer_idx, 14 + 12 * layer_idx)
            stream, saved = layer_forward(stream, pieces[span], pieces16[span], tables)
            saved_layers.append(saved)
        normed = rounded(layer_norm(stream, tail_params[0], tail_params[1]))
        predicted = linear_forward(normed, tail16[2], tail_params[3])
        errors = predicted - targets[:, roll_step].astype(jnp.float32)
        loss_sum = loss_sum + jnp.sum(weighted * jnp.sum(errors * errors, axis=-1))
        history.append((inputs, saved_layers, stream, normed, errors))
        inputs = rounded(predicted * cell_masks[..., None])
    loss_all = lax.psum(loss_sum, ("row", "col"))
    gradients = [jnp.zeros_like(piece) for piece in pieces]
    carried = jnp.zeros_like(inputs)
    for roll_step in reversed(range(STEPS)):
        inputs, saved_layers, stream, normed, errors = history[roll_step]
        grad_pred = 2.0 * weighted[..., None] * errors / total_weight + carried
        grad_normed, grad_head, grad_hbias = linear_backward(grad_pred, normed, tail16[2])
        _, pullback = jax.vjp(layer_norm, stream, tail_params[0], tail_params[1])
        grad_stream, grad_gain3, grad_shift3 = pullback(rounded(grad_normed))
        gradients = add_into(
            gradients, 2 + 12 * LAYERS, [grad_gain3, grad_shift3, grad_head, grad_hbias]
        )
        for layer_idx in reversed(range(LAYERS)):
            span = slice(2 + 12 * layer_idx, 14 + 12 * layer_idx)
            grad_stream, layer_grads = layer_backward(
                grad_stream, saved_layers[layer_idx], pieces[span], pieces16[span], tables
            )
            gradients = add_into(gradients, 2 + 12 * layer_idx, layer_grads)
        grad_inputs, grad_embed, grad_ebias = linear_backward(grad_stream, inputs, pieces16[0])
        gradients = add_into(gradients, 0, [grad_embed, grad_ebias])
        carried = cell_masks[..., None] * rounded(grad_inputs)
    flat_grad = jnp.concatenate([piece.ravel() for piece in gradients])
    padding = master.shape[0] * row_devices * col_devices - flat_grad.shape[0]
    flat_grad = jnp.concatenate([flat_grad, jnp.zeros((padding,), jnp.float32)])
    grad_table = flat_grad.reshape(-1, LANES)
    reduced = lax.psum_scatter(grad_table, ("row", "col"), scatter_dimension=0, tiled=True).reshape(
        -1
    )
    squares = jnp.sum(reduced * reduced)
    square_all = lax.psum(squares, ("row", "col"))
    grad_norm = jnp.sqrt(square_all)
    clipped = reduced * (CLIP / jnp.maximum(grad_norm, CLIP))
    first_out = BETA_ONE * first_moment + (1.0 - BETA_ONE) * clipped
    second_out = BETA_TWO * second_moment + (1.0 - BETA_TWO) * clipped * clipped
    corrected_one = first_out / (1.0 - BETA_ONE**ADAM_STEP)
    corrected_two = second_out / (1.0 - BETA_TWO**ADAM_STEP)
    master_out = master - RATE * (
        corrected_one / (jnp.sqrt(corrected_two) + ADAM_EPS) + DECAY * master
    )
    return (
        master_out,
        first_out,
        second_out,
        master_out.astype(jnp.bfloat16),
        loss_all,
        total_weight,
        grad_norm,
    )


def solution(mesh):
    in_specs = (
        P(None, "row", "col", None),
        P(None, None, "row", "col", None),
        P(),
        P(("row", "col")),
        P(("row", "col")),
        P(("row", "col")),
    )
    out_specs = (
        P(("row", "col")),
        P(("row", "col")),
        P(("row", "col")),
        P(("row", "col")),
        P(),
        P(),
        P(),
    )
    body = local_fast if dict(mesh.shape) == {"row": 8, "col": 4} else local
    return jax.shard_map(body, mesh=mesh, in_specs=in_specs, out_specs=out_specs, check_vma=False)
```

```python
import functools
import math

import jax
import jax.numpy as jnp
import numpy as np
from jax import lax
from jax.sharding import PartitionSpec as P
from jax.experimental import pallas as pl
from jax.experimental.pallas import tpu as pltpu

D = 768
FF = 3072
NBLK = 8
BS = 96
PIN = 1280
LAYERS = 2
STEPS = 2
ADAM_STEP = 5


highest = lax.Precision.HIGHEST
NORM_EPS = 1e-05
BETA_ONE = 0.9
BETA_TWO = 0.95
ADAM_EPS = 1e-08
RATE = 0.03
DECAY = 0.05
CLIP = 0.2
LANES = 128


def block_shapes():
    return [
        (D,),
        (D,),
        (2, NBLK, BS, BS),
        (2, NBLK, BS),
        (2, NBLK, BS, BS),
        (2, NBLK, BS),
        (D,),
        (D,),
        (D, FF),
        (FF,),
        (FF, D),
        (D,),
    ]


def all_shapes():
    return [(PIN, D), (D,)] + block_shapes() * LAYERS + [(D,), (D,), (D, PIN), (PIN,)]


def unpack(flat_vec):
    pieces = []
    offset = 0
    for layout in all_shapes():
        length = math.prod(layout)
        pieces.append(flat_vec[offset : offset + length].reshape(layout))
        offset += length
    return pieces


def rounded(value):
    return lax.optimization_barrier(value.astype(jnp.bfloat16)).astype(jnp.float32)


def mult(form, left, right):
    return jnp.einsum(
        form,
        left.astype(jnp.bfloat16),
        right.astype(jnp.bfloat16),
        preferred_element_type=jnp.float32,
    )


def mult_exact(form, grad_value, other):
    upper = grad_value.astype(jnp.bfloat16)
    lower = (grad_value - upper.astype(jnp.float32)).astype(jnp.bfloat16)
    return mult(form, upper, other) + mult(form, lower, other)


def layer_norm(values, gain_vec, shift_vec):
    center = values - jnp.mean(values, axis=-1, keepdims=True)
    spread = jnp.mean(center * center, axis=-1, keepdims=True)
    return center * lax.rsqrt(spread + NORM_EPS) * gain_vec + shift_vec


def dft_tables(length, direction):
    positions = jnp.arange(length, dtype=jnp.int32)
    phases = (positions[:, None] * positions[None, :] % length).astype(jnp.float32) * (
        2.0 * math.pi / length
    )
    factor = 1.0 / math.sqrt(length)
    return (jnp.cos(phases) * factor, direction * jnp.sin(phases) * factor)


def apply_pair(tables, real_part, imag_part, form):

    def contract(table, values):
        return jnp.einsum(form, table, values, precision=highest)

    return (
        contract(tables[0], real_part) - contract(tables[1], imag_part),
        contract(tables[1], real_part) + contract(tables[0], imag_part),
    )


def spectral(real_part, imag_part, weight, bias_vec):
    blocks = (weight.shape[1], weight.shape[2])
    block_re = real_part.reshape(real_part.shape[:-1] + blocks)
    block_im = imag_part.reshape(imag_part.shape[:-1] + blocks)
    form = "...kb,kbc->...kc"
    out_re = (
        jnp.einsum(form, block_re, weight[0], precision=highest)
        - jnp.einsum(form, block_im, weight[1], precision=highest)
        + bias_vec[0]
    )
    out_im = (
        jnp.einsum(form, block_im, weight[0], precision=highest)
        + jnp.einsum(form, block_re, weight[1], precision=highest)
        + bias_vec[1]
    )
    return (out_re.reshape(real_part.shape), out_im.reshape(imag_part.shape))


def first_spectral(real_part, imag_part, weight, bias_vec):
    out_re, out_im = spectral(real_part, imag_part, weight, bias_vec)
    return (jax.nn.gelu(out_re, approximate=False), jax.nn.gelu(out_im, approximate=False))


def region_masks(regions, row_ids, col_ids, width):
    row_start = regions[:, 0, None, None]
    row_span = regions[:, 1, None, None]
    col_start = regions[:, 2, None, None]
    col_span = regions[:, 3, None, None]
    row_inside = (row_ids[None, :, None] >= row_start) & (
        row_ids[None, :, None] < row_start + row_span
    )
    col_inside = (col_ids[None, None, :] - col_start) % width < col_span
    return (row_inside & col_inside).astype(jnp.float32)


def latitude(row_ids, height):
    return jnp.cos(-1.3 + 1.3 * (row_ids.astype(jnp.float32) + 0.5) / height)


def linear_forward(values, weight16, bias_vec):
    return mult("brci,io->brco", values, weight16) + bias_vec


def linear_backward(grad_value, values, weight16):
    grad_values = mult_exact("brco,io->brci", grad_value, weight16)
    grad_weight = mult_exact("brco,brci->io", grad_value, values)
    return (grad_values, grad_weight, jnp.sum(grad_value, axis=(0, 1, 2)))


def spectrum(field, forward_w, forward_h):
    values = lax.all_to_all(field, "col", split_axis=3, concat_axis=2, tiled=True).astype(
        jnp.float32
    )
    real_part = jnp.einsum("kw,bnwc->bnkc", forward_w[0], values, precision=highest)
    imag_part = jnp.einsum("kw,bnwc->bnkc", forward_w[1], values, precision=highest)
    real_part, imag_part = apply_pair(
        forward_h,
        lax.all_to_all(
            real_part.astype(jnp.bfloat16), "row", split_axis=2, concat_axis=1, tiled=True
        ).astype(jnp.float32),
        lax.all_to_all(
            imag_part.astype(jnp.bfloat16), "row", split_axis=2, concat_axis=1, tiled=True
        ).astype(jnp.float32),
        "kh,bhwc->bkwc",
    )
    return (real_part.astype(jnp.bfloat16), imag_part.astype(jnp.bfloat16))


def grid(real_part, imag_part, inverse_w, inverse_h):
    back_re, back_im = apply_pair(
        inverse_h, real_part.astype(jnp.float32), imag_part.astype(jnp.float32), "kh,bhwc->bkwc"
    )
    values_re = lax.all_to_all(
        back_re.astype(jnp.bfloat16), "row", split_axis=1, concat_axis=2, tiled=True
    ).astype(jnp.float32)
    values_im = lax.all_to_all(
        back_im.astype(jnp.bfloat16), "row", split_axis=1, concat_axis=2, tiled=True
    ).astype(jnp.float32)
    result = jnp.einsum("kw,bnwc->bnkc", inverse_w[0], values_re, precision=highest) - jnp.einsum(
        "kw,bnwc->bnkc", inverse_w[1], values_im, precision=highest
    )
    columns_back = result.astype(jnp.bfloat16)
    return lax.all_to_all(columns_back, "col", split_axis=2, concat_axis=3, tiled=True)


def local_blocks(params):
    block_count = D // lax.axis_size("col") // BS
    first_block = lax.axis_index("col") * block_count
    chosen = [
        lax.dynamic_slice_in_dim(params[index_pos], first_block, block_count, 1)
        for index_pos in (2, 3, 4, 5)
    ]
    return (chosen, first_block)


def layer_forward(stream, params, params16, tables):
    gain_one, shift_one, _, _, _, _, gain_two, shift_two, _, bias_in, _, bias_out = params
    (local_w1, local_b1, local_w2, local_b2), _ = local_blocks(params)
    normed = layer_norm(stream, gain_one, shift_one).astype(jnp.bfloat16)
    wave_re, wave_im = spectrum(normed, tables[0], tables[1])
    hid_re, hid_im = first_spectral(
        wave_re.astype(jnp.float32), wave_im.astype(jnp.float32), local_w1, local_b1
    )
    hid_re, hid_im = (rounded(hid_re), rounded(hid_im))
    spec_re, spec_im = spectral(hid_re, hid_im, local_w2, local_b2)
    filtered = grid(
        spec_re.astype(jnp.bfloat16), spec_im.astype(jnp.bfloat16), tables[2], tables[3]
    )
    mixed = stream + filtered.astype(jnp.float32)
    normed_two = rounded(layer_norm(mixed, gain_two, shift_two))
    hidden = rounded(
        jax.nn.gelu(linear_forward(normed_two, params16[8], bias_in), approximate=False)
    )
    output = mixed + linear_forward(hidden, params16[10], bias_out)
    return (output, (stream, wave_re, wave_im, hid_re, hid_im, mixed, normed_two, hidden))


def place_blocks(local_grad, full_like, first_block):
    return lax.dynamic_update_slice_in_dim(jnp.zeros_like(full_like), local_grad, first_block, 1)


def layer_backward(grad_out, saved, params, params16, tables):
    stream, wave_re, wave_im, hid_re, hid_im, mixed, normed_two, hidden = saved
    (
        gain_one,
        shift_one,
        spec_w1,
        spec_b1,
        spec_w2,
        spec_b2,
        gain_two,
        shift_two,
        weight_in,
        bias_in,
        weight_out,
        bias_out,
    ) = params
    (local_w1, local_b1, local_w2, local_b2), first_block = local_blocks(params)
    grad_hidden, grad_wout, grad_bout = linear_backward(grad_out, hidden, params16[10])
    grad_mixed = grad_out
    before = linear_forward(normed_two, params16[8], bias_in)
    _, pullback = jax.vjp(lambda value: jax.nn.gelu(value, approximate=False), before)
    (grad_before,) = pullback(rounded(grad_hidden))
    grad_normed, grad_win, grad_bin = linear_backward(grad_before, normed_two, params16[8])
    _, pullback = jax.vjp(layer_norm, mixed, gain_two, shift_two)
    grad_extra, grad_gain2, grad_shift2 = pullback(rounded(grad_normed))
    grad_mixed = grad_mixed + grad_extra
    back_re, back_im = spectrum(grad_mixed.astype(jnp.bfloat16), tables[0], tables[1])
    _, pullback = jax.vjp(spectral, hid_re, hid_im, local_w2, local_b2)
    grad_hre, grad_him, grad_lw2, grad_lb2 = pullback(
        (back_re.astype(jnp.float32), back_im.astype(jnp.float32))
    )
    _, pullback = jax.vjp(
        first_spectral, wave_re.astype(jnp.float32), wave_im.astype(jnp.float32), local_w1, local_b1
    )
    grad_wre, grad_wim, grad_lw1, grad_lb1 = pullback((rounded(grad_hre), rounded(grad_him)))
    grad_first = grid(
        grad_wre.astype(jnp.bfloat16), grad_wim.astype(jnp.bfloat16), tables[2], tables[3]
    )
    _, pullback = jax.vjp(layer_norm, stream, gain_one, shift_one)
    grad_stream, grad_gain1, grad_shift1 = pullback(grad_first.astype(jnp.float32))
    layer_grads = [
        grad_gain1,
        grad_shift1,
        place_blocks(grad_lw1, spec_w1, first_block),
        place_blocks(grad_lb1, spec_b1, first_block),
        place_blocks(grad_lw2, spec_w2, first_block),
        place_blocks(grad_lb2, spec_b2, first_block),
        grad_gain2,
        grad_shift2,
        grad_win,
        grad_bin,
        grad_wout,
        grad_bout,
    ]
    return (grad_stream + grad_mixed, layer_grads)


def add_into(gradients, start, values):
    middle = [left + right for left, right in zip(gradients[start : start + len(values)], values)]
    return gradients[:start] + middle + gradients[start + len(values) :]


MESH = pl.DeviceIdType.MESH
CH = 2944
OWN = 2934
CHR = 2960
GROWS = 93904


CHIPS = 16
UNIT = 64
PADC = 128
f32 = jnp.float32
bf16 = jnp.bfloat16


def remote(src, dst, send_sem, recv_sem, device):
    return pltpu.make_async_remote_copy(
        src_ref=src,
        dst_ref=dst,
        send_sem=send_sem,
        recv_sem=recv_sem,
        device_id=device,
        device_id_type=MESH,
    )


def chip_device(chip, core):
    return chip // 2, (chip % 2) * 2 + core


def place():
    row = lax.axis_index("row")
    col = lax.axis_index("col")
    core = col % 2
    return row, row * 2 + col // 2, core, (row, col + 1 - 2 * core)


def greet_chips(me, core, sibling):
    barrier = pltpu.get_barrier_semaphore()

    def one(k, carry):
        pl.semaphore_signal(
            barrier,
            inc=1,
            device_id=chip_device(me ^ (CHIPS - k), core),
            device_id_type=MESH,
        )
        return carry

    lax.fori_loop(1, CHIPS, one, 0)
    pl.semaphore_signal(barrier, inc=1, device_id=sibling, device_id_type=MESH)
    return barrier


def split_units(values, units):
    blank = jnp.zeros((UNIT, PADC - BS), f32)
    for part in range(2):
        for block in range(NBLK):
            piece = values[part * UNIT : (part + 1) * UNIT, block * BS : (block + 1) * BS]
            units[part * NBLK + block] = jnp.concatenate([piece, blank], axis=1).astype(bf16)


def join_units(units, joined):
    for part in range(2):
        for block in range(NBLK):
            joined[part * UNIT : (part + 1) * UNIT, block * BS : (block + 1) * BS] = units[
                part * NBLK + block, :, 0:BS
            ].astype(f32)


def normalize(values):
    center = values - jnp.mean(values, axis=-1, keepdims=True)
    spread = jnp.mean(center * center, axis=-1, keepdims=True)
    scale = lax.rsqrt(spread + NORM_EPS)
    return center * scale, scale


def gelu_of(value):
    return 0.5 * value * (1.0 + lax.erf(value * math.sqrt(0.5)))


def gelu_slope(value):
    bell = jnp.exp(-0.5 * value * value) * (1.0 / math.sqrt(2.0 * math.pi))
    return 0.5 * (1.0 + lax.erf(value * math.sqrt(0.5))) + value * bell


def dot(left, right):
    return jnp.dot(left, right, preferred_element_type=f32)


def dot_rows(left, right):
    return lax.dot_general(left, right, (((0,), (0,)), ((), ())), preferred_element_type=f32)


def dot_cols(left, right):
    return lax.dot_general(left, right, (((1,), (1,)), ((), ())), preferred_element_type=f32)


def spread_units(me, core, sibling, units, mine, others, sems, meanwhile):
    send_a, recv_a, send_f, recv_f, local_sem = sems

    def out(k):
        chip = me ^ k
        return remote(
            units.at[chip], mine.at[me], send_a.at[k], recv_a.at[k], chip_device(chip, core)
        )

    def handed(k):
        chip = me ^ k
        return remote(mine.at[chip], others.at[chip], send_f.at[k], recv_f.at[k], sibling)

    own = pltpu.make_async_copy(units.at[me], mine.at[me], local_sem)
    own.start()

    def begin(k, carry):
        out(CHIPS - k).start()
        return carry

    lax.fori_loop(1, CHIPS, begin, 0)
    meanwhile()
    own.wait()
    handed(0).start()

    def hand(k, carry):
        out(CHIPS - k).wait_recv()
        handed(CHIPS - k).start()
        return carry

    lax.fori_loop(1, CHIPS, hand, 0)

    def arrive(k, carry):
        handed(k).wait_recv()
        return carry

    lax.fori_loop(0, CHIPS, arrive, 0)

    def finish():
        def sent(k, carry):
            out(k).wait_send()
            return carry

        lax.fori_loop(1, CHIPS, sent, 0)

        def sent_on(k, carry):
            handed(k).wait_send()
            return carry

        lax.fori_loop(0, CHIPS, sent_on, 0)

    return finish


def to_spectrum(mine, others, column_table, row_table, waves):
    for h in range(16):
        pair, part = h // 2, pl.ds(32 * (h % 2), 32)
        cells = jnp.concatenate(
            [
                mine[2 * pair, part],
                mine[2 * pair + 1, part],
                others[2 * pair, part],
                others[2 * pair + 1, part],
            ],
            axis=0,
        )
        wave = dot(column_table[...], cells).astype(bf16)
        for g in range(4):
            rows = pl.ds(16 * h, 16)
            waves[g, rows, 0:PADC] = wave[16 * g : 16 * g + 16]
            waves[g, rows, PADC : 2 * PADC] = wave[64 + 16 * g : 80 + 16 * g]
    results = []
    for g in range(4):
        both = dot(row_table[...], waves[g])
        real = both[:256, :PADC] + both[256:, PADC:]
        imag = both[:256, PADC:] - both[256:, :PADC]
        results.append(jnp.concatenate([real, imag], axis=1).astype(bf16))
    return results


def from_spectrum(g, spec, row_table, back):
    both = dot(row_table[...], spec)
    real = (both[:256, :PADC] - both[256:, PADC:]).astype(bf16)
    imag = (both[:256, PADC:] + both[256:, :PADC]).astype(bf16)
    for h in range(16):
        back[h, 16 * g : 16 * g + 16] = real[16 * h : 16 * h + 16]
        back[h, 64 + 16 * g : 80 + 16 * g] = imag[16 * h : 16 * h + 16]


def gather_units(row, me, core, sibling, back, inverse_table, bufs, sems, settle, meanwhile):
    own_sum, to_sib, from_sib, ready, landed = bufs
    send_s, recv_s, send_b, recv_b, local_sem = sems

    def swap(pair):
        rows = pl.ds(2 * pair, 2)
        return remote(
            to_sib.at[rows], from_sib.at[rows], send_s.at[pair], recv_s.at[pair], sibling
        )

    def partial(j, carry):
        pair = row ^ (7 - j)
        for half in range(2):
            sums = dot(inverse_table[...], back[2 * pair + half])
            part = pl.ds(32 * half, 32)
            for x in range(2):
                own_sum[2 * pair + x, part] = sums[32 * x : 32 * x + 32]
                to_sib[2 * pair + x, part] = sums[64 + 32 * x : 96 + 32 * x].astype(bf16)
        swap(pair).start()
        return carry

    lax.fori_loop(0, 8, partial, 0)
    settle()

    def home(chip, k):
        return remote(
            ready.at[chip], landed.at[me], send_b.at[k], recv_b.at[k], chip_device(chip, core)
        )

    own = pltpu.make_async_copy(ready.at[me], landed.at[me], local_sem)

    def total(j, carry):
        pair = row ^ (7 - j)
        swap(pair).wait_recv()
        rows = pl.ds(2 * pair, 2)
        ready[rows] = (own_sum[rows] + from_sib[rows].astype(f32)).astype(bf16)
        for x in range(2):
            chip = 2 * pair + x
            k = chip ^ me

            @pl.when(k != 0)
            def _():
                home(chip, k).start()

        return carry

    lax.fori_loop(0, 8, total, 0)
    own.start()
    meanwhile()

    def landed_all(k, carry):
        home(me ^ k, k).wait_recv()
        return carry

    lax.fori_loop(1, CHIPS, landed_all, 0)
    own.wait()

    def finish():
        def sent(k, carry):
            home(me ^ k, k).wait_send()
            return carry

        lax.fori_loop(1, CHIPS, sent, 0)

        def swapped(pair, carry):
            swap(pair).wait_send()
            return carry

        lax.fori_loop(0, 8, swapped, 0)

    return finish


def filter_scratch():
    vm = pltpu.VMEM
    dma = pltpu.SemaphoreType.DMA
    block = (CHIPS, UNIT, PADC)
    return [
        vm(block, bf16),
        vm(block, bf16),
        vm(block, bf16),
        vm((4, 256, 256), bf16),
        vm((16, 128, PADC), bf16),
        vm(block, f32),
        vm(block, bf16),
        vm(block, bf16),
        vm(block, bf16),
        vm(block, bf16),
        vm((2 * UNIT, D), f32),
        dma((CHIPS,)),
        dma((CHIPS,)),
        dma((CHIPS,)),
        dma((CHIPS,)),
        dma,
        dma((8,)),
        dma((8,)),
        dma((CHIPS,)),
        dma((CHIPS,)),
        dma,
    ]


def transform_tables(core):
    width, height = 128, 16
    order = []
    for side in range(2):
        cols = [[32 * (2 * x + (c if side == 0 else 1 - c)) + i for x in range(2) for i in range(32)] for c in range(2)]
        order.append(cols)
    column, inverse = [], []
    for c in range(2):
        cells = np.array(order[0][c] + order[1][c])
        waves = 64 * c + np.arange(64)
        angle = 2.0 * np.pi * (np.outer(waves, cells) % width) / width
        cos, sin = np.cos(angle) / np.sqrt(width), np.sin(angle) / np.sqrt(width)
        column.append(np.concatenate([cos, -sin], axis=0))
        inverse.append(np.concatenate([cos, -sin], axis=0).T)
    steps = np.arange(height)
    angle = 2.0 * np.pi * (np.outer(steps, steps) % height) / height
    eye = np.eye(16)
    rows = np.concatenate(
        [np.kron(np.cos(angle), eye), np.kron(np.sin(angle), eye)], axis=0
    ) / np.sqrt(height)
    pick = lambda both: lax.dynamic_index_in_dim(jnp.asarray(np.stack(both), bf16), core, 0, False)
    return pick(column), pick(inverse), jnp.asarray(rows, bf16)


RING = 8
GATHER_CUTS = (0, 640, 1280, 2112, 2944)
SUM_CUTS = (0, 640, 1280, 2128, 2960)


def ring_place(row):
    return jnp.where(row % 2 == 0, row // 2, 7 - row // 2)


def ring_row(spot):
    return jnp.where(spot < 4, 2 * spot, 2 * (7 - spot) + 1)


def gather_kernel(shard, flat, ring_s, ring_r, x_s, x_r, sib_s, sib_r, own_sem):
    row, me, core, sibling = place()
    x = me % 2
    spot = ring_place(row)
    beside = (row, (1 - x) * 2 + core)
    ahead = (ring_row((spot + 1) % RING), x * 2 + core)
    behind = (ring_row((spot + RING - 1) % RING), x * 2 + core)
    ways = (ahead, behind)
    barrier = pltpu.get_barrier_semaphore()
    for device in (ahead, behind, beside, sibling):
        pl.semaphore_signal(barrier, inc=1, device_id=device, device_id_type=MESH)

    def span(part):
        return GATHER_CUTS[part], GATHER_CUTS[part + 1] - GATHER_CUTS[part]

    def piece(source_spot, source_x, part):
        low, size = span(part)
        base = (ring_row(source_spot) * 4 + source_x * 2 + core) * CH
        return flat.at[pl.ds(pl.multiple_of(base + low, 16), size)]

    def mine(part):
        low, size = span(part)
        return shard.at[pl.ds(low, size)]

    def origin(hop, way):
        return (spot - hop + RING) % RING if way == 0 else (spot + hop) % RING

    def item(hop, way, what):
        part = way if what else 2 + way
        return origin(hop, way), (1 - x if what == 2 else x), part

    def ring(hop, way, what, first=False):
        to = piece(*item(hop, way, what))
        source = mine(item(hop, way, what)[2]) if first and what < 2 else to
        return remote(
            source, to, ring_s.at[what, way, hop], ring_r.at[what, way, hop], ways[way]
        )

    def cross(slot, way, first=False):
        if isinstance(slot, int) and slot == 8:
            to, source = piece(spot, x, way), mine(way)
        else:
            to = piece(origin(slot, way), x, 2 + way)
            source = mine(2 + way) if first else to
        return remote(source, to, x_s.at[way, slot], x_r.at[way, slot], beside)

    def share(where, slot, way, what):
        return remote(where, where, sib_s.at[what, way, slot], sib_r.at[what, way, slot], sibling)

    def from_beside(slot, way):
        if isinstance(slot, int) and slot == 8:
            return piece(spot, 1 - x, way)
        return piece(origin(slot, way), 1 - x, 2 + way)

    base = pl.multiple_of((row * 4 + x * 2 + core) * CH, 16)
    whole = flat.at[pl.ds(base, CH)]
    own = pltpu.make_async_copy(shard, whole, own_sem)
    own.start()
    pl.semaphore_wait(barrier, 4)
    for way in range(2):
        ring(0, way, 0, True).start()
        cross(8, way).start()
    for way in range(2):
        ring(0, way, 1, True).start()
        cross(0, way, True).start()
    given = remote(shard, whole, sib_s.at[3, 0, 9], sib_r.at[3, 0, 9], sibling)
    given.start()
    for way in range(2):
        cross(8, way).wait_recv()
        ring(0, way, 2).start()
        share(from_beside(8, way), 8, way, 3).start()

    def step(hop, carry):
        for what in range(3):
            for way in range(2):
                ring(hop - 1, way, what).wait_recv()

                @pl.when(hop < RING - 1)
                def _():
                    ring(hop, way, what).start()

                if what == 0:
                    cross(hop, way).start()
                share(piece(*item(hop, way, what)), hop - 1, way, what).start()
        for way in range(2):
            cross(hop - 1, way).wait_recv()
            share(from_beside(hop - 1, way), hop - 1, way, 3).start()
        return carry

    lax.fori_loop(1, RING, step, 0)
    for way in range(2):
        cross(RING - 1, way).wait_recv()
        share(from_beside(RING - 1, way), RING - 1, way, 3).start()
    own.wait()

    def settle(hop, carry):
        for way in range(2):
            for what in range(3):
                ring(hop, way, what).wait_send()
                share(piece(*item(hop + 1, way, what)), hop, way, what).wait()
        return carry

    lax.fori_loop(0, RING - 1, settle, 0)

    def settle_cross(slot, carry):
        for way in range(2):
            cross(slot, way).wait_send()
            share(from_beside(slot, way), slot, way, 3).wait()
        return carry

    lax.fori_loop(0, RING, settle_cross, 0)
    for way in range(2):
        cross(8, way).wait_send()
        share(from_beside(8, way), 8, way, 3).wait()
    given.wait()


def ag(shard):
    anywhere = pl.BlockSpec(memory_space=pl.ANY)
    dma = pltpu.SemaphoreType.DMA
    return pl.pallas_call(
        gather_kernel,
        out_shape=jax.ShapeDtypeStruct((32 * CH, 128), bf16),
        in_specs=[anywhere],
        out_specs=anywhere,
        scratch_shapes=[
            dma((3, 2, 7)),
            dma((3, 2, 7)),
            dma((2, 9)),
            dma((2, 9)),
            dma((4, 2, 10)),
            dma((4, 2, 10)),
            dma,
        ],
        compiler_params=pltpu.CompilerParams(collective_id=0, has_side_effects=True),
        name="gather_weights",
    )(shard)


def sum_kernel(
    grad, loss, total, stats,
    own, sib, xin, rin_b, rin_a, xlast, st_mine, st_sib, st_sum, st_all,
    own_s, sib_s, sib_r, x_s, x_r, last_s, last_r, ring_s, ring_r, tell_s, tell_r, pair_s, pair_r,
):
    row, me, core, sibling = place()
    x = me % 2
    spot = ring_place(row)
    beside = (row, (1 - x) * 2 + core)
    ahead = (ring_row((spot + 1) % RING), x * 2 + core)
    behind = (ring_row((spot + RING - 1) % RING), x * 2 + core)
    ways = (ahead, behind)
    barrier = greet_chips(me, core, sibling)
    sizes = [SUM_CUTS[k + 1] - SUM_CUTS[k] for k in range(4)]

    def owner(turn, way):
        return (spot - 1 - turn + 2 * RING) % RING if way == 0 else (spot + 1 + turn) % RING

    def source(turn, way, other_x, part, side):
        owner_x = (1 - x) if other_x else x
        base = (ring_row(owner(turn, way)) * 4 + owner_x * 2 + side) * OWN // 16 * 16
        return grad.at[pl.ds(pl.multiple_of(base + SUM_CUTS[part], 16), sizes[part])]

    def part_of(way, what):
        return way if what >= 2 else 2 + way

    def held(buf, turn, way, what):
        part = part_of(way, what)
        return buf.at[what % 2, turn, pl.ds(SUM_CUTS[part], sizes[part])]

    def load(turn, way, what):
        return pltpu.make_async_copy(
            source(turn, way, what % 2, part_of(way, what), core),
            held(own, turn, way, what),
            own_s.at[what, way, turn],
        )

    def give(turn, way, what):
        return remote(
            source(turn, way, what % 2, part_of(way, what), 1 - core),
            held(sib, turn, way, what),
            sib_s.at[what, way, turn],
            sib_r.at[what, way, turn],
            sibling,
        )

    def cross(turn, way):
        return remote(
            held(own, turn, way, 1),
            xin.at[turn, pl.ds(SUM_CUTS[2 + way] - SUM_CUTS[2], sizes[2 + way])],
            x_s.at[way, turn],
            x_r.at[way, turn],
            beside,
        )

    def got(way, slot, what):
        if what == 0:
            return rin_b.at[slot, pl.ds(SUM_CUTS[2 + way] - SUM_CUTS[2], sizes[2 + way])]
        return rin_a.at[what - 2, slot, pl.ds(SUM_CUTS[way], sizes[way])]

    def ring(turn, way, what, first=False):
        where = held(own, turn, way, what) if first else got(way, turn - 1, what)
        return remote(
            where,
            got(way, turn, what),
            ring_s.at[what, way, turn],
            ring_r.at[what, way, turn],
            ways[way],
        )

    order = (1, 3, 2, 0)

    def begin_own(turn, carry):
        for what in order:
            for way in range(2):
                load(turn, way, what).start()
        return carry

    def begin_sib(turn, carry):
        for what in order:
            for way in range(2):
                give(turn, way, what).start()
        return carry

    begin_own(0, 0)
    pl.semaphore_wait(barrier, CHIPS)
    begin_sib(0, 0)
    lax.fori_loop(1, RING, lambda t, c: begin_sib(t, begin_own(t, c)), 0)

    def both(turn, way, what):
        load(turn, way, what).wait()
        give(turn, way, what).wait_recv()
        return held(own, turn, way, what)[...].astype(f32) + held(sib, turn, way, what)[...].astype(f32)

    def send_across(turn):
        for way in range(2):
            held(own, turn, way, 1)[...] = both(turn, way, 1).astype(bf16)
            cross(turn, way).start()

    def across(turn, way):
        cross(turn, way).wait_recv()
        return xin[turn, pl.ds(SUM_CUTS[2 + way] - SUM_CUTS[2], sizes[2 + way])].astype(f32)

    send_across(0)
    for what in (3, 2):
        for way in range(2):
            held(own, 0, way, what)[...] = both(0, way, what).astype(bf16)
            ring(0, way, what, True).start()
    send_across(1)
    for way in range(2):
        held(own, 0, way, 0)[...] = (both(0, way, 0) + across(0, way)).astype(bf16)
        ring(0, way, 0, True).start()

    def step(turn, carry):
        send_across(turn + 1)
        for what in (3, 2, 0):
            for way in range(2):
                part = both(turn, way, what)
                if what == 0:
                    part = part + across(turn, way)
                ring(turn - 1, way, what, True).wait_recv()
                where = got(way, turn - 1, what)
                where[...] = (where[...].astype(f32) + part).astype(bf16)
                ring(turn, way, what).start()
        return carry

    lax.fori_loop(1, RING - 1, step, 0)
    last = RING - 1
    def to_beside(way):
        return remote(
            got(way, last - 1, 3),
            xlast.at[pl.ds(SUM_CUTS[way], sizes[way])],
            last_s.at[way],
            last_r.at[way],
            beside,
        )

    for way in range(2):
        part = both(last, way, 3)
        ring(last - 1, way, 3, True).wait_recv()
        where = got(way, last - 1, 3)
        where[...] = (where[...].astype(f32) + part).astype(bf16)
        to_beside(way).start()
    for what in (2, 0):
        for way in range(2):
            part = both(last, way, what)
            if what == 0:
                part = part + across(last, way)
            ring(last - 1, way, what, True).wait_recv()
            low = SUM_CUTS[part_of(way, what)]
            total[low : low + sizes[part_of(way, what)]] = got(way, last - 1, what)[...].astype(f32) + part
    for way in range(2):
        to_beside(way).wait_recv()
        low = SUM_CUTS[way]
        total[low : low + sizes[way]] += xlast[low : low + sizes[way]].astype(f32)

    first = ((row * 4 + x * 2 + core) * OWN) % 16
    rows = lax.broadcasted_iota(jnp.int32, (CHR, 128), 0)
    value = total[...]
    squares = jnp.where((rows >= first) & (rows < first + OWN), value * value, 0.0)
    st_mine[0:8] = jnp.sum(squares.reshape(CHR // 8, 8, 128), axis=0)
    st_mine[8:16] = loss[...]
    pair = remote(st_mine, st_sib, pair_s, pair_r, sibling)
    pair.start()
    pair.wait_recv()
    st_sum[...] = st_mine[...] + st_sib[...]
    st_all[me] = st_sum[...]

    def tell(k):
        return remote(
            st_sum, st_all.at[me], tell_s.at[k], tell_r.at[k],
            chip_device(lax.rem(me + k, CHIPS), core),
        )

    def tell_one(k, carry):
        tell(k).start()
        return carry

    lax.fori_loop(1, CHIPS, tell_one, 0)

    def settle(turn, carry):
        for way in range(2):
            for what in range(4):
                give(turn, way, what).wait_send()
            cross(turn, way).wait_send()

            @pl.when(turn < RING - 1)
            def _():
                for what in (0, 2, 3):
                    ring(turn, way, what, True).wait_send()

        return carry

    lax.fori_loop(0, RING, settle, 0)
    for way in range(2):
        to_beside(way).wait_send()

    def told(k, carry):
        tell(k).wait_recv()
        return carry

    lax.fori_loop(1, CHIPS, told, 0)
    everything = st_all[0]
    for k in range(1, CHIPS):
        everything = everything + st_all[k]
    stats[...] = everything

    def tell_done(k, carry):
        tell(k).wait_send()
        return carry

    lax.fori_loop(1, CHIPS, tell_done, 0)
    pair.wait_send()


def rs(grad, loss):
    vm, dma = pltpu.VMEM, pltpu.SemaphoreType.DMA
    first, second = SUM_CUTS[2], SUM_CUTS[4] - SUM_CUTS[2]
    shape = jax.ShapeDtypeStruct
    return pl.pallas_call(
        sum_kernel,
        out_shape=[shape((CHR, 128), f32), shape((16, 128), f32)],
        in_specs=[pl.BlockSpec(memory_space=pl.ANY), pl.BlockSpec(memory_space=vm)],
        out_specs=[pl.BlockSpec(memory_space=vm)] * 2,
        scratch_shapes=[
            vm((2, RING, CHR, 128), bf16),
            vm((2, RING, CHR, 128), bf16),
            vm((RING, second, 128), bf16),
            vm((RING - 1, second, 128), bf16),
            vm((2, RING - 1, first, 128), bf16),
            vm((first, 128), bf16),
            vm((16, 128), f32),
            vm((16, 128), f32),
            vm((16, 128), f32),
            vm((CHIPS, 16, 128), f32),
            dma((4, 2, RING)),
            dma((4, 2, RING)),
            dma((4, 2, RING)),
            dma((2, RING)),
            dma((2, RING)),
            dma((2,)),
            dma((2,)),
            dma((4, 2, RING - 1)),
            dma((4, 2, RING - 1)),
            dma((CHIPS,)),
            dma((CHIPS,)),
            dma,
            dma,
        ],
        compiler_params=pltpu.CompilerParams(
            collective_id=1, has_side_effects=True, vmem_limit_bytes=56 << 20
        ),
        name="sum_gradients",
    )(grad, loss)


MATS = [(PIN, D), (D, FF), (FF, D), (D, FF), (FF, D), (D, PIN)]
SMALL_LAYER = 2352
SMALLS = [6 + SMALL_LAYER, 24, 6 + SMALL_LAYER, 24, 18, 10]
PIECE = 256


def flat_sections():
    at = 0
    found = []
    for (depth, cols), small in zip(MATS, SMALLS):
        per_row = cols // LANES
        found.append((at, depth, per_row, at + depth * per_row, small))
        at += depth * per_row + small
    return found


def piece_rows(depth, per_row):
    rows = depth
    while rows * per_row > 7680:
        rows -= PIECE
        while depth % rows:
            rows -= PIECE
    return rows


def put_rows(wide, at, value):
    for k in range(value.shape[1] // LANES):
        wide[at + k : at + k + 1] = value[:, k * LANES : (k + 1) * LANES]


def put_block_weight(wide, at, block, grad, square):
    wide[at : at + 2 * NBLK * BLOCK_ROWS] = jnp.zeros((2 * NBLK * BLOCK_ROWS, LANES), f32)
    square[0] = grad[:PADC, :PADC] + grad[PADC:, PADC:]
    square[1] = grad[:PADC, PADC:] - grad[PADC:, :PADC]
    for part in range(2):
        a, b, c, d = (square[part, pl.ds(q, 24, stride=4), :] for q in range(4))
        rows = (
            jnp.concatenate([a[:, :96], b[:, :32]], axis=1),
            jnp.concatenate([b[:, 32:96], c[:, :64]], axis=1),
            jnp.concatenate([c[:, 64:96], d[:, :96]], axis=1),
        )
        for q, value in enumerate(rows):
            wide[pl.ds(at + (part * NBLK + block) * BLOCK_ROWS + q, 24, stride=3), :] = value


def put_block_bias(wide, at, block, grad):
    found = []
    for part in range(2):
        piece = grad[:, part * PADC : part * PADC + BS]
        found += [jnp.where(block == k, piece, 0.0) for k in range(NBLK)]
    put_rows(wide, at, jnp.concatenate(found, axis=1))


def write_section(i, xs, gs, bufs):
    across, side, wide, narrow, edge, flat, sem = bufs
    start, depth, per_row, _, _ = flat_sections()[i]
    cols = per_row * LANES
    for half in range(2):
        for part in range(0, depth, PIECE):
            across[part : part + PIECE, half * 128 : half * 128 + 128] = xs[half][
                :, part : part + PIECE
            ].T
        side[half * 128 : half * 128 + 128, 0:cols] = gs[half][...]
    rows = piece_rows(depth, per_row)
    full = rows * per_row
    shift = start % 16
    skip = 16 if shift else 0
    turns = depth // rows

    def emit(at, low):
        return pltpu.make_async_copy(
            narrow.at[pl.ds(low, full - low)], flat.at[pl.ds(at + low, full - low)], sem
        )

    def step(it, carry):
        top = pl.multiple_of(it * rows, PIECE)
        for part in range(0, rows, PIECE):
            left = across[pl.ds(pl.multiple_of(top + part, PIECE), PIECE), :]
            for j in range(0, per_row, 2):
                value = dot(left, side[:, j * LANES : (j + 2) * LANES])
                for by in range(2):
                    wide[pl.ds(shift + part * per_row + j + by, PIECE, stride=per_row), :] = value[
                        :, by * LANES : (by + 1) * LANES
                    ]

        @pl.when(it == 1)
        def _():
            emit(0, skip).wait()

        @pl.when(it > 1)
        def _():
            emit(0, 0).wait()

        narrow[0:full] = wide[0:full].astype(bf16)

        @pl.when(it == 0)
        def _():
            edge[2 * i] = wide[0:16]
            emit(start - shift, skip).start()

        @pl.when(it > 0)
        def _():
            emit(pl.multiple_of(start - shift + it * full, 16), 0).start()

        wide[0:16] = wide[full : full + 16]
        return carry

    lax.fori_loop(0, turns, step, 0)
    edge[2 * i + 1] = wide[0:16]
    emit(0, skip if turns == 1 else 0).wait()


def write_small(i, put, bufs):
    _, _, wide, narrow, edge, flat, sem = bufs
    _, _, _, at, count = flat_sections()[i]
    shift = at % 16
    wide[0:16] = edge[2 * i + 1]
    put(i, shift)
    end = shift + count
    total = GROWS - at + shift if i == 5 else -(-end // 16) * 16
    if i == 5:
        wide[end:total] = jnp.zeros((total - end, LANES), f32)
    elif total > end:
        wide[end:total] = edge[2 * i + 2, 16 - (total - end) : 16]
    narrow[0:total] = wide[0:total].astype(bf16)
    done = pltpu.make_async_copy(
        narrow.at[pl.ds(0, total)], flat.at[pl.ds(at - shift, total)], sem
    )
    done.start()
    done.wait()


CELLS = 2 * UNIT
FCHUNK = 1024
FILTER_SEMS = 10


def norm_adjoint(values, gain, grad):
    normed, scale = normalize(values)
    inner = grad * gain
    along = jnp.mean(inner * normed, axis=-1, keepdims=True)
    flat = jnp.mean(inner, axis=-1, keepdims=True)
    return (
        scale * (inner - flat - normed * along),
        jnp.sum(grad * normed, axis=0, keepdims=True),
        jnp.sum(grad, axis=0, keepdims=True),
    )


SMALL_AT = []
for _count in SMALLS:
    SMALL_AT.append(SMALL_AT[-1] + -(-SMALLS[len(SMALL_AT) - 1] // 8) * 8 if SMALL_AT else 0)
SMALL_ROWS = SMALL_AT[-1] + 16
AT_NORM = (0, 6, 2340, 2346)
AT_W1, AT_B1, AT_W2, AT_B2 = 12, 1164, 1176, 2328
BLOCK_ROWS = BS * BS // LANES


def aligned_part(at, count):
    low = at // 16 * 16
    return low, -(-(at + count - low) // 16) * 16


def unpack_sections(flat, raw, wide, in_sem, wanted):
    steps = []
    for i, target in wanted:
        start, depth, per_row, _, _ = flat_sections()[i]
        rows = piece_rows(depth, per_row)
        for top in range(0, depth, rows):
            steps.append((start + top * per_row, per_row, top, rows, target))

    def fetch(n):
        at, per_row, _, rows, _ = steps[n]
        low, size = aligned_part(at, rows * per_row)
        return pltpu.make_async_copy(
            flat.at[pl.ds(low, size)], raw.at[n % 2, pl.ds(0, size)], in_sem.at[n % 2]
        ), size

    fetch(0)[0].start()
    for n, (at, per_row, top, rows, target) in enumerate(steps):
        if n + 1 < len(steps):
            fetch(n + 1)[0].start()
        copy, size = fetch(n)
        copy.wait()
        wide[0:size] = raw[n % 2, 0:size].astype(f32)
        for part in range(0, rows, PIECE):
            for j in range(per_row):
                target[top + part : top + part + PIECE, j * LANES : (j + 1) * LANES] = wide[
                    pl.ds(at % 16 + part * per_row + j, PIECE, stride=per_row), :
                ].astype(bf16)


def unpack_small(flat, raw, wide, in_sem, small):
    def fetch(n):
        _, _, _, at, count = flat_sections()[n]
        low, size = aligned_part(at, count)
        return pltpu.make_async_copy(
            flat.at[pl.ds(low, size)], raw.at[n % 2, pl.ds(0, size)], in_sem.at[n % 2]
        ), size, at - low, count

    fetch(0)[0].start()
    for n in range(6):
        if n < 5:
            fetch(n + 1)[0].start()
        copy, size, shift, count = fetch(n)
        copy.wait()
        wide[0:size] = raw[n % 2, 0:size].astype(f32)
        small[SMALL_AT[n] : SMALL_AT[n] + count] = wide[shift : shift + count]


def long_row(small, at, count):
    return jnp.concatenate([small[at + k : at + k + 1] for k in range(count)], axis=1)


def block_weight(small, at, block, square, out):
    blank = jnp.zeros((24, PADC - BS), f32)
    square[...] = jnp.zeros_like(square)
    for part in range(2):
        base = at + (part * NBLK + block) * BLOCK_ROWS
        a, b, c = (small[pl.ds(base + q, 24, stride=3), :] for q in range(3))
        pieces = (
            a[:, :96],
            jnp.concatenate([a[:, 96:], b[:, :64]], axis=1),
            jnp.concatenate([b[:, 64:], c[:, :32]], axis=1),
            c[:, 32:],
        )
        for q, piece in enumerate(pieces):
            piece = jnp.concatenate([piece, blank], axis=1)
            if part == 0:
                square[0, pl.ds(q, 24, stride=4), :] = piece
                square[3, pl.ds(q, 24, stride=4), :] = piece
            else:
                square[1, pl.ds(q, 24, stride=4), :] = piece
                square[2, pl.ds(q, 24, stride=4), :] = -piece
    for quarter in range(4):
        top, left = quarter // 2 * PADC, quarter % 2 * PADC
        out[top : top + PADC, left : left + PADC] = square[quarter].astype(bf16)


def block_bias(small, at, block):
    blank = jnp.zeros((1, PADC - BS), f32)
    both = long_row(small, at, 12)
    found = []
    for part in range(2):
        value = jnp.zeros((1, BS), f32)
        for k in range(NBLK):
            low = (part * NBLK + k) * BS
            value = value + jnp.where(block == k, both[:, low : low + BS], 0.0)
        found += [value, blank]
    return jnp.concatenate(found, axis=1)


def forward_kernel(*refs):
    x0, goals, mask, weight, column, inverse, rows, flat = refs[:8]
    (streams, waves_o, mixeds, normeds, befores, hiddens, lasts, tails, errors,
     embed_h, in0, out0, in1, out1, head_h, x1, loss, norms, tail, w1, b1, w2) = refs[8:30]
    (embed, w_in, w_out, head, flow, x_now, s_stream, s_waves, s_mixed, s_norm, s_before, s_hidden,
     s_tail, s_error, raw, wide, small, square, b2, c1, c2, embed_b, head_b,
     weight_sem, out_sem, tail_sem, in_sem) = refs[30:57]
    units, mine, others, waves, back, own_sum, to_sib, from_sib, ready, landed, joined = refs[57:68]
    sems = refs[68:]
    row, me, core, sibling = place()
    barrier = greet_chips(me, core, sibling)
    stores = [
        pltpu.make_async_copy(source, target, weight_sem.at[k])
        for k, (source, target) in enumerate(
            [(embed, embed_h), (w_in.at[0], in0), (w_out.at[0], out0), (w_in.at[1], in1),
             (w_out.at[1], out1), (head, head_h)]
        )
    ]
    block = me % NBLK
    unpack_small(flat, raw, wide, in_sem, small)
    embed_b[...] = long_row(small, SMALL_AT[0], 6)
    head_b[...] = long_row(small, SMALL_AT[5], 10)
    for layer in range(LAYERS):
        base = SMALL_AT[2 * layer] + 6
        for k, at in enumerate(AT_NORM):
            norms[layer, k : k + 1] = long_row(small, base + at, 6)
        c1[layer] = long_row(small, SMALL_AT[2 * layer + 1], 24)
        c2[layer] = long_row(small, SMALL_AT[2 * layer + 2], 6)
        block_weight(small, base + AT_W1, block, square, w1.at[layer])
        block_weight(small, base + AT_W2, block, square, w2.at[layer])
        b1[layer] = block_bias(small, base + AT_B1, block)
        b2[layer] = block_bias(small, base + AT_B2, block)
    tail[0:1] = long_row(small, SMALL_AT[4] + 6, 6)
    tail[1:2] = long_row(small, SMALL_AT[4] + 12, 6)
    unpack_sections(flat, raw, wide, in_sem, [(0, embed)])
    stores[0].start()
    x_now[...] = x0[...]
    loss[...] = jnp.zeros_like(loss)

    def saves(it):
        pairs = [(s_stream, streams), (s_waves, waves_o), (s_mixed, mixeds), (s_norm, normeds),
                 (s_before, befores), (s_hidden, hiddens)]
        return [
            pltpu.make_async_copy(source, target.at[it], out_sem.at[k])
            for k, (source, target) in enumerate(pairs)
        ]

    def tail_saves(step):
        pairs = [(flow, lasts), (s_tail, tails), (s_error, errors)]
        return [
            pltpu.make_async_copy(source, target.at[step], tail_sem.at[k])
            for k, (source, target) in enumerate(pairs)
        ]

    def when_it(cond, action):
        @pl.when(cond)
        def _():
            action()

    def unpack_when(it, number, wanted, done):
        def go():
            unpack_sections(flat, raw, wide, in_sem, wanted)
            for k in done:
                stores[k].start()

        when_it(it == number, go)

    def meanwhile_in(it):
        unpack_when(it, 0, [(1, w_in.at[0])], [1])
        unpack_when(it, 1, [(3, w_in.at[1])], [3])

    def meanwhile_out(it):
        unpack_when(it, 0, [(2, w_out.at[0])], [2])
        unpack_when(it, 1, [(4, w_out.at[1]), (5, head)], [4, 5])

    def body(it, carry):
        step, layer = it // 2, it % 2

        def start_step():
            flow[...] = dot(x_now[...], embed[...]) + embed_b[...]

        def tail_done():
            for save in tail_saves(0):
                save.wait()

        when_it(it == 2, tail_done)
        when_it(layer == 0, start_step)

        def saved():
            for save in saves(it):
                save.wait()

        when_it(it > 0, saved)
        s_stream[...] = flow[...]
        normed, _ = normalize(flow[...])
        split_units(normed * norms[layer, 0:1] + norms[layer, 1:2], units)
        when_it(it == 0, lambda: pl.semaphore_wait(barrier, CHIPS))

        finish_one = spread_units(
            me, core, sibling, units, mine, others, sems[:5], lambda: meanwhile_in(it)
        )
        groups = to_spectrum(mine, others, column, rows, waves)
        for g in range(4):
            s_waves[g] = groups[g]
            hidden = gelu_of(dot(groups[g], w1[layer]) + b1[layer]).astype(bf16)
            spec = (dot(hidden, w2[layer]) + b2[layer]).astype(bf16)
            from_spectrum(g, spec, rows, back)
        finish_two = gather_units(
            row, me, core, sibling, back, inverse,
            (own_sum, to_sib, from_sib, ready, landed), sems[5:], finish_one,
            lambda: meanwhile_out(it),
        )
        join_units(landed, joined)
        mixed = flow[...] + joined[...]
        s_mixed[...] = mixed
        normed, _ = normalize(mixed)
        s_norm[...] = (normed * norms[layer, 2:3] + norms[layer, 3:4]).astype(bf16)
        flow[...] = mixed + c2[layer]

        def chunk(c, carry):
            part = pl.ds(c * FCHUNK, FCHUNK)
            before = dot(s_norm[...], w_in[layer, :, part]) + c1[layer, :, part]
            s_before[:, part] = before.astype(bf16)
            hidden = gelu_of(before).astype(bf16)
            s_hidden[:, part] = hidden
            flow[...] += dot(hidden, w_out[layer, part, :])
            return carry

        for c in range(FF // FCHUNK):
            chunk(c, 0)
        for save in saves(it):
            save.start()
        finish_two()
        def end_step():
            normed, _ = normalize(flow[...])
            s_tail[...] = (normed * tail[0:1] + tail[1:2]).astype(bf16)
            predicted = dot(s_tail[...], head[...]) + head_b[...]
            error = predicted - goals[step].astype(f32)
            s_error[...] = error
            loss[...] += weight[...] * jnp.sum(error * error, axis=-1, keepdims=True)
            x_now[...] = (predicted * mask[...]).astype(bf16)
            for save in tail_saves(step):
                save.start()

        when_it(layer == 1, end_step)
        when_it(it == 1, lambda: x1.__setitem__(Ellipsis, x_now[...]))
        return carry

    lax.fori_loop(0, 4, body, 0)
    for save in saves(3):
        save.wait()
    for save in tail_saves(1):
        save.wait()
    for store in stores:
        store.wait()


def forward_pass(*args):
    vm, dma = pltpu.VMEM, pltpu.SemaphoreType.DMA
    whole, anywhere = pl.BlockSpec(memory_space=vm), pl.BlockSpec(memory_space=pl.ANY)
    shape = jax.ShapeDtypeStruct
    return pl.pallas_call(
        forward_kernel,
        out_shape=[
            shape((4, CELLS, D), f32),
            shape((4, 4, 256, 256), bf16),
            shape((4, CELLS, D), f32),
            shape((4, CELLS, D), bf16),
            shape((4, CELLS, FF), bf16),
            shape((4, CELLS, FF), bf16),
            shape((2, CELLS, D), f32),
            shape((2, CELLS, D), bf16),
            shape((2, CELLS, PIN), f32),
            *[shape(dims, bf16) for dims in MATS],
            shape((CELLS, PIN), bf16),
            shape((CELLS, 1), f32),
            shape((2, 4, D), f32),
            shape((2, D), f32),
            shape((2, 256, 256), bf16),
            shape((2, 1, 256), f32),
            shape((2, 256, 256), bf16),
        ],
        in_specs=[whole] * 7 + [anywhere],
        out_specs=[anywhere] * 15 + [whole] * 7,
        scratch_shapes=[
            vm((PIN, D), bf16),
            vm((2, D, FF), bf16),
            vm((2, FF, D), bf16),
            vm((D, PIN), bf16),
            vm((CELLS, D), f32),
            vm((CELLS, PIN), bf16),
            vm((CELLS, D), f32),
            vm((4, 256, 256), bf16),
            vm((CELLS, D), f32),
            vm((CELLS, D), bf16),
            vm((CELLS, FF), bf16),
            vm((CELLS, FF), bf16),
            vm((CELLS, D), bf16),
            vm((CELLS, PIN), f32),
            vm((2, 7696, LANES), bf16),
            vm((7696, LANES), f32),
            vm((SMALL_ROWS, LANES), f32),
            vm((4, PADC, PADC), f32),
            vm((2, 1, 256), f32),
            vm((2, 1, FF), f32),
            vm((2, 1, D), f32),
            vm((1, D), f32),
            vm((1, PIN), f32),
            dma((6,)),
            dma((6,)),
            dma((3,)),
            dma((2,)),
        ]
        + filter_scratch(),
        compiler_params=pltpu.CompilerParams(
            collective_id=2, has_side_effects=True, vmem_limit_bytes=56 << 20
        ),
        name="forward_pass",
    )(*args)


def backward_kernel(*refs):
    (gscale, mask, norms, tail, column, inverse, rows, w1, b1, w2,
     embed_h, in0, out0, in1, out1, head_h,
     streams, waves_h, mixeds, befores, lasts, errors, inputs, x1, normeds, hiddens, tails) = refs[:27]
    flat = refs[27]
    (sum_norm, sum_c1, sum_tail, sum_head, grad_w1, grad_w2, grad_b,
     embed, w_in, w_out, head, flow, carried, i_stream, i_waves, i_mixed, i_before, i_last, i_error,
     s_pred, s_out, s_pre, s_embed, g_norm, x_in, x_out, x_tail,
     across, side, wide, narrow, edge, square,
     weight_sem, in_sem, tail_in, section_sem, flat_sem) = refs[28:66]
    units, mine, others, waves, back, own_sum, to_sib, from_sib, ready, landed, joined = refs[66:77]
    sems = refs[77:]
    bufs = (across, side, wide, narrow, edge, flat, flat_sem)
    row, me, core, sibling = place()
    barrier = greet_chips(me, core, sibling)

    def when_it(cond, action):
        @pl.when(cond)
        def _():
            action()

    loads = [
        pltpu.make_async_copy(source, target, weight_sem.at[k])
        for k, (source, target) in enumerate(
            [(head_h, head), (out1, w_out.at[1]), (in1, w_in.at[1]), (out0, w_out.at[0]),
             (in0, w_in.at[0]), (embed_h, embed)]
        )
    ]

    def inst(it):
        return 3 - it

    def fetch(it):
        slot = it % 2
        pairs = [(streams, i_stream), (waves_h, i_waves), (mixeds, i_mixed), (befores, i_before)]
        return [
            pltpu.make_async_copy(source.at[inst(it)], target.at[slot], in_sem.at[k, slot])
            for k, (source, target) in enumerate(pairs)
        ]

    tail_loads = [
        pltpu.make_async_copy(lasts, i_last, tail_in.at[0]),
        pltpu.make_async_copy(errors, i_error, tail_in.at[1]),
    ]
    late_load = pltpu.make_async_copy(tails, x_tail, tail_in.at[2])
    for load in tail_loads:
        load.start()
    loads[0].start()
    for load in fetch(0):
        load.start()
    for load in loads[1:]:
        load.start()
    for target in (sum_norm, sum_c1, sum_tail, sum_head, grad_w1, grad_w2, grad_b, carried):
        target[...] = jnp.zeros_like(target)

    late_load.start()

    def section_loads(layer):
        return [
            pltpu.make_async_copy(source.at[2 * step + layer], target.at[step], section_sem.at[n, step])
            for n, (source, target) in enumerate([(normeds, x_in), (hiddens, x_out)])
            for step in range(2)
        ]

    def write_when(it, number, work):
        when_it(it == number, lambda: [write_section(i, xs, gs, bufs) for i, xs, gs in work] and None)

    def pairs_out(layer):
        return (2 + 2 * layer, (x_out.at[0], x_out.at[1]), (s_out.at[2], s_out.at[layer]))

    def pairs_in(layer):
        return (1 + 2 * layer, (x_in.at[0], x_in.at[1]), (s_pre.at[2], s_pre.at[layer]))

    def meanwhile_in(it):
        write_when(it, 2, [(5, (x_tail.at[0], x_tail.at[1]), (s_pred.at[0], s_pred.at[1])), pairs_out(1)])
        write_when(it, 3, [pairs_out(0)])

    def meanwhile_out(it):
        write_when(it, 2, [pairs_in(1)])
        write_when(it, 3, [pairs_in(0)])

    def body(it, carry):
        step, layer, slot = 1 - it // 2, 1 - it % 2, it % 2
        keep = jnp.where(step == 1, layer, 2)

        def fetch_section(wanted):
            for load in section_loads(wanted):
                load.start()

        when_it(it == 2, lambda: fetch_section(1))
        when_it(it == 3, lambda: fetch_section(0))

        def first():
            for load in tail_loads:
                load.wait()
            loads[0].wait()

        when_it(it == 0, first)

        def head_adjoint():
            grad = i_error[step] * gscale[...] + carried[...]
            grad16 = grad.astype(bf16)
            s_pred[step] = grad16
            sum_head[0:1] += jnp.sum(grad, axis=0, keepdims=True)
            back_n = dot_cols(grad16, head[...]).astype(bf16).astype(f32)
            value, gain, shift = norm_adjoint(i_last[step], tail[0:1], back_n)
            flow[...] = value
            sum_tail[0:1] += gain
            sum_tail[1:2] += shift

        when_it(layer == 1, head_adjoint)

        def prefetch():
            for load in fetch(it + 1):
                load.start()

        when_it(it < 3, prefetch)

        s_out[keep] = flow[...].astype(bf16)
        sum_norm[layer, 4:5] += jnp.sum(flow[...], axis=0, keepdims=True)
        for load in fetch(it):
            load.wait()

        def second_layer():
            loads[1].wait()
            loads[2].wait()

        def first_layer():
            loads[3].wait()
            loads[4].wait()

        when_it(it == 0, second_layer)
        when_it(it == 1, first_layer)
        g_norm[...] = jnp.zeros_like(g_norm)

        def chunk(c, carry):
            part = pl.ds(c * FCHUNK, FCHUNK)
            grad = dot_cols(s_out[keep], w_out[layer, part, :]).astype(bf16).astype(f32)
            grad = grad * gelu_slope(i_before[slot, :, part].astype(f32))
            sum_c1[layer, 0:1, part] += jnp.sum(grad, axis=0, keepdims=True)
            grad16 = grad.astype(bf16)
            s_pre[keep, :, part] = grad16
            g_norm[...] += dot_cols(grad16, w_in[layer, :, part])
            return carry

        for c in range(FF // FCHUNK):
            chunk(c, 0)

        def section_ready():
            for load in section_loads(0):
                load.wait()

        when_it(it >= 2, section_ready)
        when_it(it == 2, late_load.wait)
        value, gain, shift = norm_adjoint(
            i_mixed[slot], norms[layer, 2:3], g_norm[...].astype(bf16).astype(f32)
        )
        flow[...] += value
        sum_norm[layer, 2:3] += gain
        sum_norm[layer, 3:4] += shift
        split_units(flow[...], units)
        when_it(it == 0, lambda: pl.semaphore_wait(barrier, CHIPS))
        finish_one = spread_units(
            me, core, sibling, units, mine, others, sems[:5], lambda: meanwhile_in(it)
        )
        groups = to_spectrum(mine, others, column, rows, waves)
        for g in range(4):
            before = dot(i_waves[slot, g], w1[layer]) + b1[layer]
            hidden = gelu_of(before).astype(bf16)
            grad_hidden = dot_cols(groups[g], w2[layer]).astype(bf16).astype(f32)
            grad_before = grad_hidden * gelu_slope(before)
            grad_before16 = grad_before.astype(bf16)
            grad_w2[layer] += dot_rows(hidden, groups[g])
            grad_w1[layer] += dot_rows(i_waves[slot, g], grad_before16)
            grad_b[layer, 0:1] += jnp.sum(grad_before, axis=0, keepdims=True)
            grad_b[layer, 1:2] += jnp.sum(groups[g].astype(f32), axis=0, keepdims=True)
            from_spectrum(g, dot_cols(grad_before16, w1[layer]).astype(bf16), rows, back)
        finish_two = gather_units(
            row, me, core, sibling, back, inverse,
            (own_sum, to_sib, from_sib, ready, landed), sems[5:], finish_one,
            lambda: meanwhile_out(it),
        )
        join_units(landed, joined)
        value, gain, shift = norm_adjoint(i_stream[slot], norms[layer, 0:1], joined[...])
        flow[...] += value
        sum_norm[layer, 0:1] += gain
        sum_norm[layer, 1:2] += shift
        when_it(it == 1, loads[5].wait)

        def embed_adjoint():
            s_embed[step] = flow[...].astype(bf16)
            sum_tail[2:3] += jnp.sum(flow[...], axis=0, keepdims=True)

        when_it(layer == 0, embed_adjoint)

        def carry_back():
            carried[...] = mask[...] * dot_cols(s_embed[1], embed[...]).astype(bf16).astype(f32)

        when_it(it == 1, carry_back)
        finish_two()
        return carry

    lax.fori_loop(0, 4, body, 0)
    block = me % NBLK

    def put_layer(at, idx):
        put_rows(wide, at, sum_norm[idx, 0:1])
        put_rows(wide, at + 6, sum_norm[idx, 1:2])
        put_block_weight(wide, at + AT_W1, block, grad_w1[idx], square)
        put_block_bias(wide, at + AT_B1, block, grad_b[idx, 0:1])
        put_block_weight(wide, at + AT_W2, block, grad_w2[idx], square)
        put_block_bias(wide, at + AT_B2, block, grad_b[idx, 1:2])
        put_rows(wide, at + AT_NORM[2], sum_norm[idx, 2:3])
        put_rows(wide, at + AT_NORM[3], sum_norm[idx, 3:4])

    def put_small(i, at):
        if i == 0:
            put_rows(wide, at, sum_tail[2:3])
            put_layer(at + 6, 0)
        elif i == 2:
            put_rows(wide, at, sum_norm[0, 4:5])
            put_layer(at + 6, 1)
        elif i == 4:
            put_rows(wide, at, sum_norm[1, 4:5])
            put_rows(wide, at + 6, sum_tail[0:1])
            put_rows(wide, at + 12, sum_tail[1:2])
        elif i == 5:
            put_rows(wide, at, sum_head[0:1])
        else:
            put_rows(wide, at, sum_c1[i // 2, 0:1])

    write_section(0, (inputs, x1), (s_embed.at[0], s_embed.at[1]), bufs)
    for i in range(6):
        write_small(i, put_small, bufs)


def backward_pass(*args):
    vm, dma = pltpu.VMEM, pltpu.SemaphoreType.DMA
    whole, anywhere = pl.BlockSpec(memory_space=vm), pl.BlockSpec(memory_space=pl.ANY)
    shape = jax.ShapeDtypeStruct
    return pl.pallas_call(
        backward_kernel,
        out_shape=shape((GROWS, LANES), bf16),
        in_specs=[whole] * 10 + [anywhere] * 12 + [whole] * 2 + [anywhere] * 3,
        out_specs=anywhere,
        scratch_shapes=[
            vm((2, 8, D), f32),
            vm((2, 8, FF), f32),
            vm((8, D), f32),
            vm((8, PIN), f32),
            vm((2, 256, 256), f32),
            vm((2, 256, 256), f32),
            vm((2, 8, 256), f32),
            vm((PIN, D), bf16),
            vm((2, D, FF), bf16),
            vm((2, FF, D), bf16),
            vm((D, PIN), bf16),
            vm((CELLS, D), f32),
            vm((CELLS, PIN), f32),
            vm((2, CELLS, D), f32),
            vm((2, 4, 256, 256), bf16),
            vm((2, CELLS, D), f32),
            vm((2, CELLS, FF), bf16),
            vm((2, CELLS, D), f32),
            vm((2, CELLS, PIN), f32),
            vm((2, CELLS, PIN), bf16),
            vm((3, CELLS, D), bf16),
            vm((3, CELLS, FF), bf16),
            vm((2, CELLS, D), bf16),
            vm((CELLS, D), f32),
            vm((2, CELLS, D), bf16),
            vm((2, CELLS, FF), bf16),
            vm((2, CELLS, D), bf16),
            vm((FF, 256), bf16),
            vm((256, FF), bf16),
            vm((7712, LANES), f32),
            vm((7712, LANES), bf16),
            vm((12, 16, LANES), f32),
            vm((2, PADC, PADC), f32),
            dma((6,)),
            dma((4, 2)),
            dma((3,)),
            dma((2, 2)),
            dma,
        ]
        + filter_scratch(),
        compiler_params=pltpu.CompilerParams(
            collective_id=3, has_side_effects=True, vmem_limit_bytes=60 << 20
        ),
        name="backward_pass",
    )(*args)


def local_fast(frames, targets, regions, master, first_moment, second_moment):
    height, width = 16, 128
    device = lax.axis_index("row") * 4 + lax.axis_index("col")
    core = lax.axis_index("col") % 2
    shard = master.astype(bf16).reshape(OWN, LANES)
    halo = lax.ppermute(shard[:320], ("row", "col"), [(k + 1, k) for k in range(31)])
    chunk = lax.dynamic_slice_in_dim(jnp.concatenate([shard, halo]), 10 * device, CH, 0)
    flat = ag(chunk)
    tables = transform_tables(core)
    row_ids = lax.axis_index("row") * 2 + jnp.arange(2, dtype=jnp.int32)
    col_ids = lax.axis_index("col") * 32 + jnp.arange(32, dtype=jnp.int32)
    cell_masks = region_masks(regions, row_ids, col_ids, width)
    weighted = latitude(row_ids, height)[None, :, None] * cell_masks
    every_row = jnp.arange(height, dtype=jnp.int32)
    every_col = jnp.arange(width, dtype=jnp.int32)
    total_weight = (
        jnp.sum(
            latitude(every_row, height)[None, :, None]
            * region_masks(regions, every_row, every_col, width)
        )
        * STEPS
    )
    flat_mask = cell_masks.reshape(128, 1)
    flat_weight = weighted.reshape(128, 1)
    inputs = (frames.reshape(128, PIN).astype(f32) * flat_mask).astype(bf16)
    goals = jnp.stack([targets[:, s].reshape(128, PIN) for s in range(STEPS)])
    (streams, waves, mixeds, normeds, befores, hiddens, lasts, tails, errors, *rest) = forward_pass(
        inputs, goals, flat_mask, flat_weight, *tables, flat
    )
    mats, (x1, loss, norms, tail, w1, b1, w2) = rest[:6], rest[6:]
    flat_grad = backward_pass(
        flat_weight * (2.0 / total_weight), flat_mask, norms, tail, *tables, w1, b1, w2, *mats,
        streams, waves, mixeds, befores, lasts, errors, inputs, x1, normeds, hiddens, tails,
    )
    loss_tile = jnp.concatenate([loss.reshape(1, LANES), jnp.zeros((7, LANES), f32)])
    summed, stats = rs(flat_grad, loss_tile)
    reduced = lax.dynamic_slice_in_dim(summed, (device * OWN) % 16, OWN, 0).reshape(-1)
    grad_norm = jnp.sqrt(jnp.sum(stats[:8]))
    return finish_step(
        reduced, grad_norm, master, first_moment, second_moment, jnp.sum(stats[8:]), total_weight
    )


def finish_step(reduced, grad_norm, master, first_moment, second_moment, loss_all, total_weight):
    clipped = reduced * (CLIP / jnp.maximum(grad_norm, CLIP))
    first_out = BETA_ONE * first_moment + (1.0 - BETA_ONE) * clipped
    second_out = BETA_TWO * second_moment + (1.0 - BETA_TWO) * clipped * clipped
    corrected_one = first_out / (1.0 - BETA_ONE**ADAM_STEP)
    corrected_two = second_out / (1.0 - BETA_TWO**ADAM_STEP)
    master_out = master - RATE * (
        corrected_one / (jnp.sqrt(corrected_two) + ADAM_EPS) + DECAY * master
    )
    return (
        master_out,
        first_out,
        second_out,
        master_out.astype(bf16),
        loss_all,
        total_weight,
        grad_norm,
    )


def local(frames, targets, regions, master, first_moment, second_moment):
    row_devices = lax.axis_size("row")
    col_devices = lax.axis_size("col")
    local_rows = frames.shape[1]
    local_cols = frames.shape[2]
    height = local_rows * row_devices
    width = local_cols * col_devices
    weights = lax.all_gather(master.astype(jnp.bfloat16), ("row", "col"), axis=0, tiled=True)
    pieces16 = unpack(weights)
    pieces = unpack(weights.astype(jnp.float32))
    tail_params = pieces[2 + 12 * LAYERS :]
    tail16 = pieces16[2 + 12 * LAYERS :]
    tables = (
        dft_tables(width, -1.0),
        dft_tables(height, -1.0),
        dft_tables(width, 1.0),
        dft_tables(height, 1.0),
    )
    row_ids = lax.axis_index("row") * local_rows + jnp.arange(local_rows, dtype=jnp.int32)
    col_ids = lax.axis_index("col") * local_cols + jnp.arange(local_cols, dtype=jnp.int32)
    cell_masks = region_masks(regions, row_ids, col_ids, width)
    weighted = latitude(row_ids, height)[None, :, None] * cell_masks
    every_row = jnp.arange(height, dtype=jnp.int32)
    every_col = jnp.arange(width, dtype=jnp.int32)
    total_weight = (
        jnp.sum(
            latitude(every_row, height)[None, :, None]
            * region_masks(regions, every_row, every_col, width)
        )
        * STEPS
    )
    inputs = frames.astype(jnp.float32) * cell_masks[..., None]
    loss_sum = jnp.zeros((), jnp.float32)
    history = []
    for roll_step in range(STEPS):
        stream = linear_forward(inputs, pieces16[0], pieces[1])
        saved_layers = []
        for layer_idx in range(LAYERS):
            span = slice(2 + 12 * layer_idx, 14 + 12 * layer_idx)
            stream, saved = layer_forward(stream, pieces[span], pieces16[span], tables)
            saved_layers.append(saved)
        normed = rounded(layer_norm(stream, tail_params[0], tail_params[1]))
        predicted = linear_forward(normed, tail16[2], tail_params[3])
        errors = predicted - targets[:, roll_step].astype(jnp.float32)
        loss_sum = loss_sum + jnp.sum(weighted * jnp.sum(errors * errors, axis=-1))
        history.append((inputs, saved_layers, stream, normed, errors))
        inputs = rounded(predicted * cell_masks[..., None])
    loss_all = lax.psum(loss_sum, ("row", "col"))
    gradients = [jnp.zeros_like(piece) for piece in pieces]
    carried = jnp.zeros_like(inputs)
    for roll_step in reversed(range(STEPS)):
        inputs, saved_layers, stream, normed, errors = history[roll_step]
        grad_pred = 2.0 * weighted[..., None] * errors / total_weight + carried
        grad_normed, grad_head, grad_hbias = linear_backward(grad_pred, normed, tail16[2])
        _, pullback = jax.vjp(layer_norm, stream, tail_params[0], tail_params[1])
        grad_stream, grad_gain3, grad_shift3 = pullback(rounded(grad_normed))
        gradients = add_into(
            gradients, 2 + 12 * LAYERS, [grad_gain3, grad_shift3, grad_head, grad_hbias]
        )
        for layer_idx in reversed(range(LAYERS)):
            span = slice(2 + 12 * layer_idx, 14 + 12 * layer_idx)
            grad_stream, layer_grads = layer_backward(
                grad_stream, saved_layers[layer_idx], pieces[span], pieces16[span], tables
            )
            gradients = add_into(gradients, 2 + 12 * layer_idx, layer_grads)
        grad_inputs, grad_embed, grad_ebias = linear_backward(grad_stream, inputs, pieces16[0])
        gradients = add_into(gradients, 0, [grad_embed, grad_ebias])
        carried = cell_masks[..., None] * rounded(grad_inputs)
    flat_grad = jnp.concatenate([piece.ravel() for piece in gradients])
    padding = master.shape[0] * row_devices * col_devices - flat_grad.shape[0]
    flat_grad = jnp.concatenate([flat_grad, jnp.zeros((padding,), jnp.float32)])
    grad_table = flat_grad.reshape(-1, LANES)
    reduced = lax.psum_scatter(grad_table, ("row", "col"), scatter_dimension=0, tiled=True).reshape(
        -1
    )
    squares = jnp.sum(reduced * reduced)
    square_all = lax.psum(squares, ("row", "col"))
    grad_norm = jnp.sqrt(square_all)
    clipped = reduced * (CLIP / jnp.maximum(grad_norm, CLIP))
    first_out = BETA_ONE * first_moment + (1.0 - BETA_ONE) * clipped
    second_out = BETA_TWO * second_moment + (1.0 - BETA_TWO) * clipped * clipped
    corrected_one = first_out / (1.0 - BETA_ONE**ADAM_STEP)
    corrected_two = second_out / (1.0 - BETA_TWO**ADAM_STEP)
    master_out = master - RATE * (
        corrected_one / (jnp.sqrt(corrected_two) + ADAM_EPS) + DECAY * master
    )
    return (
        master_out,
        first_out,
        second_out,
        master_out.astype(jnp.bfloat16),
        loss_all,
        total_weight,
        grad_norm,
    )


def solution(mesh):
    in_specs = (
        P(None, "row", "col", None),
        P(None, None, "row", "col", None),
        P(),
        P(("row", "col")),
        P(("row", "col")),
        P(("row", "col")),
    )
    out_specs = (
        P(("row", "col")),
        P(("row", "col")),
        P(("row", "col")),
        P(("row", "col")),
        P(),
        P(),
        P(),
    )
    body = local_fast if dict(mesh.shape) == {"row": 8, "col": 4} else local
    return jax.shard_map(body, mesh=mesh, in_specs=in_specs, out_specs=out_specs, check_vma=False)
```
